32 devices in a mesh: space: 8 (over y, x, core), lane: 4 (over z).
Axes of the slice: x: 2, y: 2, z: 4, core: 2. Of those that a mesh axis runs over, the one named last changes fastest.
Arguments:
- positions: float32 [256, 3, 544], P('space'), may hold values from -6 to 6
- bend_op: float32 [544, 544], replicated, may hold values from -0.25 to 0.25
- send_list: int32 [8, 8], P('space'), may hold values from 0 to 31
- task_target: int32 [32, 12], P(('space', 'lane')), may hold values from 0 to 31, as said below
- task_source: int32 [32, 12], P(('space', 'lane')), may hold values from 0 to 39, as said below
- task_count: int32 [32], P(('space', 'lane')), may hold values from 4 to 12, as said below
Outputs:
- moved_positions: float32 [256, 3, 544], P(('space', 'lane'))
- velocity: float32 [256, 3, 544], P(('space', 'lane'))
The draws below stay inside these ranges and needn't reach their ends.
Inputs may be any that keep to these rules, and one draw needn't show every extreme that they name: `task_target`: slots at or beyond the list's task_count hold 0. `task_source`: slots at or beyond the list's task_count hold 0. Every received cell of an owner is the source of at least one live slot of that owner. `task_count`: in each owner exactly one lane has 12 live slots; every other lane has at most 7.
All inputs are finite; a program needn't handle non-finite values.
Results may differ from the reference program's by a relative error of at most 0.00015.
Values sent between devices are 32-bit elements; how exact they have to be, the bound alone decides.
No kernel may reach another device: no remote copies, remote signals or barrier semaphores. Data moves between devices by JAX's collectives and lax.ppermute only.
A program may use at most 64 MiB of HBM per device.

```python
import jax
import jax.numpy as jnp
from jax import lax

P_SIZE = 544
CD = 32
G = 1
TASK_CAP = 12
ITERS = 2
OWNERS = 8
CELLS = 256
GHOSTS = 8
LANE_ROWS = 32


def task_tables(key):
    base = jax.random.fold_in(key, 4242)
    key_count, key_busy, key_order, key_fill, key_target = jax.random.split(base, 5)
    lane_count = LANE_ROWS // OWNERS
    counts = jax.random.randint(key_count, (OWNERS, lane_count), 4, 8)
    busiest = jax.random.randint(key_busy, (OWNERS, 1), 0, lane_count)
    counts = jnp.where(jnp.arange(lane_count)[None, :] == busiest, TASK_CAP, counts).astype(jnp.int32)
    starts = jnp.cumsum(counts, axis=1) - counts
    slots = jnp.arange(TASK_CAP)[None, None, :]
    ranks = starts[:, :, None] + slots
    live_slots = slots < counts[:, :, None]
    scores = jax.random.randint(key_order, (OWNERS, GHOSTS), 0, 1 << 20) * GHOSTS + jnp.arange(GHOSTS)[None, :]
    ghost_order = jnp.argsort(scores, axis=1)
    picked = jnp.take_along_axis(ghost_order, jnp.minimum(ranks, GHOSTS - 1).reshape(OWNERS, -1), axis=1)
    picked = picked.reshape(ranks.shape)
    filler = jax.random.randint(key_fill, ranks.shape, 0, CD + GHOSTS)
    sources = jnp.where(ranks < GHOSTS, CD + picked, filler)
    sources = jnp.where(live_slots, sources, 0)
    targets = jax.random.randint(key_target, ranks.shape, 0, CD)
    targets = jnp.where(live_slots, targets, 0)
    return (targets.reshape(LANE_ROWS, TASK_CAP).astype(jnp.int32), sources.reshape(LANE_ROWS, TASK_CAP).astype(jnp.int32), counts.reshape(LANE_ROWS).astype(jnp.int32))


def draw_task_target(key, part):
    return task_tables(key)[0]


def draw_task_source(key, part):
    return task_tables(key)[1]


def draw_task_count(key, part):
    return task_tables(key)[2]


def plant(array, own_key, smallest, high):
    longest = array.shape.index(max(array.shape))
    spots = []
    for shift in (0, 1):
        where = [jax.random.randint(jax.random.fold_in(own_key, axis), (), 0, length) for axis, length in enumerate(array.shape)]
        where[longest] = (where[longest] + shift) % array.shape[longest]
        spots.append(tuple(where))
    return array.at[spots[0]].set(smallest).at[spots[1]].set(high)


def shard_levels(key, dims, cuts, smallest, high):
    def one(axis_at, shards_of):
        heights = jax.random.uniform(jax.random.fold_in(jax.random.fold_in(key, 6), axis_at), (shards_of,), jnp.float32, smallest / len(cuts), high / len(cuts))
        return jnp.repeat(jnp.exp(heights), dims[axis_at] // shards_of).reshape((-1,) + (1,) * (len(dims) - axis_at - 1))

    loudness = one(*cuts[0])
    for cut in cuts[1:]:
        loudness = loudness * one(*cut)
    return loudness


def centred(rng, extent, width, limit, cuts=(), kind=jnp.bfloat16):
    array = width * jax.random.normal(rng, extent, jnp.float32)
    if cuts:
        array = array * shard_levels(rng, extent, cuts, -0.22, 0.18)
    return jnp.clip(array, -limit, limit).astype(kind)


def setup_inputs(seed: int = 0) -> dict:
    seeds = jax.random.split(jax.random.key(seed), 7)
    positions = centred(seeds[0], (CELLS, 3, P_SIZE), 1.0, 6.0, ((0, 8),), jnp.float32)
    bend_op = centred(seeds[1], (P_SIZE, P_SIZE), P_SIZE ** -0.5, 0.25, (), jnp.float32)
    send_list = plant(jax.random.randint(seeds[2], (OWNERS, GHOSTS), 0, CD), jax.random.fold_in(seeds[2], 1), 0, CD - 1).astype(jnp.int32)
    task_target = draw_task_target(jax.random.fold_in(seeds[6], 71), 0)
    task_source = draw_task_source(jax.random.fold_in(seeds[6], 71), 0)
    task_count = draw_task_count(jax.random.fold_in(seeds[6], 71), 0)
    return dict(positions=positions, bend_op=bend_op, send_list=send_list, task_target=task_target, task_source=task_source, task_count=task_count)


REGULARIZE = 0.25
TIME_STEP = 0.5

def stokes_tile(target_pos, source_pos, source_force):
    offsets = target_pos[:, :, None] - source_pos[:, None, :]
    distance_sq = lax.optimization_barrier(jnp.sum(offsets * offsets, axis=0))
    inverse = lax.rsqrt(distance_sq + REGULARIZE)
    inverse_cube = inverse * inverse * inverse
    projected = lax.optimization_barrier(jnp.sum(offsets * source_force[:, None, :], axis=0))
    direct = lax.optimization_barrier(jnp.sum(((distance_sq + 2.0 * REGULARIZE) * inverse_cube)[None] * source_force[:, None, :], axis=2))
    tensor_part = lax.optimization_barrier(jnp.sum((projected * inverse_cube)[None] * offsets, axis=2))
    return (direct + tensor_part) / source_pos.shape[1]

def reference(positions, bend_op, send_list, task_target, task_source, task_count):
    owners = send_list.shape[0]
    cells_owner = positions.shape[0] // owners
    lane_count = task_count.shape[0] // owners
    points = positions.shape[2]
    targets = task_target.reshape(owners, lane_count, -1)
    sources = task_source.reshape(owners, lane_count, -1)
    counts = task_count.reshape(owners, lane_count)
    ghost_local = jnp.transpose(send_list.reshape(owners, owners, G), (1, 0, 2)).reshape(owners, owners * G)
    ghost_owner = jnp.repeat(jnp.arange(owners, dtype=jnp.int32), G)
    ghost_global = (ghost_owner[None, :] * cells_owner + ghost_local).astype(jnp.int32)
    current = positions
    velocity = jnp.zeros_like(positions)
    for iteration in range(ITERS):
        forces = jnp.dot(current.reshape(-1, points), bend_op, precision=lax.Precision.HIGHEST, preferred_element_type=jnp.float32).reshape(current.shape)
        own_pos = current.reshape(owners, cells_owner, 3, points)
        own_frc = forces.reshape(owners, cells_owner, 3, points)
        pool_pos = jnp.concatenate([own_pos, current[ghost_global]], axis=1)
        pool_frc = jnp.concatenate([own_frc, forces[ghost_global]], axis=1)

        def owner_speeds(bundle):
            owner_pos, owner_frc, owner_tgt, owner_src, owner_cnt = bundle

            def lane_pass(lane, speeds):

                def task_pass(task, inner):
                    target_row = owner_tgt[lane, task]
                    source_row = owner_src[lane, task]
                    tile_sum = stokes_tile(owner_pos[target_row], owner_pos[source_row], owner_frc[source_row])
                    return inner.at[target_row].add(tile_sum)
                return lax.fori_loop(0, owner_cnt[lane], task_pass, speeds)
            start = jnp.zeros((cells_owner, 3, points), dtype=jnp.float32)
            return lax.fori_loop(0, lane_count, lane_pass, start)
        velocity = lax.map(owner_speeds, (pool_pos, pool_frc, targets, sources, counts)).reshape(current.shape)
        current = current + TIME_STEP * velocity
    return (current, velocity)
```

```python
import functools
from types import SimpleNamespace

import jax
import jax.numpy as jnp
from jax import lax
from jax.experimental import pallas as pl
from jax.experimental.pallas import tpu as pltpu
from jax.sharding import PartitionSpec as P

REGULARIZE = 0.25
TIME_STEP = 0.5
UNROLL = 3
SOURCE_ROWS = 24
SUM_ROWS = 16

F32 = jnp.float32
BF16 = jnp.bfloat16
VMEM = pl.BlockSpec(memory_space=pltpu.VMEM)
SMEM = pl.BlockSpec(memory_space=pltpu.SMEM)
ANY = pl.BlockSpec(memory_space=pl.ANY)


def up(value, step):
    return -(-value // step) * step


def sizes(owners, lanes, cells, points, cap, listed):
    main = 128 * (points // (128 * lanes))
    rest = (points - main * lanes) // lanes
    group = listed // owners
    pool = up(cells + (owners - 1) * group, 8)
    per_pack = 128 // rest
    return SimpleNamespace(
        owners=owners,
        lanes=lanes,
        cells=cells,
        points=points,
        cap=cap,
        group=group,
        width=up(points, 128),
        tiles=up(points, 128) // 128,
        main=main,
        rest=rest,
        rest_tiles=up(rest * lanes, 128) // 128,
        chunk=main + rest,
        chunk_wide=main + up(rest, 128),
        chunk_tiles=(main + up(rest, 128)) // 128,
        per_pack=per_pack,
        pool=pool,
        share=cells // lanes,
        slots=up(lanes * cap + UNROLL, 8),
        rows=cells + 8,
    )


def pack_rows(sz, rows):
    return (3 * rows * sz.main // 128) + 8 * up(3 * rows // 8, sz.per_pack) // sz.per_pack


def split2(value):
    high = value.astype(BF16)
    return high, (value - high.astype(F32)).astype(BF16)


def split3(value):
    first = value.astype(BF16).astype(F32)
    left = value - first
    second = left.astype(BF16).astype(F32)
    return first, second, left - second


def lane_iota(rows):
    return lax.broadcasted_iota(jnp.int32, (rows, 128), 1)


def gather_kernel(sz, send, target, source, count, positions, *rest):
    outs, task_list, sems = rest[: sz.owners - 1], rest[sz.owners - 1], rest[sz.owners]
    me = lax.axis_index("space")
    copies = []
    for k in range(1, sz.owners):
        for g in range(sz.group):
            cell = send[0, (me ^ k) * sz.group + g]
            copies.append(
                pltpu.make_async_copy(
                    positions.at[pl.ds(cell, 1)], outs[k - 1].at[pl.ds(g, 1)], sems.at[k - 1, g]
                )
            )
    for copy in copies:
        copy.start()
    for j in range(sz.cap):
        task_list[0, j] = target[0, j]
        task_list[0, sz.cap + j] = source[0, j]
    task_list[0, 2 * sz.cap] = count[0]
    for copy in copies:
        copy.wait()


def build_list(sz, me, lists, send, tasks):
    total = jnp.int32(0)
    for one in lists:

        def step(j, total, one=one):
            source = one[0, sz.cap + j]
            ghost = jnp.maximum(source - sz.cells, 0)
            owner = lax.div(ghost, jnp.int32(sz.group))
            slot = sz.cells + ((owner ^ me) - 1) * sz.group + ghost - owner * sz.group
            received = jnp.where(owner == me, send[0, ghost], slot)
            tasks[0, total] = one[0, j]
            tasks[1, total] = jnp.where(source < sz.cells, source, received)
            return total + 1

        total = lax.fori_loop(0, one[0, 2 * sz.cap], step, total)
    for u in range(UNROLL):
        tasks[0, total + u] = jnp.int32(sz.cells)
        tasks[1, total + u] = jnp.int32(0)
    return total


def own_chunk(sz, lane, pool, first, rows):
    parts = []
    if sz.main:
        parts.append(pool[pl.ds(first, rows), pl.ds(pl.multiple_of(lane * sz.main, 128), sz.main)])
    start = sz.rest * lane
    lanes = lane_iota(rows)
    rest = jnp.zeros((rows, 128), F32)
    for tile in range(sz.rest_tiles):
        offset = sz.main * sz.lanes + 128 * tile
        block = pool[pl.ds(first, rows), offset : offset + 128]
        inside = (lanes + 128 * tile >= start) & (lanes + 128 * tile < start + sz.rest)
        rest = rest + jnp.where(inside, block, 0.0)
    rest = pltpu.roll(rest, lax.rem(128 * sz.rest_tiles - start, 128), 1)
    parts.append(rest)
    return jnp.concatenate(parts, axis=1) if len(parts) > 1 else parts[0]


def prepare(sz, lane, pool, bend, source_rows, centres, targets):
    value = pool[...]
    high, low = split2(value[:, : sz.points])
    bend_high, bend_low = split2(bend[...])
    dot = functools.partial(jnp.dot, preferred_element_type=F32)
    forces = dot(high, bend_high) + dot(low, bend_high) + dot(high, bend_low)
    forces = jnp.concatenate(
        [forces, jnp.zeros((3 * sz.pool, sz.width - sz.points), F32)], axis=1
    )
    middle = jnp.sum(value, axis=1, keepdims=True) / sz.points
    centres[...] = jnp.zeros_like(centres)
    for g in range(sz.pool // 8):
        where = [i * sz.pool + 8 * g for i in range(3)]
        middles = [jnp.broadcast_to(middle[w : w + 8], (8, 128)) for w in where]
        for i in range(3):
            centres[pl.ds(64 * g + i, 8, stride=8), :] = middles[i]
        for j in range(sz.tiles):
            cut = slice(128 * j, 128 * j + 128)
            y = [value[w : w + 8, cut] - m for w, m in zip(where, middles)]
            f = [forces[w : w + 8, cut] for w in where]
            norm = y[0] * y[0] + y[1] * y[1] + y[2] * y[2] + REGULARIZE
            along = y[0] * f[0] + y[1] * f[1] + y[2] * f[2]
            one, zero = jnp.ones((8, 128), F32), jnp.zeros((8, 128), F32)
            rows = [y[0], y[1], y[2], norm, one, zero, zero, zero]
            rows += f
            rows += [y[i] * f[k] for i in range(3) for k in range(3)]
            rows += [norm * f[i] + along * y[i] for i in range(3)]
            rows += [along]
            for k, row in enumerate(rows):
                source_rows.at[j][pl.ds(8 * SOURCE_ROWS * g + k, 8, stride=SOURCE_ROWS), :] = row
    targets[...] = jnp.zeros_like(targets)
    for g in range(sz.cells // 8):
        for i in range(3):
            chunk = own_chunk(sz, lane, pool, i * sz.pool + 8 * g, 8)
            for j in range(sz.chunk_tiles):
                targets.at[j][pl.ds(64 * g + i, 8, stride=8), :] = chunk[:, 128 * j : 128 * j + 128]


def one_task(sz, slot, tasks, source_rows, centres, targets, offsets, sums):
    target, source = tasks[0, slot], tasks[1, slot]
    centre = centres[pl.ds(pl.multiple_of(8 * source, 8), 8), :]
    row = lax.broadcasted_iota(jnp.int32, (8, 128), 0)
    pieces = []
    for j in range(sz.chunk_tiles):
        x = targets[j, pl.ds(pl.multiple_of(8 * target, 8), 8), :] - centre
        offsets.at[j][pl.ds(slot, 8, stride=sz.slots), :] = x
        square = x * x
        norm = pltpu.roll(square, 2, 0) + pltpu.roll(square, 3, 0) + pltpu.roll(square, 4, 0)
        side = jnp.where(row == 4, norm, jnp.where(row == 3, 1.0, 0.0))
        pieces.append(jnp.where(row < 3, -2.0 * x, side))
    x_side = jnp.concatenate(pieces, axis=1) if len(pieces) > 1 else pieces[0]
    x1, x2, x3 = split3(x_side)
    x_stack = jnp.concatenate([x1, x2, x1, x2, x3, x1], axis=0).astype(BF16)[:, : sz.chunk]
    held = jnp.concatenate(
        [
            source_rows[j, pl.ds(pl.multiple_of(SOURCE_ROWS * source, 8), SOURCE_ROWS), :]
            for j in range(sz.tiles)
        ],
        axis=1,
    )
    y1, y2, y3 = split3(held[:8])
    y_stack = jnp.concatenate([y1, y1, y2, y2, y1, y3], axis=0).astype(BF16)
    shifted = lax.dot_general(
        x_stack, y_stack, (((0,), (0,)), ((), ())), preferred_element_type=F32
    )
    inverse = lax.rsqrt(shifted)
    high, low = split2(inverse * inverse * inverse)
    m_stack = jnp.concatenate(split3(held[8:]), axis=0).astype(BF16)
    turned = (((1,), (1,)), ((), ()))
    result = lax.dot_general(m_stack, high, turned, preferred_element_type=F32)
    result = result + lax.dot_general(m_stack, low, turned, preferred_element_type=F32)
    result = result[:SUM_ROWS] + result[SUM_ROWS : 2 * SUM_ROWS] + result[2 * SUM_ROWS :]
    spare = sz.chunk_wide - sz.chunk
    if spare:
        result = jnp.concatenate([result, jnp.zeros((SUM_ROWS, spare), F32)], axis=1)
    for j in range(sz.chunk_tiles):
        for h in range(0, SUM_ROWS, 8):
            sums.at[j][pl.ds(h * sz.slots + slot, 8, stride=sz.slots), :] = result[
                h : h + 8, 128 * j : 128 * j + 128
            ]


def combine(sz, first, offsets, sums, speeds):
    for j in range(sz.chunk_tiles):
        x = [offsets[j, pl.ds(i * sz.slots + first, 8), :] for i in range(3)]
        s = [sums[j, pl.ds(k * sz.slots + first, 8), :] for k in range(SUM_ROWS)]
        a, b, c = s[:3], [s[3:6], s[6:9], s[9:12]], s[12:15]
        norm = x[0] * x[0] + x[1] * x[1] + x[2] * x[2] + REGULARIZE
        along = x[0] * a[0] + x[1] * a[1] + x[2] * a[2] - s[15]
        for i in range(3):
            speed = norm * a[i] + c[i] + along * x[i]
            for k in range(3):
                speed = speed - x[k] * (2.0 * b[k][i] + b[i][k])
            speeds[i, pl.ds(first, 8), 128 * j : 128 * j + 128] = speed / sz.points


def all_tiles(sz, total, tasks, source_rows, centres, targets, offsets, sums, speeds, moved):
    def several(q, carry):
        for u in range(UNROLL):
            one_task(sz, q * UNROLL + u, tasks, source_rows, centres, targets, offsets, sums)
        return carry

    lax.fori_loop(0, lax.div(total + UNROLL - 1, UNROLL), several, 0)

    def eight(q, carry):
        combine(sz, pl.multiple_of(8 * q, 8), offsets, sums, speeds)
        return carry

    lax.fori_loop(0, lax.div(total + 7, 8), eight, 0)
    moved[...] = jnp.zeros_like(moved)

    def add(t, carry):
        for i in range(3):
            place = pl.ds(i * sz.rows + tasks[0, t], 1)
            moved[place, :] = moved[place, :] + speeds[i, pl.ds(t, 1), :]
        return carry

    lax.fori_loop(0, total, add, 0)


def packed(sz, blocks):
    rows = [b[:, : sz.main] for b in blocks] if sz.main else []
    lanes = lane_iota(8)
    for p in range(0, len(blocks), sz.per_pack):
        total = jnp.zeros((8, 128), F32)
        for q, block in enumerate(blocks[p : p + sz.per_pack]):
            rest = jnp.where(lanes < sz.rest, block[:, sz.main : sz.main + 128], 0.0)
            total = total + (pltpu.roll(rest, q * sz.rest, 1) if q else rest)
        rows.append(total)
    return rows


def store_packed(sz, out, blocks):
    first = 0
    count = len(blocks)
    values = packed(sz, blocks)
    if sz.main:
        for b in range(count):
            for m in range(sz.main // 128):
                out[pl.ds(first, 8), :] = values[b][:, 128 * m : 128 * m + 128]
                first += 8
        values = values[count:]
    for value in values:
        out[pl.ds(first, 8), :] = value
        first += 8


def place_packed(sz, lane, arrived, count, store_main, add_rest):
    first = 0
    if sz.main:
        for b in range(count):
            for m in range(sz.main // 128):
                store_main(b, m, arrived[pl.ds(first, 8), :])
                first += 8
    start = sz.rest * lane
    lanes = lane_iota(8)
    for b in range(count):
        pack, q = divmod(b, sz.per_pack)
        value = arrived[pl.ds(first + 8 * pack, 8), :]
        value = pltpu.roll(value, lax.rem(start - q * sz.rest + 128, 128), 1)
        for tile in range(sz.rest_tiles):
            inside = (lanes + 128 * tile >= start) & (lanes + 128 * tile < start + sz.rest)
            add_rest(b, tile, jnp.where(inside, value, 0.0))


def first_kernel(sz, send, *refs):
    lists, refs = refs[: sz.lanes], refs[sz.lanes :]
    positions, refs = refs[0], refs[1:]
    ghosts, refs = refs[: sz.owners - 1], refs[sz.owners - 1 :]
    bend, chunk_out = refs[0], refs[1]
    ghost_out, refs = refs[2 : 1 + sz.owners], refs[1 + sz.owners :]
    pool, source_rows, centres, targets, offsets, sums, speeds, moved, tasks = refs
    me, lane = lax.axis_index("space"), lax.axis_index("lane")
    pool[...] = jnp.zeros_like(pool)
    for i in range(3):
        pool[pl.ds(i * sz.pool, sz.cells), : sz.points] = positions[:, i, :]
        for k in range(sz.owners - 1):
            for g in range(sz.group):
                place = i * sz.pool + sz.cells + k * sz.group + g
                pool[pl.ds(place, 1), : sz.points] = ghosts[k][g, pl.ds(i, 1), :]
    total = build_list(sz, me, lists, send, tasks)
    prepare(sz, lane, pool, bend, source_rows, centres, targets)
    all_tiles(sz, total, tasks, source_rows, centres, targets, offsets, sums, speeds, moved)
    blocks = []
    for i in range(3):
        for g in range(0, sz.cells, 8):
            chunk = own_chunk(sz, lane, pool, i * sz.pool + g, 8)
            place = pl.ds(i * sz.rows + g, 8)
            block = chunk + TIME_STEP * moved[place, :]
            moved[place, :] = block
            blocks.append(block)
    store_packed(sz, chunk_out, blocks)
    lanes = lane_iota(1)
    for k in range(1, sz.owners):
        for g in range(sz.group):
            cell = send[0, (me ^ k) * sz.group + g]
            rest = jnp.zeros((1, 128), F32)
            for i in range(3):
                place = pl.ds(i * sz.rows + cell, 1)
                row = moved[place, :]
                if sz.main:
                    ghost_out[k - 1][pl.ds(4 * g + i, 1), :] = row[:, :128]
                else:
                    ghost_out[k - 1][pl.ds(4 * g + i, 1), :] = jnp.zeros((1, 128), F32)
                piece = jnp.where(lanes < sz.rest, row[:, sz.main : sz.main + 128], 0.0)
                rest = rest + (pltpu.roll(piece, i * sz.rest, 1) if i else piece)
            ghost_out[k - 1][pl.ds(4 * g + 3, 1), :] = rest


def second_kernel(sz, send, *refs):
    lists, refs = refs[: sz.lanes], refs[sz.lanes :]
    chunks, refs = refs[: sz.lanes], refs[sz.lanes :]
    ghosts, refs = refs[: sz.lanes], refs[sz.lanes :]
    bend = refs[0]
    outs, refs = refs[1 : 1 + sz.lanes], refs[1 + sz.lanes :]
    share_out = refs[0]
    pool, source_rows, centres, targets, offsets, sums, speeds, moved, tasks = refs[1:]
    me, lane = lax.axis_index("space"), lax.axis_index("lane")
    pool[...] = jnp.zeros_like(pool)
    per = sz.cells // 8
    for k in range(sz.lanes):
        other = lane ^ k

        def row_of(b):
            return (b // per) * sz.pool + 8 * (b % per)

        def store_main(b, m, value):
            cut = pl.ds(pl.multiple_of(other * sz.main + 128 * m, 128), 128)
            pool[pl.ds(row_of(b), 8), cut] = value

        def add_rest(b, tile, value):
            offset = sz.main * sz.lanes + 128 * tile
            cut = (pl.ds(row_of(b), 8), slice(offset, offset + 128))
            pool[cut] = pool[cut] + value

        place_packed(sz, other, chunks[k], 3 * per, store_main, add_rest)
        start = sz.rest * other
        lanes = lane_iota(1)
        for c in range((sz.owners - 1) * sz.group):
            packed_rest = ghosts[k][pl.ds(4 * c + 3, 1), :]
            for i in range(3):
                place = pl.ds(i * sz.pool + sz.cells + c, 1)
                if sz.main:
                    cut = pl.ds(pl.multiple_of(other * sz.main, 128), 128)
                    pool[place, cut] = ghosts[k][pl.ds(4 * c + i, 1), :]
                value = pltpu.roll(packed_rest, lax.rem(start - i * sz.rest + 128, 128), 1)
                for tile in range(sz.rest_tiles):
                    offset = sz.main * sz.lanes + 128 * tile
                    inside = (lanes + 128 * tile >= start) & (
                        lanes + 128 * tile < start + sz.rest
                    )
                    cut = (place, slice(offset, offset + 128))
                    pool[cut] = pool[cut] + jnp.where(inside, value, 0.0)
    total = build_list(sz, me, lists, send, tasks)
    prepare(sz, lane, pool, bend, source_rows, centres, targets)
    all_tiles(sz, total, tasks, source_rows, centres, targets, offsets, sums, speeds, moved)
    for i in range(3):
        share_out[i] = share_rows(sz, pool, i * sz.pool, lane)
    for k in range(sz.lanes):
        blocks = [share_rows(sz, moved, i * sz.rows, lane ^ k) for i in range(3)]
        store_packed(sz, outs[k], blocks)


def share_rows(sz, ref, base, lane):
    if sz.share % 8 == 0:
        return ref[pl.ds(pl.multiple_of(base + lane * sz.share, 8), sz.share), :]
    rows = [ref[pl.ds(base + lane * sz.share + c, 1), :] for c in range(sz.share)]
    rows.append(jnp.zeros((8 - sz.share, rows[0].shape[1]), F32))
    return jnp.concatenate(rows, axis=0)


def last_kernel(sz, *refs):
    arrived, share, moved_out, velocity_out, held = (
        refs[: sz.lanes],
        refs[sz.lanes],
        refs[sz.lanes + 1],
        refs[sz.lanes + 2],
        refs[sz.lanes + 3],
    )
    lane = lax.axis_index("lane")
    held[...] = jnp.zeros_like(held)
    for k in range(sz.lanes):
        other = lane ^ k

        def store_main(b, m, value):
            held[b, :, pl.ds(pl.multiple_of(other * sz.main + 128 * m, 128), 128)] = value

        def add_rest(b, tile, value):
            offset = sz.main * sz.lanes + 128 * tile
            held[b, :, offset : offset + 128] = held[b, :, offset : offset + 128] + value

        place_packed(sz, other, arrived[k], 3, store_main, add_rest)
    for i in range(3):
        velocity = held[i]
        velocity_out[:, i, :] = velocity[: sz.share, : sz.points]
        moved_out[:, i, :] = (share[i] + TIME_STEP * velocity)[: sz.share, : sz.points]


def scratch(sz):
    return [
        pltpu.VMEM((3 * sz.pool, sz.width), F32),
        pltpu.VMEM((sz.tiles, SOURCE_ROWS * sz.pool, 128), F32),
        pltpu.VMEM((8 * sz.pool, 128), F32),
        pltpu.VMEM((sz.chunk_tiles, 8 * sz.rows, 128), F32),
        pltpu.VMEM((sz.chunk_tiles, 8 * sz.slots, 128), F32),
        pltpu.VMEM((sz.chunk_tiles, SUM_ROWS * sz.slots, 128), F32),
        pltpu.VMEM((3, sz.slots, sz.chunk_wide), F32),
        pltpu.VMEM((3 * sz.rows, sz.chunk_wide), F32),
        pltpu.SMEM((2, sz.slots), jnp.int32),
    ]


def swap(value, axis, size, k):
    return lax.ppermute(value, axis, [(d, d ^ k) for d in range(size)])


def shards(positions, bend_op, send_list, task_target, task_source, task_count):
    owners, lanes = lax.axis_size("space"), lax.axis_size("lane")
    cells, points = positions.shape[0], positions.shape[2]
    sz = sizes(owners, lanes, cells, points, task_target.shape[1], send_list.shape[1])
    params = pltpu.CompilerParams(vmem_limit_bytes=48 << 20)
    shape = jax.ShapeDtypeStruct
    cell = shape((sz.group, 3, points), F32)
    task_shape = shape((1, 2 * sz.cap + 1), jnp.int32)
    *leaving, own_list = pl.pallas_call(
        functools.partial(gather_kernel, sz),
        out_shape=[cell] * (owners - 1) + [task_shape],
        in_specs=[SMEM] * 4 + [ANY],
        out_specs=[ANY] * (owners - 1) + [SMEM],
        scratch_shapes=[pltpu.SemaphoreType.DMA((owners - 1, sz.group))],
        compiler_params=params,
        name="pick_cells",
    )(send_list, task_target, task_source, task_count, positions)
    ghosts = [swap(leaving[k - 1], "space", owners, k) for k in range(1, owners)]
    lists = [own_list] + [swap(own_list, "lane", lanes, k) for k in range(1, lanes)]
    wide = shape((pack_rows(sz, cells), 128), F32)
    narrow = shape((4 * sz.group, 128), F32)
    chunk, *leaving = pl.pallas_call(
        functools.partial(first_kernel, sz),
        out_shape=[wide] + [narrow] * (owners - 1),
        in_specs=[SMEM] * (1 + lanes) + [VMEM] * (1 + owners),
        out_specs=[VMEM] * owners,
        scratch_shapes=scratch(sz),
        compiler_params=params,
        name="first_step",
    )(send_list, *lists, positions, *ghosts, bend_op)
    arrived = [swap(leaving[k - 1], "space", owners, k) for k in range(1, owners)]
    chunks = [chunk] + [swap(chunk, "lane", lanes, k) for k in range(1, lanes)]
    arrived = jnp.concatenate(arrived, axis=0)
    ghosts = [arrived] + [swap(arrived, "lane", lanes, k) for k in range(1, lanes)]
    part = shape((pack_rows(sz, up(sz.share, 8)), 128), F32)
    share_shape = shape((3, up(sz.share, 8), sz.width), F32)
    *parts, share = pl.pallas_call(
        functools.partial(second_kernel, sz),
        out_shape=[part] * lanes + [share_shape],
        in_specs=[SMEM] * (1 + lanes) + [VMEM] * (2 * lanes + 1),
        out_specs=[VMEM] * (lanes + 1),
        scratch_shapes=scratch(sz),
        compiler_params=params,
        name="second_step",
    )(send_list, *lists, *chunks, *ghosts, bend_op)
    parts = [parts[0]] + [swap(parts[k], "lane", lanes, k) for k in range(1, lanes)]
    result = shape((sz.share, 3, points), F32)
    return pl.pallas_call(
        functools.partial(last_kernel, sz),
        out_shape=[result, result],
        in_specs=[VMEM] * (lanes + 1),
        out_specs=[VMEM] * 2,
        scratch_shapes=[pltpu.VMEM((3, up(sz.share, 8), sz.width), F32)],
        compiler_params=params,
        name="put_together",
    )(*parts, share)


def solution(mesh):
    in_specs = (
        P("space", None, None),
        P(),
        P("space", None),
        P(("space", "lane"), None),
        P(("space", "lane"), None),
        P(("space", "lane")),
    )
    out_specs = (P(("space", "lane"), None, None), P(("space", "lane"), None, None))
    return jax.shard_map(shards, mesh=mesh, in_specs=in_specs, out_specs=out_specs, check_vma=False)
```

```python
import functools
from types import SimpleNamespace

import jax
import jax.numpy as jnp
from jax import lax
from jax.experimental import pallas as pl
from jax.experimental.pallas import tpu as pltpu
from jax.sharding import PartitionSpec as P

REGULARIZE = 0.25
TIME_STEP = 0.5
UNROLL = 3
SOURCE_ROWS = 24
SUM_ROWS = 16

F32 = jnp.float32
BF16 = jnp.bfloat16
VMEM = pl.BlockSpec(memory_space=pltpu.VMEM)
SMEM = pl.BlockSpec(memory_space=pltpu.SMEM)
HBM = pl.BlockSpec(memory_space=pltpu.HBM)


def up(value, step):
    return -(-value // step) * step


def sizes(owners, lanes, cells, points, cap, listed):
    main = 128 * (points // (128 * lanes))
    rest = (points - main * lanes) // lanes
    group = listed // owners
    pool = up(cells + listed, 8)
    per_pack = 128 // rest
    return SimpleNamespace(
        owners=owners,
        lanes=lanes,
        cells=cells,
        points=points,
        cap=cap,
        group=group,
        width=up(points, 128),
        tiles=up(points, 128) // 128,
        main=main,
        rest=rest,
        rest_tiles=up(rest * lanes, 128) // 128,
        chunk=main + rest,
        chunk_wide=main + up(rest, 128),
        chunk_tiles=(main + up(rest, 128)) // 128,
        per_pack=per_pack,
        pool=pool,
        share=cells // lanes,
        slots=up(lanes * cap + UNROLL, 8),
        rows=cells + 8,
    )


def pack_rows(sz, rows):
    return (3 * rows * sz.main // 128) + 8 * up(3 * rows // 8, sz.per_pack) // sz.per_pack


def split2(value):
    high = value.astype(BF16)
    return high, (value - high.astype(F32)).astype(BF16)


def split3(value):
    first = value.astype(BF16).astype(F32)
    left = value - first
    second = left.astype(BF16).astype(F32)
    return first, second, left - second


def lane_iota(rows):
    return lax.broadcasted_iota(jnp.int32, (rows, 128), 1)


def loop(count, body):
    if count <= 8:
        for q in range(count):
            body(q)
    else:

        def step(q, carry):
            body(q)
            return carry

        lax.fori_loop(0, count, step, 0)


def own_chunk(sz, lane, ref, rows):
    parts = []
    if sz.main:
        parts.append(ref[rows, pl.ds(pl.multiple_of(lane * sz.main, 128), sz.main)])
    start = sz.rest * lane
    lanes = lane_iota(8)
    rest = jnp.zeros((8, 128), F32)
    for tile in range(sz.rest_tiles):
        offset = sz.main * sz.lanes + 128 * tile
        block = ref[rows, offset : min(offset + 128, ref.shape[-1])]
        if block.shape[1] < 128:
            block = jnp.concatenate([block, jnp.zeros((8, 128 - block.shape[1]), F32)], axis=1)
        inside = (lanes + 128 * tile >= start) & (lanes + 128 * tile < start + sz.rest)
        rest = rest + jnp.where(inside, block, 0.0)
    rest = pltpu.roll(rest, lax.rem(128 * sz.rest_tiles - start, 128), 1)
    parts.append(rest)
    return jnp.concatenate(parts, axis=1) if len(parts) > 1 else parts[0]


def send_ghosts(sz, send, chunks, out, tasks):
    lanes = lane_iota(1)

    def one(d):
        for g in range(sz.group):
            cell = send[0, d * sz.group + g]
            rows = []
            last = tasks
            for i in range(3):
                row = chunks[pl.ds(i * sz.rows + cell, 1), :]
                rows.append(row[:, :128] if sz.main else jnp.zeros((1, 128), F32))
                piece = jnp.where(lanes < sz.rest, row[:, sz.main : sz.main + 128], 0.0)
                last = last + (pltpu.roll(piece, i * sz.rest, 1) if i else piece)
            rows.append(last)
            for other in range(sz.lanes):
                first = ((d * sz.lanes + other) * sz.group + g) * 4
                for q, row in enumerate(rows):
                    out[pl.ds(first + q, 1), :] = row

    loop(sz.owners, one)


def pick_kernel(sz, send_in, lists_in, positions_in, out, send, lists, positions, chunks, sems):
    copies = [
        pltpu.make_async_copy(source, target, sems.at[q])
        for q, (source, target) in enumerate(
            [(send_in, send), (positions_in, positions), (lists_in, lists)]
        )
    ]
    for copy in copies:
        copy.start()
    for copy in copies:
        copy.wait()
    lane = lax.axis_index("lane")
    for i in range(3):
        for g in range(0, sz.cells, 8):
            value = own_chunk(sz, lane, positions.at[i], pl.ds(g, 8))
            chunks[pl.ds(i * sz.rows + g, 8), :] = value
    wide = [
        lists[...].astype(F32),
        jnp.zeros((1, 128 - 2 * sz.cap - 1), F32),
    ]
    tasks = pltpu.roll(jnp.concatenate(wide, axis=1), 3 * sz.rest, 1)
    send_ghosts(sz, send, chunks, out, tasks)


def take_ghosts(sz, arrived, pool):
    lanes = lane_iota(1)

    def one(d):
        for g in range(sz.group):
            first = [((d * sz.lanes + lane) * sz.group + g) * 4 for lane in range(sz.lanes)]
            last = [arrived[pl.ds(row + 3, 1), :] for row in first]
            for i in range(3):
                tiles = []
                if sz.main:
                    tiles += [arrived[pl.ds(row + i, 1), :] for row in first]
                for tile in range(sz.rest_tiles):
                    total = jnp.zeros((1, 128), F32)
                    for lane in range(sz.lanes):
                        start = sz.rest * lane
                        if start + sz.rest <= 128 * tile or start >= 128 * tile + 128:
                            continue
                        shift = (start - i * sz.rest) % 128
                        value = pltpu.roll(last[lane], shift, 1) if shift else last[lane]
                        at = lanes + 128 * tile
                        total = jnp.where((at >= start) & (at < start + sz.rest), value, total)
                    tiles.append(total)
                place = pl.ds(i * sz.pool + sz.cells + d * sz.group + g, 1)
                pool[place, :] = jnp.concatenate(tiles, axis=1)

    loop(sz.owners, one)


def build_list(sz, lists, tasks):
    total = jnp.int32(0)
    for lane in range(sz.lanes):

        def step(j, total, lane=lane):
            tasks[0, total] = lists[lane, j]
            tasks[1, total] = lists[lane, sz.cap + j]
            return total + 1

        total = lax.fori_loop(0, lists[lane, 2 * sz.cap], step, total)
    for u in range(UNROLL):
        tasks[0, total + u] = jnp.int32(sz.cells)
        tasks[1, total + u] = jnp.int32(0)
    tasks[2, 0] = total
    return total


def prepare(sz, lane, pool, bend, source_rows, centres, targets):
    value = pool[...]
    high, low = split2(value[:, : sz.points])
    bend_high, bend_low = split2(bend[...])
    dot = functools.partial(jnp.dot, preferred_element_type=F32)
    forces = dot(high, bend_high) + dot(low, bend_high) + dot(high, bend_low)
    forces = jnp.concatenate(
        [forces, jnp.zeros((3 * sz.pool, sz.width - sz.points), F32)], axis=1
    )
    middle = jnp.sum(value, axis=1, keepdims=True) / sz.points
    centres[...] = jnp.zeros_like(centres)
    for g in range(sz.pool // 8):
        where = [i * sz.pool + 8 * g for i in range(3)]
        middles = [jnp.broadcast_to(middle[w : w + 8], (8, 128)) for w in where]
        for i in range(3):
            centres[pl.ds(64 * g + i, 8, stride=8), :] = middles[i]
        for j in range(sz.tiles):
            cut = slice(128 * j, 128 * j + 128)
            y = [value[w : w + 8, cut] - m for w, m in zip(where, middles)]
            f = [forces[w : w + 8, cut] for w in where]
            norm = y[0] * y[0] + y[1] * y[1] + y[2] * y[2] + REGULARIZE
            along = y[0] * f[0] + y[1] * f[1] + y[2] * f[2]
            one, zero = jnp.ones((8, 128), F32), jnp.zeros((8, 128), F32)
            rows = [y[0], y[1], y[2], norm, one, zero, zero, zero]
            rows += f
            rows += [y[i] * f[k] for i in range(3) for k in range(3)]
            rows += [norm * f[i] + along * y[i] for i in range(3)]
            rows += [along]
            for k, row in enumerate(rows):
                source_rows.at[j][pl.ds(8 * SOURCE_ROWS * g + k, 8, stride=SOURCE_ROWS), :] = row
    targets[...] = jnp.zeros_like(targets)
    for g in range(sz.cells // 8):
        for i in range(3):
            chunk = own_chunk(sz, lane, pool, pl.ds(i * sz.pool + 8 * g, 8))
            for j in range(sz.chunk_tiles):
                targets.at[j][pl.ds(64 * g + i, 8, stride=8), :] = chunk[:, 128 * j : 128 * j + 128]


def one_task(sz, slot, tasks, source_rows, centres, targets, offsets, sums):
    target, source = tasks[0, slot], tasks[1, slot]
    centre = centres[pl.ds(pl.multiple_of(8 * source, 8), 8), :]
    row = lax.broadcasted_iota(jnp.int32, (8, 128), 0)
    pieces = []
    for j in range(sz.chunk_tiles):
        x = targets[j, pl.ds(pl.multiple_of(8 * target, 8), 8), :] - centre
        offsets.at[j][pl.ds(slot, 8, stride=sz.slots), :] = x
        square = x * x
        norm = pltpu.roll(square, 2, 0) + pltpu.roll(square, 3, 0) + pltpu.roll(square, 4, 0)
        side = jnp.where(row == 4, norm, jnp.where(row == 3, 1.0, 0.0))
        pieces.append(jnp.where(row < 3, -2.0 * x, side))
    x_side = jnp.concatenate(pieces, axis=1) if len(pieces) > 1 else pieces[0]
    x1, x2, x3 = split3(x_side)
    x_stack = jnp.concatenate([x1, x2, x1, x2, x3, x1], axis=0).astype(BF16)[:, : sz.chunk]
    held = jnp.concatenate(
        [
            source_rows[j, pl.ds(pl.multiple_of(SOURCE_ROWS * source, 8), SOURCE_ROWS), :]
            for j in range(sz.tiles)
        ],
        axis=1,
    )
    y1, y2, y3 = split3(held[:8])
    y_stack = jnp.concatenate([y1, y1, y2, y2, y1, y3], axis=0).astype(BF16)
    shifted = lax.dot_general(
        x_stack, y_stack, (((0,), (0,)), ((), ())), preferred_element_type=F32
    )
    inverse = lax.rsqrt(shifted)
    high, low = split2(inverse * inverse * inverse)
    m_stack = jnp.concatenate(split3(held[8:]), axis=0).astype(BF16)
    turned = (((1,), (1,)), ((), ()))
    result = lax.dot_general(m_stack, high, turned, preferred_element_type=F32)
    result = result + lax.dot_general(m_stack, low, turned, preferred_element_type=F32)
    result = result[:SUM_ROWS] + result[SUM_ROWS : 2 * SUM_ROWS] + result[2 * SUM_ROWS :]
    spare = sz.chunk_wide - sz.chunk
    if spare:
        result = jnp.concatenate([result, jnp.zeros((SUM_ROWS, spare), F32)], axis=1)
    for j in range(sz.chunk_tiles):
        for h in range(0, SUM_ROWS, 8):
            sums.at[j][pl.ds(h * sz.slots + slot, 8, stride=sz.slots), :] = result[
                h : h + 8, 128 * j : 128 * j + 128
            ]


def combine(sz, first, offsets, sums, speeds):
    for j in range(sz.chunk_tiles):
        x = [offsets[j, pl.ds(i * sz.slots + first, 8), :] for i in range(3)]
        s = [sums[j, pl.ds(k * sz.slots + first, 8), :] for k in range(SUM_ROWS)]
        a, b, c = s[:3], [s[3:6], s[6:9], s[9:12]], s[12:15]
        norm = x[0] * x[0] + x[1] * x[1] + x[2] * x[2] + REGULARIZE
        along = x[0] * a[0] + x[1] * a[1] + x[2] * a[2] - s[15]
        for i in range(3):
            speed = norm * a[i] + c[i] + along * x[i]
            for k in range(3):
                speed = speed - x[k] * (2.0 * b[k][i] + b[i][k])
            speeds[i, pl.ds(first, 8), 128 * j : 128 * j + 128] = speed / sz.points


def all_tiles(sz, total, tasks, source_rows, centres, targets, offsets, sums, speeds, moved):
    def several(q, carry):
        for u in range(UNROLL):
            one_task(sz, q * UNROLL + u, tasks, source_rows, centres, targets, offsets, sums)
        return carry

    lax.fori_loop(0, lax.div(total + UNROLL - 1, UNROLL), several, 0)

    def eight(q, carry):
        combine(sz, pl.multiple_of(8 * q, 8), offsets, sums, speeds)
        return carry

    lax.fori_loop(0, lax.div(total + 7, 8), eight, 0)
    moved[...] = jnp.zeros_like(moved)

    def add(t, carry):
        for i in range(3):
            place = pl.ds(i * sz.rows + tasks[0, t], 1)
            moved[place, :] = moved[place, :] + speeds[i, pl.ds(t, 1), :]
        return carry

    lax.fori_loop(0, total, add, 0)


def packed(sz, blocks):
    rows = [b[:, : sz.main] for b in blocks] if sz.main else []
    lanes = lane_iota(8)
    for p in range(0, len(blocks), sz.per_pack):
        total = jnp.zeros((8, 128), F32)
        for q, block in enumerate(blocks[p : p + sz.per_pack]):
            rest = jnp.where(lanes < sz.rest, block[:, sz.main : sz.main + 128], 0.0)
            total = total + (pltpu.roll(rest, q * sz.rest, 1) if q else rest)
        rows.append(total)
    return rows


def store_packed(sz, out, blocks):
    first = 0
    count = len(blocks)
    values = packed(sz, blocks)
    if sz.main:
        for b in range(count):
            for m in range(sz.main // 128):
                out[pl.ds(first, 8), :] = values[b][:, 128 * m : 128 * m + 128]
                first += 8
        values = values[count:]
    for value in values:
        out[pl.ds(first, 8), :] = value
        first += 8


def place_packed(sz, lane, arrived, count, store_main, add_rest):
    first = 0
    if sz.main:
        for b in range(count):
            for m in range(sz.main // 128):
                store_main(b, m, arrived[pl.ds(first, 8), :])
                first += 8
    start = sz.rest * lane
    lanes = lane_iota(8)
    for b in range(count):
        pack, q = divmod(b, sz.per_pack)
        value = arrived[pl.ds(first + 8 * pack, 8), :]
        value = pltpu.roll(value, lax.rem(start - q * sz.rest + 128, 128), 1)
        for tile in range(sz.rest_tiles):
            inside = (lanes + 128 * tile >= start) & (lanes + 128 * tile < start + sz.rest)
            add_rest(b, tile, jnp.where(inside, value, 0.0))


def first_kernel(sz, send, *refs):
    positions, arrived, bend, chunk_out, ghost_out, tasks = refs[:6]
    pool, source_rows, centres, targets, offsets, sums, speeds, moved = refs[6:14]
    staged, lists, sem = refs[14:]
    me, lane = lax.axis_index("space"), lax.axis_index("lane")
    for other in range(sz.lanes):
        row = ((me * sz.lanes + other) * sz.group) * 4 + 3
        value = pltpu.roll(arrived[pl.ds(row, 1), :], 128 - 3 * sz.rest, 1)
        staged[pl.ds(other, 1), :] = value.astype(jnp.int32)
    copy = pltpu.make_async_copy(staged, lists, sem)
    copy.start()
    pool[...] = jnp.zeros_like(pool)
    for i in range(3):
        pool[pl.ds(i * sz.pool, sz.cells), : sz.points] = positions[i]
    take_ghosts(sz, arrived, pool)
    prepare(sz, lane, pool, bend, source_rows, centres, targets)
    copy.wait()
    total = build_list(sz, lists, tasks)
    all_tiles(sz, total, tasks, source_rows, centres, targets, offsets, sums, speeds, moved)
    blocks = []
    for i in range(3):
        for g in range(0, sz.cells, 8):
            chunk = own_chunk(sz, lane, pool, pl.ds(i * sz.pool + g, 8))
            place = pl.ds(i * sz.rows + g, 8)
            block = chunk + TIME_STEP * moved[place, :]
            moved[place, :] = block
            blocks.append(block)
    store_packed(sz, chunk_out, blocks)
    send_ghosts(sz, send, moved, ghost_out, jnp.zeros((1, 128), F32))


def second_kernel(sz, tasks, *refs):
    chunks, refs = refs[: sz.lanes], refs[sz.lanes :]
    arrived, bend = refs[:2]
    outs, refs = refs[2 : 2 + sz.lanes], refs[2 + sz.lanes :]
    share_out = refs[0]
    pool, source_rows, centres, targets, offsets, sums, speeds, moved = refs[1:]
    lane = lax.axis_index("lane")
    pool[...] = jnp.zeros_like(pool)
    per = sz.cells // 8
    for k in range(sz.lanes):
        other = lane ^ k

        def row_of(b):
            return (b // per) * sz.pool + 8 * (b % per)

        def store_main(b, m, value):
            cut = pl.ds(pl.multiple_of(other * sz.main + 128 * m, 128), 128)
            pool[pl.ds(row_of(b), 8), cut] = value

        def add_rest(b, tile, value):
            offset = sz.main * sz.lanes + 128 * tile
            cut = (pl.ds(row_of(b), 8), slice(offset, offset + 128))
            pool[cut] = pool[cut] + value

        place_packed(sz, other, chunks[k], 3 * per, store_main, add_rest)
    take_ghosts(sz, arrived, pool)
    total = tasks[2, 0]
    prepare(sz, lane, pool, bend, source_rows, centres, targets)
    all_tiles(sz, total, tasks, source_rows, centres, targets, offsets, sums, speeds, moved)
    for i in range(3):
        share_out[i] = share_rows(sz, pool, i * sz.pool, lane)
    for k in range(sz.lanes):
        blocks = [share_rows(sz, moved, i * sz.rows, lane ^ k) for i in range(3)]
        store_packed(sz, outs[k], blocks)


def share_rows(sz, ref, base, lane):
    if sz.share % 8 == 0:
        return ref[pl.ds(pl.multiple_of(base + lane * sz.share, 8), sz.share), :]
    rows = [ref[pl.ds(base + lane * sz.share + c, 1), :] for c in range(sz.share)]
    rows.append(jnp.zeros((8 - sz.share, rows[0].shape[1]), F32))
    return jnp.concatenate(rows, axis=0)


def last_kernel(sz, *refs):
    arrived, share, moved_out, velocity_out, held = (
        refs[: sz.lanes],
        refs[sz.lanes],
        refs[sz.lanes + 1],
        refs[sz.lanes + 2],
        refs[sz.lanes + 3],
    )
    lane = lax.axis_index("lane")
    held[...] = jnp.zeros_like(held)
    for k in range(sz.lanes):
        other = lane ^ k

        def store_main(b, m, value):
            held[b, :, pl.ds(pl.multiple_of(other * sz.main + 128 * m, 128), 128)] = value

        def add_rest(b, tile, value):
            offset = sz.main * sz.lanes + 128 * tile
            held[b, :, offset : offset + 128] = held[b, :, offset : offset + 128] + value

        place_packed(sz, other, arrived[k], 3, store_main, add_rest)
    for i in range(3):
        velocity = held[i]
        velocity_out[i] = velocity[: sz.share, : sz.points]
        moved_out[i] = (share[i] + TIME_STEP * velocity)[: sz.share, : sz.points]


def scratch(sz):
    return [
        pltpu.VMEM((3 * sz.pool, sz.width), F32),
        pltpu.VMEM((sz.tiles, SOURCE_ROWS * sz.pool, 128), F32),
        pltpu.VMEM((8 * sz.pool, 128), F32),
        pltpu.VMEM((sz.chunk_tiles, 8 * sz.rows, 128), F32),
        pltpu.VMEM((sz.chunk_tiles, 8 * sz.slots, 128), F32),
        pltpu.VMEM((sz.chunk_tiles, SUM_ROWS * sz.slots, 128), F32),
        pltpu.VMEM((3, sz.slots, sz.chunk_wide), F32),
        pltpu.VMEM((3 * sz.rows, sz.chunk_wide), F32),
    ]


def swap(value, axis, size, k):
    return lax.ppermute(value, axis, [(d, d ^ k) for d in range(size)])


def shards(positions, bend_op, send_list, task_target, task_source, task_count):
    owners, lanes = lax.axis_size("space"), lax.axis_size("lane")
    cells, points = positions.shape[0], positions.shape[2]
    sz = sizes(owners, lanes, cells, points, task_target.shape[1], send_list.shape[1])
    params = pltpu.CompilerParams(vmem_limit_bytes=48 << 20)
    shape = jax.ShapeDtypeStruct
    both = ("space", "lane")
    by_component = jnp.transpose(positions, (1, 0, 2))
    own_list = jnp.concatenate([task_target, task_source, task_count[:, None]], axis=1)
    list_rows = up(lanes, 8)
    slot_shape = shape((4 * sz.group * owners * lanes, 128), F32)
    leaving = pl.pallas_call(
        functools.partial(pick_kernel, sz),
        out_shape=slot_shape,
        in_specs=[HBM] * 3,
        out_specs=VMEM,
        scratch_shapes=[
            pltpu.SMEM(send_list.shape, jnp.int32),
            pltpu.VMEM(own_list.shape, jnp.int32),
            pltpu.VMEM(by_component.shape, F32),
            pltpu.VMEM((3 * sz.rows, sz.chunk_wide), F32),
            pltpu.SemaphoreType.DMA((3,)),
        ],
        compiler_params=params,
        name="pick_cells",
    )(send_list, own_list, by_component)
    arrived = lax.all_to_all(leaving, both, split_axis=0, concat_axis=0, tiled=True)
    chunk, leaving, tasks = pl.pallas_call(
        functools.partial(first_kernel, sz),
        out_shape=[
            shape((pack_rows(sz, cells), 128), F32),
            slot_shape,
            shape((3, sz.slots), jnp.int32),
        ],
        in_specs=[SMEM] + [VMEM] * 3,
        out_specs=[VMEM, VMEM, SMEM],
        scratch_shapes=scratch(sz)
        + [
            pltpu.VMEM((list_rows, 128), jnp.int32),
            pltpu.SMEM((list_rows, 128), jnp.int32),
            pltpu.SemaphoreType.DMA,
        ],
        compiler_params=params,
        name="first_step",
    )(send_list, by_component, arrived, bend_op)
    arrived = lax.all_to_all(leaving, both, split_axis=0, concat_axis=0, tiled=True)
    chunks = [chunk] + [swap(chunk, "lane", lanes, k) for k in range(1, lanes)]
    part = shape((pack_rows(sz, up(sz.share, 8)), 128), F32)
    share_shape = shape((3, up(sz.share, 8), sz.width), F32)
    *parts, share = pl.pallas_call(
        functools.partial(second_kernel, sz),
        out_shape=[part] * lanes + [share_shape],
        in_specs=[SMEM] + [VMEM] * (lanes + 2),
        out_specs=[VMEM] * (lanes + 1),
        scratch_shapes=scratch(sz),
        compiler_params=params,
        name="second_step",
    )(tasks, *chunks, arrived, bend_op)
    parts = [parts[0]] + [swap(parts[k], "lane", lanes, k) for k in range(1, lanes)]
    result = shape((3, sz.share, points), F32)
    outputs = pl.pallas_call(
        functools.partial(last_kernel, sz),
        out_shape=[result, result],
        in_specs=[VMEM] * (lanes + 1),
        out_specs=[VMEM] * 2,
        scratch_shapes=[pltpu.VMEM((3, up(sz.share, 8), sz.width), F32)],
        compiler_params=params,
        name="put_together",
    )(*parts, share)
    return tuple(jnp.transpose(output, (1, 0, 2)) for output in outputs)


def solution(mesh):
    in_specs = (
        P("space", None, None),
        P(),
        P("space", None),
        P(("space", "lane"), None),
        P(("space", "lane"), None),
        P(("space", "lane")),
    )
    out_specs = (P(("space", "lane"), None, None), P(("space", "lane"), None, None))
    return jax.shard_map(shards, mesh=mesh, in_specs=in_specs, out_specs=out_specs, check_vma=False)
```

```python
import functools
from types import SimpleNamespace

import jax
import jax.numpy as jnp
from jax import lax
from jax.experimental import pallas as pl
from jax.experimental.pallas import tpu as pltpu
from jax.sharding import PartitionSpec as P

REGULARIZE = 0.25
TIME_STEP = 0.5
UNROLL = 4
SOURCE_ROWS = 24
SUM_ROWS = 16
STREAM = True

F32 = jnp.float32
BF16 = jnp.bfloat16
VMEM = pl.BlockSpec(memory_space=pltpu.VMEM)
SMEM = pl.BlockSpec(memory_space=pltpu.SMEM)
ANY = pl.BlockSpec(memory_space=pl.ANY)
HBM = pl.BlockSpec(memory_space=pltpu.HBM)


def up(value, step):
    return -(-value // step) * step


def sizes(owners, lanes, cells, points, cap, listed):
    main = 128 * (points // (128 * lanes))
    rest = (points - main * lanes) // lanes
    group = listed // owners
    pool = up(cells + listed, 8)
    per_pack = 128 // rest
    return SimpleNamespace(
        owners=owners,
        lanes=lanes,
        cells=cells,
        points=points,
        cap=cap,
        group=group,
        width=up(points, 128),
        tiles=up(points, 128) // 128,
        main=main,
        rest=rest,
        rest_tiles=up(rest * lanes, 128) // 128,
        chunk=main + rest,
        chunk_wide=main + up(rest, 128),
        chunk_tiles=(main + up(rest, 128)) // 128,
        per_pack=per_pack,
        pool=pool,
        share=cells // lanes,
        slots=up(lanes * cap + UNROLL, 8),
        rows=cells + 8,
        own=up(lanes * cap, 8),
    )


def pack_rows(sz, rows):
    return (3 * rows * sz.main // 128) + 8 * up(3 * rows // 8, sz.per_pack) // sz.per_pack


def split2(value):
    high = value.astype(BF16)
    return high, (value - high.astype(F32)).astype(BF16)


def split3(value):
    first = value.astype(BF16).astype(F32)
    left = value - first
    second = left.astype(BF16).astype(F32)
    return first, second, left - second


def lane_iota(rows):
    return lax.broadcasted_iota(jnp.int32, (rows, 128), 1)


def loop(count, body):
    if count <= 8:
        for q in range(count):
            body(q)
    else:

        def step(q, carry):
            body(q)
            return carry

        lax.fori_loop(0, count, step, 0)


def own_chunk(sz, lane, ref, rows):
    parts = []
    if sz.main:
        parts.append(ref[rows, pl.ds(pl.multiple_of(lane * sz.main, 128), sz.main)])
    start = sz.rest * lane
    lanes = lane_iota(8)
    rest = jnp.zeros((8, 128), F32)
    for tile in range(sz.rest_tiles):
        offset = sz.main * sz.lanes + 128 * tile
        block = ref[rows, offset : min(offset + 128, ref.shape[-1])]
        if block.shape[1] < 128:
            block = jnp.concatenate([block, jnp.zeros((8, 128 - block.shape[1]), F32)], axis=1)
        inside = (lanes + 128 * tile >= start) & (lanes + 128 * tile < start + sz.rest)
        rest = rest + jnp.where(inside, block, 0.0)
    rest = pltpu.roll(rest, lax.rem(128 * sz.rest_tiles - start, 128), 1)
    parts.append(rest)
    return jnp.concatenate(parts, axis=1) if len(parts) > 1 else parts[0]


def send_ghosts(sz, send, chunks, out, tasks):
    lanes = lane_iota(1)

    def one(d):
        for g in range(sz.group):
            cell = send[0, d * sz.group + g]
            rows = []
            last = tasks
            for i in range(3):
                row = chunks[pl.ds(i * sz.rows + cell, 1), :]
                rows.append(row[:, :128] if sz.main else jnp.zeros((1, 128), F32))
                piece = jnp.where(lanes < sz.rest, row[:, sz.main : sz.main + 128], 0.0)
                last = last + (pltpu.roll(piece, i * sz.rest, 1) if i else piece)
            rows.append(last)
            for other in range(sz.lanes):
                first = ((d * sz.lanes + other) * sz.group + g) * 4
                for q, row in enumerate(rows):
                    out[pl.ds(first + q, 1), :] = row

    loop(sz.owners, one)


def pick_kernel(sz, send_in, lists_in, positions_in, out, send, lists, positions, chunks, sems):
    copies = [
        pltpu.make_async_copy(source, target, sems.at[q])
        for q, (source, target) in enumerate(
            [(send_in, send), (positions_in, positions), (lists_in, lists)]
        )
    ]
    for copy in copies:
        copy.start()
    for copy in copies:
        copy.wait()
    lane = lax.axis_index("lane")
    for i in range(3):
        for g in range(0, sz.cells, 8):
            value = own_chunk(sz, lane, positions.at[i], pl.ds(g, 8))
            chunks[pl.ds(i * sz.rows + g, 8), :] = value
    wide = [
        lists[...].astype(F32),
        jnp.zeros((1, 128 - 2 * sz.cap - 1), F32),
    ]
    tasks = pltpu.roll(jnp.concatenate(wide, axis=1), 3 * sz.rest, 1)
    send_ghosts(sz, send, chunks, out, tasks)


def take_ghosts(sz, arrived, pool, stride, base):
    lanes = lane_iota(1)

    def one(d):
        for g in range(sz.group):
            first = [((d * sz.lanes + lane) * sz.group + g) * 4 for lane in range(sz.lanes)]
            last = [arrived[pl.ds(row + 3, 1), :] for row in first]
            for i in range(3):
                tiles = []
                if sz.main:
                    tiles += [arrived[pl.ds(row + i, 1), :] for row in first]
                for tile in range(sz.rest_tiles):
                    total = jnp.zeros((1, 128), F32)
                    for lane in range(sz.lanes):
                        start = sz.rest * lane
                        if start + sz.rest <= 128 * tile or start >= 128 * tile + 128:
                            continue
                        shift = (start - i * sz.rest) % 128
                        value = pltpu.roll(last[lane], shift, 1) if shift else last[lane]
                        at = lanes + 128 * tile
                        total = jnp.where((at >= start) & (at < start + sz.rest), value, total)
                    tiles.append(total)
                place = pl.ds(i * stride + base + d * sz.group + g, 1)
                pool[place, :] = jnp.concatenate(tiles, axis=1)

    loop(sz.owners, one)


def build_list(sz, lists, tasks):
    total = jnp.int32(0)
    for lane in range(sz.lanes):

        def step(j, total, lane=lane):
            tasks[0, total] = lists[lane, j]
            tasks[1, total] = lists[lane, sz.cap + j]
            return total + 1

        total = lax.fori_loop(0, lists[lane, 2 * sz.cap], step, total)
    for u in range(UNROLL):
        tasks[0, total + u] = jnp.int32(sz.cells)
        tasks[1, total + u] = jnp.int32(0)
    tasks[2, 0] = total
    return total


def own_list(sz, lane, tasks, mine):
    first = lane * sz.share

    def step(t, count):
        target = tasks[0, t] - first
        mine[0, count] = target
        mine[1, count] = tasks[1, t]
        return count + ((target >= 0) & (target < sz.share)).astype(jnp.int32)

    return lax.fori_loop(0, tasks[2, 0], step, jnp.int32(0))


def products(value, bend_high, bend_low):
    high, low = split2(value)
    dot = functools.partial(jnp.dot, preferred_element_type=F32)
    return dot(high, bend_high) + dot(low, bend_high) + dot(high, bend_low)


def make_sources(sz, value, bend_high, bend_low, source_rows, centres, first):
    count = value.shape[0] // 3
    forces = products(value[:, : sz.points], bend_high, bend_low)
    forces = jnp.concatenate(
        [forces, jnp.zeros((3 * count, sz.width - sz.points), F32)], axis=1
    )
    middle = jnp.sum(value, axis=1, keepdims=True) / sz.points
    for g in range(count // 8):
        where = [i * count + 8 * g for i in range(3)]
        middles = [jnp.broadcast_to(middle[w : w + 8], (8, 128)) for w in where]
        middles += [jnp.zeros((8, 128), F32)] * 5
        for i, row in enumerate(middles):
            centres[pl.ds(8 * (first + 8 * g) + i, 8, stride=8), :] = row
        for j in range(sz.tiles):
            cut = slice(128 * j, 128 * j + 128)
            y = [value[w : w + 8, cut] - m for w, m in zip(where, middles)]
            f = [forces[w : w + 8, cut] for w in where]
            norm = y[0] * y[0] + y[1] * y[1] + y[2] * y[2] + REGULARIZE
            along = y[0] * f[0] + y[1] * f[1] + y[2] * f[2]
            one, zero = jnp.ones((8, 128), F32), jnp.zeros((8, 128), F32)
            rows = [y[0], y[1], y[2], norm, one, zero, zero, zero]
            rows += f
            rows += [y[i] * f[k] for i in range(3) for k in range(3)]
            rows += [norm * f[i] + along * y[i] for i in range(3)]
            rows += [along]
            for k, row in enumerate(rows):
                place = pl.ds(SOURCE_ROWS * (first + 8 * g) + k, 8, stride=SOURCE_ROWS)
                source_rows.at[j][place, :] = row


def make_targets(sz, blocks, targets):
    targets[...] = jnp.zeros_like(targets)
    for g in range(sz.cells // 8):
        for i in range(3):
            block = blocks(i, g)
            for j in range(targets.shape[0]):
                cut = slice(128 * j, 128 * j + 128)
                targets.at[j][pl.ds(64 * g + i, 8, stride=8), :] = block[:, cut]


def load_source(sz, source, source_rows):
    held = [
        source_rows[j, pl.ds(pl.multiple_of(SOURCE_ROWS * source, 8), SOURCE_ROWS), :]
        for j in range(sz.tiles)
    ]
    held = jnp.concatenate(held, axis=1)
    y1, y2, y3 = split3(held[:8])
    y_stack = jnp.concatenate([y1, y1, y2, y2, y1, y3], axis=0).astype(BF16)
    m_stack = jnp.concatenate(split3(held[8:]), axis=0).astype(BF16)
    return y_stack, m_stack


def load_target(j, target, slot, centre, targets, offsets):
    row = lax.broadcasted_iota(jnp.int32, (8, 128), 0)
    x = targets[j, pl.ds(pl.multiple_of(8 * target, 8), 8), :] - centre
    square = x * x
    norm = pltpu.roll(square, 2, 0) + pltpu.roll(square, 3, 0) + pltpu.roll(square, 4, 0)
    side = jnp.where(row == 4, norm, jnp.where(row == 3, 1.0, 0.0))
    x_side = jnp.where(row < 3, -2.0 * x, side)
    x1, x2, x3 = split3(x_side)
    return x, jnp.concatenate([x1, x2, x1, x2, x3, x1], axis=0).astype(BF16)


def distances(x_stack, y_stack):
    return lax.dot_general(
        x_stack, y_stack, (((0,), (0,)), ((), ())), preferred_element_type=F32
    )


def weights(shifted):
    inverse = lax.rsqrt(shifted)
    return split2(inverse * inverse * inverse)


def tile_sums(high, low, m_stack):
    turned = (((1,), (1,)), ((), ()))
    if STREAM:
        result = lax.dot_general(high, m_stack, turned, preferred_element_type=F32)
        result = result + lax.dot_general(low, m_stack, turned, preferred_element_type=F32)
        result = jnp.transpose(result)
    else:
        result = lax.dot_general(m_stack, high, turned, preferred_element_type=F32)
        result = result + lax.dot_general(m_stack, low, turned, preferred_element_type=F32)
    result = result[:SUM_ROWS] + result[SUM_ROWS : 2 * SUM_ROWS] + result[2 * SUM_ROWS :]
    spare = -result.shape[1] % 128
    if spare:
        result = jnp.concatenate([result, jnp.zeros((SUM_ROWS, spare), F32)], axis=1)
    return result


def store_sums(slots, slot, j, x, result, offsets, sums):
    offsets.at[j][pl.ds(slot, 8, stride=slots), :] = x
    for h in range(0, SUM_ROWS, 8):
        sums.at[j][pl.ds(h * slots + slot, 8, stride=slots), :] = result[h : h + 8]


def mark(slot, target, hot):
    hot[pl.ds(slot, 1), :] = jnp.where(lane_iota(1) == target, 1.0, 0.0)


def combine(sz, slots, first, total, offsets, sums, speeds):
    live = lax.broadcasted_iota(jnp.int32, (8, 128), 0) + first < total
    for j in range(offsets.shape[0]):
        x = [offsets[j, pl.ds(i * slots + first, 8), :] for i in range(3)]
        s = [sums[j, pl.ds(k * slots + first, 8), :] for k in range(SUM_ROWS)]
        a, b, c = s[:3], [s[3:6], s[6:9], s[9:12]], s[12:15]
        norm = x[0] * x[0] + x[1] * x[1] + x[2] * x[2] + REGULARIZE
        along = x[0] * a[0] + x[1] * a[1] + x[2] * a[2] - s[15]
        for i in range(3):
            speed = norm * a[i] + c[i] + along * x[i]
            for k in range(3):
                speed = speed - x[k] * (2.0 * b[k][i] + b[i][k])
            speed = jnp.where(live, speed / sz.points, 0.0)
            speeds[i, pl.ds(first, 8), 128 * j : 128 * j + 128] = speed


def add_up(sz, slots, total, rows, offsets, sums, speeds, hot):
    def eight(q, carry):
        combine(sz, slots, pl.multiple_of(8 * q, 8), total, offsets, sums, speeds)
        return carry

    lax.fori_loop(0, lax.div(total + 7, 8), eight, 0)
    one_hot = hot[...].astype(BF16)
    result = []
    for i in range(3):
        first, second, third = split3(speeds[i])
        parts = [
            lax.dot_general(
                one_hot, part.astype(BF16), (((0,), (0,)), ((), ())), preferred_element_type=F32
            )
            for part in (first, second, third)
        ]
        result.append((parts[0] + parts[1] + parts[2])[:rows])
    return result


def tiles_of_chunk(sz, total, tasks, source_rows, centres, targets, offsets, sums, hot):
    def several(q, carry):
        slots = [q * UNROLL + u for u in range(UNROLL)]
        picks = [(tasks[0, slot], tasks[1, slot]) for slot in slots]
        sources = [load_source(sz, source, source_rows) for _, source in picks]
        points = []
        for slot, (target, source) in zip(slots, picks):
            centre = centres[pl.ds(pl.multiple_of(8 * source, 8), 8), :]
            points.append(
                [
                    load_target(j, target, slot, centre, targets, offsets)
                    for j in range(sz.chunk_tiles)
                ]
            )
        stacks = [
            jnp.concatenate([stack for _, stack in point], axis=1)[:, : sz.chunk]
            for point in points
        ]
        shifted = [distances(stack, y) for stack, (y, _) in zip(stacks, sources)]
        pairs = [weights(one) for one in shifted]
        results = [tile_sums(*pair, m) for pair, (_, m) in zip(pairs, sources)]
        for slot, (target, _), point, result in zip(slots, picks, points, results):
            for j in range(sz.chunk_tiles):
                cut = result[:, 128 * j : 128 * j + 128]
                store_sums(sz.slots, slot, j, point[j][0], cut, offsets, sums)
            mark(slot, target, hot)
        return carry

    lax.fori_loop(0, lax.div(total + UNROLL - 1, UNROLL), several, 0)


def tiles_of_cells(sz, first, total, mine, source_rows, centres, targets, offsets, sums, hot):
    def single(slot, carry):
        target, source = mine[0, slot], mine[1, slot]
        y_stack, m_stack = load_source(sz, source, source_rows)
        centre = centres[pl.ds(pl.multiple_of(8 * source, 8), 8), :]
        points = [
            load_target(j, target + first, slot, centre, targets, offsets)
            for j in range(sz.tiles)
        ]
        stacks = [
            stack[:, : min(128, sz.points - 128 * j)] for j, (_, stack) in enumerate(points)
        ]
        shifted = [distances(stack, y_stack) for stack in stacks]
        pairs = [weights(one) for one in shifted]
        results = [tile_sums(*pair, m_stack) for pair in pairs]
        for j in range(sz.tiles):
            store_sums(sz.own, slot, j, points[j][0], results[j], offsets, sums)
        mark(slot, target, hot)
        return carry

    lax.fori_loop(0, total, single, 0)


def packed(sz, blocks):
    rows = [b[:, : sz.main] for b in blocks] if sz.main else []
    lanes = lane_iota(8)
    for p in range(0, len(blocks), sz.per_pack):
        total = jnp.zeros((8, 128), F32)
        for q, block in enumerate(blocks[p : p + sz.per_pack]):
            rest = jnp.where(lanes < sz.rest, block[:, sz.main : sz.main + 128], 0.0)
            total = total + (pltpu.roll(rest, q * sz.rest, 1) if q else rest)
        rows.append(total)
    return rows


def store_packed(sz, out, blocks):
    first = 0
    count = len(blocks)
    values = packed(sz, blocks)
    if sz.main:
        for b in range(count):
            for m in range(sz.main // 128):
                out[pl.ds(first, 8), :] = values[b][:, 128 * m : 128 * m + 128]
                first += 8
        values = values[count:]
    for value in values:
        out[pl.ds(first, 8), :] = value
        first += 8


def place_packed(sz, lane, arrived, count, store_main, add_rest):
    first = 0
    if sz.main:
        for b in range(count):
            for m in range(sz.main // 128):
                store_main(b, m, arrived[pl.ds(first, 8), :])
                first += 8
    start = sz.rest * lane
    lanes = lane_iota(8)
    for b in range(count):
        pack, q = divmod(b, sz.per_pack)
        value = arrived[pl.ds(first + 8 * pack, 8), :]
        value = pltpu.roll(value, lax.rem(start - q * sz.rest + 128, 128), 1)
        for tile in range(sz.rest_tiles):
            inside = (lanes + 128 * tile >= start) & (lanes + 128 * tile < start + sz.rest)
            add_rest(b, tile, jnp.where(inside, value, 0.0))


def source_kernel(sz, positions, bend, high_out, low_out, source_rows, centres):
    high_out[...], low_out[...] = split2(bend[...])
    value = jnp.concatenate([positions[i] for i in range(3)], axis=0)
    value = jnp.concatenate(
        [value, jnp.zeros((3 * sz.cells, sz.width - sz.points), F32)], axis=1
    )
    make_sources(sz, value, high_out[...], low_out[...], source_rows, centres, 0)


def first_kernel(sz, send, *refs):
    positions, arrived, high, low, own_rows, own_centres = refs[:6]
    chunk_out, ghost_out, tasks = refs[6:9]
    source_rows, centres, targets, offsets, sums, speeds, hot, moved, pool = refs[9:18]
    staged, lists, sems = refs[18:]
    me, lane = lax.axis_index("space"), lax.axis_index("lane")
    for other in range(sz.lanes):
        row = ((me * sz.lanes + other) * sz.group) * 4 + 3
        value = pltpu.roll(arrived[pl.ds(row, 1), :], 128 - 3 * sz.rest, 1)
        staged[pl.ds(other, 1), :] = value.astype(jnp.int32)
    copies = [
        pltpu.make_async_copy(staged, lists, sems.at[0]),
        pltpu.make_async_copy(
            own_rows, source_rows.at[:, pl.ds(0, SOURCE_ROWS * sz.cells)], sems.at[1]
        ),
        pltpu.make_async_copy(own_centres, centres.at[pl.ds(0, 8 * sz.cells)], sems.at[2]),
    ]
    for copy in copies:
        copy.start()
    pool[...] = jnp.zeros_like(pool)
    take_ghosts(sz, arrived, pool, up(sz.owners * sz.group, 8), 0)
    make_sources(sz, pool[...], high[...], low[...], source_rows, centres, sz.cells)
    make_targets(
        sz, lambda i, g: own_chunk(sz, lane, positions.at[i], pl.ds(8 * g, 8)), targets
    )
    hot[...] = jnp.zeros_like(hot)
    speeds[...] = jnp.zeros_like(speeds)
    for copy in copies:
        copy.wait()
    total = build_list(sz, lists, tasks)
    tiles_of_chunk(sz, total, tasks, source_rows, centres, targets, offsets, sums, hot)
    velocity = add_up(sz, sz.slots, total, sz.cells, offsets, sums, speeds, hot)
    blocks = []
    for i in range(3):
        for g in range(0, sz.cells, 8):
            chunk = own_chunk(sz, lane, positions.at[i], pl.ds(g, 8))
            block = chunk + TIME_STEP * velocity[i][g : g + 8]
            moved[pl.ds(i * sz.rows + g, 8), :] = block
            blocks.append(block)
    store_packed(sz, chunk_out, blocks)
    send_ghosts(sz, send, moved, ghost_out, jnp.zeros((1, 128), F32))


def second_kernel(sz, tasks, *refs):
    chunks, refs = refs[: sz.lanes], refs[sz.lanes :]
    arrived, high, low, moved_out, velocity_out = refs[:5]
    source_rows, centres, targets, offsets, sums, speeds, hot, pool, mine = refs[5:]
    lane = lax.axis_index("lane")
    pool[...] = jnp.zeros_like(pool)
    per = sz.cells // 8
    for k in range(sz.lanes):
        other = lane ^ k

        def row_of(b):
            return (b // per) * sz.pool + 8 * (b % per)

        def store_main(b, m, value):
            cut = pl.ds(pl.multiple_of(other * sz.main + 128 * m, 128), 128)
            pool[pl.ds(row_of(b), 8), cut] = value

        def add_rest(b, tile, value):
            offset = sz.main * sz.lanes + 128 * tile
            cut = (pl.ds(row_of(b), 8), slice(offset, offset + 128))
            pool[cut] = pool[cut] + value

        place_packed(sz, other, chunks[k], 3 * per, store_main, add_rest)
    take_ghosts(sz, arrived, pool, sz.pool, sz.cells)
    total = own_list(sz, lane, tasks, mine)
    make_sources(sz, pool[...], high[...], low[...], source_rows, centres, 0)
    make_targets(sz, lambda i, g: pool[pl.ds(i * sz.pool + 8 * g, 8), :], targets)
    hot[...] = jnp.zeros_like(hot)
    speeds[...] = jnp.zeros_like(speeds)
    first = lane * sz.share
    tiles_of_cells(sz, first, total, mine, source_rows, centres, targets, offsets, sums, hot)
    velocity = add_up(sz, sz.own, total, up(sz.share, 8), offsets, sums, speeds, hot)
    for i in range(3):
        speed = velocity[i]
        moved = share_rows(sz, pool, i * sz.pool, lane) + TIME_STEP * speed
        velocity_out[i] = speed[: sz.share, : sz.points]
        moved_out[i] = moved[: sz.share, : sz.points]


def share_rows(sz, ref, base, lane):
    if sz.share % 8 == 0:
        return ref[pl.ds(pl.multiple_of(base + lane * sz.share, 8), sz.share), :]
    rows = [ref[pl.ds(base + lane * sz.share + c, 1), :] for c in range(sz.share)]
    rows.append(jnp.zeros((8 - sz.share, rows[0].shape[1]), F32))
    return jnp.concatenate(rows, axis=0)


def scratch(sz, tiles, slots):
    return [
        pltpu.VMEM((sz.tiles, SOURCE_ROWS * sz.pool, 128), F32),
        pltpu.VMEM((8 * sz.pool, 128), F32),
        pltpu.VMEM((tiles, 8 * sz.rows, 128), F32),
        pltpu.VMEM((tiles, 8 * slots, 128), F32),
        pltpu.VMEM((tiles, SUM_ROWS * slots, 128), F32),
        pltpu.VMEM((3, slots, 128 * tiles), F32),
        pltpu.VMEM((slots, 128), F32),
    ]


def swap(value, axis, size, k):
    return lax.ppermute(value, axis, [(d, d ^ k) for d in range(size)])


def shards(positions, bend_op, send_list, task_target, task_source, task_count):
    owners, lanes = lax.axis_size("space"), lax.axis_size("lane")
    cells, points = positions.shape[0], positions.shape[2]
    sz = sizes(owners, lanes, cells, points, task_target.shape[1], send_list.shape[1])
    params = pltpu.CompilerParams(vmem_limit_bytes=48 << 20)
    shape = jax.ShapeDtypeStruct
    both = ("space", "lane")
    by_component = jnp.transpose(positions, (1, 0, 2))
    own_list = jnp.concatenate([task_target, task_source, task_count[:, None]], axis=1)
    list_rows = up(lanes, 8)
    slot_shape = shape((4 * sz.group * owners * lanes, 128), F32)
    leaving = pl.pallas_call(
        functools.partial(pick_kernel, sz),
        out_shape=slot_shape,
        in_specs=[HBM] * 3,
        out_specs=VMEM,
        scratch_shapes=[
            pltpu.SMEM(send_list.shape, jnp.int32),
            pltpu.VMEM(own_list.shape, jnp.int32),
            pltpu.VMEM(by_component.shape, F32),
            pltpu.VMEM((3 * sz.rows, sz.chunk_wide), F32),
            pltpu.SemaphoreType.DMA((3,)),
        ],
        compiler_params=params,
        name="pick_cells",
    )(send_list, own_list, by_component)
    arrived = lax.all_to_all(leaving, both, split_axis=0, concat_axis=0, tiled=True)
    high, low, own_rows, own_centres = pl.pallas_call(
        functools.partial(source_kernel, sz),
        out_shape=[
            shape(bend_op.shape, BF16),
            shape(bend_op.shape, BF16),
            shape((sz.tiles, SOURCE_ROWS * cells, 128), F32),
            shape((8 * cells, 128), F32),
        ],
        in_specs=[VMEM] * 2,
        out_specs=[VMEM] * 4,
        compiler_params=params,
        cost_estimate=pl.CostEstimate(flops=10**9, bytes_accessed=10**7, transcendentals=0),
        name="first_sources",
    )(by_component, bend_op)
    chunk, leaving, tasks = pl.pallas_call(
        functools.partial(first_kernel, sz),
        out_shape=[
            shape((pack_rows(sz, cells), 128), F32),
            slot_shape,
            shape((3, sz.slots), jnp.int32),
        ],
        in_specs=[SMEM] + [VMEM] * 4 + [ANY] * 2,
        out_specs=[VMEM, VMEM, SMEM],
        scratch_shapes=scratch(sz, sz.chunk_tiles, sz.slots)
        + [
            pltpu.VMEM((3 * sz.rows, sz.chunk_wide), F32),
            pltpu.VMEM((3 * up(sz.owners * sz.group, 8), sz.width), F32),
            pltpu.VMEM((list_rows, 128), jnp.int32),
            pltpu.SMEM((list_rows, 128), jnp.int32),
            pltpu.SemaphoreType.DMA((3,)),
        ],
        compiler_params=params,
        name="first_step",
    )(send_list, by_component, arrived, high, low, own_rows, own_centres)
    arrived = lax.all_to_all(leaving, both, split_axis=0, concat_axis=0, tiled=True)
    chunks = [chunk] + [swap(chunk, "lane", lanes, k) for k in range(1, lanes)]
    result = shape((3, sz.share, points), F32)
    outputs = pl.pallas_call(
        functools.partial(second_kernel, sz),
        out_shape=[result, result],
        in_specs=[SMEM] + [VMEM] * (lanes + 3),
        out_specs=[VMEM] * 2,
        scratch_shapes=scratch(sz, sz.tiles, sz.own)
        + [
            pltpu.VMEM((3 * sz.pool, sz.width), F32),
            pltpu.SMEM((2, sz.own + 8), jnp.int32),
        ],
        compiler_params=params,
        name="second_step",
    )(tasks, *chunks, arrived, high, low)
    return tuple(jnp.transpose(output, (1, 0, 2)) for output in outputs)


def solution(mesh):
    in_specs = (
        P("space", None, None),
        P(),
        P("space", None),
        P(("space", "lane"), None),
        P(("space", "lane"), None),
        P(("space", "lane")),
    )
    out_specs = (P(("space", "lane"), None, None), P(("space", "lane"), None, None))
    return jax.shard_map(shards, mesh=mesh, in_specs=in_specs, out_specs=out_specs, check_vma=False)
```

```python
import functools
from types import SimpleNamespace

import jax
import jax.numpy as jnp
from jax import lax
from jax.experimental import pallas as pl
from jax.experimental.pallas import tpu as pltpu
from jax.sharding import PartitionSpec as P

REGULARIZE = 0.25
TIME_STEP = 0.5
UNROLL = 4
SOURCE_ROWS = 24
SUM_ROWS = 16

F32 = jnp.float32
BF16 = jnp.bfloat16
VMEM = pl.BlockSpec(memory_space=pltpu.VMEM)
SMEM = pl.BlockSpec(memory_space=pltpu.SMEM)
ANY = pl.BlockSpec(memory_space=pl.ANY)
HBM = pl.BlockSpec(memory_space=pltpu.HBM)


def up(value, step):
    return -(-value // step) * step


def sizes(owners, lanes, cells, points, cap, listed):
    main = 128 * (points // (128 * lanes))
    rest = (points - main * lanes) // lanes
    group = listed // owners
    pool = up(cells + listed, 8)
    per_pack = 128 // rest
    return SimpleNamespace(
        owners=owners,
        lanes=lanes,
        cells=cells,
        points=points,
        cap=cap,
        group=group,
        width=up(points, 128),
        tiles=up(points, 128) // 128,
        main=main,
        rest=rest,
        rest_tiles=up(rest * lanes, 128) // 128,
        chunk=main + rest,
        chunk_wide=main + up(rest, 128),
        chunk_tiles=(main + up(rest, 128)) // 128,
        per_pack=per_pack,
        pool=pool,
        share=cells // lanes,
        slots=up(lanes * cap + UNROLL, 8),
        rows=cells + 8,
        own=up(lanes * cap, 8),
    )


def pack_rows(sz, rows):
    return (3 * rows * sz.main // 128) + 8 * up(3 * rows // 8, sz.per_pack) // sz.per_pack


def split2(value):
    high = value.astype(BF16)
    return high, (value - high.astype(F32)).astype(BF16)


def split3(value):
    first = value.astype(BF16).astype(F32)
    left = value - first
    second = left.astype(BF16).astype(F32)
    return first, second, left - second


def lane_iota(rows):
    return lax.broadcasted_iota(jnp.int32, (rows, 128), 1)


def loop(count, body):
    if count <= 8:
        for q in range(count):
            body(q)
    else:

        def step(q, carry):
            body(q)
            return carry

        lax.fori_loop(0, count, step, 0)


def own_chunk(sz, lane, ref, rows):
    parts = []
    if sz.main:
        parts.append(ref[rows, pl.ds(pl.multiple_of(lane * sz.main, 128), sz.main)])
    start = sz.rest * lane
    lanes = lane_iota(8)
    rest = jnp.zeros((8, 128), F32)
    for tile in range(sz.rest_tiles):
        offset = sz.main * sz.lanes + 128 * tile
        block = ref[rows, offset : min(offset + 128, ref.shape[-1])]
        if block.shape[1] < 128:
            block = jnp.concatenate([block, jnp.zeros((8, 128 - block.shape[1]), F32)], axis=1)
        inside = (lanes + 128 * tile >= start) & (lanes + 128 * tile < start + sz.rest)
        rest = rest + jnp.where(inside, block, 0.0)
    rest = pltpu.roll(rest, lax.rem(128 * sz.rest_tiles - start, 128), 1)
    parts.append(rest)
    return jnp.concatenate(parts, axis=1) if len(parts) > 1 else parts[0]


def send_ghosts(sz, send, chunks, out, tasks):
    lanes = lane_iota(1)

    def one(d):
        for g in range(sz.group):
            cell = send[0, d * sz.group + g]
            rows = []
            last = tasks
            for i in range(3):
                row = chunks[pl.ds(i * sz.rows + cell, 1), :]
                rows.append(row[:, :128] if sz.main else jnp.zeros((1, 128), F32))
                piece = jnp.where(lanes < sz.rest, row[:, sz.main : sz.main + 128], 0.0)
                last = last + (pltpu.roll(piece, i * sz.rest, 1) if i else piece)
            rows.append(last)
            for other in range(sz.lanes):
                first = ((d * sz.lanes + other) * sz.group + g) * 4
                for q, row in enumerate(rows):
                    out[pl.ds(first + q, 1), :] = row

    loop(sz.owners, one)


def pick_kernel(sz, *refs):
    inputs, (out, send_out), held, (chunks, sems) = refs[:5], refs[5:7], refs[7:12], refs[12:]
    copies = [
        pltpu.make_async_copy(source, target, sems.at[q])
        for q, (source, target) in enumerate(zip(inputs, held))
    ]
    for copy in copies:
        copy.start()
    for copy in copies:
        copy.wait()
    send, target, source, count, positions = held
    for j in range(send_out.shape[1]):
        send_out[0, j] = send[0, j]
    lane = lax.axis_index("lane")
    for i in range(3):
        for g in range(0, sz.cells, 8):
            value = own_chunk(sz, lane, positions.at[i], pl.ds(g, 8))
            chunks[pl.ds(i * sz.rows + g, 8), :] = value
    spare = jnp.zeros((1, 128 - sz.cap), F32)
    tasks = jnp.where(lane_iota(1) == 3 * sz.rest + 2 * sz.cap, count[0].astype(F32), 0.0)
    for q, row in enumerate((target, source)):
        wide = jnp.concatenate([row[...].astype(F32), spare], axis=1)
        tasks = tasks + pltpu.roll(wide, 3 * sz.rest + q * sz.cap, 1)
    send_ghosts(sz, send, chunks, out, tasks)


def take_ghosts(sz, arrived, pool, stride, base):
    lanes = lane_iota(1)

    def one(d):
        for g in range(sz.group):
            first = [((d * sz.lanes + lane) * sz.group + g) * 4 for lane in range(sz.lanes)]
            last = [arrived[pl.ds(row + 3, 1), :] for row in first]
            for i in range(3):
                tiles = []
                if sz.main:
                    tiles += [arrived[pl.ds(row + i, 1), :] for row in first]
                for tile in range(sz.rest_tiles):
                    total = jnp.zeros((1, 128), F32)
                    for lane in range(sz.lanes):
                        start = sz.rest * lane
                        if start + sz.rest <= 128 * tile or start >= 128 * tile + 128:
                            continue
                        shift = (start - i * sz.rest) % 128
                        value = pltpu.roll(last[lane], shift, 1) if shift else last[lane]
                        at = lanes + 128 * tile
                        total = jnp.where((at >= start) & (at < start + sz.rest), value, total)
                    tiles.append(total)
                place = pl.ds(i * stride + base + d * sz.group + g, 1)
                pool[place, :] = jnp.concatenate(tiles, axis=1)

    loop(sz.owners, one)


def build_list(sz, lists, tasks):
    total = jnp.int32(0)
    for lane in range(sz.lanes):

        def step(j, total, lane=lane):
            tasks[0, total] = lists[lane, j]
            tasks[1, total] = lists[lane, sz.cap + j]
            return total + 1

        total = lax.fori_loop(0, lists[lane, 2 * sz.cap], step, total)
    for u in range(UNROLL):
        tasks[0, total + u] = jnp.int32(sz.cells)
        tasks[1, total + u] = jnp.int32(0)
    tasks[2, 0] = total
    return total


def own_list(sz, lane, tasks, mine):
    first = lane * sz.share

    def step(t, count):
        target = tasks[0, t] - first
        mine[0, count] = target
        mine[1, count] = tasks[1, t]
        return count + ((target >= 0) & (target < sz.share)).astype(jnp.int32)

    return lax.fori_loop(0, tasks[2, 0], step, jnp.int32(0))


def products(value, bend_high, bend_low):
    high, low = split2(value)
    dot = functools.partial(jnp.dot, preferred_element_type=F32)
    return dot(high, bend_high) + dot(low, bend_high) + dot(high, bend_low)


def make_sources(sz, value, bend_high, bend_low, source_rows, centres, first):
    count = value.shape[0] // 3
    forces = products(value[:, : sz.points], bend_high, bend_low)
    forces = jnp.concatenate(
        [forces, jnp.zeros((3 * count, sz.width - sz.points), F32)], axis=1
    )
    middle = jnp.sum(value, axis=1, keepdims=True) / sz.points
    for g in range(count // 8):
        where = [i * count + 8 * g for i in range(3)]
        middles = [jnp.broadcast_to(middle[w : w + 8], (8, 128)) for w in where]
        middles += [jnp.zeros((8, 128), F32)] * 5
        for i, row in enumerate(middles):
            centres[pl.ds(8 * (first + 8 * g) + i, 8, stride=8), :] = row
        for j in range(sz.tiles):
            cut = slice(128 * j, 128 * j + 128)
            y = [value[w : w + 8, cut] - m for w, m in zip(where, middles)]
            f = [forces[w : w + 8, cut] for w in where]
            norm = y[0] * y[0] + y[1] * y[1] + y[2] * y[2] + REGULARIZE
            along = y[0] * f[0] + y[1] * f[1] + y[2] * f[2]
            one, zero = jnp.ones((8, 128), F32), jnp.zeros((8, 128), F32)
            rows = [y[0], y[1], y[2], norm, one, zero, zero, zero]
            rows += f
            rows += [y[i] * f[k] for i in range(3) for k in range(3)]
            rows += [norm * f[i] + along * y[i] for i in range(3)]
            rows += [along]
            for k, row in enumerate(rows):
                place = pl.ds(SOURCE_ROWS * (first + 8 * g) + k, 8, stride=SOURCE_ROWS)
                source_rows.at[j][place, :] = row


def make_targets(sz, blocks, targets):
    targets[...] = jnp.zeros_like(targets)
    for g in range(sz.cells // 8):
        for i in range(3):
            block = blocks(i, g)
            for j in range(targets.shape[0]):
                cut = slice(128 * j, 128 * j + 128)
                targets.at[j][pl.ds(64 * g + i, 8, stride=8), :] = block[:, cut]


def load_source(sz, source, source_rows):
    held = [
        source_rows[j, pl.ds(pl.multiple_of(SOURCE_ROWS * source, 8), SOURCE_ROWS), :]
        for j in range(sz.tiles)
    ]
    count = sz.points // 128
    whole = jnp.concatenate(held[:count], axis=1)
    y1, y2, y3 = split3(whole[:8])
    y_stack = jnp.concatenate([y1, y1, y2, y2, y1, y3], axis=0).astype(BF16)
    m_stack = jnp.concatenate(split3(whole[8:]), axis=0).astype(BF16)
    m_stack = jnp.concatenate([m_stack, m_stack], axis=1)
    if count == sz.tiles:
        return y_stack, m_stack, None, None
    last = sz.points - 128 * count
    y1, y2, y3 = split3(held[count][:8])
    y_last = jnp.concatenate([y1, y1, y2, y2, y1, y3], axis=0).astype(BF16)[:, :last]
    m_last = jnp.concatenate(split3(held[count][8:]), axis=0)
    m_last = (m_last + pltpu.roll(m_last, last, 1)).astype(BF16)[:, : 2 * last]
    return y_stack, m_stack, y_last, m_last


def load_target(j, target, slot, centre, targets, offsets):
    row = lax.broadcasted_iota(jnp.int32, (8, 128), 0)
    x = targets[j, pl.ds(pl.multiple_of(8 * target, 8), 8), :] - centre
    square = x * x
    norm = pltpu.roll(square, 2, 0) + pltpu.roll(square, 3, 0) + pltpu.roll(square, 4, 0)
    side = jnp.where(row == 4, norm, jnp.where(row == 3, 1.0, 0.0))
    x_side = jnp.where(row < 3, -2.0 * x, side)
    x1, x2, x3 = split3(x_side)
    return x, jnp.concatenate([x1, x2, x1, x2, x3, x1], axis=0).astype(BF16)


def distances(x_stack, y_stack):
    return lax.dot_general(
        x_stack, y_stack, (((0,), (0,)), ((), ())), preferred_element_type=F32
    )


def weights(shifted, axis):
    inverse = lax.rsqrt(shifted)
    return jnp.concatenate(split2(inverse * inverse * inverse), axis=axis)


def tile_sums(whole, last, m_stack, m_last):
    turned = (((1,), (1,)), ((), ()))
    result = lax.dot_general(whole, m_stack, turned, preferred_element_type=F32)
    result = jnp.transpose(result)
    if last is not None:
        result = result + jnp.dot(m_last, last, preferred_element_type=F32)
    result = result[:SUM_ROWS] + result[SUM_ROWS : 2 * SUM_ROWS] + result[2 * SUM_ROWS :]
    spare = -result.shape[1] % 128
    if spare:
        result = jnp.concatenate([result, jnp.zeros((SUM_ROWS, spare), F32)], axis=1)
    return result


def sum_blocks(blocks, source):
    y_stack, m_stack, y_last, m_last = source
    whole = [distances(block, y_stack) for block in blocks]
    whole = [weights(one, 1) for one in whole]
    last = [None] * len(blocks)
    if y_last is not None:
        last = [weights(distances(y_last, block), 0) for block in blocks]
    return [tile_sums(*pair, m_stack, m_last) for pair in zip(whole, last)]


def store_sums(slots, slot, j, x, result, offsets, sums):
    offsets.at[j][pl.ds(slot, 8, stride=slots), :] = x
    for h in range(0, SUM_ROWS, 8):
        sums.at[j][pl.ds(h * slots + slot, 8, stride=slots), :] = result[h : h + 8]


def mark(slot, target, hot):
    hot[pl.ds(slot, 1), :] = jnp.where(lane_iota(1) == target, 1.0, 0.0)


def combine(sz, slots, first, total, offsets, sums, speeds):
    live = lax.broadcasted_iota(jnp.int32, (8, 128), 0) + first < total
    for j in range(offsets.shape[0]):
        x = [offsets[j, pl.ds(i * slots + first, 8), :] for i in range(3)]
        s = [sums[j, pl.ds(k * slots + first, 8), :] for k in range(SUM_ROWS)]
        a, b, c = s[:3], [s[3:6], s[6:9], s[9:12]], s[12:15]
        norm = x[0] * x[0] + x[1] * x[1] + x[2] * x[2] + REGULARIZE
        along = x[0] * a[0] + x[1] * a[1] + x[2] * a[2] - s[15]
        for i in range(3):
            speed = norm * a[i] + c[i] + along * x[i]
            for k in range(3):
                speed = speed - x[k] * (2.0 * b[k][i] + b[i][k])
            speed = jnp.where(live, speed / sz.points, 0.0)
            speeds[i, pl.ds(first, 8), 128 * j : 128 * j + 128] = speed


def add_up(sz, slots, total, rows, offsets, sums, speeds, hot):
    def eight(q, carry):
        combine(sz, slots, pl.multiple_of(8 * q, 8), total, offsets, sums, speeds)
        return carry

    lax.fori_loop(0, lax.div(total + 7, 8), eight, 0)
    one_hot = hot[...].astype(BF16)
    result = []
    for i in range(3):
        first, second, third = split3(speeds[i])
        parts = [
            lax.dot_general(
                one_hot, part.astype(BF16), (((0,), (0,)), ((), ())), preferred_element_type=F32
            )
            for part in (first, second, third)
        ]
        result.append((parts[0] + parts[1] + parts[2])[:rows])
    return result


def tiles_of_chunk(sz, total, tasks, source_rows, centres, targets, offsets, sums, hot):
    def several(q, carry):
        slots = [q * UNROLL + u for u in range(UNROLL)]
        picks = [(tasks[0, slot], tasks[1, slot]) for slot in slots]
        sources = [load_source(sz, source, source_rows) for _, source in picks]
        points = []
        for slot, (target, source) in zip(slots, picks):
            centre = centres[pl.ds(pl.multiple_of(8 * source, 8), 8), :]
            points.append(
                [
                    load_target(j, target, slot, centre, targets, offsets)
                    for j in range(sz.chunk_tiles)
                ]
            )
        stacks = [
            jnp.concatenate([stack for _, stack in point], axis=1)[:, : sz.chunk]
            for point in points
        ]
        whole = [distances(stack, source[0]) for stack, source in zip(stacks, sources)]
        whole = [weights(one, 1) for one in whole]
        last = [None] * UNROLL
        if sources[0][2] is not None:
            last = [distances(source[2], stack) for stack, source in zip(stacks, sources)]
            last = [weights(one, 0) for one in last]
        results = [
            tile_sums(*pair, source[1], source[3])
            for pair, source in zip(zip(whole, last), sources)
        ]
        for slot, (target, _), point, result in zip(slots, picks, points, results):
            for j in range(sz.chunk_tiles):
                cut = result[:, 128 * j : 128 * j + 128]
                store_sums(sz.slots, slot, j, point[j][0], cut, offsets, sums)
            mark(slot, target, hot)
        return carry

    lax.fori_loop(0, lax.div(total + UNROLL - 1, UNROLL), several, 0)


def tiles_of_cells(sz, first, total, mine, source_rows, centres, targets, offsets, sums, hot):
    def single(slot, carry):
        target, source = mine[0, slot], mine[1, slot]
        held = load_source(sz, source, source_rows)
        centre = centres[pl.ds(pl.multiple_of(8 * source, 8), 8), :]
        points = [
            load_target(j, target + first, slot, centre, targets, offsets)
            for j in range(sz.tiles)
        ]
        stacks = [
            stack[:, : min(128, sz.points - 128 * j)] for j, (_, stack) in enumerate(points)
        ]
        results = sum_blocks(stacks, held)
        for j in range(sz.tiles):
            store_sums(sz.own, slot, j, points[j][0], results[j], offsets, sums)
        mark(slot, target, hot)
        return carry

    lax.fori_loop(0, total, single, 0)


def packed(sz, blocks):
    rows = [b[:, : sz.main] for b in blocks] if sz.main else []
    lanes = lane_iota(8)
    for p in range(0, len(blocks), sz.per_pack):
        total = jnp.zeros((8, 128), F32)
        for q, block in enumerate(blocks[p : p + sz.per_pack]):
            rest = jnp.where(lanes < sz.rest, block[:, sz.main : sz.main + 128], 0.0)
            total = total + (pltpu.roll(rest, q * sz.rest, 1) if q else rest)
        rows.append(total)
    return rows


def store_packed(sz, out, blocks):
    first = 0
    count = len(blocks)
    values = packed(sz, blocks)
    if sz.main:
        for b in range(count):
            for m in range(sz.main // 128):
                out[pl.ds(first, 8), :] = values[b][:, 128 * m : 128 * m + 128]
                first += 8
        values = values[count:]
    for value in values:
        out[pl.ds(first, 8), :] = value
        first += 8


def place_packed(sz, lane, arrived, count, store_main, add_rest):
    first = 0
    if sz.main:
        for b in range(count):
            for m in range(sz.main // 128):
                store_main(b, m, arrived[pl.ds(first, 8), :])
                first += 8
    start = sz.rest * lane
    lanes = lane_iota(8)
    for b in range(count):
        pack, q = divmod(b, sz.per_pack)
        value = arrived[pl.ds(first + 8 * pack, 8), :]
        value = pltpu.roll(value, lax.rem(start - q * sz.rest + 128, 128), 1)
        for tile in range(sz.rest_tiles):
            inside = (lanes + 128 * tile >= start) & (lanes + 128 * tile < start + sz.rest)
            add_rest(b, tile, jnp.where(inside, value, 0.0))


def source_kernel(sz, positions, bend, high_out, low_out, source_rows, centres):
    high_out[...], low_out[...] = split2(bend[...])
    value = jnp.concatenate([positions[i] for i in range(3)], axis=0)
    value = jnp.concatenate(
        [value, jnp.zeros((3 * sz.cells, sz.width - sz.points), F32)], axis=1
    )
    make_sources(sz, value, high_out[...], low_out[...], source_rows, centres, 0)


def first_kernel(sz, send, *refs):
    positions, arrived, high, low, own_rows, own_centres = refs[:6]
    chunk_out, ghost_out, tasks = refs[6:9]
    source_rows, centres, targets, offsets, sums, speeds, hot, moved, pool = refs[9:18]
    staged, lists, sems = refs[18:]
    me, lane = lax.axis_index("space"), lax.axis_index("lane")
    for other in range(sz.lanes):
        row = ((me * sz.lanes + other) * sz.group) * 4 + 3
        value = pltpu.roll(arrived[pl.ds(row, 1), :], 128 - 3 * sz.rest, 1)
        staged[pl.ds(other, 1), :] = value.astype(jnp.int32)
    copies = [
        pltpu.make_async_copy(staged, lists, sems.at[0]),
        pltpu.make_async_copy(
            own_rows, source_rows.at[:, pl.ds(0, SOURCE_ROWS * sz.cells)], sems.at[1]
        ),
        pltpu.make_async_copy(own_centres, centres.at[pl.ds(0, 8 * sz.cells)], sems.at[2]),
    ]
    for copy in copies:
        copy.start()
    pool[...] = jnp.zeros_like(pool)
    take_ghosts(sz, arrived, pool, up(sz.owners * sz.group, 8), 0)
    make_sources(sz, pool[...], high[...], low[...], source_rows, centres, sz.cells)
    make_targets(
        sz, lambda i, g: own_chunk(sz, lane, positions.at[i], pl.ds(8 * g, 8)), targets
    )
    hot[...] = jnp.zeros_like(hot)
    speeds[...] = jnp.zeros_like(speeds)
    for copy in copies:
        copy.wait()
    total = build_list(sz, lists, tasks)
    tiles_of_chunk(sz, total, tasks, source_rows, centres, targets, offsets, sums, hot)
    velocity = add_up(sz, sz.slots, total, sz.cells, offsets, sums, speeds, hot)
    blocks = []
    for i in range(3):
        for g in range(0, sz.cells, 8):
            chunk = own_chunk(sz, lane, positions.at[i], pl.ds(g, 8))
            block = chunk + TIME_STEP * velocity[i][g : g + 8]
            moved[pl.ds(i * sz.rows + g, 8), :] = block
            blocks.append(block)
    store_packed(sz, chunk_out, blocks)
    send_ghosts(sz, send, moved, ghost_out, jnp.zeros((1, 128), F32))


def second_kernel(sz, tasks, *refs):
    chunks, refs = refs[: sz.lanes], refs[sz.lanes :]
    arrived, high, low, moved_out, velocity_out = refs[:5]
    source_rows, centres, targets, offsets, sums, speeds, hot, pool, mine = refs[5:]
    lane = lax.axis_index("lane")
    pool[...] = jnp.zeros_like(pool)
    per = sz.cells // 8
    for k in range(sz.lanes):
        other = lane ^ k

        def row_of(b):
            return (b // per) * sz.pool + 8 * (b % per)

        def store_main(b, m, value):
            cut = pl.ds(pl.multiple_of(other * sz.main + 128 * m, 128), 128)
            pool[pl.ds(row_of(b), 8), cut] = value

        def add_rest(b, tile, value):
            offset = sz.main * sz.lanes + 128 * tile
            cut = (pl.ds(row_of(b), 8), slice(offset, offset + 128))
            pool[cut] = pool[cut] + value

        place_packed(sz, other, chunks[k], 3 * per, store_main, add_rest)
    take_ghosts(sz, arrived, pool, sz.pool, sz.cells)
    total = own_list(sz, lane, tasks, mine)
    make_sources(sz, pool[...], high[...], low[...], source_rows, centres, 0)
    make_targets(sz, lambda i, g: pool[pl.ds(i * sz.pool + 8 * g, 8), :], targets)
    hot[...] = jnp.zeros_like(hot)
    speeds[...] = jnp.zeros_like(speeds)
    first = lane * sz.share
    tiles_of_cells(sz, first, total, mine, source_rows, centres, targets, offsets, sums, hot)
    velocity = add_up(sz, sz.own, total, up(sz.share, 8), offsets, sums, speeds, hot)
    for i in range(3):
        speed = velocity[i]
        moved = share_rows(sz, pool, i * sz.pool, lane) + TIME_STEP * speed
        velocity_out[i] = speed[: sz.share, : sz.points]
        moved_out[i] = moved[: sz.share, : sz.points]


def share_rows(sz, ref, base, lane):
    if sz.share % 8 == 0:
        return ref[pl.ds(pl.multiple_of(base + lane * sz.share, 8), sz.share), :]
    rows = [ref[pl.ds(base + lane * sz.share + c, 1), :] for c in range(sz.share)]
    rows.append(jnp.zeros((8 - sz.share, rows[0].shape[1]), F32))
    return jnp.concatenate(rows, axis=0)


def scratch(sz, tiles, slots):
    return [
        pltpu.VMEM((sz.tiles, SOURCE_ROWS * sz.pool, 128), F32),
        pltpu.VMEM((8 * sz.pool, 128), F32),
        pltpu.VMEM((tiles, 8 * sz.rows, 128), F32),
        pltpu.VMEM((tiles, 8 * slots, 128), F32),
        pltpu.VMEM((tiles, SUM_ROWS * slots, 128), F32),
        pltpu.VMEM((3, slots, 128 * tiles), F32),
        pltpu.VMEM((slots, 128), F32),
    ]


def swap(value, axis, size, k):
    return lax.ppermute(value, axis, [(d, d ^ k) for d in range(size)])


def shards(positions, bend_op, send_list, task_target, task_source, task_count):
    owners, lanes = lax.axis_size("space"), lax.axis_size("lane")
    cells, points = positions.shape[0], positions.shape[2]
    sz = sizes(owners, lanes, cells, points, task_target.shape[1], send_list.shape[1])
    params = pltpu.CompilerParams(vmem_limit_bytes=min(4 * lanes, 40) << 20)
    shape = jax.ShapeDtypeStruct
    both = ("space", "lane")
    by_component = jnp.transpose(positions, (1, 0, 2))
    list_rows = up(lanes, 8)
    slot_shape = shape((4 * sz.group * owners * lanes, 128), F32)
    leaving, send = pl.pallas_call(
        functools.partial(pick_kernel, sz),
        out_shape=[slot_shape, shape(send_list.shape, jnp.int32)],
        in_specs=[HBM] * 5,
        out_specs=[VMEM, SMEM],
        scratch_shapes=[
            pltpu.SMEM(send_list.shape, jnp.int32),
            pltpu.VMEM(task_target.shape, jnp.int32),
            pltpu.VMEM(task_source.shape, jnp.int32),
            pltpu.SMEM(task_count.shape, jnp.int32),
            pltpu.VMEM(by_component.shape, F32),
            pltpu.VMEM((3 * sz.rows, sz.chunk_wide), F32),
            pltpu.SemaphoreType.DMA((5,)),
        ],
        compiler_params=pltpu.CompilerParams(vmem_limit_bytes=60 << 20),
        name="pick_cells",
    )(send_list, task_target, task_source, task_count, by_component)
    arrived = lax.all_to_all(leaving, both, split_axis=0, concat_axis=0, tiled=True)
    high, low, own_rows, own_centres = pl.pallas_call(
        functools.partial(source_kernel, sz),
        out_shape=[
            shape(bend_op.shape, BF16),
            shape(bend_op.shape, BF16),
            shape((sz.tiles, SOURCE_ROWS * cells, 128), F32),
            shape((8 * cells, 128), F32),
        ],
        in_specs=[VMEM] * 2,
        out_specs=[VMEM] * 4,
        compiler_params=params,
        cost_estimate=pl.CostEstimate(flops=10**9, bytes_accessed=10**7, transcendentals=0),
        name="first_sources",
    )(by_component, bend_op)
    chunk, leaving, tasks = pl.pallas_call(
        functools.partial(first_kernel, sz),
        out_shape=[
            shape((pack_rows(sz, cells), 128), F32),
            slot_shape,
            shape((3, sz.slots), jnp.int32),
        ],
        in_specs=[SMEM] + [VMEM] * 4 + [ANY] * 2,
        out_specs=[VMEM, VMEM, SMEM],
        scratch_shapes=scratch(sz, sz.chunk_tiles, sz.slots)
        + [
            pltpu.VMEM((3 * sz.rows, sz.chunk_wide), F32),
            pltpu.VMEM((3 * up(sz.owners * sz.group, 8), sz.width), F32),
            pltpu.VMEM((list_rows, 128), jnp.int32),
            pltpu.SMEM((list_rows, 128), jnp.int32),
            pltpu.SemaphoreType.DMA((3,)),
        ],
        compiler_params=params,
        name="first_step",
    )(send, by_component, arrived, high, low, own_rows, own_centres)
    arrived = lax.all_to_all(leaving, both, split_axis=0, concat_axis=0, tiled=True)
    chunks = [chunk] + [swap(chunk, "lane", lanes, k) for k in range(1, lanes)]
    result = shape((3, sz.share, points), F32)
    outputs = pl.pallas_call(
        functools.partial(second_kernel, sz),
        out_shape=[result, result],
        in_specs=[SMEM] + [VMEM] * (lanes + 3),
        out_specs=[VMEM] * 2,
        scratch_shapes=scratch(sz, sz.tiles, sz.own)
        + [
            pltpu.VMEM((3 * sz.pool, sz.width), F32),
            pltpu.SMEM((2, sz.own + 8), jnp.int32),
        ],
        compiler_params=params,
        name="second_step",
    )(tasks, *chunks, arrived, high, low)
    return tuple(jnp.transpose(output, (1, 0, 2)) for output in outputs)


def solution(mesh):
    in_specs = (
        P("space", None, None),
        P(),
        P("space", None),
        P(("space", "lane"), None),
        P(("space", "lane"), None),
        P(("space", "lane")),
    )
    out_specs = (P(("space", "lane"), None, None), P(("space", "lane"), None, None))
    return jax.shard_map(shards, mesh=mesh, in_specs=in_specs, out_specs=out_specs, check_vma=False)
```

```python
import functools
from types import SimpleNamespace

import jax
import jax.numpy as jnp
from jax import lax
from jax.experimental import pallas as pl
from jax.experimental.pallas import tpu as pltpu
from jax.sharding import PartitionSpec as P

REGULARIZE = 0.25
TIME_STEP = 0.5
UNROLL = 4
SOURCE_ROWS = 24
SUM_ROWS = 16

F32 = jnp.float32
BF16 = jnp.bfloat16
VMEM = pl.BlockSpec(memory_space=pltpu.VMEM)
SMEM = pl.BlockSpec(memory_space=pltpu.SMEM)
HBM = pl.BlockSpec(memory_space=pltpu.HBM)


def up(value, step):
    return -(-value // step) * step


def sizes(owners, lanes, cells, points, cap, listed):
    main = 128 * (points // (128 * lanes))
    rest = (points - main * lanes) // lanes
    group = listed // owners
    pool = up(cells + listed, 8)
    per_pack = 128 // rest
    return SimpleNamespace(
        owners=owners,
        lanes=lanes,
        cells=cells,
        points=points,
        cap=cap,
        group=group,
        width=up(points, 128),
        tiles=up(points, 128) // 128,
        main=main,
        rest=rest,
        rest_tiles=up(rest * lanes, 128) // 128,
        chunk=main + rest,
        chunk_wide=main + up(rest, 128),
        chunk_tiles=(main + up(rest, 128)) // 128,
        per_pack=per_pack,
        pool=pool,
        share=cells // lanes,
        slots=up(lanes * cap + UNROLL, 8),
        rows=cells + 8,
        own=up(lanes * cap, 8),
    )


def pack_rows(sz, rows):
    return (3 * rows * sz.main // 128) + 8 * up(3 * rows // 8, sz.per_pack) // sz.per_pack


def split2(value):
    high = value.astype(BF16)
    return high, (value - high.astype(F32)).astype(BF16)


def split3(value):
    first = value.astype(BF16).astype(F32)
    left = value - first
    second = left.astype(BF16).astype(F32)
    return first, second, left - second


def lane_iota(rows):
    return lax.broadcasted_iota(jnp.int32, (rows, 128), 1)


def fetch(sources, targets, sems):
    copies = [
        pltpu.make_async_copy(source, target, sems.at[q])
        for q, (source, target) in enumerate(zip(sources, targets))
    ]
    for copy in copies:
        copy.start()
    return copies


def loop(count, body):
    if count <= 8:
        for q in range(count):
            body(q)
    else:

        def step(q, carry):
            body(q)
            return carry

        lax.fori_loop(0, count, step, 0)


def own_chunk(sz, lane, ref, rows):
    parts = []
    if sz.main:
        parts.append(ref[rows, pl.ds(pl.multiple_of(lane * sz.main, 128), sz.main)])
    start = sz.rest * lane
    lanes = lane_iota(8)
    rest = jnp.zeros((8, 128), F32)
    for tile in range(sz.rest_tiles):
        offset = sz.main * sz.lanes + 128 * tile
        block = ref[rows, offset : min(offset + 128, ref.shape[-1])]
        if block.shape[1] < 128:
            block = jnp.concatenate([block, jnp.zeros((8, 128 - block.shape[1]), F32)], axis=1)
        inside = (lanes + 128 * tile >= start) & (lanes + 128 * tile < start + sz.rest)
        rest = rest + jnp.where(inside, block, 0.0)
    rest = pltpu.roll(rest, lax.rem(128 * sz.rest_tiles - start, 128), 1)
    parts.append(rest)
    return jnp.concatenate(parts, axis=1) if len(parts) > 1 else parts[0]


def send_ghosts(sz, send, chunks, out, tasks):
    lanes = lane_iota(1)

    def one(d):
        for g in range(sz.group):
            cell = send[0, d * sz.group + g]
            rows = []
            last = tasks
            for i in range(3):
                row = chunks[pl.ds(i * sz.rows + cell, 1), :]
                rows.append(row[:, :128] if sz.main else jnp.zeros((1, 128), F32))
                piece = jnp.where(lanes < sz.rest, row[:, sz.main : sz.main + 128], 0.0)
                last = last + (pltpu.roll(piece, i * sz.rest, 1) if i else piece)
            rows.append(last)
            for other in range(sz.lanes):
                first = ((d * sz.lanes + other) * sz.group + g) * 4
                for q, row in enumerate(rows):
                    out[pl.ds(first + q, 1), :] = row

    loop(sz.owners, one)


def pick_kernel(sz, *refs):
    inputs, (out, send_out), held, (chunks, sems) = refs[:5], refs[5:7], refs[7:12], refs[12:]
    for copy in fetch(inputs, held, sems):
        copy.wait()
    send, target, source, count, positions = held
    for j in range(send_out.shape[1]):
        send_out[0, j] = send[0, j]
    lane = lax.axis_index("lane")
    for i in range(3):
        for g in range(0, sz.cells, 8):
            value = own_chunk(sz, lane, positions.at[i], pl.ds(g, 8))
            chunks[pl.ds(i * sz.rows + g, 8), :] = value
    spare = jnp.zeros((1, 128 - sz.cap), F32)
    tasks = jnp.where(lane_iota(1) == 3 * sz.rest + 2 * sz.cap, count[0].astype(F32), 0.0)
    for q, row in enumerate((target, source)):
        wide = jnp.concatenate([row[...].astype(F32), spare], axis=1)
        tasks = tasks + pltpu.roll(wide, 3 * sz.rest + q * sz.cap, 1)
    send_ghosts(sz, send, chunks, out, tasks)


def take_ghosts(sz, arrived, pool, stride, base):
    lanes = lane_iota(1)

    def one(d):
        for g in range(sz.group):
            first = [((d * sz.lanes + lane) * sz.group + g) * 4 for lane in range(sz.lanes)]
            last = [arrived[pl.ds(row + 3, 1), :] for row in first]
            for i in range(3):
                tiles = []
                if sz.main:
                    tiles += [arrived[pl.ds(row + i, 1), :] for row in first]
                for tile in range(sz.rest_tiles):
                    total = jnp.zeros((1, 128), F32)
                    for lane in range(sz.lanes):
                        start = sz.rest * lane
                        if start + sz.rest <= 128 * tile or start >= 128 * tile + 128:
                            continue
                        shift = (start - i * sz.rest) % 128
                        value = pltpu.roll(last[lane], shift, 1) if shift else last[lane]
                        at = lanes + 128 * tile
                        total = jnp.where((at >= start) & (at < start + sz.rest), value, total)
                    tiles.append(total)
                place = pl.ds(i * stride + base + d * sz.group + g, 1)
                pool[place, :] = jnp.concatenate(tiles, axis=1)

    loop(sz.owners, one)


def build_list(sz, lists, tasks):
    total = jnp.int32(0)
    for lane in range(sz.lanes):

        def step(j, total, lane=lane):
            tasks[0, total] = lists[lane, j]
            tasks[1, total] = lists[lane, sz.cap + j]
            return total + 1

        total = lax.fori_loop(0, lists[lane, 2 * sz.cap], step, total)
    for u in range(UNROLL):
        tasks[0, total + u] = jnp.int32(sz.cells)
        tasks[1, total + u] = jnp.int32(0)
    tasks[2, 0] = total
    return total


def own_list(sz, lane, tasks, mine):
    first = lane * sz.share

    def step(t, count):
        target = tasks[0, t] - first
        mine[0, count] = target
        mine[1, count] = tasks[1, t]
        return count + ((target >= 0) & (target < sz.share)).astype(jnp.int32)

    return lax.fori_loop(0, tasks[2, 0], step, jnp.int32(0))


def products(value, bend_high, bend_low):
    high, low = split2(value)
    dot = functools.partial(jnp.dot, preferred_element_type=F32)
    return dot(high, bend_high) + dot(low, bend_high) + dot(high, bend_low)


def make_sources(sz, value, bend_high, bend_low, source_rows, centres, first):
    count = value.shape[0] // 3
    forces = products(value[:, : sz.points], bend_high, bend_low)
    forces = jnp.concatenate(
        [forces, jnp.zeros((3 * count, sz.width - sz.points), F32)], axis=1
    )
    middle = jnp.sum(value, axis=1, keepdims=True) / sz.points
    for g in range(count // 8):
        where = [i * count + 8 * g for i in range(3)]
        middles = [jnp.broadcast_to(middle[w : w + 8], (8, 128)) for w in where]
        middles += [jnp.zeros((8, 128), F32)] * 5
        for i, row in enumerate(middles):
            centres[pl.ds(8 * (first + 8 * g) + i, 8, stride=8), :] = row
        for j in range(sz.tiles):
            cut = slice(128 * j, 128 * j + 128)
            y = [value[w : w + 8, cut] - m for w, m in zip(where, middles)]
            f = [forces[w : w + 8, cut] for w in where]
            norm = y[0] * y[0] + y[1] * y[1] + y[2] * y[2] + REGULARIZE
            along = y[0] * f[0] + y[1] * f[1] + y[2] * f[2]
            one, zero = jnp.ones((8, 128), F32), jnp.zeros((8, 128), F32)
            rows = [y[0], y[1], y[2], norm, one, zero, zero, zero]
            rows += f
            rows += [y[i] * f[k] for i in range(3) for k in range(3)]
            rows += [norm * f[i] + along * y[i] for i in range(3)]
            rows += [along]
            for k, row in enumerate(rows):
                place = pl.ds(SOURCE_ROWS * (first + 8 * g) + k, 8, stride=SOURCE_ROWS)
                source_rows.at[j][place, :] = row


def make_targets(sz, blocks, targets):
    targets[...] = jnp.zeros_like(targets)
    for g in range(sz.cells // 8):
        for i in range(3):
            block = blocks(i, g)
            for j in range(targets.shape[0]):
                cut = slice(128 * j, 128 * j + 128)
                targets.at[j][pl.ds(64 * g + i, 8, stride=8), :] = block[:, cut]


def load_source(sz, source, source_rows):
    held = [
        source_rows[j, pl.ds(pl.multiple_of(SOURCE_ROWS * source, 8), SOURCE_ROWS), :]
        for j in range(sz.tiles)
    ]
    count = sz.points // 128
    whole = jnp.concatenate(held[:count], axis=1)
    y1, y2, y3 = split3(whole[:8])
    y_stack = jnp.concatenate([y1, y1, y2, y2, y1, y3], axis=0).astype(BF16)
    m_stack = jnp.concatenate(split3(whole[8:]), axis=0).astype(BF16)
    m_stack = jnp.concatenate([m_stack, m_stack], axis=1)
    if count == sz.tiles:
        return y_stack, m_stack, None, None
    last = sz.points - 128 * count
    y1, y2, y3 = split3(held[count][:8])
    y_last = jnp.concatenate([y1, y1, y2, y2, y1, y3], axis=0).astype(BF16)[:, :last]
    m_last = jnp.concatenate(split3(held[count][8:]), axis=0)
    m_last = (m_last + pltpu.roll(m_last, last, 1)).astype(BF16)[:, : 2 * last]
    return y_stack, m_stack, y_last, m_last


def load_target(j, target, slot, centre, targets, offsets):
    row = lax.broadcasted_iota(jnp.int32, (8, 128), 0)
    x = targets[j, pl.ds(pl.multiple_of(8 * target, 8), 8), :] - centre
    square = x * x
    norm = pltpu.roll(square, 2, 0) + pltpu.roll(square, 3, 0) + pltpu.roll(square, 4, 0)
    side = jnp.where(row == 4, norm, jnp.where(row == 3, 1.0, 0.0))
    x_side = jnp.where(row < 3, -2.0 * x, side)
    x1, x2, x3 = split3(x_side)
    return x, jnp.concatenate([x1, x2, x1, x2, x3, x1], axis=0).astype(BF16)


def distances(x_stack, y_stack):
    return lax.dot_general(
        x_stack, y_stack, (((0,), (0,)), ((), ())), preferred_element_type=F32
    )


def weights(shifted, axis):
    return jnp.concatenate(split2(jnp.exp2(-1.5 * jnp.log2(shifted))), axis=axis)


def tile_sums(whole, last, m_stack, m_last):
    turned = (((1,), (1,)), ((), ()))
    result = lax.dot_general(whole, m_stack, turned, preferred_element_type=F32)
    result = jnp.transpose(result)
    if last is not None:
        result = result + jnp.dot(m_last, last, preferred_element_type=F32)
    result = result[:SUM_ROWS] + result[SUM_ROWS : 2 * SUM_ROWS] + result[2 * SUM_ROWS :]
    spare = -result.shape[1] % 128
    if spare:
        result = jnp.concatenate([result, jnp.zeros((SUM_ROWS, spare), F32)], axis=1)
    return result


def sum_blocks(blocks, source):
    y_stack, m_stack, y_last, m_last = source
    whole = [distances(block, y_stack) for block in blocks]
    whole = [weights(one, 1) for one in whole]
    last = [None] * len(blocks)
    if y_last is not None:
        last = [weights(distances(y_last, block), 0) for block in blocks]
    return [tile_sums(*pair, m_stack, m_last) for pair in zip(whole, last)]


def store_sums(slots, slot, j, x, result, offsets, sums):
    offsets.at[j][pl.ds(slot, 8, stride=slots), :] = x
    for h in range(0, SUM_ROWS, 8):
        sums.at[j][pl.ds(h * slots + slot, 8, stride=slots), :] = result[h : h + 8]


def mark(slot, target, hot):
    hot[pl.ds(slot, 1), :] = jnp.where(lane_iota(1) == target, 1.0, 0.0)


def combine(sz, slots, first, total, offsets, sums, speeds):
    live = lax.broadcasted_iota(jnp.int32, (8, 128), 0) + first < total
    for j in range(offsets.shape[0]):
        x = [offsets[j, pl.ds(i * slots + first, 8), :] for i in range(3)]
        s = [sums[j, pl.ds(k * slots + first, 8), :] for k in range(SUM_ROWS)]
        a, b, c = s[:3], [s[3:6], s[6:9], s[9:12]], s[12:15]
        norm = x[0] * x[0] + x[1] * x[1] + x[2] * x[2] + REGULARIZE
        along = x[0] * a[0] + x[1] * a[1] + x[2] * a[2] - s[15]
        for i in range(3):
            speed = norm * a[i] + c[i] + along * x[i]
            for k in range(3):
                speed = speed - x[k] * (2.0 * b[k][i] + b[i][k])
            speed = jnp.where(live, speed / sz.points, 0.0)
            speeds[i, pl.ds(first, 8), 128 * j : 128 * j + 128] = speed


def add_up(sz, slots, total, rows, offsets, sums, speeds, hot):
    def eight(q, carry):
        combine(sz, slots, pl.multiple_of(8 * q, 8), total, offsets, sums, speeds)
        return carry

    lax.fori_loop(0, lax.div(total + 7, 8), eight, 0)
    one_hot = hot[...].astype(BF16)
    result = []
    for i in range(3):
        first, second, third = split3(speeds[i])
        parts = [
            lax.dot_general(
                one_hot, part.astype(BF16), (((0,), (0,)), ((), ())), preferred_element_type=F32
            )
            for part in (first, second, third)
        ]
        result.append((parts[0] + parts[1] + parts[2])[:rows])
    return result


def tiles_of_chunk(sz, total, tasks, source_rows, centres, targets, offsets, sums, hot):
    def several(q, carry):
        slots = [q * UNROLL + u for u in range(UNROLL)]
        picks = [(tasks[0, slot], tasks[1, slot]) for slot in slots]
        sources = [load_source(sz, source, source_rows) for _, source in picks]
        points = []
        for slot, (target, source) in zip(slots, picks):
            centre = centres[pl.ds(pl.multiple_of(8 * source, 8), 8), :]
            points.append(
                [
                    load_target(j, target, slot, centre, targets, offsets)
                    for j in range(sz.chunk_tiles)
                ]
            )
        stacks = [
            jnp.concatenate([stack for _, stack in point], axis=1)[:, : sz.chunk]
            for point in points
        ]
        whole = [distances(stack, source[0]) for stack, source in zip(stacks, sources)]
        whole = [weights(one, 1) for one in whole]
        last = [None] * UNROLL
        if sources[0][2] is not None:
            last = [distances(source[2], stack) for stack, source in zip(stacks, sources)]
            last = [weights(one, 0) for one in last]
        results = [
            tile_sums(*pair, source[1], source[3])
            for pair, source in zip(zip(whole, last), sources)
        ]
        for slot, (target, _), point, result in zip(slots, picks, points, results):
            for j in range(sz.chunk_tiles):
                cut = result[:, 128 * j : 128 * j + 128]
                store_sums(sz.slots, slot, j, point[j][0], cut, offsets, sums)
            mark(slot, target, hot)
        return carry

    lax.fori_loop(0, lax.div(total + UNROLL - 1, UNROLL), several, 0)


def tiles_of_cells(sz, first, total, mine, source_rows, centres, targets, offsets, sums, hot):
    def single(slot, carry):
        target, source = mine[0, slot], mine[1, slot]
        held = load_source(sz, source, source_rows)
        centre = centres[pl.ds(pl.multiple_of(8 * source, 8), 8), :]
        points = [
            load_target(j, target + first, slot, centre, targets, offsets)
            for j in range(sz.tiles)
        ]
        stacks = [
            stack[:, : min(128, sz.points - 128 * j)] for j, (_, stack) in enumerate(points)
        ]
        results = sum_blocks(stacks, held)
        for j in range(sz.tiles):
            store_sums(sz.own, slot, j, points[j][0], results[j], offsets, sums)
        mark(slot, target, hot)
        return carry

    lax.fori_loop(0, total, single, 0)


def packed(sz, blocks):
    rows = [b[:, : sz.main] for b in blocks] if sz.main else []
    lanes = lane_iota(8)
    for p in range(0, len(blocks), sz.per_pack):
        total = jnp.zeros((8, 128), F32)
        for q, block in enumerate(blocks[p : p + sz.per_pack]):
            rest = jnp.where(lanes < sz.rest, block[:, sz.main : sz.main + 128], 0.0)
            total = total + (pltpu.roll(rest, q * sz.rest, 1) if q else rest)
        rows.append(total)
    return rows


def store_packed(sz, out, blocks):
    first = 0
    count = len(blocks)
    values = packed(sz, blocks)
    if sz.main:
        for b in range(count):
            for m in range(sz.main // 128):
                out[pl.ds(first, 8), :] = values[b][:, 128 * m : 128 * m + 128]
                first += 8
        values = values[count:]
    for value in values:
        out[pl.ds(first, 8), :] = value
        first += 8


def place_packed(sz, lane, arrived, count, store_main, add_rest):
    first = 0
    if sz.main:
        for b in range(count):
            for m in range(sz.main // 128):
                store_main(b, m, arrived[pl.ds(first, 8), :])
                first += 8
    start = sz.rest * lane
    lanes = lane_iota(8)
    for b in range(count):
        pack, q = divmod(b, sz.per_pack)
        value = arrived[pl.ds(first + 8 * pack, 8), :]
        value = pltpu.roll(value, lax.rem(start - q * sz.rest + 128, 128), 1)
        for tile in range(sz.rest_tiles):
            inside = (lanes + 128 * tile >= start) & (lanes + 128 * tile < start + sz.rest)
            add_rest(b, tile, jnp.where(inside, value, 0.0))


def source_kernel(sz, *refs):
    inputs, (high_out, low_out, source_rows, centres), held, sems = (
        refs[:2],
        refs[2:6],
        refs[6:8],
        refs[8],
    )
    for copy in fetch(inputs, held, sems):
        copy.wait()
    positions, bend = held
    high_out[...], low_out[...] = split2(bend[...])
    value = jnp.concatenate([positions[i] for i in range(3)], axis=0)
    value = jnp.concatenate(
        [value, jnp.zeros((3 * sz.cells, sz.width - sz.points), F32)], axis=1
    )
    make_sources(sz, value, high_out[...], low_out[...], source_rows, centres, 0)


def first_kernel(sz, *refs):
    inputs, (chunk_out, ghost_out, tasks), refs = refs[:7], refs[7:10], refs[10:]
    source_rows, centres, targets, offsets, sums, speeds, hot, moved, pool = refs[:9]
    send, positions, arrived, high, low, staged, lists, sems = refs[9:]
    me, lane = lax.axis_index("space"), lax.axis_index("lane")
    own_rows = source_rows.at[:, pl.ds(0, SOURCE_ROWS * sz.cells)]
    own_centres = centres.at[pl.ds(0, 8 * sz.cells)]
    held = [arrived, send, positions, high, low, own_rows, own_centres]
    copies = fetch(inputs, held, sems)
    copies[0].wait()
    for other in range(sz.lanes):
        row = ((me * sz.lanes + other) * sz.group) * 4 + 3
        value = pltpu.roll(arrived[pl.ds(row, 1), :], 128 - 3 * sz.rest, 1)
        staged[pl.ds(other, 1), :] = value.astype(jnp.int32)
    copies.append(pltpu.make_async_copy(staged, lists, sems.at[7]))
    copies[7].start()
    pool[...] = jnp.zeros_like(pool)
    take_ghosts(sz, arrived, pool, up(sz.owners * sz.group, 8), 0)
    hot[...] = jnp.zeros_like(hot)
    speeds[...] = jnp.zeros_like(speeds)
    for copy in copies[1:5]:
        copy.wait()
    make_sources(sz, pool[...], high[...], low[...], source_rows, centres, sz.cells)
    make_targets(
        sz, lambda i, g: own_chunk(sz, lane, positions.at[i], pl.ds(8 * g, 8)), targets
    )
    for copy in copies[5:]:
        copy.wait()
    total = build_list(sz, lists, tasks)
    tiles_of_chunk(sz, total, tasks, source_rows, centres, targets, offsets, sums, hot)
    velocity = add_up(sz, sz.slots, total, sz.cells, offsets, sums, speeds, hot)
    blocks = []
    for i in range(3):
        for g in range(0, sz.cells, 8):
            chunk = own_chunk(sz, lane, positions.at[i], pl.ds(g, 8))
            block = chunk + TIME_STEP * velocity[i][g : g + 8]
            moved[pl.ds(i * sz.rows + g, 8), :] = block
            blocks.append(block)
    store_packed(sz, chunk_out, blocks)
    send_ghosts(sz, send, moved, ghost_out, jnp.zeros((1, 128), F32))


def second_kernel(sz, *refs):
    count = sz.lanes + 4
    inputs, (moved_out, velocity_out), refs = refs[:count], refs[count : count + 2], refs[count + 2 :]
    source_rows, centres, targets, offsets, sums, speeds, hot, pool, mine = refs[:9]
    held, sems = refs[9:-1], refs[-1]
    copies = fetch(inputs, held, sems)
    tasks, arrived, chunks, (high, low) = held[0], held[1], held[2:-2], held[-2:]
    hot[...] = jnp.zeros_like(hot)
    speeds[...] = jnp.zeros_like(speeds)
    lane = lax.axis_index("lane")
    pool[...] = jnp.zeros_like(pool)
    for copy in copies[:-2]:
        copy.wait()
    per = sz.cells // 8
    for k in range(sz.lanes):
        other = lane ^ k

        def row_of(b):
            return (b // per) * sz.pool + 8 * (b % per)

        def store_main(b, m, value):
            cut = pl.ds(pl.multiple_of(other * sz.main + 128 * m, 128), 128)
            pool[pl.ds(row_of(b), 8), cut] = value

        def add_rest(b, tile, value):
            offset = sz.main * sz.lanes + 128 * tile
            cut = (pl.ds(row_of(b), 8), slice(offset, offset + 128))
            pool[cut] = pool[cut] + value

        place_packed(sz, other, chunks[k], 3 * per, store_main, add_rest)
    take_ghosts(sz, arrived, pool, sz.pool, sz.cells)
    total = own_list(sz, lane, tasks, mine)
    for copy in copies[-2:]:
        copy.wait()
    make_sources(sz, pool[...], high[...], low[...], source_rows, centres, 0)
    make_targets(sz, lambda i, g: pool[pl.ds(i * sz.pool + 8 * g, 8), :], targets)
    first = lane * sz.share
    tiles_of_cells(sz, first, total, mine, source_rows, centres, targets, offsets, sums, hot)
    velocity = add_up(sz, sz.own, total, up(sz.share, 8), offsets, sums, speeds, hot)
    for i in range(3):
        speed = velocity[i]
        moved = share_rows(sz, pool, i * sz.pool, lane) + TIME_STEP * speed
        velocity_out[i] = speed[: sz.share, : sz.points]
        moved_out[i] = moved[: sz.share, : sz.points]


def share_rows(sz, ref, base, lane):
    if sz.share % 8 == 0:
        return ref[pl.ds(pl.multiple_of(base + lane * sz.share, 8), sz.share), :]
    rows = [ref[pl.ds(base + lane * sz.share + c, 1), :] for c in range(sz.share)]
    rows.append(jnp.zeros((8 - sz.share, rows[0].shape[1]), F32))
    return jnp.concatenate(rows, axis=0)


def scratch(sz, tiles, slots):
    return [
        pltpu.VMEM((sz.tiles, SOURCE_ROWS * sz.pool, 128), F32),
        pltpu.VMEM((8 * sz.pool, 128), F32),
        pltpu.VMEM((tiles, 8 * sz.rows, 128), F32),
        pltpu.VMEM((tiles, 8 * slots, 128), F32),
        pltpu.VMEM((tiles, SUM_ROWS * slots, 128), F32),
        pltpu.VMEM((3, slots, 128 * tiles), F32),
        pltpu.VMEM((slots, 128), F32),
    ]


def swap(value, axis, size, k):
    return lax.ppermute(value, axis, [(d, d ^ k) for d in range(size)])


def shards(positions, bend_op, send_list, task_target, task_source, task_count):
    owners, lanes = lax.axis_size("space"), lax.axis_size("lane")
    cells, points = positions.shape[0], positions.shape[2]
    sz = sizes(owners, lanes, cells, points, task_target.shape[1], send_list.shape[1])
    params = pltpu.CompilerParams(vmem_limit_bytes=60 << 20)
    shape = jax.ShapeDtypeStruct
    both = ("space", "lane")
    by_component = jnp.transpose(positions, (1, 0, 2))
    list_rows = up(lanes, 8)
    slot_shape = shape((4 * sz.group * owners * lanes, 128), F32)
    leaving, send = pl.pallas_call(
        functools.partial(pick_kernel, sz),
        out_shape=[slot_shape, shape(send_list.shape, jnp.int32)],
        in_specs=[HBM] * 5,
        out_specs=[VMEM, SMEM],
        scratch_shapes=[
            pltpu.SMEM(send_list.shape, jnp.int32),
            pltpu.VMEM(task_target.shape, jnp.int32),
            pltpu.VMEM(task_source.shape, jnp.int32),
            pltpu.SMEM(task_count.shape, jnp.int32),
            pltpu.VMEM(by_component.shape, F32),
            pltpu.VMEM((3 * sz.rows, sz.chunk_wide), F32),
            pltpu.SemaphoreType.DMA((5,)),
        ],
        compiler_params=params,
        name="pick_cells",
    )(send_list, task_target, task_source, task_count, by_component)
    arrived = lax.all_to_all(leaving, both, split_axis=0, concat_axis=0, tiled=True)
    high, low, own_rows, own_centres = pl.pallas_call(
        functools.partial(source_kernel, sz),
        out_shape=[
            shape(bend_op.shape, BF16),
            shape(bend_op.shape, BF16),
            shape((sz.tiles, SOURCE_ROWS * cells, 128), F32),
            shape((8 * cells, 128), F32),
        ],
        in_specs=[HBM] * 2,
        out_specs=[VMEM] * 4,
        scratch_shapes=[
            pltpu.VMEM(by_component.shape, F32),
            pltpu.VMEM(bend_op.shape, F32),
            pltpu.SemaphoreType.DMA((2,)),
        ],
        compiler_params=params,
        cost_estimate=pl.CostEstimate(flops=10**9, bytes_accessed=10**7, transcendentals=0),
        name="first_sources",
    )(by_component, bend_op)
    chunk, leaving, tasks = pl.pallas_call(
        functools.partial(first_kernel, sz),
        out_shape=[
            shape((pack_rows(sz, cells), 128), F32),
            slot_shape,
            shape((3, sz.slots), jnp.int32),
        ],
        in_specs=[HBM] * 7,
        out_specs=[VMEM, VMEM, SMEM],
        scratch_shapes=scratch(sz, sz.chunk_tiles, sz.slots)
        + [
            pltpu.VMEM((3 * sz.rows, sz.chunk_wide), F32),
            pltpu.VMEM((3 * up(sz.owners * sz.group, 8), sz.width), F32),
            pltpu.SMEM(send_list.shape, jnp.int32),
            pltpu.VMEM(by_component.shape, F32),
            pltpu.VMEM(slot_shape.shape, F32),
            pltpu.VMEM(bend_op.shape, BF16),
            pltpu.VMEM(bend_op.shape, BF16),
            pltpu.VMEM((list_rows, 128), jnp.int32),
            pltpu.SMEM((list_rows, 128), jnp.int32),
            pltpu.SemaphoreType.DMA((8,)),
        ],
        compiler_params=params,
        name="first_step",
    )(arrived, send, by_component, high, low, own_rows, own_centres)
    arrived = lax.all_to_all(leaving, both, split_axis=0, concat_axis=0, tiled=True)
    chunks = [chunk] + [swap(chunk, "lane", lanes, k) for k in range(1, lanes)]
    result = shape((3, sz.share, points), F32)
    outputs = pl.pallas_call(
        functools.partial(second_kernel, sz),
        out_shape=[result, result],
        in_specs=[HBM] * (lanes + 4),
        out_specs=[VMEM] * 2,
        scratch_shapes=scratch(sz, sz.tiles, sz.own)
        + [
            pltpu.VMEM((3 * sz.pool, sz.width), F32),
            pltpu.SMEM((2, sz.own + 8), jnp.int32),
            pltpu.SMEM(tasks.shape, jnp.int32),
            pltpu.VMEM(slot_shape.shape, F32),
        ]
        + [pltpu.VMEM(chunk.shape, F32)] * lanes
        + [pltpu.VMEM(bend_op.shape, BF16)] * 2
        + [pltpu.SemaphoreType.DMA((lanes + 4,))],
        compiler_params=params,
        name="second_step",
    )(tasks, arrived, *chunks, high, low)
    return tuple(jnp.transpose(output, (1, 0, 2)) for output in outputs)


def solution(mesh):
    in_specs = (
        P("space", None, None),
        P(),
        P("space", None),
        P(("space", "lane"), None),
        P(("space", "lane"), None),
        P(("space", "lane")),
    )
    out_specs = (P(("space", "lane"), None, None), P(("space", "lane"), None, None))
    return jax.shard_map(shards, mesh=mesh, in_specs=in_specs, out_specs=out_specs, check_vma=False)
```

```python
import functools
from types import SimpleNamespace

import jax
import jax.numpy as jnp
from jax import lax
from jax.experimental import pallas as pl
from jax.experimental.pallas import tpu as pltpu
from jax.sharding import PartitionSpec as P

REGULARIZE = 0.25
TIME_STEP = 0.5
UNROLL = 4
SOURCE_ROWS = 24
SUM_ROWS = 16

F32 = jnp.float32
BF16 = jnp.bfloat16
VMEM = pl.BlockSpec(memory_space=pltpu.VMEM)
SMEM = pl.BlockSpec(memory_space=pltpu.SMEM)
HBM = pl.BlockSpec(memory_space=pltpu.HBM)


def up(value, step):
    return -(-value // step) * step


def sizes(owners, lanes, cells, points, cap, listed):
    main = 128 * (points // (128 * lanes))
    rest = (points - main * lanes) // lanes
    group = listed // owners
    pool = up(cells + listed, 8)
    per_pack = 128 // rest
    return SimpleNamespace(
        owners=owners,
        lanes=lanes,
        cells=cells,
        points=points,
        cap=cap,
        group=group,
        width=up(points, 128),
        tiles=up(points, 128) // 128,
        main=main,
        rest=rest,
        rest_tiles=up(rest * lanes, 128) // 128,
        chunk=main + rest,
        chunk_wide=main + up(rest, 128),
        chunk_tiles=(main + up(rest, 128)) // 128,
        per_pack=per_pack,
        pool=pool,
        share=cells // lanes,
        slots=up(lanes * cap + UNROLL, 8),
        rows=cells + 8,
        own=up(lanes * cap, 8),
    )


def pack_rows(sz, rows):
    return (3 * rows * sz.main // 128) + 8 * up(3 * rows // 8, sz.per_pack) // sz.per_pack


def split2(value):
    high = value.astype(BF16)
    return high, (value - high.astype(F32)).astype(BF16)


def split3(value):
    first = value.astype(BF16).astype(F32)
    left = value - first
    second = left.astype(BF16).astype(F32)
    return first, second, left - second


def lane_iota(rows):
    return lax.broadcasted_iota(jnp.int32, (rows, 128), 1)


def fetch(sources, targets, sems):
    copies = [
        pltpu.make_async_copy(source, target, sems.at[q])
        for q, (source, target) in enumerate(zip(sources, targets))
    ]
    for copy in copies:
        copy.start()
    return copies


def loop(count, body):
    if count <= 8:
        for q in range(count):
            body(q)
    else:

        def step(q, carry):
            body(q)
            return carry

        lax.fori_loop(0, count, step, 0)


def own_chunk(sz, lane, ref, rows):
    parts = []
    if sz.main:
        parts.append(ref[rows, pl.ds(pl.multiple_of(lane * sz.main, 128), sz.main)])
    start = sz.rest * lane
    lanes = lane_iota(8)
    rest = jnp.zeros((8, 128), F32)
    for tile in range(sz.rest_tiles):
        offset = sz.main * sz.lanes + 128 * tile
        block = ref[rows, offset : min(offset + 128, ref.shape[-1])]
        if block.shape[1] < 128:
            block = jnp.concatenate([block, jnp.zeros((8, 128 - block.shape[1]), F32)], axis=1)
        inside = (lanes + 128 * tile >= start) & (lanes + 128 * tile < start + sz.rest)
        rest = rest + jnp.where(inside, block, 0.0)
    rest = pltpu.roll(rest, lax.rem(128 * sz.rest_tiles - start, 128), 1)
    parts.append(rest)
    return jnp.concatenate(parts, axis=1) if len(parts) > 1 else parts[0]


def send_ghosts(sz, send, chunks, out, tasks):
    lanes = lane_iota(1)

    def one(d):
        for g in range(sz.group):
            cell = send[0, d * sz.group + g]
            rows = []
            last = tasks
            for i in range(3):
                row = chunks[pl.ds(i * sz.rows + cell, 1), :]
                rows.append(row[:, :128] if sz.main else jnp.zeros((1, 128), F32))
                piece = jnp.where(lanes < sz.rest, row[:, sz.main : sz.main + 128], 0.0)
                last = last + (pltpu.roll(piece, i * sz.rest, 1) if i else piece)
            rows.append(last)
            for other in range(sz.lanes):
                first = ((d * sz.lanes + other) * sz.group + g) * 4
                for q, row in enumerate(rows):
                    out[pl.ds(first + q, 1), :] = row

    loop(sz.owners, one)


def pick_kernel(sz, *refs):
    inputs, (out, send_out), held, (chunks, sems) = refs[:5], refs[5:7], refs[7:12], refs[12:]
    for copy in fetch(inputs, held, sems):
        copy.wait()
    send, target, source, count, positions = held
    for j in range(send_out.shape[1]):
        send_out[0, j] = send[0, j]
    lane = lax.axis_index("lane")
    for i in range(3):
        for g in range(0, sz.cells, 8):
            value = own_chunk(sz, lane, positions.at[i], pl.ds(g, 8))
            chunks[pl.ds(i * sz.rows + g, 8), :] = value
    spare = jnp.zeros((1, 128 - sz.cap), F32)
    tasks = jnp.where(lane_iota(1) == 3 * sz.rest + 2 * sz.cap, count[0].astype(F32), 0.0)
    for q, row in enumerate((target, source)):
        wide = jnp.concatenate([row[...].astype(F32), spare], axis=1)
        tasks = tasks + pltpu.roll(wide, 3 * sz.rest + q * sz.cap, 1)
    send_ghosts(sz, send, chunks, out, tasks)


def take_ghosts(sz, arrived, pool, stride, base):
    lanes = lane_iota(1)

    def one(d):
        for g in range(sz.group):
            first = [((d * sz.lanes + lane) * sz.group + g) * 4 for lane in range(sz.lanes)]
            last = [arrived[pl.ds(row + 3, 1), :] for row in first]
            for i in range(3):
                tiles = []
                if sz.main:
                    tiles += [arrived[pl.ds(row + i, 1), :] for row in first]
                for tile in range(sz.rest_tiles):
                    total = jnp.zeros((1, 128), F32)
                    for lane in range(sz.lanes):
                        start = sz.rest * lane
                        if start + sz.rest <= 128 * tile or start >= 128 * tile + 128:
                            continue
                        shift = (start - i * sz.rest) % 128
                        value = pltpu.roll(last[lane], shift, 1) if shift else last[lane]
                        at = lanes + 128 * tile
                        total = jnp.where((at >= start) & (at < start + sz.rest), value, total)
                    tiles.append(total)
                place = pl.ds(i * stride + base + d * sz.group + g, 1)
                pool[place, :] = jnp.concatenate(tiles, axis=1)

    loop(sz.owners, one)


def build_list(sz, lists, tasks):
    total = jnp.int32(0)
    for lane in range(sz.lanes):

        def step(j, total, lane=lane):
            tasks[0, total] = lists[lane, j]
            tasks[1, total] = lists[lane, sz.cap + j]
            return total + 1

        total = lax.fori_loop(0, lists[lane, 2 * sz.cap], step, total)
    for u in range(UNROLL):
        tasks[0, total + u] = jnp.int32(sz.cells)
        tasks[1, total + u] = jnp.int32(0)
    tasks[2, 0] = total
    return total


def own_list(sz, lane, tasks, mine):
    first = lane * sz.share

    def step(t, count):
        target = tasks[0, t] - first
        mine[0, count] = target
        mine[1, count] = tasks[1, t]
        return count + ((target >= 0) & (target < sz.share)).astype(jnp.int32)

    return lax.fori_loop(0, tasks[2, 0], step, jnp.int32(0))


def products(value, bend_high, bend_low):
    high, low = split2(value)
    dot = functools.partial(jnp.dot, preferred_element_type=F32)
    return dot(high, bend_high) + dot(low, bend_high) + dot(high, bend_low)


def make_sources(sz, value, bend_high, bend_low, source_rows, centres, first):
    count = value.shape[0] // 3
    forces = products(value[:, : sz.points], bend_high, bend_low)
    forces = jnp.concatenate(
        [forces, jnp.zeros((3 * count, sz.width - sz.points), F32)], axis=1
    )
    middle = jnp.sum(value, axis=1, keepdims=True) / sz.points
    for g in range(count // 8):
        where = [i * count + 8 * g for i in range(3)]
        middles = [jnp.broadcast_to(middle[w : w + 8], (8, 128)) for w in where]
        middles += [jnp.zeros((8, 128), F32)] * 5
        for i, row in enumerate(middles):
            centres[pl.ds(8 * (first + 8 * g) + i, 8, stride=8), :] = row
        for j in range(sz.tiles):
            cut = slice(128 * j, 128 * j + 128)
            y = [value[w : w + 8, cut] - m for w, m in zip(where, middles)]
            f = [forces[w : w + 8, cut] for w in where]
            norm = y[0] * y[0] + y[1] * y[1] + y[2] * y[2] + REGULARIZE
            along = y[0] * f[0] + y[1] * f[1] + y[2] * f[2]
            one, zero = jnp.ones((8, 128), F32), jnp.zeros((8, 128), F32)
            rows = [y[0], y[1], y[2], norm, one, zero, zero, zero]
            rows += f
            rows += [y[i] * f[k] for i in range(3) for k in range(3)]
            rows += [norm * f[i] + along * y[i] for i in range(3)]
            rows += [along]
            for k, row in enumerate(rows):
                place = pl.ds(SOURCE_ROWS * (first + 8 * g) + k, 8, stride=SOURCE_ROWS)
                source_rows.at[j][place, :] = row


def make_targets(sz, blocks, targets):
    targets[...] = jnp.zeros_like(targets)
    for g in range(sz.cells // 8):
        for i in range(3):
            block = blocks(i, g)
            for j in range(targets.shape[0]):
                cut = slice(128 * j, 128 * j + 128)
                targets.at[j][pl.ds(64 * g + i, 8, stride=8), :] = block[:, cut]


def load_source(sz, source, source_rows):
    held = [
        source_rows[j, pl.ds(pl.multiple_of(SOURCE_ROWS * source, 8), SOURCE_ROWS), :]
        for j in range(sz.tiles)
    ]
    count = sz.points // 128
    whole = jnp.concatenate(held[:count], axis=1)
    y1, y2, y3 = split3(whole[:8])
    y_stack = jnp.concatenate([y1, y1, y2, y2, y1, y3], axis=0).astype(BF16)
    m_stack = jnp.transpose(jnp.concatenate(split3(whole[8:]), axis=0).astype(BF16))
    m_stack = jnp.concatenate([m_stack, m_stack], axis=0)
    if count == sz.tiles:
        return y_stack, m_stack, None, None
    last = sz.points - 128 * count
    y1, y2, y3 = split3(held[count][:8])
    y_last = jnp.concatenate([y1, y1, y2, y2, y1, y3], axis=0).astype(BF16)
    y_last = jnp.transpose(y_last)[:last]
    m_last = jnp.concatenate(split3(held[count][8:]), axis=0)
    m_last = (m_last + pltpu.roll(m_last, last, 1)).astype(BF16)[:, : 2 * last]
    return y_stack, m_stack, y_last, m_last


def load_target(j, target, slot, centre, targets, offsets):
    row = lax.broadcasted_iota(jnp.int32, (8, 128), 0)
    x = targets[j, pl.ds(pl.multiple_of(8 * target, 8), 8), :] - centre
    square = x * x
    norm = pltpu.roll(square, 2, 0) + pltpu.roll(square, 3, 0) + pltpu.roll(square, 4, 0)
    side = jnp.where(row == 4, norm, jnp.where(row == 3, 1.0, 0.0))
    x_side = jnp.where(row < 3, -2.0 * x, side)
    x1, x2, x3 = split3(x_side)
    return x, jnp.concatenate([x1, x2, x1, x2, x3, x1], axis=0).astype(BF16)


def distances(one_stack, other_stack):
    return jnp.dot(one_stack, other_stack, preferred_element_type=F32)


def weights(shifted, axis):
    inverse = lax.rsqrt(shifted)
    return jnp.concatenate(split2(inverse * inverse * inverse), axis=axis)


def tile_sums(whole, last, m_stack, m_last):
    result = jnp.transpose(jnp.dot(whole, m_stack, preferred_element_type=F32))
    if last is not None:
        result = result + jnp.dot(m_last, last, preferred_element_type=F32)
    result = result[:SUM_ROWS] + result[SUM_ROWS : 2 * SUM_ROWS] + result[2 * SUM_ROWS :]
    spare = -result.shape[1] % 128
    if spare:
        result = jnp.concatenate([result, jnp.zeros((SUM_ROWS, spare), F32)], axis=1)
    return result


def sum_blocks(blocks, source):
    y_stack, m_stack, y_last, m_last = source
    whole = [distances(jnp.transpose(block), y_stack) for block in blocks]
    whole = [weights(one, 1) for one in whole]
    last = [None] * len(blocks)
    if y_last is not None:
        last = [weights(distances(y_last, block), 0) for block in blocks]
    return [tile_sums(*pair, m_stack, m_last) for pair in zip(whole, last)]


def store_sums(slots, slot, j, x, result, offsets, sums):
    offsets.at[j][pl.ds(slot, 8, stride=slots), :] = x
    for h in range(0, SUM_ROWS, 8):
        sums.at[j][pl.ds(h * slots + slot, 8, stride=slots), :] = result[h : h + 8]


def mark(slot, target, hot):
    hot[pl.ds(slot, 1), :] = jnp.where(lane_iota(1) == target, 1.0, 0.0)


def combine(sz, slots, first, total, offsets, sums, speeds):
    live = lax.broadcasted_iota(jnp.int32, (8, 128), 0) + first < total
    for j in range(offsets.shape[0]):
        x = [offsets[j, pl.ds(i * slots + first, 8), :] for i in range(3)]
        s = [sums[j, pl.ds(k * slots + first, 8), :] for k in range(SUM_ROWS)]
        a, b, c = s[:3], [s[3:6], s[6:9], s[9:12]], s[12:15]
        norm = x[0] * x[0] + x[1] * x[1] + x[2] * x[2] + REGULARIZE
        along = x[0] * a[0] + x[1] * a[1] + x[2] * a[2] - s[15]
        for i in range(3):
            speed = norm * a[i] + c[i] + along * x[i]
            for k in range(3):
                speed = speed - x[k] * (2.0 * b[k][i] + b[i][k])
            speed = jnp.where(live, speed / sz.points, 0.0)
            speeds[i, pl.ds(first, 8), 128 * j : 128 * j + 128] = speed


def add_up(sz, slots, total, rows, offsets, sums, speeds, hot):
    def eight(q, carry):
        combine(sz, slots, pl.multiple_of(8 * q, 8), total, offsets, sums, speeds)
        return carry

    lax.fori_loop(0, lax.div(total + 7, 8), eight, 0)
    one_hot = hot[...].astype(BF16)
    result = []
    for i in range(3):
        first, second, third = split3(speeds[i])
        parts = [
            lax.dot_general(
                one_hot, part.astype(BF16), (((0,), (0,)), ((), ())), preferred_element_type=F32
            )
            for part in (first, second, third)
        ]
        result.append((parts[0] + parts[1] + parts[2])[:rows])
    return result


def tiles_of_chunk(sz, total, tasks, source_rows, centres, targets, offsets, sums, hot):
    def several(q, carry):
        slots = [q * UNROLL + u for u in range(UNROLL)]
        picks = [(tasks[0, slot], tasks[1, slot]) for slot in slots]
        sources = [load_source(sz, source, source_rows) for _, source in picks]
        points = []
        for slot, (target, source) in zip(slots, picks):
            centre = centres[pl.ds(pl.multiple_of(8 * source, 8), 8), :]
            points.append(
                [
                    load_target(j, target, slot, centre, targets, offsets)
                    for j in range(sz.chunk_tiles)
                ]
            )
        stacks = [
            jnp.concatenate([stack for _, stack in point], axis=1)[:, : sz.chunk]
            for point in points
        ]
        whole = [
            distances(jnp.transpose(stack), source[0]) for stack, source in zip(stacks, sources)
        ]
        whole = [weights(one, 1) for one in whole]
        last = [None] * UNROLL
        if sources[0][2] is not None:
            last = [distances(source[2], stack) for stack, source in zip(stacks, sources)]
            last = [weights(one, 0) for one in last]
        results = [
            tile_sums(*pair, source[1], source[3])
            for pair, source in zip(zip(whole, last), sources)
        ]
        for slot, (target, _), point, result in zip(slots, picks, points, results):
            for j in range(sz.chunk_tiles):
                cut = result[:, 128 * j : 128 * j + 128]
                store_sums(sz.slots, slot, j, point[j][0], cut, offsets, sums)
            mark(slot, target, hot)
        return carry

    lax.fori_loop(0, lax.div(total + UNROLL - 1, UNROLL), several, 0)


def tiles_of_cells(sz, first, total, mine, source_rows, centres, targets, offsets, sums, hot):
    def single(slot, carry):
        target, source = mine[0, slot], mine[1, slot]
        held = load_source(sz, source, source_rows)
        centre = centres[pl.ds(pl.multiple_of(8 * source, 8), 8), :]
        points = [
            load_target(j, target + first, slot, centre, targets, offsets)
            for j in range(sz.tiles)
        ]
        stacks = [
            stack[:, : min(128, sz.points - 128 * j)] for j, (_, stack) in enumerate(points)
        ]
        results = sum_blocks(stacks, held)
        for j in range(sz.tiles):
            store_sums(sz.own, slot, j, points[j][0], results[j], offsets, sums)
        mark(slot, target, hot)
        return carry

    lax.fori_loop(0, total, single, 0)


def packed(sz, blocks):
    rows = [b[:, : sz.main] for b in blocks] if sz.main else []
    lanes = lane_iota(8)
    for p in range(0, len(blocks), sz.per_pack):
        total = jnp.zeros((8, 128), F32)
        for q, block in enumerate(blocks[p : p + sz.per_pack]):
            rest = jnp.where(lanes < sz.rest, block[:, sz.main : sz.main + 128], 0.0)
            total = total + (pltpu.roll(rest, q * sz.rest, 1) if q else rest)
        rows.append(total)
    return rows


def store_packed(sz, out, blocks):
    first = 0
    count = len(blocks)
    values = packed(sz, blocks)
    if sz.main:
        for b in range(count):
            for m in range(sz.main // 128):
                out[pl.ds(first, 8), :] = values[b][:, 128 * m : 128 * m + 128]
                first += 8
        values = values[count:]
    for value in values:
        out[pl.ds(first, 8), :] = value
        first += 8


def place_packed(sz, lane, arrived, count, store_main, add_rest):
    first = 0
    if sz.main:
        for b in range(count):
            for m in range(sz.main // 128):
                store_main(b, m, arrived[pl.ds(first, 8), :])
                first += 8
    start = sz.rest * lane
    lanes = lane_iota(8)
    for b in range(count):
        pack, q = divmod(b, sz.per_pack)
        value = arrived[pl.ds(first + 8 * pack, 8), :]
        value = pltpu.roll(value, lax.rem(start - q * sz.rest + 128, 128), 1)
        for tile in range(sz.rest_tiles):
            inside = (lanes + 128 * tile >= start) & (lanes + 128 * tile < start + sz.rest)
            add_rest(b, tile, jnp.where(inside, value, 0.0))


def source_kernel(sz, *refs):
    inputs, (high_out, low_out, source_rows, centres), held, sems = (
        refs[:2],
        refs[2:6],
        refs[6:8],
        refs[8],
    )
    for copy in fetch(inputs, held, sems):
        copy.wait()
    positions, bend = held
    high_out[...], low_out[...] = split2(bend[...])
    value = jnp.concatenate([positions[i] for i in range(3)], axis=0)
    value = jnp.concatenate(
        [value, jnp.zeros((3 * sz.cells, sz.width - sz.points), F32)], axis=1
    )
    make_sources(sz, value, high_out[...], low_out[...], source_rows, centres, 0)


def first_kernel(sz, *refs):
    inputs, (chunk_out, ghost_out, tasks), refs = refs[:7], refs[7:10], refs[10:]
    source_rows, centres, targets, offsets, sums, speeds, hot, moved, pool = refs[:9]
    send, positions, arrived, high, low, staged, lists, sems = refs[9:]
    me, lane = lax.axis_index("space"), lax.axis_index("lane")
    own_rows = source_rows.at[:, pl.ds(0, SOURCE_ROWS * sz.cells)]
    own_centres = centres.at[pl.ds(0, 8 * sz.cells)]
    held = [arrived, send, positions, high, low, own_rows, own_centres]
    copies = fetch(inputs, held, sems)
    copies[0].wait()
    for other in range(sz.lanes):
        row = ((me * sz.lanes + other) * sz.group) * 4 + 3
        value = pltpu.roll(arrived[pl.ds(row, 1), :], 128 - 3 * sz.rest, 1)
        staged[pl.ds(other, 1), :] = value.astype(jnp.int32)
    copies.append(pltpu.make_async_copy(staged, lists, sems.at[7]))
    copies[7].start()
    pool[...] = jnp.zeros_like(pool)
    take_ghosts(sz, arrived, pool, up(sz.owners * sz.group, 8), 0)
    hot[...] = jnp.zeros_like(hot)
    speeds[...] = jnp.zeros_like(speeds)
    for copy in copies[1:5]:
        copy.wait()
    make_sources(sz, pool[...], high[...], low[...], source_rows, centres, sz.cells)
    make_targets(
        sz, lambda i, g: own_chunk(sz, lane, positions.at[i], pl.ds(8 * g, 8)), targets
    )
    for copy in copies[5:]:
        copy.wait()
    total = build_list(sz, lists, tasks)
    tiles_of_chunk(sz, total, tasks, source_rows, centres, targets, offsets, sums, hot)
    velocity = add_up(sz, sz.slots, total, sz.cells, offsets, sums, speeds, hot)
    blocks = []
    for i in range(3):
        for g in range(0, sz.cells, 8):
            chunk = own_chunk(sz, lane, positions.at[i], pl.ds(g, 8))
            block = chunk + TIME_STEP * velocity[i][g : g + 8]
            moved[pl.ds(i * sz.rows + g, 8), :] = block
            blocks.append(block)
    store_packed(sz, chunk_out, blocks)
    send_ghosts(sz, send, moved, ghost_out, jnp.zeros((1, 128), F32))


def second_kernel(sz, *refs):
    count = sz.lanes + 4
    inputs, (moved_out, velocity_out), refs = refs[:count], refs[count : count + 2], refs[count + 2 :]
    source_rows, centres, targets, offsets, sums, speeds, hot, pool, mine = refs[:9]
    held, sems = refs[9:-1], refs[-1]
    copies = fetch(inputs, held, sems)
    tasks, arrived, chunks, (high, low) = held[0], held[1], held[2:-2], held[-2:]
    hot[...] = jnp.zeros_like(hot)
    speeds[...] = jnp.zeros_like(speeds)
    lane = lax.axis_index("lane")
    pool[...] = jnp.zeros_like(pool)
    for copy in copies[:-2]:
        copy.wait()
    per = sz.cells // 8
    for k in range(sz.lanes):
        other = lane ^ k

        def row_of(b):
            return (b // per) * sz.pool + 8 * (b % per)

        def store_main(b, m, value):
            cut = pl.ds(pl.multiple_of(other * sz.main + 128 * m, 128), 128)
            pool[pl.ds(row_of(b), 8), cut] = value

        def add_rest(b, tile, value):
            offset = sz.main * sz.lanes + 128 * tile
            cut = (pl.ds(row_of(b), 8), slice(offset, offset + 128))
            pool[cut] = pool[cut] + value

        place_packed(sz, other, chunks[k], 3 * per, store_main, add_rest)
    take_ghosts(sz, arrived, pool, sz.pool, sz.cells)
    total = own_list(sz, lane, tasks, mine)
    for copy in copies[-2:]:
        copy.wait()
    make_sources(sz, pool[...], high[...], low[...], source_rows, centres, 0)
    make_targets(sz, lambda i, g: pool[pl.ds(i * sz.pool + 8 * g, 8), :], targets)
    first = lane * sz.share
    tiles_of_cells(sz, first, total, mine, source_rows, centres, targets, offsets, sums, hot)
    velocity = add_up(sz, sz.own, total, up(sz.share, 8), offsets, sums, speeds, hot)
    for i in range(3):
        speed = velocity[i]
        moved = share_rows(sz, pool, i * sz.pool, lane) + TIME_STEP * speed
        velocity_out[i] = speed[: sz.share, : sz.points]
        moved_out[i] = moved[: sz.share, : sz.points]


def share_rows(sz, ref, base, lane):
    if sz.share % 8 == 0:
        return ref[pl.ds(pl.multiple_of(base + lane * sz.share, 8), sz.share), :]
    rows = [ref[pl.ds(base + lane * sz.share + c, 1), :] for c in range(sz.share)]
    rows.append(jnp.zeros((8 - sz.share, rows[0].shape[1]), F32))
    return jnp.concatenate(rows, axis=0)


def scratch(sz, tiles, slots):
    return [
        pltpu.VMEM((sz.tiles, SOURCE_ROWS * sz.pool, 128), F32),
        pltpu.VMEM((8 * sz.pool, 128), F32),
        pltpu.VMEM((tiles, 8 * sz.rows, 128), F32),
        pltpu.VMEM((tiles, 8 * slots, 128), F32),
        pltpu.VMEM((tiles, SUM_ROWS * slots, 128), F32),
        pltpu.VMEM((3, slots, 128 * tiles), F32),
        pltpu.VMEM((slots, 128), F32),
    ]


def swap(value, axis, size, k):
    return lax.ppermute(value, axis, [(d, d ^ k) for d in range(size)])


def shards(positions, bend_op, send_list, task_target, task_source, task_count):
    owners, lanes = lax.axis_size("space"), lax.axis_size("lane")
    cells, points = positions.shape[0], positions.shape[2]
    sz = sizes(owners, lanes, cells, points, task_target.shape[1], send_list.shape[1])
    params = pltpu.CompilerParams(vmem_limit_bytes=60 << 20)
    shape = jax.ShapeDtypeStruct
    both = ("space", "lane")
    by_component = jnp.transpose(positions, (1, 0, 2))
    list_rows = up(lanes, 8)
    slot_shape = shape((4 * sz.group * owners * lanes, 128), F32)
    leaving, send = pl.pallas_call(
        functools.partial(pick_kernel, sz),
        out_shape=[slot_shape, shape(send_list.shape, jnp.int32)],
        in_specs=[HBM] * 5,
        out_specs=[VMEM, SMEM],
        scratch_shapes=[
            pltpu.SMEM(send_list.shape, jnp.int32),
            pltpu.VMEM(task_target.shape, jnp.int32),
            pltpu.VMEM(task_source.shape, jnp.int32),
            pltpu.SMEM(task_count.shape, jnp.int32),
            pltpu.VMEM(by_component.shape, F32),
            pltpu.VMEM((3 * sz.rows, sz.chunk_wide), F32),
            pltpu.SemaphoreType.DMA((5,)),
        ],
        compiler_params=params,
        name="pick_cells",
    )(send_list, task_target, task_source, task_count, by_component)
    arrived = lax.all_to_all(leaving, both, split_axis=0, concat_axis=0, tiled=True)
    high, low, own_rows, own_centres = pl.pallas_call(
        functools.partial(source_kernel, sz),
        out_shape=[
            shape(bend_op.shape, BF16),
            shape(bend_op.shape, BF16),
            shape((sz.tiles, SOURCE_ROWS * cells, 128), F32),
            shape((8 * cells, 128), F32),
        ],
        in_specs=[HBM] * 2,
        out_specs=[VMEM] * 4,
        scratch_shapes=[
            pltpu.VMEM(by_component.shape, F32),
            pltpu.VMEM(bend_op.shape, F32),
            pltpu.SemaphoreType.DMA((2,)),
        ],
        compiler_params=params,
        cost_estimate=pl.CostEstimate(flops=10**9, bytes_accessed=10**7, transcendentals=0),
        name="first_sources",
    )(by_component, bend_op)
    chunk, leaving, tasks = pl.pallas_call(
        functools.partial(first_kernel, sz),
        out_shape=[
            shape((pack_rows(sz, cells), 128), F32),
            slot_shape,
            shape((3, sz.slots), jnp.int32),
        ],
        in_specs=[HBM] * 7,
        out_specs=[VMEM, VMEM, SMEM],
        scratch_shapes=scratch(sz, sz.chunk_tiles, sz.slots)
        + [
            pltpu.VMEM((3 * sz.rows, sz.chunk_wide), F32),
            pltpu.VMEM((3 * up(sz.owners * sz.group, 8), sz.width), F32),
            pltpu.SMEM(send_list.shape, jnp.int32),
            pltpu.VMEM(by_component.shape, F32),
            pltpu.VMEM(slot_shape.shape, F32),
            pltpu.VMEM(bend_op.shape, BF16),
            pltpu.VMEM(bend_op.shape, BF16),
            pltpu.VMEM((list_rows, 128), jnp.int32),
            pltpu.SMEM((list_rows, 128), jnp.int32),
            pltpu.SemaphoreType.DMA((8,)),
        ],
        compiler_params=params,
        name="first_step",
    )(arrived, send, by_component, high, low, own_rows, own_centres)
    arrived = lax.all_to_all(leaving, both, split_axis=0, concat_axis=0, tiled=True)
    chunks = [chunk] + [swap(chunk, "lane", lanes, k) for k in range(1, lanes)]
    result = shape((3, sz.share, points), F32)
    outputs = pl.pallas_call(
        functools.partial(second_kernel, sz),
        out_shape=[result, result],
        in_specs=[HBM] * (lanes + 4),
        out_specs=[VMEM] * 2,
        scratch_shapes=scratch(sz, sz.tiles, sz.own)
        + [
            pltpu.VMEM((3 * sz.pool, sz.width), F32),
            pltpu.SMEM((2, sz.own + 8), jnp.int32),
            pltpu.SMEM(tasks.shape, jnp.int32),
            pltpu.VMEM(slot_shape.shape, F32),
        ]
        + [pltpu.VMEM(chunk.shape, F32)] * lanes
        + [pltpu.VMEM(bend_op.shape, BF16)] * 2
        + [pltpu.SemaphoreType.DMA((lanes + 4,))],
        compiler_params=params,
        name="second_step",
    )(tasks, arrived, *chunks, high, low)
    return tuple(jnp.transpose(output, (1, 0, 2)) for output in outputs)


def solution(mesh):
    in_specs = (
        P("space", None, None),
        P(),
        P("space", None),
        P(("space", "lane"), None),
        P(("space", "lane"), None),
        P(("space", "lane")),
    )
    out_specs = (P(("space", "lane"), None, None), P(("space", "lane"), None, None))
    return jax.shard_map(shards, mesh=mesh, in_specs=in_specs, out_specs=out_specs, check_vma=False)
```

```python
import functools
from types import SimpleNamespace

import jax
import jax.numpy as jnp
from jax import lax
from jax.experimental import pallas as pl
from jax.experimental.pallas import tpu as pltpu
from jax.sharding import PartitionSpec as P

REGULARIZE = 0.25
TIME_STEP = 0.5
UNROLL = 4
SOURCE_ROWS = 24
SUM_ROWS = 16

F32 = jnp.float32
BF16 = jnp.bfloat16
VMEM = pl.BlockSpec(memory_space=pltpu.VMEM)
SMEM = pl.BlockSpec(memory_space=pltpu.SMEM)
HBM = pl.BlockSpec(memory_space=pltpu.HBM)


def up(value, step):
    return -(-value // step) * step


def sizes(owners, lanes, cells, points, cap, listed):
    main = 128 * (points // (128 * lanes))
    rest = (points - main * lanes) // lanes
    group = listed // owners
    pool = up(cells + listed, 8)
    per_pack = 128 // rest
    return SimpleNamespace(
        owners=owners,
        lanes=lanes,
        cells=cells,
        points=points,
        cap=cap,
        group=group,
        width=up(points, 128),
        tiles=up(points, 128) // 128,
        main=main,
        rest=rest,
        rest_tiles=up(rest * lanes, 128) // 128,
        chunk=main + rest,
        chunk_wide=main + up(rest, 128),
        chunk_tiles=(main + up(rest, 128)) // 128,
        per_pack=per_pack,
        pool=pool,
        share=cells // lanes,
        slots=up(lanes * cap + UNROLL, 8),
        rows=cells + 8,
        own=up(lanes * cap, 8),
    )


def pack_rows(sz, rows):
    return (3 * rows * sz.main // 128) + 8 * up(3 * rows // 8, sz.per_pack) // sz.per_pack


def split2(value):
    high = value.astype(BF16)
    return high, (value - high.astype(F32)).astype(BF16)


def split3(value):
    first = value.astype(BF16).astype(F32)
    left = value - first
    second = left.astype(BF16).astype(F32)
    return first, second, left - second


def lane_iota(rows):
    return lax.broadcasted_iota(jnp.int32, (rows, 128), 1)


def fetch(sources, targets, sems):
    copies = [
        pltpu.make_async_copy(source, target, sems.at[q])
        for q, (source, target) in enumerate(zip(sources, targets))
    ]
    for copy in copies:
        copy.start()
    return copies


def loop(count, body):
    if count <= 8:
        for q in range(count):
            body(q)
    else:

        def step(q, carry):
            body(q)
            return carry

        lax.fori_loop(0, count, step, 0)


def own_chunk(sz, lane, ref, rows):
    parts = []
    if sz.main:
        parts.append(ref[rows, pl.ds(pl.multiple_of(lane * sz.main, 128), sz.main)])
    start = sz.rest * lane
    lanes = lane_iota(8)
    rest = jnp.zeros((8, 128), F32)
    for tile in range(sz.rest_tiles):
        offset = sz.main * sz.lanes + 128 * tile
        block = ref[rows, offset : min(offset + 128, ref.shape[-1])]
        if block.shape[1] < 128:
            block = jnp.concatenate([block, jnp.zeros((8, 128 - block.shape[1]), F32)], axis=1)
        inside = (lanes + 128 * tile >= start) & (lanes + 128 * tile < start + sz.rest)
        rest = rest + jnp.where(inside, block, 0.0)
    rest = pltpu.roll(rest, lax.rem(128 * sz.rest_tiles - start, 128), 1)
    parts.append(rest)
    return jnp.concatenate(parts, axis=1) if len(parts) > 1 else parts[0]


def send_ghosts(sz, send, chunks, out, tasks):
    lanes = lane_iota(1)

    def one(d):
        for g in range(sz.group):
            cell = send[0, d * sz.group + g]
            rows = []
            last = tasks
            for i in range(3):
                row = chunks[pl.ds(i * sz.rows + cell, 1), :]
                rows.append(row[:, :128] if sz.main else jnp.zeros((1, 128), F32))
                piece = jnp.where(lanes < sz.rest, row[:, sz.main : sz.main + 128], 0.0)
                last = last + (pltpu.roll(piece, i * sz.rest, 1) if i else piece)
            rows.append(last)
            for other in range(sz.lanes):
                first = ((d * sz.lanes + other) * sz.group + g) * 4
                for q, row in enumerate(rows):
                    out[pl.ds(first + q, 1), :] = row

    loop(sz.owners, one)


def pick_kernel(sz, *refs):
    inputs, (out, send_out), held, (chunks, sems) = refs[:5], refs[5:7], refs[7:12], refs[12:]
    for copy in fetch(inputs, held, sems):
        copy.wait()
    send, target, source, count, positions = held
    for j in range(send_out.shape[1]):
        send_out[0, j] = send[0, j]
    lane = lax.axis_index("lane")
    for i in range(3):
        for g in range(0, sz.cells, 8):
            value = own_chunk(sz, lane, positions.at[i], pl.ds(g, 8))
            chunks[pl.ds(i * sz.rows + g, 8), :] = value
    spare = jnp.zeros((1, 128 - sz.cap), F32)
    tasks = jnp.where(lane_iota(1) == 3 * sz.rest + 2 * sz.cap, count[0].astype(F32), 0.0)
    for q, row in enumerate((target, source)):
        wide = jnp.concatenate([row[...].astype(F32), spare], axis=1)
        tasks = tasks + pltpu.roll(wide, 3 * sz.rest + q * sz.cap, 1)
    send_ghosts(sz, send, chunks, out, tasks)


def take_ghosts(sz, arrived, pool, stride, base):
    lanes = lane_iota(1)

    def one(d):
        for g in range(sz.group):
            first = [((d * sz.lanes + lane) * sz.group + g) * 4 for lane in range(sz.lanes)]
            last = [arrived[pl.ds(row + 3, 1), :] for row in first]
            for i in range(3):
                tiles = []
                if sz.main:
                    tiles += [arrived[pl.ds(row + i, 1), :] for row in first]
                for tile in range(sz.rest_tiles):
                    total = jnp.zeros((1, 128), F32)
                    for lane in range(sz.lanes):
                        start = sz.rest * lane
                        if start + sz.rest <= 128 * tile or start >= 128 * tile + 128:
                            continue
                        shift = (start - i * sz.rest) % 128
                        value = pltpu.roll(last[lane], shift, 1) if shift else last[lane]
                        at = lanes + 128 * tile
                        total = jnp.where((at >= start) & (at < start + sz.rest), value, total)
                    tiles.append(total)
                place = pl.ds(i * stride + base + d * sz.group + g, 1)
                pool[place, :] = jnp.concatenate(tiles, axis=1)

    loop(sz.owners, one)


def build_list(sz, lists, tasks):
    total = jnp.int32(0)
    for lane in range(sz.lanes):

        def step(j, total, lane=lane):
            tasks[0, total] = lists[lane, j]
            tasks[1, total] = lists[lane, sz.cap + j]
            return total + 1

        total = lax.fori_loop(0, lists[lane, 2 * sz.cap], step, total)
    for u in range(UNROLL):
        tasks[0, total + u] = jnp.int32(sz.cells)
        tasks[1, total + u] = jnp.int32(0)
    tasks[2, 0] = total
    return total


def own_list(sz, lane, tasks, mine):
    first = lane * sz.share

    def step(t, count):
        target = tasks[0, t] - first
        mine[0, count] = target
        mine[1, count] = tasks[1, t]
        return count + ((target >= 0) & (target < sz.share)).astype(jnp.int32)

    return lax.fori_loop(0, tasks[2, 0], step, jnp.int32(0))


def products(value, bend_high, bend_low):
    high, low = split2(value)
    dot = functools.partial(jnp.dot, preferred_element_type=F32)
    return dot(high, bend_high) + dot(low, bend_high) + dot(high, bend_low)


def make_sources(sz, value, bend_high, bend_low, source_rows, centres, first):
    count = value.shape[0] // 3
    forces = products(value[:, : sz.points], bend_high, bend_low)
    forces = jnp.concatenate(
        [forces, jnp.zeros((3 * count, sz.width - sz.points), F32)], axis=1
    )
    middle = jnp.sum(value, axis=1, keepdims=True) / sz.points
    for g in range(count // 8):
        where = [i * count + 8 * g for i in range(3)]
        middles = [jnp.broadcast_to(middle[w : w + 8], (8, 128)) for w in where]
        middles += [jnp.zeros((8, 128), F32)] * 5
        for i, row in enumerate(middles):
            centres[pl.ds(8 * (first + 8 * g) + i, 8, stride=8), :] = row
        for j in range(sz.tiles):
            cut = slice(128 * j, 128 * j + 128)
            y = [value[w : w + 8, cut] - m for w, m in zip(where, middles)]
            f = [forces[w : w + 8, cut] for w in where]
            norm = y[0] * y[0] + y[1] * y[1] + y[2] * y[2] + REGULARIZE
            along = y[0] * f[0] + y[1] * f[1] + y[2] * f[2]
            one, zero = jnp.ones((8, 128), F32), jnp.zeros((8, 128), F32)
            rows = [y[0], y[1], y[2], norm, one, zero, zero, zero]
            rows += f
            rows += [y[i] * f[k] for i in range(3) for k in range(3)]
            rows += [norm * f[i] + along * y[i] for i in range(3)]
            rows += [along]
            for k, row in enumerate(rows):
                place = pl.ds(SOURCE_ROWS * (first + 8 * g) + k, 8, stride=SOURCE_ROWS)
                source_rows.at[j][place, :] = row


def make_targets(sz, blocks, targets):
    targets[...] = jnp.zeros_like(targets)
    for g in range(sz.cells // 8):
        for i in range(3):
            block = blocks(i, g)
            for j in range(targets.shape[0]):
                cut = slice(128 * j, 128 * j + 128)
                targets.at[j][pl.ds(64 * g + i, 8, stride=8), :] = block[:, cut]


def load_source(sz, source, source_rows):
    held = [
        source_rows[j, pl.ds(pl.multiple_of(SOURCE_ROWS * source, 8), SOURCE_ROWS), :]
        for j in range(sz.tiles)
    ]
    count = sz.points // 128
    whole = jnp.concatenate(held[:count], axis=1)
    y1, y2, y3 = split3(whole[:8])
    y_stack = jnp.concatenate([y1, y1, y2, y2, y1, y3], axis=0).astype(BF16)
    m_stack = jnp.transpose(jnp.concatenate(split3(whole[8:]), axis=0).astype(BF16))
    m_stack = jnp.concatenate([m_stack, m_stack], axis=0)
    if count == sz.tiles:
        return y_stack, m_stack, None, None
    last = sz.points - 128 * count
    y1, y2, y3 = split3(held[count][:8])
    y_last = jnp.concatenate([y1, y1, y2, y2, y1, y3], axis=0).astype(BF16)
    y_last = jnp.transpose(y_last)[:last]
    m_last = jnp.concatenate(split3(held[count][8:]), axis=0)
    m_last = (m_last + pltpu.roll(m_last, last, 1)).astype(BF16)[:, : 2 * last]
    return y_stack, m_stack, y_last, m_last


def load_target(j, target, slot, centre, targets, offsets):
    row = lax.broadcasted_iota(jnp.int32, (8, 128), 0)
    x = targets[j, pl.ds(pl.multiple_of(8 * target, 8), 8), :] - centre
    square = x * x
    norm = pltpu.roll(square, 2, 0) + pltpu.roll(square, 3, 0) + pltpu.roll(square, 4, 0)
    side = jnp.where(row == 4, norm, jnp.where(row == 3, 1.0, 0.0))
    x_side = jnp.where(row < 3, -2.0 * x, side)
    x1, x2, x3 = split3(x_side)
    return x, jnp.concatenate([x1, x2, x1, x2, x3, x1], axis=0).astype(BF16)


def distances(one_stack, other_stack):
    return jnp.dot(one_stack, other_stack, preferred_element_type=F32)


def weights(shifted, axis):
    inverse = lax.rsqrt(shifted.astype(BF16)).astype(F32)
    square = inverse * inverse
    result = inverse * square * (5.0 / 3.0 - shifted * square)
    return jnp.concatenate(split2(result), axis=axis)


def tile_sums(whole, last, m_stack, m_last):
    result = jnp.transpose(jnp.dot(whole, m_stack, preferred_element_type=F32))
    if last is not None:
        result = result + jnp.dot(m_last, last, preferred_element_type=F32)
    result = result[:SUM_ROWS] + result[SUM_ROWS : 2 * SUM_ROWS] + result[2 * SUM_ROWS :]
    spare = -result.shape[1] % 128
    if spare:
        result = jnp.concatenate([result, jnp.zeros((SUM_ROWS, spare), F32)], axis=1)
    return result


def sum_blocks(blocks, source):
    y_stack, m_stack, y_last, m_last = source
    whole = [distances(jnp.transpose(block), y_stack) for block in blocks]
    whole = [weights(one, 1) for one in whole]
    last = [None] * len(blocks)
    if y_last is not None:
        last = [weights(distances(y_last, block), 0) for block in blocks]
    return [tile_sums(*pair, m_stack, m_last) for pair in zip(whole, last)]


def store_sums(slots, slot, j, x, result, offsets, sums):
    offsets.at[j][pl.ds(slot, 8, stride=slots), :] = x
    for h in range(0, SUM_ROWS, 8):
        sums.at[j][pl.ds(h * slots + slot, 8, stride=slots), :] = result[h : h + 8]


def mark(slot, target, hot):
    hot[pl.ds(slot, 1), :] = jnp.where(lane_iota(1) == target, 1.0, 0.0)


def combine(sz, slots, first, total, offsets, sums, speeds):
    live = lax.broadcasted_iota(jnp.int32, (8, 128), 0) + first < total
    for j in range(offsets.shape[0]):
        x = [offsets[j, pl.ds(i * slots + first, 8), :] for i in range(3)]
        s = [sums[j, pl.ds(k * slots + first, 8), :] for k in range(SUM_ROWS)]
        a, b, c = s[:3], [s[3:6], s[6:9], s[9:12]], s[12:15]
        norm = x[0] * x[0] + x[1] * x[1] + x[2] * x[2] + REGULARIZE
        along = x[0] * a[0] + x[1] * a[1] + x[2] * a[2] - s[15]
        for i in range(3):
            speed = norm * a[i] + c[i] + along * x[i]
            for k in range(3):
                speed = speed - x[k] * (2.0 * b[k][i] + b[i][k])
            speed = jnp.where(live, speed * (1.5 / sz.points), 0.0)
            speeds[i, pl.ds(first, 8), 128 * j : 128 * j + 128] = speed


def add_up(sz, slots, total, rows, offsets, sums, speeds, hot):
    def eight(q, carry):
        combine(sz, slots, pl.multiple_of(8 * q, 8), total, offsets, sums, speeds)
        return carry

    lax.fori_loop(0, lax.div(total + 7, 8), eight, 0)
    one_hot = hot[...].astype(BF16)
    result = []
    for i in range(3):
        first, second, third = split3(speeds[i])
        parts = [
            lax.dot_general(
                one_hot, part.astype(BF16), (((0,), (0,)), ((), ())), preferred_element_type=F32
            )
            for part in (first, second, third)
        ]
        result.append((parts[0] + parts[1] + parts[2])[:rows])
    return result


def tiles_of_chunk(sz, total, tasks, source_rows, centres, targets, offsets, sums, hot):
    def several(q, carry):
        slots = [q * UNROLL + u for u in range(UNROLL)]
        picks = [(tasks[0, slot], tasks[1, slot]) for slot in slots]
        sources = [load_source(sz, source, source_rows) for _, source in picks]
        points = []
        for slot, (target, source) in zip(slots, picks):
            centre = centres[pl.ds(pl.multiple_of(8 * source, 8), 8), :]
            points.append(
                [
                    load_target(j, target, slot, centre, targets, offsets)
                    for j in range(sz.chunk_tiles)
                ]
            )
        stacks = [
            jnp.concatenate([stack for _, stack in point], axis=1)[:, : sz.chunk]
            for point in points
        ]
        whole = [
            distances(jnp.transpose(stack), source[0]) for stack, source in zip(stacks, sources)
        ]
        whole = [weights(one, 1) for one in whole]
        last = [None] * UNROLL
        if sources[0][2] is not None:
            last = [distances(source[2], stack) for stack, source in zip(stacks, sources)]
            last = [weights(one, 0) for one in last]
        results = [
            tile_sums(*pair, source[1], source[3])
            for pair, source in zip(zip(whole, last), sources)
        ]
        for slot, (target, _), point, result in zip(slots, picks, points, results):
            for j in range(sz.chunk_tiles):
                cut = result[:, 128 * j : 128 * j + 128]
                store_sums(sz.slots, slot, j, point[j][0], cut, offsets, sums)
            mark(slot, target, hot)
        return carry

    lax.fori_loop(0, lax.div(total + UNROLL - 1, UNROLL), several, 0)


def tiles_of_cells(sz, first, total, mine, source_rows, centres, targets, offsets, sums, hot):
    def single(slot, carry):
        target, source = mine[0, slot], mine[1, slot]
        held = load_source(sz, source, source_rows)
        centre = centres[pl.ds(pl.multiple_of(8 * source, 8), 8), :]
        points = [
            load_target(j, target + first, slot, centre, targets, offsets)
            for j in range(sz.tiles)
        ]
        stacks = [
            stack[:, : min(128, sz.points - 128 * j)] for j, (_, stack) in enumerate(points)
        ]
        results = sum_blocks(stacks, held)
        for j in range(sz.tiles):
            store_sums(sz.own, slot, j, points[j][0], results[j], offsets, sums)
        mark(slot, target, hot)
        return carry

    lax.fori_loop(0, total, single, 0)


def packed(sz, blocks):
    rows = [b[:, : sz.main] for b in blocks] if sz.main else []
    lanes = lane_iota(8)
    for p in range(0, len(blocks), sz.per_pack):
        total = jnp.zeros((8, 128), F32)
        for q, block in enumerate(blocks[p : p + sz.per_pack]):
            rest = jnp.where(lanes < sz.rest, block[:, sz.main : sz.main + 128], 0.0)
            total = total + (pltpu.roll(rest, q * sz.rest, 1) if q else rest)
        rows.append(total)
    return rows


def store_packed(sz, out, blocks):
    first = 0
    count = len(blocks)
    values = packed(sz, blocks)
    if sz.main:
        for b in range(count):
            for m in range(sz.main // 128):
                out[pl.ds(first, 8), :] = values[b][:, 128 * m : 128 * m + 128]
                first += 8
        values = values[count:]
    for value in values:
        out[pl.ds(first, 8), :] = value
        first += 8


def place_packed(sz, lane, arrived, count, store_main, add_rest):
    first = 0
    if sz.main:
        for b in range(count):
            for m in range(sz.main // 128):
                store_main(b, m, arrived[pl.ds(first, 8), :])
                first += 8
    start = sz.rest * lane
    lanes = lane_iota(8)
    for b in range(count):
        pack, q = divmod(b, sz.per_pack)
        value = arrived[pl.ds(first + 8 * pack, 8), :]
        value = pltpu.roll(value, lax.rem(start - q * sz.rest + 128, 128), 1)
        for tile in range(sz.rest_tiles):
            inside = (lanes + 128 * tile >= start) & (lanes + 128 * tile < start + sz.rest)
            add_rest(b, tile, jnp.where(inside, value, 0.0))


def source_kernel(sz, *refs):
    inputs, (high_out, low_out, source_rows, centres), held, sems = (
        refs[:2],
        refs[2:6],
        refs[6:8],
        refs[8],
    )
    for copy in fetch(inputs, held, sems):
        copy.wait()
    positions, bend = held
    high_out[...], low_out[...] = split2(bend[...])
    value = jnp.concatenate([positions[i] for i in range(3)], axis=0)
    value = jnp.concatenate(
        [value, jnp.zeros((3 * sz.cells, sz.width - sz.points), F32)], axis=1
    )
    make_sources(sz, value, high_out[...], low_out[...], source_rows, centres, 0)


def first_kernel(sz, *refs):
    inputs, (chunk_out, ghost_out, tasks), refs = refs[:7], refs[7:10], refs[10:]
    source_rows, centres, targets, offsets, sums, speeds, hot, moved, pool = refs[:9]
    send, positions, arrived, high, low, staged, lists, sems = refs[9:]
    me, lane = lax.axis_index("space"), lax.axis_index("lane")
    own_rows = source_rows.at[:, pl.ds(0, SOURCE_ROWS * sz.cells)]
    own_centres = centres.at[pl.ds(0, 8 * sz.cells)]
    held = [arrived, send, positions, high, low, own_rows, own_centres]
    copies = fetch(inputs, held, sems)
    copies[0].wait()
    for other in range(sz.lanes):
        row = ((me * sz.lanes + other) * sz.group) * 4 + 3
        value = pltpu.roll(arrived[pl.ds(row, 1), :], 128 - 3 * sz.rest, 1)
        staged[pl.ds(other, 1), :] = value.astype(jnp.int32)
    copies.append(pltpu.make_async_copy(staged, lists, sems.at[7]))
    copies[7].start()
    pool[...] = jnp.zeros_like(pool)
    take_ghosts(sz, arrived, pool, up(sz.owners * sz.group, 8), 0)
    hot[...] = jnp.zeros_like(hot)
    speeds[...] = jnp.zeros_like(speeds)
    for copy in copies[1:5]:
        copy.wait()
    make_sources(sz, pool[...], high[...], low[...], source_rows, centres, sz.cells)
    make_targets(
        sz, lambda i, g: own_chunk(sz, lane, positions.at[i], pl.ds(8 * g, 8)), targets
    )
    for copy in copies[5:]:
        copy.wait()
    total = build_list(sz, lists, tasks)
    tiles_of_chunk(sz, total, tasks, source_rows, centres, targets, offsets, sums, hot)
    velocity = add_up(sz, sz.slots, total, sz.cells, offsets, sums, speeds, hot)
    blocks = []
    for i in range(3):
        for g in range(0, sz.cells, 8):
            chunk = own_chunk(sz, lane, positions.at[i], pl.ds(g, 8))
            block = chunk + TIME_STEP * velocity[i][g : g + 8]
            moved[pl.ds(i * sz.rows + g, 8), :] = block
            blocks.append(block)
    store_packed(sz, chunk_out, blocks)
    send_ghosts(sz, send, moved, ghost_out, jnp.zeros((1, 128), F32))


def second_kernel(sz, *refs):
    count = sz.lanes + 4
    inputs, (moved_out, velocity_out), refs = refs[:count], refs[count : count + 2], refs[count + 2 :]
    source_rows, centres, targets, offsets, sums, speeds, hot, pool, mine = refs[:9]
    held, sems = refs[9:-1], refs[-1]
    copies = fetch(inputs, held, sems)
    tasks, arrived, chunks, (high, low) = held[0], held[1], held[2:-2], held[-2:]
    hot[...] = jnp.zeros_like(hot)
    speeds[...] = jnp.zeros_like(speeds)
    lane = lax.axis_index("lane")
    pool[...] = jnp.zeros_like(pool)
    for copy in copies[:-2]:
        copy.wait()
    per = sz.cells // 8
    for k in range(sz.lanes):
        other = lane ^ k

        def row_of(b):
            return (b // per) * sz.pool + 8 * (b % per)

        def store_main(b, m, value):
            cut = pl.ds(pl.multiple_of(other * sz.main + 128 * m, 128), 128)
            pool[pl.ds(row_of(b), 8), cut] = value

        def add_rest(b, tile, value):
            offset = sz.main * sz.lanes + 128 * tile
            cut = (pl.ds(row_of(b), 8), slice(offset, offset + 128))
            pool[cut] = pool[cut] + value

        place_packed(sz, other, chunks[k], 3 * per, store_main, add_rest)
    take_ghosts(sz, arrived, pool, sz.pool, sz.cells)
    total = own_list(sz, lane, tasks, mine)
    for copy in copies[-2:]:
        copy.wait()
    make_sources(sz, pool[...], high[...], low[...], source_rows, centres, 0)
    make_targets(sz, lambda i, g: pool[pl.ds(i * sz.pool + 8 * g, 8), :], targets)
    first = lane * sz.share
    tiles_of_cells(sz, first, total, mine, source_rows, centres, targets, offsets, sums, hot)
    velocity = add_up(sz, sz.own, total, up(sz.share, 8), offsets, sums, speeds, hot)
    for i in range(3):
        speed = velocity[i]
        moved = share_rows(sz, pool, i * sz.pool, lane) + TIME_STEP * speed
        velocity_out[i] = speed[: sz.share, : sz.points]
        moved_out[i] = moved[: sz.share, : sz.points]


def share_rows(sz, ref, base, lane):
    if sz.share % 8 == 0:
        return ref[pl.ds(pl.multiple_of(base + lane * sz.share, 8), sz.share), :]
    rows = [ref[pl.ds(base + lane * sz.share + c, 1), :] for c in range(sz.share)]
    rows.append(jnp.zeros((8 - sz.share, rows[0].shape[1]), F32))
    return jnp.concatenate(rows, axis=0)


def scratch(sz, tiles, slots):
    return [
        pltpu.VMEM((sz.tiles, SOURCE_ROWS * sz.pool, 128), F32),
        pltpu.VMEM((8 * sz.pool, 128), F32),
        pltpu.VMEM((tiles, 8 * sz.rows, 128), F32),
        pltpu.VMEM((tiles, 8 * slots, 128), F32),
        pltpu.VMEM((tiles, SUM_ROWS * slots, 128), F32),
        pltpu.VMEM((3, slots, 128 * tiles), F32),
        pltpu.VMEM((slots, 128), F32),
    ]


def swap(value, axis, size, k):
    return lax.ppermute(value, axis, [(d, d ^ k) for d in range(size)])


def shards(positions, bend_op, send_list, task_target, task_source, task_count):
    owners, lanes = lax.axis_size("space"), lax.axis_size("lane")
    cells, points = positions.shape[0], positions.shape[2]
    sz = sizes(owners, lanes, cells, points, task_target.shape[1], send_list.shape[1])
    params = pltpu.CompilerParams(vmem_limit_bytes=60 << 20)
    shape = jax.ShapeDtypeStruct
    both = ("space", "lane")
    by_component = jnp.transpose(positions, (1, 0, 2))
    list_rows = up(lanes, 8)
    slot_shape = shape((4 * sz.group * owners * lanes, 128), F32)
    leaving, send = pl.pallas_call(
        functools.partial(pick_kernel, sz),
        out_shape=[slot_shape, shape(send_list.shape, jnp.int32)],
        in_specs=[HBM] * 5,
        out_specs=[VMEM, SMEM],
        scratch_shapes=[
            pltpu.SMEM(send_list.shape, jnp.int32),
            pltpu.VMEM(task_target.shape, jnp.int32),
            pltpu.VMEM(task_source.shape, jnp.int32),
            pltpu.SMEM(task_count.shape, jnp.int32),
            pltpu.VMEM(by_component.shape, F32),
            pltpu.VMEM((3 * sz.rows, sz.chunk_wide), F32),
            pltpu.SemaphoreType.DMA((5,)),
        ],
        compiler_params=params,
        name="pick_cells",
    )(send_list, task_target, task_source, task_count, by_component)
    arrived = lax.all_to_all(leaving, both, split_axis=0, concat_axis=0, tiled=True)
    high, low, own_rows, own_centres = pl.pallas_call(
        functools.partial(source_kernel, sz),
        out_shape=[
            shape(bend_op.shape, BF16),
            shape(bend_op.shape, BF16),
            shape((sz.tiles, SOURCE_ROWS * cells, 128), F32),
            shape((8 * cells, 128), F32),
        ],
        in_specs=[HBM] * 2,
        out_specs=[VMEM] * 4,
        scratch_shapes=[
            pltpu.VMEM(by_component.shape, F32),
            pltpu.VMEM(bend_op.shape, F32),
            pltpu.SemaphoreType.DMA((2,)),
        ],
        compiler_params=params,
        cost_estimate=pl.CostEstimate(flops=10**9, bytes_accessed=10**7, transcendentals=0),
        name="first_sources",
    )(by_component, bend_op)
    chunk, leaving, tasks = pl.pallas_call(
        functools.partial(first_kernel, sz),
        out_shape=[
            shape((pack_rows(sz, cells), 128), F32),
            slot_shape,
            shape((3, sz.slots), jnp.int32),
        ],
        in_specs=[HBM] * 7,
        out_specs=[VMEM, VMEM, SMEM],
        scratch_shapes=scratch(sz, sz.chunk_tiles, sz.slots)
        + [
            pltpu.VMEM((3 * sz.rows, sz.chunk_wide), F32),
            pltpu.VMEM((3 * up(sz.owners * sz.group, 8), sz.width), F32),
            pltpu.SMEM(send_list.shape, jnp.int32),
            pltpu.VMEM(by_component.shape, F32),
            pltpu.VMEM(slot_shape.shape, F32),
            pltpu.VMEM(bend_op.shape, BF16),
            pltpu.VMEM(bend_op.shape, BF16),
            pltpu.VMEM((list_rows, 128), jnp.int32),
            pltpu.SMEM((list_rows, 128), jnp.int32),
            pltpu.SemaphoreType.DMA((8,)),
        ],
        compiler_params=params,
        name="first_step",
    )(arrived, send, by_component, high, low, own_rows, own_centres)
    arrived = lax.all_to_all(leaving, both, split_axis=0, concat_axis=0, tiled=True)
    chunks = [chunk] + [swap(chunk, "lane", lanes, k) for k in range(1, lanes)]
    result = shape((3, sz.share, points), F32)
    outputs = pl.pallas_call(
        functools.partial(second_kernel, sz),
        out_shape=[result, result],
        in_specs=[HBM] * (lanes + 4),
        out_specs=[VMEM] * 2,
        scratch_shapes=scratch(sz, sz.tiles, sz.own)
        + [
            pltpu.VMEM((3 * sz.pool, sz.width), F32),
            pltpu.SMEM((2, sz.own + 8), jnp.int32),
            pltpu.SMEM(tasks.shape, jnp.int32),
            pltpu.VMEM(slot_shape.shape, F32),
        ]
        + [pltpu.VMEM(chunk.shape, F32)] * lanes
        + [pltpu.VMEM(bend_op.shape, BF16)] * 2
        + [pltpu.SemaphoreType.DMA((lanes + 4,))],
        compiler_params=params,
        name="second_step",
    )(tasks, arrived, *chunks, high, low)
    return tuple(jnp.transpose(output, (1, 0, 2)) for output in outputs)


def solution(mesh):
    in_specs = (
        P("space", None, None),
        P(),
        P("space", None),
        P(("space", "lane"), None),
        P(("space", "lane"), None),
        P(("space", "lane")),
    )
    out_specs = (P(("space", "lane"), None, None), P(("space", "lane"), None, None))
    return jax.shard_map(shards, mesh=mesh, in_specs=in_specs, out_specs=out_specs, check_vma=False)
```

```python
import functools
from types import SimpleNamespace

import jax
import jax.numpy as jnp
from jax import lax
from jax.experimental import pallas as pl
from jax.experimental.pallas import tpu as pltpu
from jax.sharding import PartitionSpec as P

REGULARIZE = 0.25
TIME_STEP = 0.5
UNROLL = 4
SOURCE_ROWS = 24
SUM_ROWS = 16

F32 = jnp.float32
BF16 = jnp.bfloat16
VMEM = pl.BlockSpec(memory_space=pltpu.VMEM)
SMEM = pl.BlockSpec(memory_space=pltpu.SMEM)
HBM = pl.BlockSpec(memory_space=pltpu.HBM)


def up(value, step):
    return -(-value // step) * step


def sizes(owners, lanes, cells, points, cap, listed):
    main = 128 * (points // (128 * lanes))
    rest = (points - main * lanes) // lanes
    group = listed // owners
    pool = up(cells + listed, 8)
    per_pack = 128 // rest
    return SimpleNamespace(
        owners=owners,
        lanes=lanes,
        cells=cells,
        points=points,
        cap=cap,
        group=group,
        width=up(points, 128),
        tiles=up(points, 128) // 128,
        main=main,
        rest=rest,
        rest_tiles=up(rest * lanes, 128) // 128,
        chunk=main + rest,
        chunk_wide=main + up(rest, 128),
        chunk_tiles=(main + up(rest, 128)) // 128,
        per_pack=per_pack,
        pool=pool,
        share=cells // lanes,
        slots=up(lanes * cap + UNROLL, 8),
        rows=cells + 8,
        own=up(lanes * cap, 8),
    )


def pack_rows(sz, rows):
    return (3 * rows * sz.main // 128) + 8 * up(3 * rows // 8, sz.per_pack) // sz.per_pack


def split2(value):
    high = value.astype(BF16)
    return high, (value - high.astype(F32)).astype(BF16)


def split3(value):
    first = value.astype(BF16).astype(F32)
    left = value - first
    second = left.astype(BF16).astype(F32)
    return first, second, left - second


def lane_iota(rows):
    return lax.broadcasted_iota(jnp.int32, (rows, 128), 1)


def fetch(sources, targets, sems):
    copies = [
        pltpu.make_async_copy(source, target, sems.at[q])
        for q, (source, target) in enumerate(zip(sources, targets))
    ]
    for copy in copies:
        copy.start()
    return copies


def loop(count, body):
    if count <= 8:
        for q in range(count):
            body(q)
    else:

        def step(q, carry):
            body(q)
            return carry

        lax.fori_loop(0, count, step, 0)


def own_chunk(sz, lane, ref, rows):
    parts = []
    if sz.main:
        parts.append(ref[rows, pl.ds(pl.multiple_of(lane * sz.main, 128), sz.main)])
    start = sz.rest * lane
    lanes = lane_iota(8)
    rest = jnp.zeros((8, 128), F32)
    for tile in range(sz.rest_tiles):
        offset = sz.main * sz.lanes + 128 * tile
        block = ref[rows, offset : min(offset + 128, ref.shape[-1])]
        if block.shape[1] < 128:
            block = jnp.concatenate([block, jnp.zeros((8, 128 - block.shape[1]), F32)], axis=1)
        inside = (lanes + 128 * tile >= start) & (lanes + 128 * tile < start + sz.rest)
        rest = rest + jnp.where(inside, block, 0.0)
    rest = pltpu.roll(rest, lax.rem(128 * sz.rest_tiles - start, 128), 1)
    parts.append(rest)
    return jnp.concatenate(parts, axis=1) if len(parts) > 1 else parts[0]


def send_ghosts(sz, send, chunks, out, tasks):
    lanes = lane_iota(1)

    def one(d):
        for g in range(sz.group):
            cell = send[0, d * sz.group + g]
            rows = []
            last = tasks
            for i in range(3):
                row = chunks[pl.ds(i * sz.rows + cell, 1), :]
                rows.append(row[:, :128] if sz.main else jnp.zeros((1, 128), F32))
                piece = jnp.where(lanes < sz.rest, row[:, sz.main : sz.main + 128], 0.0)
                last = last + (pltpu.roll(piece, i * sz.rest, 1) if i else piece)
            rows.append(last)
            for other in range(sz.lanes):
                first = ((d * sz.lanes + other) * sz.group + g) * 4
                for q, row in enumerate(rows):
                    out[pl.ds(first + q, 1), :] = row

    loop(sz.owners, one)


def pick_kernel(sz, *refs):
    inputs, (out, send_out), held, (chunks, sems) = refs[:5], refs[5:7], refs[7:12], refs[12:]
    for copy in fetch(inputs, held, sems):
        copy.wait()
    send, target, source, count, positions = held
    for j in range(send_out.shape[1]):
        send_out[0, j] = send[0, j]
    lane = lax.axis_index("lane")
    for i in range(3):
        for g in range(0, sz.cells, 8):
            value = own_chunk(sz, lane, positions.at[i], pl.ds(g, 8))
            chunks[pl.ds(i * sz.rows + g, 8), :] = value
    spare = jnp.zeros((1, 128 - sz.cap), F32)
    tasks = jnp.where(lane_iota(1) == 3 * sz.rest + 2 * sz.cap, count[0].astype(F32), 0.0)
    for q, row in enumerate((target, source)):
        wide = jnp.concatenate([row[...].astype(F32), spare], axis=1)
        tasks = tasks + pltpu.roll(wide, 3 * sz.rest + q * sz.cap, 1)
    send_ghosts(sz, send, chunks, out, tasks)


def take_ghosts(sz, arrived, pool, stride, base):
    lanes = lane_iota(1)

    def one(d):
        for g in range(sz.group):
            first = [((d * sz.lanes + lane) * sz.group + g) * 4 for lane in range(sz.lanes)]
            last = [arrived[pl.ds(row + 3, 1), :] for row in first]
            for i in range(3):
                tiles = []
                if sz.main:
                    tiles += [arrived[pl.ds(row + i, 1), :] for row in first]
                for tile in range(sz.rest_tiles):
                    total = jnp.zeros((1, 128), F32)
                    for lane in range(sz.lanes):
                        start = sz.rest * lane
                        if start + sz.rest <= 128 * tile or start >= 128 * tile + 128:
                            continue
                        shift = (start - i * sz.rest) % 128
                        value = pltpu.roll(last[lane], shift, 1) if shift else last[lane]
                        at = lanes + 128 * tile
                        total = jnp.where((at >= start) & (at < start + sz.rest), value, total)
                    tiles.append(total)
                place = pl.ds(i * stride + base + d * sz.group + g, 1)
                pool[place, :] = jnp.concatenate(tiles, axis=1)

    loop(sz.owners, one)


def build_list(sz, lists, tasks):
    total = jnp.int32(0)
    for lane in range(sz.lanes):

        def step(j, total, lane=lane):
            tasks[0, total] = lists[lane, j]
            tasks[1, total] = lists[lane, sz.cap + j]
            return total + 1

        total = lax.fori_loop(0, lists[lane, 2 * sz.cap], step, total)
    for u in range(UNROLL):
        tasks[0, total + u] = jnp.int32(sz.cells)
        tasks[1, total + u] = jnp.int32(0)
    tasks[2, 0] = total
    return total


def own_list(sz, lane, tasks, mine):
    first = lane * sz.share

    def step(t, count):
        target = tasks[0, t] - first
        mine[0, count] = target
        mine[1, count] = tasks[1, t]
        return count + ((target >= 0) & (target < sz.share)).astype(jnp.int32)

    return lax.fori_loop(0, tasks[2, 0], step, jnp.int32(0))


def products(value, bend_high, bend_low):
    high, low = split2(value)
    dot = functools.partial(jnp.dot, preferred_element_type=F32)
    return dot(high, bend_high) + dot(low, bend_high) + dot(high, bend_low)


def make_sources(sz, value, bend_high, bend_low, source_rows, centres, first):
    count = value.shape[0] // 3
    forces = products(value[:, : sz.points], bend_high, bend_low)
    forces = jnp.concatenate(
        [forces, jnp.zeros((3 * count, sz.width - sz.points), F32)], axis=1
    )
    middle = jnp.sum(value, axis=1, keepdims=True) / sz.points
    for g in range(count // 8):
        where = [i * count + 8 * g for i in range(3)]
        middles = [jnp.broadcast_to(middle[w : w + 8], (8, 128)) for w in where]
        middles += [jnp.zeros((8, 128), F32)] * 5
        for i, row in enumerate(middles):
            centres[pl.ds(8 * (first + 8 * g) + i, 8, stride=8), :] = row
        for j in range(sz.tiles):
            cut = slice(128 * j, 128 * j + 128)
            y = [value[w : w + 8, cut] - m for w, m in zip(where, middles)]
            f = [forces[w : w + 8, cut] for w in where]
            norm = y[0] * y[0] + y[1] * y[1] + y[2] * y[2] + REGULARIZE
            along = y[0] * f[0] + y[1] * f[1] + y[2] * f[2]
            one, zero = jnp.ones((8, 128), F32), jnp.zeros((8, 128), F32)
            rows = [y[0], y[1], y[2], norm, one, zero, zero, zero]
            rows += f
            rows += [y[i] * f[k] for i in range(3) for k in range(3)]
            rows += [norm * f[i] + along * y[i] for i in range(3)]
            rows += [along]
            for k, row in enumerate(rows):
                place = pl.ds(SOURCE_ROWS * (first + 8 * g) + k, 8, stride=SOURCE_ROWS)
                source_rows.at[j][place, :] = row


def make_targets(sz, blocks, targets):
    targets[...] = jnp.zeros_like(targets)
    for g in range(sz.cells // 8):
        for i in range(3):
            block = blocks(i, g)
            for j in range(targets.shape[0]):
                cut = slice(128 * j, 128 * j + 128)
                targets.at[j][pl.ds(64 * g + i, 8, stride=8), :] = block[:, cut]


def load_source(sz, source, source_rows):
    held = [
        source_rows[j, pl.ds(pl.multiple_of(SOURCE_ROWS * source, 8), SOURCE_ROWS), :]
        for j in range(sz.tiles)
    ]
    count = sz.points // 128
    whole = jnp.concatenate(held[:count], axis=1)
    y1, y2, y3 = split3(whole[:8])
    y_stack = jnp.concatenate([y1, y1, y2, y2, y1, y3], axis=0).astype(BF16)
    m_stack = jnp.transpose(jnp.concatenate(split3(whole[8:]), axis=0).astype(BF16))
    m_stack = jnp.concatenate([m_stack, m_stack], axis=0)
    if count == sz.tiles:
        return y_stack, m_stack, None, None
    last = sz.points - 128 * count
    y1, y2, y3 = split3(held[count][:8])
    y_last = jnp.concatenate([y1, y1, y2, y2, y1, y3], axis=0).astype(BF16)
    y_last = jnp.transpose(y_last)[:last]
    m_last = jnp.concatenate(split3(held[count][8:]), axis=0)
    m_last = (m_last + pltpu.roll(m_last, last, 1)).astype(BF16)[:, : 2 * last]
    return y_stack, m_stack, y_last, m_last


def load_target(j, target, slot, centre, targets, offsets):
    row = lax.broadcasted_iota(jnp.int32, (8, 128), 0)
    x = targets[j, pl.ds(pl.multiple_of(8 * target, 8), 8), :] - centre
    square = x * x
    norm = pltpu.roll(square, 2, 0) + pltpu.roll(square, 3, 0) + pltpu.roll(square, 4, 0)
    side = jnp.where(row == 4, norm, jnp.where(row == 3, 1.0, 0.0))
    x_side = jnp.where(row < 3, -2.0 * x, side)
    x1, x2, x3 = split3(x_side)
    return x, jnp.concatenate([x1, x2, x1, x2, x3, x1], axis=0).astype(BF16)


def distances(one_stack, other_stack):
    return jnp.dot(one_stack, other_stack, preferred_element_type=F32)


def weights(shifted, axis):
    inverse = lax.rsqrt(shifted)
    return jnp.concatenate(split2(inverse * inverse * inverse), axis=axis)


def tile_sums(whole, last, m_stack, m_last):
    result = jnp.transpose(jnp.dot(whole, m_stack, preferred_element_type=F32))
    if last is not None:
        result = result + jnp.dot(m_last, last, preferred_element_type=F32)
    result = result[:SUM_ROWS] + result[SUM_ROWS : 2 * SUM_ROWS] + result[2 * SUM_ROWS :]
    spare = -result.shape[1] % 128
    if spare:
        result = jnp.concatenate([result, jnp.zeros((SUM_ROWS, spare), F32)], axis=1)
    return result


def store_sums(slots, slot, j, x, result, offsets, sums):
    offsets.at[j][pl.ds(slot, 8, stride=slots), :] = x
    for h in range(0, SUM_ROWS, 8):
        sums.at[j][pl.ds(h * slots + slot, 8, stride=slots), :] = result[h : h + 8]


def mark(slot, target, hot):
    hot[pl.ds(slot, 1), :] = jnp.where(lane_iota(1) == target, 1.0, 0.0)


def combine(sz, slots, first, total, offsets, sums, speeds):
    live = lax.broadcasted_iota(jnp.int32, (8, 128), 0) + first < total
    for j in range(offsets.shape[0]):
        x = [offsets[j, pl.ds(i * slots + first, 8), :] for i in range(3)]
        s = [sums[j, pl.ds(k * slots + first, 8), :] for k in range(SUM_ROWS)]
        a, b, c = s[:3], [s[3:6], s[6:9], s[9:12]], s[12:15]
        norm = x[0] * x[0] + x[1] * x[1] + x[2] * x[2] + REGULARIZE
        along = x[0] * a[0] + x[1] * a[1] + x[2] * a[2] - s[15]
        for i in range(3):
            speed = norm * a[i] + c[i] + along * x[i]
            for k in range(3):
                speed = speed - x[k] * (2.0 * b[k][i] + b[i][k])
            speed = jnp.where(live, speed / sz.points, 0.0)
            speeds[i, pl.ds(first, 8), 128 * j : 128 * j + 128] = speed


def add_up(sz, slots, total, rows, offsets, sums, speeds, hot):
    def eight(q, carry):
        combine(sz, slots, pl.multiple_of(8 * q, 8), total, offsets, sums, speeds)
        return carry

    lax.fori_loop(0, lax.div(total + 7, 8), eight, 0)
    one_hot = hot[...].astype(BF16)
    result = []
    for i in range(3):
        first, second, third = split3(speeds[i])
        parts = [
            lax.dot_general(
                one_hot, part.astype(BF16), (((0,), (0,)), ((), ())), preferred_element_type=F32
            )
            for part in (first, second, third)
        ]
        result.append((parts[0] + parts[1] + parts[2])[:rows])
    return result


def tiles_of_chunk(sz, total, tasks, source_rows, centres, targets, offsets, sums, hot):
    def several(q, carry):
        slots = [q * UNROLL + u for u in range(UNROLL)]
        picks = [(tasks[0, slot], tasks[1, slot]) for slot in slots]
        sources = [load_source(sz, source, source_rows) for _, source in picks]
        points = []
        for slot, (target, source) in zip(slots, picks):
            centre = centres[pl.ds(pl.multiple_of(8 * source, 8), 8), :]
            points.append(
                [
                    load_target(j, target, slot, centre, targets, offsets)
                    for j in range(sz.chunk_tiles)
                ]
            )
        stacks = [
            jnp.concatenate([stack for _, stack in point], axis=1)[:, : sz.chunk]
            for point in points
        ]
        whole = [
            distances(jnp.transpose(stack), source[0]) for stack, source in zip(stacks, sources)
        ]
        whole = [weights(one, 1) for one in whole]
        last = [None] * UNROLL
        if sources[0][2] is not None:
            last = [distances(source[2], stack) for stack, source in zip(stacks, sources)]
            last = [weights(one, 0) for one in last]
        results = [
            tile_sums(*pair, source[1], source[3])
            for pair, source in zip(zip(whole, last), sources)
        ]
        for slot, (target, _), point, result in zip(slots, picks, points, results):
            for j in range(sz.chunk_tiles):
                cut = result[:, 128 * j : 128 * j + 128]
                store_sums(sz.slots, slot, j, point[j][0], cut, offsets, sums)
            mark(slot, target, hot)
        return carry

    lax.fori_loop(0, lax.div(total + UNROLL - 1, UNROLL), several, 0)


def tiles_of_cells(sz, first, total, mine, source_rows, centres, targets, offsets, sums, hot):
    def single(slot, carry):
        target, source = mine[0, slot], mine[1, slot]
        y_stack, m_stack, y_last, m_last = load_source(sz, source, source_rows)
        centre = centres[pl.ds(pl.multiple_of(8 * source, 8), 8), :]
        points = [
            load_target(j, target + first, slot, centre, targets, offsets)
            for j in range(sz.tiles)
        ]
        stack = jnp.concatenate([stack for _, stack in points], axis=1)
        whole = weights(distances(jnp.transpose(stack)[: sz.points], y_stack), 1)
        last = None if y_last is None else weights(distances(y_last, stack[:, : sz.points]), 0)
        result = tile_sums(whole, last, m_stack, m_last)
        for j in range(sz.tiles):
            cut = result[:, 128 * j : 128 * j + 128]
            store_sums(sz.own, slot, j, points[j][0], cut, offsets, sums)
        mark(slot, target, hot)
        return carry

    lax.fori_loop(0, total, single, 0)


def packed(sz, blocks):
    rows = [b[:, : sz.main] for b in blocks] if sz.main else []
    lanes = lane_iota(8)
    for p in range(0, len(blocks), sz.per_pack):
        total = jnp.zeros((8, 128), F32)
        for q, block in enumerate(blocks[p : p + sz.per_pack]):
            rest = jnp.where(lanes < sz.rest, block[:, sz.main : sz.main + 128], 0.0)
            total = total + (pltpu.roll(rest, q * sz.rest, 1) if q else rest)
        rows.append(total)
    return rows


def store_packed(sz, out, blocks):
    first = 0
    count = len(blocks)
    values = packed(sz, blocks)
    if sz.main:
        for b in range(count):
            for m in range(sz.main // 128):
                out[pl.ds(first, 8), :] = values[b][:, 128 * m : 128 * m + 128]
                first += 8
        values = values[count:]
    for value in values:
        out[pl.ds(first, 8), :] = value
        first += 8


def place_packed(sz, lane, arrived, count, store_main, add_rest):
    first = 0
    if sz.main:
        for b in range(count):
            for m in range(sz.main // 128):
                store_main(b, m, arrived[pl.ds(first, 8), :])
                first += 8
    start = sz.rest * lane
    lanes = lane_iota(8)
    for b in range(count):
        pack, q = divmod(b, sz.per_pack)
        value = arrived[pl.ds(first + 8 * pack, 8), :]
        value = pltpu.roll(value, lax.rem(start - q * sz.rest + 128, 128), 1)
        for tile in range(sz.rest_tiles):
            inside = (lanes + 128 * tile >= start) & (lanes + 128 * tile < start + sz.rest)
            add_rest(b, tile, jnp.where(inside, value, 0.0))


def source_kernel(sz, *refs):
    inputs, (high_out, low_out, source_rows, centres), held, sems = (
        refs[:2],
        refs[2:6],
        refs[6:8],
        refs[8],
    )
    for copy in fetch(inputs, held, sems):
        copy.wait()
    positions, bend = held
    high_out[...], low_out[...] = split2(bend[...])
    value = jnp.concatenate([positions[i] for i in range(3)], axis=0)
    value = jnp.concatenate(
        [value, jnp.zeros((3 * sz.cells, sz.width - sz.points), F32)], axis=1
    )
    make_sources(sz, value, high_out[...], low_out[...], source_rows, centres, 0)


def first_kernel(sz, *refs):
    inputs, (chunk_out, ghost_out, tasks), refs = refs[:7], refs[7:10], refs[10:]
    source_rows, centres, targets, offsets, sums, speeds, hot, moved, pool = refs[:9]
    send, positions, arrived, high, low, staged, lists, sems = refs[9:]
    me, lane = lax.axis_index("space"), lax.axis_index("lane")
    own_rows = source_rows.at[:, pl.ds(0, SOURCE_ROWS * sz.cells)]
    own_centres = centres.at[pl.ds(0, 8 * sz.cells)]
    held = [arrived, send, positions, high, low, own_rows, own_centres]
    copies = fetch(inputs, held, sems)
    copies[0].wait()
    for other in range(sz.lanes):
        row = ((me * sz.lanes + other) * sz.group) * 4 + 3
        value = pltpu.roll(arrived[pl.ds(row, 1), :], 128 - 3 * sz.rest, 1)
        staged[pl.ds(other, 1), :] = value.astype(jnp.int32)
    copies.append(pltpu.make_async_copy(staged, lists, sems.at[7]))
    copies[7].start()
    pool[...] = jnp.zeros_like(pool)
    take_ghosts(sz, arrived, pool, up(sz.owners * sz.group, 8), 0)
    hot[...] = jnp.zeros_like(hot)
    speeds[...] = jnp.zeros_like(speeds)
    for copy in copies[1:5]:
        copy.wait()
    make_sources(sz, pool[...], high[...], low[...], source_rows, centres, sz.cells)
    make_targets(
        sz, lambda i, g: own_chunk(sz, lane, positions.at[i], pl.ds(8 * g, 8)), targets
    )
    for copy in copies[5:]:
        copy.wait()
    total = build_list(sz, lists, tasks)
    tiles_of_chunk(sz, total, tasks, source_rows, centres, targets, offsets, sums, hot)
    velocity = add_up(sz, sz.slots, total, sz.cells, offsets, sums, speeds, hot)
    blocks = []
    for i in range(3):
        for g in range(0, sz.cells, 8):
            chunk = own_chunk(sz, lane, positions.at[i], pl.ds(g, 8))
            block = chunk + TIME_STEP * velocity[i][g : g + 8]
            moved[pl.ds(i * sz.rows + g, 8), :] = block
            blocks.append(block)
    store_packed(sz, chunk_out, blocks)
    send_ghosts(sz, send, moved, ghost_out, jnp.zeros((1, 128), F32))


def second_kernel(sz, *refs):
    count = sz.lanes + 4
    inputs, (moved_out, velocity_out), refs = refs[:count], refs[count : count + 2], refs[count + 2 :]
    source_rows, centres, targets, offsets, sums, speeds, hot, pool, mine = refs[:9]
    held, sems = refs[9:-1], refs[-1]
    copies = fetch(inputs, held, sems)
    tasks, arrived, chunks, (high, low) = held[0], held[1], held[2:-2], held[-2:]
    hot[...] = jnp.zeros_like(hot)
    speeds[...] = jnp.zeros_like(speeds)
    lane = lax.axis_index("lane")
    pool[...] = jnp.zeros_like(pool)
    for copy in copies[:-2]:
        copy.wait()
    per = sz.cells // 8
    for k in range(sz.lanes):
        other = lane ^ k

        def row_of(b):
            return (b // per) * sz.pool + 8 * (b % per)

        def store_main(b, m, value):
            cut = pl.ds(pl.multiple_of(other * sz.main + 128 * m, 128), 128)
            pool[pl.ds(row_of(b), 8), cut] = value

        def add_rest(b, tile, value):
            offset = sz.main * sz.lanes + 128 * tile
            cut = (pl.ds(row_of(b), 8), slice(offset, offset + 128))
            pool[cut] = pool[cut] + value

        place_packed(sz, other, chunks[k], 3 * per, store_main, add_rest)
    take_ghosts(sz, arrived, pool, sz.pool, sz.cells)
    total = own_list(sz, lane, tasks, mine)
    for copy in copies[-2:]:
        copy.wait()
    make_sources(sz, pool[...], high[...], low[...], source_rows, centres, 0)
    make_targets(sz, lambda i, g: pool[pl.ds(i * sz.pool + 8 * g, 8), :], targets)
    first = lane * sz.share
    tiles_of_cells(sz, first, total, mine, source_rows, centres, targets, offsets, sums, hot)
    velocity = add_up(sz, sz.own, total, up(sz.share, 8), offsets, sums, speeds, hot)
    for i in range(3):
        speed = velocity[i]
        moved = share_rows(sz, pool, i * sz.pool, lane) + TIME_STEP * speed
        velocity_out[i] = speed[: sz.share, : sz.points]
        moved_out[i] = moved[: sz.share, : sz.points]


def share_rows(sz, ref, base, lane):
    if sz.share % 8 == 0:
        return ref[pl.ds(pl.multiple_of(base + lane * sz.share, 8), sz.share), :]
    rows = [ref[pl.ds(base + lane * sz.share + c, 1), :] for c in range(sz.share)]
    rows.append(jnp.zeros((8 - sz.share, rows[0].shape[1]), F32))
    return jnp.concatenate(rows, axis=0)


def scratch(sz, tiles, slots):
    return [
        pltpu.VMEM((sz.tiles, SOURCE_ROWS * sz.pool, 128), F32),
        pltpu.VMEM((8 * sz.pool, 128), F32),
        pltpu.VMEM((tiles, 8 * sz.rows, 128), F32),
        pltpu.VMEM((tiles, 8 * slots, 128), F32),
        pltpu.VMEM((tiles, SUM_ROWS * slots, 128), F32),
        pltpu.VMEM((3, slots, 128 * tiles), F32),
        pltpu.VMEM((slots, 128), F32),
    ]


def swap(value, axis, size, k):
    return lax.ppermute(value, axis, [(d, d ^ k) for d in range(size)])


def shards(positions, bend_op, send_list, task_target, task_source, task_count):
    owners, lanes = lax.axis_size("space"), lax.axis_size("lane")
    cells, points = positions.shape[0], positions.shape[2]
    sz = sizes(owners, lanes, cells, points, task_target.shape[1], send_list.shape[1])
    params = pltpu.CompilerParams(vmem_limit_bytes=60 << 20)
    shape = jax.ShapeDtypeStruct
    both = ("space", "lane")
    by_component = jnp.transpose(positions, (1, 0, 2))
    list_rows = up(lanes, 8)
    slot_shape = shape((4 * sz.group * owners * lanes, 128), F32)
    leaving, send = pl.pallas_call(
        functools.partial(pick_kernel, sz),
        out_shape=[slot_shape, shape(send_list.shape, jnp.int32)],
        in_specs=[HBM] * 5,
        out_specs=[VMEM, SMEM],
        scratch_shapes=[
            pltpu.SMEM(send_list.shape, jnp.int32),
            pltpu.VMEM(task_target.shape, jnp.int32),
            pltpu.VMEM(task_source.shape, jnp.int32),
            pltpu.SMEM(task_count.shape, jnp.int32),
            pltpu.VMEM(by_component.shape, F32),
            pltpu.VMEM((3 * sz.rows, sz.chunk_wide), F32),
            pltpu.SemaphoreType.DMA((5,)),
        ],
        compiler_params=params,
        name="pick_cells",
    )(send_list, task_target, task_source, task_count, by_component)
    arrived = lax.all_to_all(leaving, both, split_axis=0, concat_axis=0, tiled=True)
    high, low, own_rows, own_centres = pl.pallas_call(
        functools.partial(source_kernel, sz),
        out_shape=[
            shape(bend_op.shape, BF16),
            shape(bend_op.shape, BF16),
            shape((sz.tiles, SOURCE_ROWS * cells, 128), F32),
            shape((8 * cells, 128), F32),
        ],
        in_specs=[HBM] * 2,
        out_specs=[VMEM] * 4,
        scratch_shapes=[
            pltpu.VMEM(by_component.shape, F32),
            pltpu.VMEM(bend_op.shape, F32),
            pltpu.SemaphoreType.DMA((2,)),
        ],
        compiler_params=params,
        cost_estimate=pl.CostEstimate(flops=10**9, bytes_accessed=10**7, transcendentals=0),
        name="first_sources",
    )(by_component, bend_op)
    chunk, leaving, tasks = pl.pallas_call(
        functools.partial(first_kernel, sz),
        out_shape=[
            shape((pack_rows(sz, cells), 128), F32),
            slot_shape,
            shape((3, sz.slots), jnp.int32),
        ],
        in_specs=[HBM] * 7,
        out_specs=[VMEM, VMEM, SMEM],
        scratch_shapes=scratch(sz, sz.chunk_tiles, sz.slots)
        + [
            pltpu.VMEM((3 * sz.rows, sz.chunk_wide), F32),
            pltpu.VMEM((3 * up(sz.owners * sz.group, 8), sz.width), F32),
            pltpu.SMEM(send_list.shape, jnp.int32),
            pltpu.VMEM(by_component.shape, F32),
            pltpu.VMEM(slot_shape.shape, F32),
            pltpu.VMEM(bend_op.shape, BF16),
            pltpu.VMEM(bend_op.shape, BF16),
            pltpu.VMEM((list_rows, 128), jnp.int32),
            pltpu.SMEM((list_rows, 128), jnp.int32),
            pltpu.SemaphoreType.DMA((8,)),
        ],
        compiler_params=params,
        name="first_step",
    )(arrived, send, by_component, high, low, own_rows, own_centres)
    arrived = lax.all_to_all(leaving, both, split_axis=0, concat_axis=0, tiled=True)
    chunks = [chunk] + [swap(chunk, "lane", lanes, k) for k in range(1, lanes)]
    result = shape((3, sz.share, points), F32)
    outputs = pl.pallas_call(
        functools.partial(second_kernel, sz),
        out_shape=[result, result],
        in_specs=[HBM] * (lanes + 4),
        out_specs=[VMEM] * 2,
        scratch_shapes=scratch(sz, sz.tiles, sz.own)
        + [
            pltpu.VMEM((3 * sz.pool, sz.width), F32),
            pltpu.SMEM((2, sz.own + 8), jnp.int32),
            pltpu.SMEM(tasks.shape, jnp.int32),
            pltpu.VMEM(slot_shape.shape, F32),
        ]
        + [pltpu.VMEM(chunk.shape, F32)] * lanes
        + [pltpu.VMEM(bend_op.shape, BF16)] * 2
        + [pltpu.SemaphoreType.DMA((lanes + 4,))],
        compiler_params=params,
        name="second_step",
    )(tasks, arrived, *chunks, high, low)
    return tuple(jnp.transpose(output, (1, 0, 2)) for output in outputs)


def solution(mesh):
    in_specs = (
        P("space", None, None),
        P(),
        P("space", None),
        P(("space", "lane"), None),
        P(("space", "lane"), None),
        P(("space", "lane")),
    )
    out_specs = (P(("space", "lane"), None, None), P(("space", "lane"), None, None))
    return jax.shard_map(shards, mesh=mesh, in_specs=in_specs, out_specs=out_specs, check_vma=False)
```

```python
import functools
from types import SimpleNamespace

import jax
import jax.numpy as jnp
from jax import lax
from jax.experimental import pallas as pl
from jax.experimental.pallas import tpu as pltpu
from jax.sharding import PartitionSpec as P

REGULARIZE = 0.25
TIME_STEP = 0.5
UNROLL = 4
SOURCE_ROWS = 24
SUM_ROWS = 16

F32 = jnp.float32
BF16 = jnp.bfloat16
VMEM = pl.BlockSpec(memory_space=pltpu.VMEM)
SMEM = pl.BlockSpec(memory_space=pltpu.SMEM)
HBM = pl.BlockSpec(memory_space=pltpu.HBM)


def up(value, step):
    return -(-value // step) * step


def sizes(owners, lanes, cells, points, cap, listed):
    main = 128 * (points // (128 * lanes))
    rest = (points - main * lanes) // lanes
    group = listed // owners
    pool = up(cells + listed, 8)
    per_pack = 128 // rest
    return SimpleNamespace(
        owners=owners,
        lanes=lanes,
        cells=cells,
        points=points,
        cap=cap,
        group=group,
        width=up(points, 128),
        tiles=up(points, 128) // 128,
        main=main,
        rest=rest,
        rest_tiles=up(rest * lanes, 128) // 128,
        chunk=main + rest,
        chunk_wide=main + up(rest, 128),
        chunk_tiles=(main + up(rest, 128)) // 128,
        per_pack=per_pack,
        pool=pool,
        share=cells // lanes,
        slots=up(lanes * cap + UNROLL, 8),
        rows=cells + 8,
        own=up(lanes * cap, 8),
    )


def pack_rows(sz, rows):
    return (3 * rows * sz.main // 128) + 8 * up(3 * rows // 8, sz.per_pack) // sz.per_pack


def split2(value):
    high = value.astype(BF16)
    return high, (value - high.astype(F32)).astype(BF16)


def split3(value):
    first = value.astype(BF16).astype(F32)
    left = value - first
    second = left.astype(BF16).astype(F32)
    return first, second, left - second


def lane_iota(rows):
    return lax.broadcasted_iota(jnp.int32, (rows, 128), 1)


def fetch(sources, targets, sems):
    copies = [
        pltpu.make_async_copy(source, target, sems.at[q])
        for q, (source, target) in enumerate(zip(sources, targets))
    ]
    for copy in copies:
        copy.start()
    return copies


def loop(count, body):
    if count <= 8:
        for q in range(count):
            body(q)
    else:

        def step(q, carry):
            body(q)
            return carry

        lax.fori_loop(0, count, step, 0)


def own_chunk(sz, lane, ref, rows):
    parts = []
    if sz.main:
        parts.append(ref[rows, pl.ds(pl.multiple_of(lane * sz.main, 128), sz.main)])
    start = sz.rest * lane
    lanes = lane_iota(8)
    rest = jnp.zeros((8, 128), F32)
    for tile in range(sz.rest_tiles):
        offset = sz.main * sz.lanes + 128 * tile
        block = ref[rows, offset : min(offset + 128, ref.shape[-1])]
        if block.shape[1] < 128:
            block = jnp.concatenate([block, jnp.zeros((8, 128 - block.shape[1]), F32)], axis=1)
        inside = (lanes + 128 * tile >= start) & (lanes + 128 * tile < start + sz.rest)
        rest = rest + jnp.where(inside, block, 0.0)
    rest = pltpu.roll(rest, lax.rem(128 * sz.rest_tiles - start, 128), 1)
    parts.append(rest)
    return jnp.concatenate(parts, axis=1) if len(parts) > 1 else parts[0]


def send_ghosts(sz, send, chunks, out, tasks):
    lanes = lane_iota(1)

    def one(d):
        for g in range(sz.group):
            cell = send[0, d * sz.group + g]
            rows = []
            last = tasks
            for i in range(3):
                row = chunks[pl.ds(i * sz.rows + cell, 1), :]
                rows.append(row[:, :128] if sz.main else jnp.zeros((1, 128), F32))
                piece = jnp.where(lanes < sz.rest, row[:, sz.main : sz.main + 128], 0.0)
                last = last + (pltpu.roll(piece, i * sz.rest, 1) if i else piece)
            rows.append(last)
            for other in range(sz.lanes):
                first = ((d * sz.lanes + other) * sz.group + g) * 4
                for q, row in enumerate(rows):
                    out[pl.ds(first + q, 1), :] = row

    loop(sz.owners, one)


def pick_kernel(sz, *refs):
    inputs, (out, send_out), held, (chunks, sems) = refs[:5], refs[5:7], refs[7:12], refs[12:]
    for copy in fetch(inputs, held, sems):
        copy.wait()
    send, target, source, count, positions = held
    for j in range(send_out.shape[1]):
        send_out[0, j] = send[0, j]
    lane = lax.axis_index("lane")
    for i in range(3):
        for g in range(0, sz.cells, 8):
            value = own_chunk(sz, lane, positions.at[i], pl.ds(g, 8))
            chunks[pl.ds(i * sz.rows + g, 8), :] = value
    spare = jnp.zeros((1, 128 - sz.cap), F32)
    tasks = jnp.where(lane_iota(1) == 3 * sz.rest + 2 * sz.cap, count[0].astype(F32), 0.0)
    for q, row in enumerate((target, source)):
        wide = jnp.concatenate([row[...].astype(F32), spare], axis=1)
        tasks = tasks + pltpu.roll(wide, 3 * sz.rest + q * sz.cap, 1)
    send_ghosts(sz, send, chunks, out, tasks)


def take_ghosts(sz, arrived, pool, stride, base):
    lanes = lane_iota(1)

    def one(d):
        for g in range(sz.group):
            first = [((d * sz.lanes + lane) * sz.group + g) * 4 for lane in range(sz.lanes)]
            last = [arrived[pl.ds(row + 3, 1), :] for row in first]
            for i in range(3):
                tiles = []
                if sz.main:
                    tiles += [arrived[pl.ds(row + i, 1), :] for row in first]
                for tile in range(sz.rest_tiles):
                    total = jnp.zeros((1, 128), F32)
                    for lane in range(sz.lanes):
                        start = sz.rest * lane
                        if start + sz.rest <= 128 * tile or start >= 128 * tile + 128:
                            continue
                        shift = (start - i * sz.rest) % 128
                        value = pltpu.roll(last[lane], shift, 1) if shift else last[lane]
                        at = lanes + 128 * tile
                        total = jnp.where((at >= start) & (at < start + sz.rest), value, total)
                    tiles.append(total)
                place = pl.ds(i * stride + base + d * sz.group + g, 1)
                pool[place, :] = jnp.concatenate(tiles, axis=1)

    loop(sz.owners, one)


def build_list(sz, lists, tasks):
    total = jnp.int32(0)
    for lane in range(sz.lanes):

        def step(j, total, lane=lane):
            tasks[0, total] = lists[lane, j]
            tasks[1, total] = lists[lane, sz.cap + j]
            return total + 1

        total = lax.fori_loop(0, lists[lane, 2 * sz.cap], step, total)
    for u in range(UNROLL):
        tasks[0, total + u] = jnp.int32(sz.cells)
        tasks[1, total + u] = jnp.int32(0)
    tasks[2, 0] = total
    return total


def own_list(sz, lane, tasks, mine):
    first = lane * sz.share

    def step(t, count):
        target = tasks[0, t] - first
        mine[0, count] = target
        mine[1, count] = tasks[1, t]
        return count + ((target >= 0) & (target < sz.share)).astype(jnp.int32)

    return lax.fori_loop(0, tasks[2, 0], step, jnp.int32(0))


def products(value, bend_high, bend_low):
    high, low = split2(value)
    dot = functools.partial(jnp.dot, preferred_element_type=F32)
    return dot(high, bend_high) + dot(low, bend_high) + dot(high, bend_low)


def make_sources(sz, value, bend_high, bend_low, source_rows, centres, first):
    count = value.shape[0] // 3
    forces = products(value[:, : sz.points], bend_high, bend_low)
    forces = jnp.concatenate(
        [forces, jnp.zeros((3 * count, sz.width - sz.points), F32)], axis=1
    )
    middle = jnp.sum(value, axis=1, keepdims=True) / sz.points
    for g in range(count // 8):
        where = [i * count + 8 * g for i in range(3)]
        middles = [jnp.broadcast_to(middle[w : w + 8], (8, 128)) for w in where]
        middles += [jnp.zeros((8, 128), F32)] * 5
        for i, row in enumerate(middles):
            centres[pl.ds(8 * (first + 8 * g) + i, 8, stride=8), :] = row
        for j in range(sz.tiles):
            cut = slice(128 * j, 128 * j + 128)
            y = [value[w : w + 8, cut] - m for w, m in zip(where, middles)]
            f = [forces[w : w + 8, cut] for w in where]
            norm = y[0] * y[0] + y[1] * y[1] + y[2] * y[2] + REGULARIZE
            along = y[0] * f[0] + y[1] * f[1] + y[2] * f[2]
            one, zero = jnp.ones((8, 128), F32), jnp.zeros((8, 128), F32)
            rows = [y[0], y[1], y[2], norm, one, zero, zero, zero]
            rows += f
            rows += [y[i] * f[k] for i in range(3) for k in range(3)]
            rows += [norm * f[i] + along * y[i] for i in range(3)]
            rows += [along]
            for k, row in enumerate(rows):
                place = pl.ds(SOURCE_ROWS * (first + 8 * g) + k, 8, stride=SOURCE_ROWS)
                source_rows.at[j][place, :] = row


def make_targets(sz, blocks, targets):
    targets[...] = jnp.zeros_like(targets)
    for g in range(sz.cells // 8):
        for i in range(3):
            block = blocks(i, g)
            for j in range(targets.shape[0]):
                cut = slice(128 * j, 128 * j + 128)
                targets.at[j][pl.ds(64 * g + i, 8, stride=8), :] = block[:, cut]


def load_source(sz, source, source_rows):
    held = [
        source_rows[j, pl.ds(pl.multiple_of(SOURCE_ROWS * source, 8), SOURCE_ROWS), :]
        for j in range(sz.tiles)
    ]
    held = jnp.concatenate(held, axis=1)
    y1, y2, y3 = split3(held[:8])
    y_stack = jnp.concatenate([y1, y1, y2, y2, y1, y3], axis=0).astype(BF16)
    m_stack = jnp.concatenate(split3(held[8:]), axis=0)
    whole = 128 * (sz.points // 128)
    parts = [m_stack[:, :whole].astype(BF16)] * 2
    if whole < sz.points:
        last = m_stack[:, whole:]
        last = last + pltpu.roll(last, sz.points - whole, 1)
        parts.append(last.astype(BF16)[:, : 2 * (sz.points - whole)])
    m_stack = jnp.concatenate(parts, axis=1)
    return jnp.transpose(y_stack)[: sz.points], y_stack[:, : sz.points], m_stack


def load_target(j, target, slot, centre, targets, offsets):
    row = lax.broadcasted_iota(jnp.int32, (8, 128), 0)
    x = targets[j, pl.ds(pl.multiple_of(8 * target, 8), 8), :] - centre
    square = x * x
    norm = pltpu.roll(square, 2, 0) + pltpu.roll(square, 3, 0) + pltpu.roll(square, 4, 0)
    side = jnp.where(row == 4, norm, jnp.where(row == 3, 1.0, 0.0))
    x_side = jnp.where(row < 3, -2.0 * x, side)
    x1, x2, x3 = split3(x_side)
    return x, jnp.concatenate([x1, x2, x1, x2, x3, x1], axis=0).astype(BF16)


def distances(one_stack, other_stack):
    return jnp.dot(one_stack, other_stack, preferred_element_type=F32)


def weights(shifted):
    inverse = lax.rsqrt(shifted)
    return split2(inverse * inverse * inverse)


def tile_sums(sz, main, rest, source):
    y_turned, y_stack, m_stack = source
    whole = 128 * (sz.points // 128)
    results = []
    if main is not None:
        high, low = weights(distances(y_turned, main))
        parts = [high[:whole], low[:whole], high[whole:], low[whole:]]
        stack = jnp.concatenate(parts[: 4 if whole < sz.points else 2], axis=0)
        results.append(jnp.dot(m_stack, stack, preferred_element_type=F32))
    if rest is not None:
        high, low = weights(distances(jnp.transpose(rest), y_stack))
        parts = [high[:, :whole], low[:, :whole]]
        if whole < sz.points:
            parts += [high[:, whole:], low[:, whole:]]
        stack = jnp.concatenate(parts, axis=1)
        result = lax.dot_general(
            m_stack, stack, (((1,), (1,)), ((), ())), preferred_element_type=F32
        )
        spare = jnp.zeros((result.shape[0], 128 - result.shape[1]), F32)
        results.append(jnp.concatenate([result, spare], axis=1))
    result = jnp.concatenate(results, axis=1) if len(results) > 1 else results[0]
    return result[:SUM_ROWS] + result[SUM_ROWS : 2 * SUM_ROWS] + result[2 * SUM_ROWS :]


def blocks_of(stacks, main, rest):
    whole = stacks[: main // 128]
    first = jnp.concatenate(whole, axis=1) if whole else None
    return first, stacks[main // 128][:, :rest] if rest else None


def store_sums(slots, slot, j, x, result, offsets, sums):
    offsets.at[j][pl.ds(slot, 8, stride=slots), :] = x
    for h in range(0, SUM_ROWS, 8):
        sums.at[j][pl.ds(h * slots + slot, 8, stride=slots), :] = result[h : h + 8]


def mark(slot, target, hot):
    hot[pl.ds(slot, 1), :] = jnp.where(lane_iota(1) == target, 1.0, 0.0)


def combine(sz, slots, first, total, offsets, sums, speeds):
    live = lax.broadcasted_iota(jnp.int32, (8, 128), 0) + first < total
    for j in range(offsets.shape[0]):
        x = [offsets[j, pl.ds(i * slots + first, 8), :] for i in range(3)]
        s = [sums[j, pl.ds(k * slots + first, 8), :] for k in range(SUM_ROWS)]
        a, b, c = s[:3], [s[3:6], s[6:9], s[9:12]], s[12:15]
        norm = x[0] * x[0] + x[1] * x[1] + x[2] * x[2] + REGULARIZE
        along = x[0] * a[0] + x[1] * a[1] + x[2] * a[2] - s[15]
        for i in range(3):
            speed = norm * a[i] + c[i] + along * x[i]
            for k in range(3):
                speed = speed - x[k] * (2.0 * b[k][i] + b[i][k])
            speed = jnp.where(live, speed / sz.points, 0.0)
            speeds[i, pl.ds(first, 8), 128 * j : 128 * j + 128] = speed


def add_up(sz, slots, total, rows, offsets, sums, speeds, hot):
    def eight(q, carry):
        combine(sz, slots, pl.multiple_of(8 * q, 8), total, offsets, sums, speeds)
        return carry

    lax.fori_loop(0, lax.div(total + 7, 8), eight, 0)
    one_hot = hot[...].astype(BF16)
    result = []
    for i in range(3):
        first, second, third = split3(speeds[i])
        parts = [
            lax.dot_general(
                one_hot, part.astype(BF16), (((0,), (0,)), ((), ())), preferred_element_type=F32
            )
            for part in (first, second, third)
        ]
        result.append((parts[0] + parts[1] + parts[2])[:rows])
    return result


def tiles_of_chunk(sz, total, tasks, source_rows, centres, targets, offsets, sums, hot):
    def several(q, carry):
        slots = [q * UNROLL + u for u in range(UNROLL)]
        picks = [(tasks[0, slot], tasks[1, slot]) for slot in slots]
        sources = [load_source(sz, source, source_rows) for _, source in picks]
        points = []
        for slot, (target, source) in zip(slots, picks):
            centre = centres[pl.ds(pl.multiple_of(8 * source, 8), 8), :]
            points.append(
                [
                    load_target(j, target, slot, centre, targets, offsets)
                    for j in range(sz.chunk_tiles)
                ]
            )
        blocks = [blocks_of([t for _, t in point], sz.main, sz.rest) for point in points]
        results = [tile_sums(sz, *block, source) for block, source in zip(blocks, sources)]
        for slot, (target, _), point, result in zip(slots, picks, points, results):
            for j in range(sz.chunk_tiles):
                cut = result[:, 128 * j : 128 * j + 128]
                store_sums(sz.slots, slot, j, point[j][0], cut, offsets, sums)
            mark(slot, target, hot)
        return carry

    lax.fori_loop(0, lax.div(total + UNROLL - 1, UNROLL), several, 0)


def tiles_of_cells(sz, first, total, mine, source_rows, centres, targets, offsets, sums, hot):
    def single(slot, carry):
        target, source = mine[0, slot], mine[1, slot]
        held = load_source(sz, source, source_rows)
        centre = centres[pl.ds(pl.multiple_of(8 * source, 8), 8), :]
        points = [
            load_target(j, target + first, slot, centre, targets, offsets)
            for j in range(sz.tiles)
        ]
        whole = 128 * (sz.points // 128)
        block = blocks_of([stack for _, stack in points], whole, sz.points - whole)
        result = tile_sums(sz, *block, held)
        for j in range(sz.tiles):
            cut = result[:, 128 * j : 128 * j + 128]
            store_sums(sz.own, slot, j, points[j][0], cut, offsets, sums)
        mark(slot, target, hot)
        return carry

    lax.fori_loop(0, total, single, 0)


def packed(sz, blocks):
    rows = [b[:, : sz.main] for b in blocks] if sz.main else []
    lanes = lane_iota(8)
    for p in range(0, len(blocks), sz.per_pack):
        total = jnp.zeros((8, 128), F32)
        for q, block in enumerate(blocks[p : p + sz.per_pack]):
            rest = jnp.where(lanes < sz.rest, block[:, sz.main : sz.main + 128], 0.0)
            total = total + (pltpu.roll(rest, q * sz.rest, 1) if q else rest)
        rows.append(total)
    return rows


def store_packed(sz, out, blocks):
    first = 0
    count = len(blocks)
    values = packed(sz, blocks)
    if sz.main:
        for b in range(count):
            for m in range(sz.main // 128):
                out[pl.ds(first, 8), :] = values[b][:, 128 * m : 128 * m + 128]
                first += 8
        values = values[count:]
    for value in values:
        out[pl.ds(first, 8), :] = value
        first += 8


def place_packed(sz, lane, arrived, count, store_main, add_rest):
    first = 0
    if sz.main:
        for b in range(count):
            for m in range(sz.main // 128):
                store_main(b, m, arrived[pl.ds(first, 8), :])
                first += 8
    start = sz.rest * lane
    lanes = lane_iota(8)
    for b in range(count):
        pack, q = divmod(b, sz.per_pack)
        value = arrived[pl.ds(first + 8 * pack, 8), :]
        value = pltpu.roll(value, lax.rem(start - q * sz.rest + 128, 128), 1)
        for tile in range(sz.rest_tiles):
            inside = (lanes + 128 * tile >= start) & (lanes + 128 * tile < start + sz.rest)
            add_rest(b, tile, jnp.where(inside, value, 0.0))


def source_kernel(sz, *refs):
    inputs, (high_out, low_out, source_rows, centres), held, sems = (
        refs[:2],
        refs[2:6],
        refs[6:8],
        refs[8],
    )
    for copy in fetch(inputs, held, sems):
        copy.wait()
    positions, bend = held
    high_out[...], low_out[...] = split2(bend[...])
    value = jnp.concatenate([positions[i] for i in range(3)], axis=0)
    value = jnp.concatenate(
        [value, jnp.zeros((3 * sz.cells, sz.width - sz.points), F32)], axis=1
    )
    make_sources(sz, value, high_out[...], low_out[...], source_rows, centres, 0)


def first_kernel(sz, *refs):
    inputs, (chunk_out, ghost_out, tasks), refs = refs[:7], refs[7:10], refs[10:]
    source_rows, centres, targets, offsets, sums, speeds, hot, moved, pool = refs[:9]
    send, positions, arrived, high, low, staged, lists, sems = refs[9:]
    me, lane = lax.axis_index("space"), lax.axis_index("lane")
    own_rows = source_rows.at[:, pl.ds(0, SOURCE_ROWS * sz.cells)]
    own_centres = centres.at[pl.ds(0, 8 * sz.cells)]
    held = [arrived, send, positions, high, low, own_rows, own_centres]
    copies = fetch(inputs, held, sems)
    copies[0].wait()
    for other in range(sz.lanes):
        row = ((me * sz.lanes + other) * sz.group) * 4 + 3
        value = pltpu.roll(arrived[pl.ds(row, 1), :], 128 - 3 * sz.rest, 1)
        staged[pl.ds(other, 1), :] = value.astype(jnp.int32)
    copies.append(pltpu.make_async_copy(staged, lists, sems.at[7]))
    copies[7].start()
    pool[...] = jnp.zeros_like(pool)
    take_ghosts(sz, arrived, pool, up(sz.owners * sz.group, 8), 0)
    hot[...] = jnp.zeros_like(hot)
    speeds[...] = jnp.zeros_like(speeds)
    for copy in copies[1:5]:
        copy.wait()
    make_sources(sz, pool[...], high[...], low[...], source_rows, centres, sz.cells)
    make_targets(
        sz, lambda i, g: own_chunk(sz, lane, positions.at[i], pl.ds(8 * g, 8)), targets
    )
    for copy in copies[5:]:
        copy.wait()
    total = build_list(sz, lists, tasks)
    tiles_of_chunk(sz, total, tasks, source_rows, centres, targets, offsets, sums, hot)
    velocity = add_up(sz, sz.slots, total, sz.cells, offsets, sums, speeds, hot)
    blocks = []
    for i in range(3):
        for g in range(0, sz.cells, 8):
            chunk = own_chunk(sz, lane, positions.at[i], pl.ds(g, 8))
            block = chunk + TIME_STEP * velocity[i][g : g + 8]
            moved[pl.ds(i * sz.rows + g, 8), :] = block
            blocks.append(block)
    store_packed(sz, chunk_out, blocks)
    send_ghosts(sz, send, moved, ghost_out, jnp.zeros((1, 128), F32))


def second_kernel(sz, *refs):
    count = sz.lanes + 4
    inputs, (moved_out, velocity_out), refs = refs[:count], refs[count : count + 2], refs[count + 2 :]
    source_rows, centres, targets, offsets, sums, speeds, hot, pool, mine = refs[:9]
    held, sems = refs[9:-1], refs[-1]
    copies = fetch(inputs, held, sems)
    tasks, arrived, chunks, (high, low) = held[0], held[1], held[2:-2], held[-2:]
    hot[...] = jnp.zeros_like(hot)
    speeds[...] = jnp.zeros_like(speeds)
    lane = lax.axis_index("lane")
    pool[...] = jnp.zeros_like(pool)
    for copy in copies[:-2]:
        copy.wait()
    per = sz.cells // 8
    for k in range(sz.lanes):
        other = lane ^ k

        def row_of(b):
            return (b // per) * sz.pool + 8 * (b % per)

        def store_main(b, m, value):
            cut = pl.ds(pl.multiple_of(other * sz.main + 128 * m, 128), 128)
            pool[pl.ds(row_of(b), 8), cut] = value

        def add_rest(b, tile, value):
            offset = sz.main * sz.lanes + 128 * tile
            cut = (pl.ds(row_of(b), 8), slice(offset, offset + 128))
            pool[cut] = pool[cut] + value

        place_packed(sz, other, chunks[k], 3 * per, store_main, add_rest)
    take_ghosts(sz, arrived, pool, sz.pool, sz.cells)
    total = own_list(sz, lane, tasks, mine)
    for copy in copies[-2:]:
        copy.wait()
    make_sources(sz, pool[...], high[...], low[...], source_rows, centres, 0)
    make_targets(sz, lambda i, g: pool[pl.ds(i * sz.pool + 8 * g, 8), :], targets)
    first = lane * sz.share
    tiles_of_cells(sz, first, total, mine, source_rows, centres, targets, offsets, sums, hot)
    velocity = add_up(sz, sz.own, total, up(sz.share, 8), offsets, sums, speeds, hot)
    for i in range(3):
        speed = velocity[i]
        moved = share_rows(sz, pool, i * sz.pool, lane) + TIME_STEP * speed
        velocity_out[i] = speed[: sz.share, : sz.points]
        moved_out[i] = moved[: sz.share, : sz.points]


def share_rows(sz, ref, base, lane):
    if sz.share % 8 == 0:
        return ref[pl.ds(pl.multiple_of(base + lane * sz.share, 8), sz.share), :]
    rows = [ref[pl.ds(base + lane * sz.share + c, 1), :] for c in range(sz.share)]
    rows.append(jnp.zeros((8 - sz.share, rows[0].shape[1]), F32))
    return jnp.concatenate(rows, axis=0)


def scratch(sz, tiles, slots):
    return [
        pltpu.VMEM((sz.tiles, SOURCE_ROWS * sz.pool, 128), F32),
        pltpu.VMEM((8 * sz.pool, 128), F32),
        pltpu.VMEM((tiles, 8 * sz.rows, 128), F32),
        pltpu.VMEM((tiles, 8 * slots, 128), F32),
        pltpu.VMEM((tiles, SUM_ROWS * slots, 128), F32),
        pltpu.VMEM((3, slots, 128 * tiles), F32),
        pltpu.VMEM((slots, 128), F32),
    ]


def swap(value, axis, size, k):
    return lax.ppermute(value, axis, [(d, d ^ k) for d in range(size)])


def shards(positions, bend_op, send_list, task_target, task_source, task_count):
    owners, lanes = lax.axis_size("space"), lax.axis_size("lane")
    cells, points = positions.shape[0], positions.shape[2]
    sz = sizes(owners, lanes, cells, points, task_target.shape[1], send_list.shape[1])
    params = pltpu.CompilerParams(vmem_limit_bytes=60 << 20)
    shape = jax.ShapeDtypeStruct
    both = ("space", "lane")
    by_component = jnp.transpose(positions, (1, 0, 2))
    list_rows = up(lanes, 8)
    slot_shape = shape((4 * sz.group * owners * lanes, 128), F32)
    leaving, send = pl.pallas_call(
        functools.partial(pick_kernel, sz),
        out_shape=[slot_shape, shape(send_list.shape, jnp.int32)],
        in_specs=[HBM] * 5,
        out_specs=[VMEM, SMEM],
        scratch_shapes=[
            pltpu.SMEM(send_list.shape, jnp.int32),
            pltpu.VMEM(task_target.shape, jnp.int32),
            pltpu.VMEM(task_source.shape, jnp.int32),
            pltpu.SMEM(task_count.shape, jnp.int32),
            pltpu.VMEM(by_component.shape, F32),
            pltpu.VMEM((3 * sz.rows, sz.chunk_wide), F32),
            pltpu.SemaphoreType.DMA((5,)),
        ],
        compiler_params=params,
        name="pick_cells",
    )(send_list, task_target, task_source, task_count, by_component)
    arrived = lax.all_to_all(leaving, both, split_axis=0, concat_axis=0, tiled=True)
    high, low, own_rows, own_centres = pl.pallas_call(
        functools.partial(source_kernel, sz),
        out_shape=[
            shape(bend_op.shape, BF16),
            shape(bend_op.shape, BF16),
            shape((sz.tiles, SOURCE_ROWS * cells, 128), F32),
            shape((8 * cells, 128), F32),
        ],
        in_specs=[HBM] * 2,
        out_specs=[VMEM] * 4,
        scratch_shapes=[
            pltpu.VMEM(by_component.shape, F32),
            pltpu.VMEM(bend_op.shape, F32),
            pltpu.SemaphoreType.DMA((2,)),
        ],
        compiler_params=params,
        cost_estimate=pl.CostEstimate(flops=10**9, bytes_accessed=10**7, transcendentals=0),
        name="first_sources",
    )(by_component, bend_op)
    chunk, leaving, tasks = pl.pallas_call(
        functools.partial(first_kernel, sz),
        out_shape=[
            shape((pack_rows(sz, cells), 128), F32),
            slot_shape,
            shape((3, sz.slots), jnp.int32),
        ],
        in_specs=[HBM] * 7,
        out_specs=[VMEM, VMEM, SMEM],
        scratch_shapes=scratch(sz, sz.chunk_tiles, sz.slots)
        + [
            pltpu.VMEM((3 * sz.rows, sz.chunk_wide), F32),
            pltpu.VMEM((3 * up(sz.owners * sz.group, 8), sz.width), F32),
            pltpu.SMEM(send_list.shape, jnp.int32),
            pltpu.VMEM(by_component.shape, F32),
            pltpu.VMEM(slot_shape.shape, F32),
            pltpu.VMEM(bend_op.shape, BF16),
            pltpu.VMEM(bend_op.shape, BF16),
            pltpu.VMEM((list_rows, 128), jnp.int32),
            pltpu.SMEM((list_rows, 128), jnp.int32),
            pltpu.SemaphoreType.DMA((8,)),
        ],
        compiler_params=params,
        name="first_step",
    )(arrived, send, by_component, high, low, own_rows, own_centres)
    arrived = lax.all_to_all(leaving, both, split_axis=0, concat_axis=0, tiled=True)
    chunks = [chunk] + [swap(chunk, "lane", lanes, k) for k in range(1, lanes)]
    result = shape((3, sz.share, points), F32)
    outputs = pl.pallas_call(
        functools.partial(second_kernel, sz),
        out_shape=[result, result],
        in_specs=[HBM] * (lanes + 4),
        out_specs=[VMEM] * 2,
        scratch_shapes=scratch(sz, sz.tiles, sz.own)
        + [
            pltpu.VMEM((3 * sz.pool, sz.width), F32),
            pltpu.SMEM((2, sz.own + 8), jnp.int32),
            pltpu.SMEM(tasks.shape, jnp.int32),
            pltpu.VMEM(slot_shape.shape, F32),
        ]
        + [pltpu.VMEM(chunk.shape, F32)] * lanes
        + [pltpu.VMEM(bend_op.shape, BF16)] * 2
        + [pltpu.SemaphoreType.DMA((lanes + 4,))],
        compiler_params=params,
        name="second_step",
    )(tasks, arrived, *chunks, high, low)
    return tuple(jnp.transpose(output, (1, 0, 2)) for output in outputs)


def solution(mesh):
    in_specs = (
        P("space", None, None),
        P(),
        P("space", None),
        P(("space", "lane"), None),
        P(("space", "lane"), None),
        P(("space", "lane")),
    )
    out_specs = (P(("space", "lane"), None, None), P(("space", "lane"), None, None))
    return jax.shard_map(shards, mesh=mesh, in_specs=in_specs, out_specs=out_specs, check_vma=False)
```

```python
import functools
from types import SimpleNamespace

import jax
import jax.numpy as jnp
from jax import lax
from jax.experimental import pallas as pl
from jax.experimental.pallas import tpu as pltpu
from jax.sharding import PartitionSpec as P

REGULARIZE = 0.25
TIME_STEP = 0.5
UNROLL = 4
SOURCE_ROWS = 24
SUM_ROWS = 16

F32 = jnp.float32
BF16 = jnp.bfloat16
VMEM = pl.BlockSpec(memory_space=pltpu.VMEM)
SMEM = pl.BlockSpec(memory_space=pltpu.SMEM)
HBM = pl.BlockSpec(memory_space=pltpu.HBM)


def up(value, step):
    return -(-value // step) * step


def sizes(owners, lanes, cells, points, cap, listed):
    main = 128 * (points // (128 * lanes))
    rest = (points - main * lanes) // lanes
    group = listed // owners
    pool = up(cells + listed, 8)
    per_pack = 128 // rest
    return SimpleNamespace(
        owners=owners,
        lanes=lanes,
        cells=cells,
        points=points,
        cap=cap,
        group=group,
        width=up(points, 128),
        tiles=up(points, 128) // 128,
        main=main,
        rest=rest,
        rest_tiles=up(rest * lanes, 128) // 128,
        chunk=main + rest,
        chunk_wide=main + up(rest, 128),
        chunk_tiles=(main + up(rest, 128)) // 128,
        per_pack=per_pack,
        pool=pool,
        share=cells // lanes,
        slots=up(lanes * cap + UNROLL, 8),
        rows=cells + 8,
        own=up(lanes * cap, 8),
    )


def pack_rows(sz, rows):
    return (3 * rows * sz.main // 128) + 8 * up(3 * rows // 8, sz.per_pack) // sz.per_pack


def split2(value):
    high = value.astype(BF16)
    return high, (value - high.astype(F32)).astype(BF16)


def split3(value):
    first = value.astype(BF16).astype(F32)
    left = value - first
    second = left.astype(BF16).astype(F32)
    return first, second, left - second


def lane_iota(rows):
    return lax.broadcasted_iota(jnp.int32, (rows, 128), 1)


def fetch(sources, targets, sems):
    copies = [
        pltpu.make_async_copy(source, target, sems.at[q])
        for q, (source, target) in enumerate(zip(sources, targets))
    ]
    for copy in copies:
        copy.start()
    return copies


def loop(count, body):
    if count <= 8:
        for q in range(count):
            body(q)
    else:

        def step(q, carry):
            body(q)
            return carry

        lax.fori_loop(0, count, step, 0)


def own_chunk(sz, lane, ref, rows):
    parts = []
    if sz.main:
        parts.append(ref[rows, pl.ds(pl.multiple_of(lane * sz.main, 128), sz.main)])
    start = sz.rest * lane
    lanes = lane_iota(8)
    rest = jnp.zeros((8, 128), F32)
    for tile in range(sz.rest_tiles):
        offset = sz.main * sz.lanes + 128 * tile
        block = ref[rows, offset : min(offset + 128, ref.shape[-1])]
        if block.shape[1] < 128:
            block = jnp.concatenate([block, jnp.zeros((8, 128 - block.shape[1]), F32)], axis=1)
        inside = (lanes + 128 * tile >= start) & (lanes + 128 * tile < start + sz.rest)
        rest = rest + jnp.where(inside, block, 0.0)
    rest = pltpu.roll(rest, lax.rem(128 * sz.rest_tiles - start, 128), 1)
    parts.append(rest)
    return jnp.concatenate(parts, axis=1) if len(parts) > 1 else parts[0]


def send_ghosts(sz, send, chunks, out, tasks):
    lanes = lane_iota(1)

    def one(d):
        for g in range(sz.group):
            cell = send[0, d * sz.group + g]
            rows = []
            last = tasks
            for i in range(3):
                row = chunks[pl.ds(i * sz.rows + cell, 1), :]
                rows.append(row[:, :128] if sz.main else jnp.zeros((1, 128), F32))
                piece = jnp.where(lanes < sz.rest, row[:, sz.main : sz.main + 128], 0.0)
                last = last + (pltpu.roll(piece, i * sz.rest, 1) if i else piece)
            rows.append(last)
            for other in range(sz.lanes):
                first = ((d * sz.lanes + other) * sz.group + g) * 4
                for q, row in enumerate(rows):
                    out[pl.ds(first + q, 1), :] = row

    loop(sz.owners, one)


def pick_kernel(sz, *refs):
    inputs, (out, send_out), held, (chunks, sems) = refs[:5], refs[5:7], refs[7:12], refs[12:]
    for copy in fetch(inputs, held, sems):
        copy.wait()
    send, target, source, count, positions = held
    for j in range(send_out.shape[1]):
        send_out[0, j] = send[0, j]
    lane = lax.axis_index("lane")
    for i in range(3):
        for g in range(0, sz.cells, 8):
            value = own_chunk(sz, lane, positions.at[i], pl.ds(g, 8))
            chunks[pl.ds(i * sz.rows + g, 8), :] = value
    spare = jnp.zeros((1, 128 - sz.cap), F32)
    tasks = jnp.where(lane_iota(1) == 3 * sz.rest + 2 * sz.cap, count[0].astype(F32), 0.0)
    for q, row in enumerate((target, source)):
        wide = jnp.concatenate([row[...].astype(F32), spare], axis=1)
        tasks = tasks + pltpu.roll(wide, 3 * sz.rest + q * sz.cap, 1)
    send_ghosts(sz, send, chunks, out, tasks)


def take_ghosts(sz, arrived, pool, stride, base):
    lanes = lane_iota(1)

    def one(d):
        for g in range(sz.group):
            first = [((d * sz.lanes + lane) * sz.group + g) * 4 for lane in range(sz.lanes)]
            last = [arrived[pl.ds(row + 3, 1), :] for row in first]
            for i in range(3):
                tiles = []
                if sz.main:
                    tiles += [arrived[pl.ds(row + i, 1), :] for row in first]
                for tile in range(sz.rest_tiles):
                    total = jnp.zeros((1, 128), F32)
                    for lane in range(sz.lanes):
                        start = sz.rest * lane
                        if start + sz.rest <= 128 * tile or start >= 128 * tile + 128:
                            continue
                        shift = (start - i * sz.rest) % 128
                        value = pltpu.roll(last[lane], shift, 1) if shift else last[lane]
                        at = lanes + 128 * tile
                        total = jnp.where((at >= start) & (at < start + sz.rest), value, total)
                    tiles.append(total)
                place = pl.ds(i * stride + base + d * sz.group + g, 1)
                pool[place, :] = jnp.concatenate(tiles, axis=1)

    loop(sz.owners, one)


def build_list(sz, lists, tasks):
    total = jnp.int32(0)
    for lane in range(sz.lanes):

        def step(j, total, lane=lane):
            tasks[0, total] = lists[lane, j]
            tasks[1, total] = lists[lane, sz.cap + j]
            return total + 1

        total = lax.fori_loop(0, lists[lane, 2 * sz.cap], step, total)
    for u in range(UNROLL):
        tasks[0, total + u] = jnp.int32(sz.cells)
        tasks[1, total + u] = jnp.int32(0)
    tasks[2, 0] = total
    return total


def own_list(sz, lane, tasks, mine):
    first = lane * sz.share

    def step(t, count):
        target = tasks[0, t] - first
        mine[0, count] = target
        mine[1, count] = tasks[1, t]
        return count + ((target >= 0) & (target < sz.share)).astype(jnp.int32)

    return lax.fori_loop(0, tasks[2, 0], step, jnp.int32(0))


def products(value, bend_high, bend_low):
    high, low = split2(value)
    dot = functools.partial(jnp.dot, preferred_element_type=F32)
    return dot(high, bend_high) + dot(low, bend_high) + dot(high, bend_low)


def make_sources(sz, value, bend_high, bend_low, source_rows, centres, first):
    count = value.shape[0] // 3
    forces = products(value[:, : sz.points], bend_high, bend_low)
    forces = jnp.concatenate(
        [forces, jnp.zeros((3 * count, sz.width - sz.points), F32)], axis=1
    )
    middle = jnp.sum(value, axis=1, keepdims=True) / sz.points
    for g in range(count // 8):
        where = [i * count + 8 * g for i in range(3)]
        middles = [jnp.broadcast_to(middle[w : w + 8], (8, 128)) for w in where]
        middles += [jnp.zeros((8, 128), F32)] * 5
        for i, row in enumerate(middles):
            centres[pl.ds(8 * (first + 8 * g) + i, 8, stride=8), :] = row
        for j in range(sz.tiles):
            cut = slice(128 * j, 128 * j + 128)
            y = [value[w : w + 8, cut] - m for w, m in zip(where, middles)]
            f = [forces[w : w + 8, cut] for w in where]
            norm = y[0] * y[0] + y[1] * y[1] + y[2] * y[2] + REGULARIZE
            along = y[0] * f[0] + y[1] * f[1] + y[2] * f[2]
            one, zero = jnp.ones((8, 128), F32), jnp.zeros((8, 128), F32)
            rows = [y[0], y[1], y[2], norm, one, zero, zero, zero]
            rows += f
            rows += [y[i] * f[k] for i in range(3) for k in range(3)]
            rows += [norm * f[i] + along * y[i] for i in range(3)]
            rows += [along]
            for k, row in enumerate(rows):
                place = pl.ds(SOURCE_ROWS * (first + 8 * g) + k, 8, stride=SOURCE_ROWS)
                source_rows.at[j][place, :] = row


def make_targets(sz, blocks, targets):
    targets[...] = jnp.zeros_like(targets)
    for g in range(sz.cells // 8):
        for i in range(3):
            block = blocks(i, g)
            for j in range(targets.shape[0]):
                cut = slice(128 * j, 128 * j + 128)
                targets.at[j][pl.ds(64 * g + i, 8, stride=8), :] = block[:, cut]


def source_operands(sz, source, source_rows):
    held = [
        source_rows[j, pl.ds(pl.multiple_of(SOURCE_ROWS * source, 8), SOURCE_ROWS), :]
        for j in range(sz.tiles)
    ]
    held = jnp.concatenate(held, axis=1)
    y1, y2, y3 = split3(held[:8])
    y_stack = jnp.concatenate([y1, y1, y2, y2, y1, y3], axis=0).astype(BF16)
    return y_stack, jnp.concatenate(split3(held[8:]), axis=0)


def pieces(points, step):
    return [(p, min(p + step, points)) for p in range(0, points, step)]


def twice(piece, count):
    if count % 128 == 0:
        return jnp.concatenate([piece.astype(BF16)] * 2, axis=1)
    return (piece + pltpu.roll(piece, count, 1)).astype(BF16)[:, : 2 * count]


def load_target(j, target, slot, centre, targets, offsets):
    row = lax.broadcasted_iota(jnp.int32, (8, 128), 0)
    x = targets[j, pl.ds(pl.multiple_of(8 * target, 8), 8), :] - centre
    square = x * x
    norm = pltpu.roll(square, 2, 0) + pltpu.roll(square, 3, 0) + pltpu.roll(square, 4, 0)
    side = jnp.where(row == 4, norm, jnp.where(row == 3, 1.0, 0.0))
    x_side = jnp.where(row < 3, -2.0 * x, side)
    x1, x2, x3 = split3(x_side)
    return x, jnp.concatenate([x1, x2, x1, x2, x3, x1], axis=0).astype(BF16)


def distances(one_stack, other_stack):
    return jnp.dot(one_stack, other_stack, preferred_element_type=F32)


def weights(shifted):
    inverse = lax.rsqrt(shifted)
    return split2(inverse * inverse * inverse)


def fold(result):
    return result[:SUM_ROWS] + result[SUM_ROWS : 2 * SUM_ROWS] + result[2 * SUM_ROWS :]


def tall_sums(sz, targets, y_stack, m_stack):
    targets = jnp.transpose(targets)
    total = None
    for first, end in pieces(128 * (sz.points // 128), 256):
        high, low = weights(distances(targets, y_stack[:, first:end]))
        m_piece = jnp.transpose(m_stack[:, first:end].astype(BF16))
        stack = jnp.concatenate([high, low], axis=1)
        m_piece = jnp.concatenate([m_piece, m_piece], axis=0)
        result = jnp.dot(stack, m_piece, preferred_element_type=F32)
        total = result if total is None else total + result
    return jnp.transpose(total)


def wide_sums(sz, targets, y_turned, m_stack, start, step):
    total = None
    for first, end in pieces(sz.points, step):
        if first < start:
            continue
        high, low = weights(distances(y_turned[first:end], targets))
        stack = jnp.concatenate([high, low], axis=0)
        m_piece = m_stack[:, first : up(end, 128)]
        result = jnp.dot(twice(m_piece, end - first), stack, preferred_element_type=F32)
        total = result if total is None else total + result
    return total


def store_sums(slots, slot, j, x, result, offsets, sums):
    offsets.at[j][pl.ds(slot, 8, stride=slots), :] = x
    for h in range(0, SUM_ROWS, 8):
        sums.at[j][pl.ds(h * slots + slot, 8, stride=slots), :] = result[h : h + 8]


def mark(slot, target, hot):
    hot[pl.ds(slot, 1), :] = jnp.where(lane_iota(1) == target, 1.0, 0.0)


def combine(sz, slots, first, total, offsets, sums, speeds):
    live = lax.broadcasted_iota(jnp.int32, (8, 128), 0) + first < total
    for j in range(offsets.shape[0]):
        x = [offsets[j, pl.ds(i * slots + first, 8), :] for i in range(3)]
        s = [sums[j, pl.ds(k * slots + first, 8), :] for k in range(SUM_ROWS)]
        a, b, c = s[:3], [s[3:6], s[6:9], s[9:12]], s[12:15]
        norm = x[0] * x[0] + x[1] * x[1] + x[2] * x[2] + REGULARIZE
        along = x[0] * a[0] + x[1] * a[1] + x[2] * a[2] - s[15]
        for i in range(3):
            speed = norm * a[i] + c[i] + along * x[i]
            for k in range(3):
                speed = speed - x[k] * (2.0 * b[k][i] + b[i][k])
            speed = jnp.where(live, speed / sz.points, 0.0)
            speeds[i, pl.ds(first, 8), 128 * j : 128 * j + 128] = speed


def add_up(sz, slots, total, rows, offsets, sums, speeds, hot):
    def eight(q, carry):
        combine(sz, slots, pl.multiple_of(8 * q, 8), total, offsets, sums, speeds)
        return carry

    lax.fori_loop(0, lax.div(total + 7, 8), eight, 0)
    one_hot = hot[...].astype(BF16)
    result = []
    for i in range(3):
        first, second, third = split3(speeds[i])
        parts = [
            lax.dot_general(
                one_hot, part.astype(BF16), (((0,), (0,)), ((), ())), preferred_element_type=F32
            )
            for part in (first, second, third)
        ]
        result.append((parts[0] + parts[1] + parts[2])[:rows])
    return result


def tiles_of_chunk(sz, total, tasks, source_rows, centres, targets, offsets, sums, hot):
    whole = 128 * (sz.points // 128)

    def one(slot):
        target, source = tasks[0, slot], tasks[1, slot]
        y_stack, m_stack = source_operands(sz, source, source_rows)
        centre = centres[pl.ds(pl.multiple_of(8 * source, 8), 8), :]
        points = [
            load_target(j, target, slot, centre, targets, offsets) for j in range(sz.chunk_tiles)
        ]
        stack = jnp.concatenate([stack for _, stack in points], axis=1)[:, : sz.chunk]
        result = tall_sums(sz, stack, y_stack, m_stack)
        if whole < sz.points:
            y_turned = jnp.transpose(y_stack[:, whole:])
            y_turned = jnp.concatenate([jnp.zeros((whole, y_turned.shape[1]), BF16), y_turned])
            result = result + wide_sums(sz, stack, y_turned, m_stack, whole, 128)
        result = fold(result)
        spare = -result.shape[1] % 128
        if spare:
            result = jnp.concatenate([result, jnp.zeros((SUM_ROWS, spare), F32)], axis=1)
        for j in range(sz.chunk_tiles):
            cut = result[:, 128 * j : 128 * j + 128]
            store_sums(sz.slots, slot, j, points[j][0], cut, offsets, sums)
        mark(slot, target, hot)

    def several(q, carry):
        for u in range(UNROLL):
            one(q * UNROLL + u)
        return carry

    lax.fori_loop(0, lax.div(total + UNROLL - 1, UNROLL), several, 0)


def tiles_of_cells(sz, first, total, mine, source_rows, centres, targets, offsets, sums, hot):
    whole = 128 * (sz.points // 128)

    def single(slot, carry):
        target, source = mine[0, slot], mine[1, slot]
        y_stack, m_stack = source_operands(sz, source, source_rows)
        y_turned = jnp.transpose(y_stack)
        centre = centres[pl.ds(pl.multiple_of(8 * source, 8), 8), :]
        points = [
            load_target(j, target + first, slot, centre, targets, offsets)
            for j in range(sz.tiles)
        ]
        results = []
        for begin, end in pieces(whole, 256):
            stack = [stack for _, stack in points[begin // 128 : end // 128]]
            stack = jnp.concatenate(stack, axis=1)
            results.append(fold(wide_sums(sz, stack, y_turned, m_stack, 0, 128)))
        if whole < sz.points:
            rest = jnp.transpose(points[-1][1])[: sz.points - whole]
            high, low = weights(distances(rest, y_stack))
            m_whole = m_stack.astype(BF16)
            turned = (((1,), (1,)), ((), ()))
            result = lax.dot_general(m_whole, high, turned, preferred_element_type=F32)
            result += lax.dot_general(m_whole, low, turned, preferred_element_type=F32)
            spare = jnp.zeros((SUM_ROWS, 128 - result.shape[1]), F32)
            results.append(jnp.concatenate([fold(result), spare], axis=1))
        result = jnp.concatenate(results, axis=1)
        for j in range(sz.tiles):
            cut = result[:, 128 * j : 128 * j + 128]
            store_sums(sz.own, slot, j, points[j][0], cut, offsets, sums)
        mark(slot, target, hot)
        return carry

    lax.fori_loop(0, total, single, 0)


def packed(sz, blocks):
    rows = [b[:, : sz.main] for b in blocks] if sz.main else []
    lanes = lane_iota(8)
    for p in range(0, len(blocks), sz.per_pack):
        total = jnp.zeros((8, 128), F32)
        for q, block in enumerate(blocks[p : p + sz.per_pack]):
            rest = jnp.where(lanes < sz.rest, block[:, sz.main : sz.main + 128], 0.0)
            total = total + (pltpu.roll(rest, q * sz.rest, 1) if q else rest)
        rows.append(total)
    return rows


def store_packed(sz, out, blocks):
    first = 0
    count = len(blocks)
    values = packed(sz, blocks)
    if sz.main:
        for b in range(count):
            for m in range(sz.main // 128):
                out[pl.ds(first, 8), :] = values[b][:, 128 * m : 128 * m + 128]
                first += 8
        values = values[count:]
    for value in values:
        out[pl.ds(first, 8), :] = value
        first += 8


def place_packed(sz, lane, arrived, count, store_main, add_rest):
    first = 0
    if sz.main:
        for b in range(count):
            for m in range(sz.main // 128):
                store_main(b, m, arrived[pl.ds(first, 8), :])
                first += 8
    start = sz.rest * lane
    lanes = lane_iota(8)
    for b in range(count):
        pack, q = divmod(b, sz.per_pack)
        value = arrived[pl.ds(first + 8 * pack, 8), :]
        value = pltpu.roll(value, lax.rem(start - q * sz.rest + 128, 128), 1)
        for tile in range(sz.rest_tiles):
            inside = (lanes + 128 * tile >= start) & (lanes + 128 * tile < start + sz.rest)
            add_rest(b, tile, jnp.where(inside, value, 0.0))


def source_kernel(sz, *refs):
    inputs, (high_out, low_out, source_rows, centres), held, sems = (
        refs[:2],
        refs[2:6],
        refs[6:8],
        refs[8],
    )
    for copy in fetch(inputs, held, sems):
        copy.wait()
    positions, bend = held
    high_out[...], low_out[...] = split2(bend[...])
    value = jnp.concatenate([positions[i] for i in range(3)], axis=0)
    value = jnp.concatenate(
        [value, jnp.zeros((3 * sz.cells, sz.width - sz.points), F32)], axis=1
    )
    make_sources(sz, value, high_out[...], low_out[...], source_rows, centres, 0)


def first_kernel(sz, *refs):
    inputs, (chunk_out, ghost_out, tasks), refs = refs[:7], refs[7:10], refs[10:]
    source_rows, centres, targets, offsets, sums, speeds, hot, moved, pool = refs[:9]
    send, positions, arrived, high, low, staged, lists, sems = refs[9:]
    me, lane = lax.axis_index("space"), lax.axis_index("lane")
    own_rows = source_rows.at[:, pl.ds(0, SOURCE_ROWS * sz.cells)]
    own_centres = centres.at[pl.ds(0, 8 * sz.cells)]
    held = [arrived, send, positions, high, low, own_rows, own_centres]
    copies = fetch(inputs, held, sems)
    copies[0].wait()
    for other in range(sz.lanes):
        row = ((me * sz.lanes + other) * sz.group) * 4 + 3
        value = pltpu.roll(arrived[pl.ds(row, 1), :], 128 - 3 * sz.rest, 1)
        staged[pl.ds(other, 1), :] = value.astype(jnp.int32)
    copies.append(pltpu.make_async_copy(staged, lists, sems.at[7]))
    copies[7].start()
    pool[...] = jnp.zeros_like(pool)
    take_ghosts(sz, arrived, pool, up(sz.owners * sz.group, 8), 0)
    hot[...] = jnp.zeros_like(hot)
    speeds[...] = jnp.zeros_like(speeds)
    for copy in copies[1:5]:
        copy.wait()
    make_sources(sz, pool[...], high[...], low[...], source_rows, centres, sz.cells)
    make_targets(
        sz, lambda i, g: own_chunk(sz, lane, positions.at[i], pl.ds(8 * g, 8)), targets
    )
    for copy in copies[5:]:
        copy.wait()
    total = build_list(sz, lists, tasks)
    tiles_of_chunk(sz, total, tasks, source_rows, centres, targets, offsets, sums, hot)
    velocity = add_up(sz, sz.slots, total, sz.cells, offsets, sums, speeds, hot)
    blocks = []
    for i in range(3):
        for g in range(0, sz.cells, 8):
            chunk = own_chunk(sz, lane, positions.at[i], pl.ds(g, 8))
            block = chunk + TIME_STEP * velocity[i][g : g + 8]
            moved[pl.ds(i * sz.rows + g, 8), :] = block
            blocks.append(block)
    store_packed(sz, chunk_out, blocks)
    send_ghosts(sz, send, moved, ghost_out, jnp.zeros((1, 128), F32))


def second_kernel(sz, *refs):
    count = sz.lanes + 4
    inputs, (moved_out, velocity_out), refs = refs[:count], refs[count : count + 2], refs[count + 2 :]
    source_rows, centres, targets, offsets, sums, speeds, hot, pool, mine = refs[:9]
    held, sems = refs[9:-1], refs[-1]
    copies = fetch(inputs, held, sems)
    tasks, arrived, chunks, (high, low) = held[0], held[1], held[2:-2], held[-2:]
    hot[...] = jnp.zeros_like(hot)
    speeds[...] = jnp.zeros_like(speeds)
    lane = lax.axis_index("lane")
    pool[...] = jnp.zeros_like(pool)
    for copy in copies[:-2]:
        copy.wait()
    per = sz.cells // 8
    for k in range(sz.lanes):
        other = lane ^ k

        def row_of(b):
            return (b // per) * sz.pool + 8 * (b % per)

        def store_main(b, m, value):
            cut = pl.ds(pl.multiple_of(other * sz.main + 128 * m, 128), 128)
            pool[pl.ds(row_of(b), 8), cut] = value

        def add_rest(b, tile, value):
            offset = sz.main * sz.lanes + 128 * tile
            cut = (pl.ds(row_of(b), 8), slice(offset, offset + 128))
            pool[cut] = pool[cut] + value

        place_packed(sz, other, chunks[k], 3 * per, store_main, add_rest)
    take_ghosts(sz, arrived, pool, sz.pool, sz.cells)
    total = own_list(sz, lane, tasks, mine)
    for copy in copies[-2:]:
        copy.wait()
    make_sources(sz, pool[...], high[...], low[...], source_rows, centres, 0)
    make_targets(sz, lambda i, g: pool[pl.ds(i * sz.pool + 8 * g, 8), :], targets)
    first = lane * sz.share
    tiles_of_cells(sz, first, total, mine, source_rows, centres, targets, offsets, sums, hot)
    velocity = add_up(sz, sz.own, total, up(sz.share, 8), offsets, sums, speeds, hot)
    for i in range(3):
        speed = velocity[i]
        moved = share_rows(sz, pool, i * sz.pool, lane) + TIME_STEP * speed
        velocity_out[i] = speed[: sz.share, : sz.points]
        moved_out[i] = moved[: sz.share, : sz.points]


def share_rows(sz, ref, base, lane):
    if sz.share % 8 == 0:
        return ref[pl.ds(pl.multiple_of(base + lane * sz.share, 8), sz.share), :]
    rows = [ref[pl.ds(base + lane * sz.share + c, 1), :] for c in range(sz.share)]
    rows.append(jnp.zeros((8 - sz.share, rows[0].shape[1]), F32))
    return jnp.concatenate(rows, axis=0)


def scratch(sz, tiles, slots):
    return [
        pltpu.VMEM((sz.tiles, SOURCE_ROWS * sz.pool, 128), F32),
        pltpu.VMEM((8 * sz.pool, 128), F32),
        pltpu.VMEM((tiles, 8 * sz.rows, 128), F32),
        pltpu.VMEM((tiles, 8 * slots, 128), F32),
        pltpu.VMEM((tiles, SUM_ROWS * slots, 128), F32),
        pltpu.VMEM((3, slots, 128 * tiles), F32),
        pltpu.VMEM((slots, 128), F32),
    ]


def swap(value, axis, size, k):
    return lax.ppermute(value, axis, [(d, d ^ k) for d in range(size)])


def shards(positions, bend_op, send_list, task_target, task_source, task_count):
    owners, lanes = lax.axis_size("space"), lax.axis_size("lane")
    cells, points = positions.shape[0], positions.shape[2]
    sz = sizes(owners, lanes, cells, points, task_target.shape[1], send_list.shape[1])
    params = pltpu.CompilerParams(vmem_limit_bytes=60 << 20)
    shape = jax.ShapeDtypeStruct
    both = ("space", "lane")
    by_component = jnp.transpose(positions, (1, 0, 2))
    list_rows = up(lanes, 8)
    slot_shape = shape((4 * sz.group * owners * lanes, 128), F32)
    leaving, send = pl.pallas_call(
        functools.partial(pick_kernel, sz),
        out_shape=[slot_shape, shape(send_list.shape, jnp.int32)],
        in_specs=[HBM] * 5,
        out_specs=[VMEM, SMEM],
        scratch_shapes=[
            pltpu.SMEM(send_list.shape, jnp.int32),
            pltpu.VMEM(task_target.shape, jnp.int32),
            pltpu.VMEM(task_source.shape, jnp.int32),
            pltpu.SMEM(task_count.shape, jnp.int32),
            pltpu.VMEM(by_component.shape, F32),
            pltpu.VMEM((3 * sz.rows, sz.chunk_wide), F32),
            pltpu.SemaphoreType.DMA((5,)),
        ],
        compiler_params=params,
        name="pick_cells",
    )(send_list, task_target, task_source, task_count, by_component)
    arrived = lax.all_to_all(leaving, both, split_axis=0, concat_axis=0, tiled=True)
    high, low, own_rows, own_centres = pl.pallas_call(
        functools.partial(source_kernel, sz),
        out_shape=[
            shape(bend_op.shape, BF16),
            shape(bend_op.shape, BF16),
            shape((sz.tiles, SOURCE_ROWS * cells, 128), F32),
            shape((8 * cells, 128), F32),
        ],
        in_specs=[HBM] * 2,
        out_specs=[VMEM] * 4,
        scratch_shapes=[
            pltpu.VMEM(by_component.shape, F32),
            pltpu.VMEM(bend_op.shape, F32),
            pltpu.SemaphoreType.DMA((2,)),
        ],
        compiler_params=params,
        cost_estimate=pl.CostEstimate(flops=10**9, bytes_accessed=10**7, transcendentals=0),
        name="first_sources",
    )(by_component, bend_op)
    chunk, leaving, tasks = pl.pallas_call(
        functools.partial(first_kernel, sz),
        out_shape=[
            shape((pack_rows(sz, cells), 128), F32),
            slot_shape,
            shape((3, sz.slots), jnp.int32),
        ],
        in_specs=[HBM] * 7,
        out_specs=[VMEM, VMEM, SMEM],
        scratch_shapes=scratch(sz, sz.chunk_tiles, sz.slots)
        + [
            pltpu.VMEM((3 * sz.rows, sz.chunk_wide), F32),
            pltpu.VMEM((3 * up(sz.owners * sz.group, 8), sz.width), F32),
            pltpu.SMEM(send_list.shape, jnp.int32),
            pltpu.VMEM(by_component.shape, F32),
            pltpu.VMEM(slot_shape.shape, F32),
            pltpu.VMEM(bend_op.shape, BF16),
            pltpu.VMEM(bend_op.shape, BF16),
            pltpu.VMEM((list_rows, 128), jnp.int32),
            pltpu.SMEM((list_rows, 128), jnp.int32),
            pltpu.SemaphoreType.DMA((8,)),
        ],
        compiler_params=params,
        name="first_step",
    )(arrived, send, by_component, high, low, own_rows, own_centres)
    arrived = lax.all_to_all(leaving, both, split_axis=0, concat_axis=0, tiled=True)
    chunks = [chunk] + [swap(chunk, "lane", lanes, k) for k in range(1, lanes)]
    result = shape((3, sz.share, points), F32)
    outputs = pl.pallas_call(
        functools.partial(second_kernel, sz),
        out_shape=[result, result],
        in_specs=[HBM] * (lanes + 4),
        out_specs=[VMEM] * 2,
        scratch_shapes=scratch(sz, sz.tiles, sz.own)
        + [
            pltpu.VMEM((3 * sz.pool, sz.width), F32),
            pltpu.SMEM((2, sz.own + 8), jnp.int32),
            pltpu.SMEM(tasks.shape, jnp.int32),
            pltpu.VMEM(slot_shape.shape, F32),
        ]
        + [pltpu.VMEM(chunk.shape, F32)] * lanes
        + [pltpu.VMEM(bend_op.shape, BF16)] * 2
        + [pltpu.SemaphoreType.DMA((lanes + 4,))],
        compiler_params=params,
        name="second_step",
    )(tasks, arrived, *chunks, high, low)
    return tuple(jnp.transpose(output, (1, 0, 2)) for output in outputs)


def solution(mesh):
    in_specs = (
        P("space", None, None),
        P(),
        P("space", None),
        P(("space", "lane"), None),
        P(("space", "lane"), None),
        P(("space", "lane")),
    )
    out_specs = (P(("space", "lane"), None, None), P(("space", "lane"), None, None))
    return jax.shard_map(shards, mesh=mesh, in_specs=in_specs, out_specs=out_specs, check_vma=False)
```

```python
import functools
from types import SimpleNamespace

import jax
import jax.numpy as jnp
from jax import lax
from jax.experimental import pallas as pl
from jax.experimental.pallas import tpu as pltpu
from jax.sharding import PartitionSpec as P

REGULARIZE = 0.25
TIME_STEP = 0.5
UNROLL = 4
PAIR = 2
SKEW = 2
SOURCE_ROWS = 24
SUM_ROWS = 16

F32 = jnp.float32
BF16 = jnp.bfloat16
VMEM = pl.BlockSpec(memory_space=pltpu.VMEM)
SMEM = pl.BlockSpec(memory_space=pltpu.SMEM)
HBM = pl.BlockSpec(memory_space=pltpu.HBM)


def up(value, step):
    return -(-value // step) * step


def sizes(owners, lanes, cells, points, cap, listed):
    main = 128 * (points // (128 * lanes))
    rest = (points - main * lanes) // lanes
    group = listed // owners
    pool = up(cells + listed, 8)
    per_pack = 128 // rest
    return SimpleNamespace(
        owners=owners,
        lanes=lanes,
        cells=cells,
        points=points,
        cap=cap,
        group=group,
        width=up(points, 128),
        tiles=up(points, 128) // 128,
        main=main,
        rest=rest,
        rest_tiles=up(rest * lanes, 128) // 128,
        chunk=main + rest,
        chunk_wide=main + up(rest, 128),
        chunk_tiles=(main + up(rest, 128)) // 128,
        per_pack=per_pack,
        pool=pool,
        share=cells // lanes,
        slots=up(lanes * cap + UNROLL, 8),
        rows=cells + 8,
        own=up(lanes * cap + PAIR, 8),
    )


def pack_rows(sz, rows):
    return (3 * rows * sz.main // 128) + 8 * up(3 * rows // 8, sz.per_pack) // sz.per_pack


def split2(value):
    high = value.astype(BF16)
    return high, (value - high.astype(F32)).astype(BF16)


def split3(value):
    first = value.astype(BF16).astype(F32)
    left = value - first
    second = left.astype(BF16).astype(F32)
    return first, second, left - second


def lane_iota(rows):
    return lax.broadcasted_iota(jnp.int32, (rows, 128), 1)


def fetch(sources, targets, sems):
    copies = [
        pltpu.make_async_copy(source, target, sems.at[q])
        for q, (source, target) in enumerate(zip(sources, targets))
    ]
    for copy in copies:
        copy.start()
    return copies


def loop(count, body):
    if count <= 8:
        for q in range(count):
            body(q)
    else:

        def step(q, carry):
            body(q)
            return carry

        lax.fori_loop(0, count, step, 0)


def own_chunk(sz, lane, ref, rows):
    parts = []
    if sz.main:
        parts.append(ref[rows, pl.ds(pl.multiple_of(lane * sz.main, 128), sz.main)])
    start = sz.rest * lane
    lanes = lane_iota(8)
    rest = jnp.zeros((8, 128), F32)
    for tile in range(sz.rest_tiles):
        offset = sz.main * sz.lanes + 128 * tile
        block = ref[rows, offset : min(offset + 128, ref.shape[-1])]
        if block.shape[1] < 128:
            block = jnp.concatenate([block, jnp.zeros((8, 128 - block.shape[1]), F32)], axis=1)
        inside = (lanes + 128 * tile >= start) & (lanes + 128 * tile < start + sz.rest)
        rest = rest + jnp.where(inside, block, 0.0)
    rest = pltpu.roll(rest, lax.rem(128 * sz.rest_tiles - start, 128), 1)
    parts.append(rest)
    return jnp.concatenate(parts, axis=1) if len(parts) > 1 else parts[0]


def send_ghosts(sz, send, chunks, out, tasks):
    lanes = lane_iota(1)

    def one(d):
        for g in range(sz.group):
            cell = send[0, d * sz.group + g]
            rows = []
            last = tasks
            for i in range(3):
                row = chunks[pl.ds(i * sz.rows + cell, 1), :]
                rows.append(row[:, :128] if sz.main else jnp.zeros((1, 128), F32))
                piece = jnp.where(lanes < sz.rest, row[:, sz.main : sz.main + 128], 0.0)
                last = last + (pltpu.roll(piece, i * sz.rest, 1) if i else piece)
            rows.append(last)
            for other in range(sz.lanes):
                first = ((d * sz.lanes + other) * sz.group + g) * 4
                for q, row in enumerate(rows):
                    out[pl.ds(first + q, 1), :] = row

    loop(sz.owners, one)


def pick_kernel(sz, *refs):
    inputs, (out, send_out), held, (chunks, sems) = refs[:5], refs[5:7], refs[7:12], refs[12:]
    for copy in fetch(inputs, held, sems):
        copy.wait()
    send, target, source, count, positions = held
    for j in range(send_out.shape[1]):
        send_out[0, j] = send[0, j]
    lane = lax.axis_index("lane")
    for i in range(3):
        for g in range(0, sz.cells, 8):
            value = own_chunk(sz, lane, positions.at[i], pl.ds(g, 8))
            chunks[pl.ds(i * sz.rows + g, 8), :] = value
    spare = jnp.zeros((1, 128 - sz.cap), F32)
    tasks = jnp.where(lane_iota(1) == 3 * sz.rest + 2 * sz.cap, count[0].astype(F32), 0.0)
    for q, row in enumerate((target, source)):
        wide = jnp.concatenate([row[...].astype(F32), spare], axis=1)
        tasks = tasks + pltpu.roll(wide, 3 * sz.rest + q * sz.cap, 1)
    send_ghosts(sz, send, chunks, out, tasks)


def take_ghosts(sz, arrived, pool, stride, base):
    lanes = lane_iota(1)

    def one(d):
        for g in range(sz.group):
            first = [((d * sz.lanes + lane) * sz.group + g) * 4 for lane in range(sz.lanes)]
            last = [arrived[pl.ds(row + 3, 1), :] for row in first]
            for i in range(3):
                tiles = []
                if sz.main:
                    tiles += [arrived[pl.ds(row + i, 1), :] for row in first]
                for tile in range(sz.rest_tiles):
                    total = jnp.zeros((1, 128), F32)
                    for lane in range(sz.lanes):
                        start = sz.rest * lane
                        if start + sz.rest <= 128 * tile or start >= 128 * tile + 128:
                            continue
                        shift = (start - i * sz.rest) % 128
                        value = pltpu.roll(last[lane], shift, 1) if shift else last[lane]
                        at = lanes + 128 * tile
                        total = jnp.where((at >= start) & (at < start + sz.rest), value, total)
                    tiles.append(total)
                place = pl.ds(i * stride + base + d * sz.group + g, 1)
                pool[place, :] = jnp.concatenate(tiles, axis=1)

    loop(sz.owners, one)


def build_list(sz, lists, tasks):
    total = jnp.int32(0)
    for lane in range(sz.lanes):

        def step(j, total, lane=lane):
            tasks[0, total] = lists[lane, j]
            tasks[1, total] = lists[lane, sz.cap + j]
            return total + 1

        total = lax.fori_loop(0, lists[lane, 2 * sz.cap], step, total)
    for u in range(UNROLL):
        tasks[0, total + u] = jnp.int32(sz.cells)
        tasks[1, total + u] = jnp.int32(0)
    tasks[2, 0] = total
    return total


def own_list(sz, lane, tasks, mine):
    first = lane * sz.share

    def step(t, count):
        target = tasks[0, t] - first
        mine[0, count] = target
        mine[1, count] = tasks[1, t]
        return count + ((target >= 0) & (target < sz.share)).astype(jnp.int32)

    total = lax.fori_loop(0, tasks[2, 0], step, jnp.int32(0))
    for u in range(PAIR):
        mine[0, total + u] = jnp.int32(-1)
        mine[1, total + u] = jnp.int32(0)
    return total


def products(value, bend_high, bend_low):
    high, low = split2(value)
    dot = functools.partial(jnp.dot, preferred_element_type=F32)
    return dot(high, bend_high) + dot(low, bend_high) + dot(high, bend_low)


def make_sources(sz, value, bend_high, bend_low, source_rows, centres, first):
    count = value.shape[0] // 3
    forces = products(value[:, : sz.points], bend_high, bend_low)
    forces = jnp.concatenate(
        [forces, jnp.zeros((3 * count, sz.width - sz.points), F32)], axis=1
    )
    middle = jnp.sum(value, axis=1, keepdims=True) / sz.points
    for g in range(count // 8):
        where = [i * count + 8 * g for i in range(3)]
        middles = [jnp.broadcast_to(middle[w : w + 8], (8, 128)) for w in where]
        middles += [jnp.zeros((8, 128), F32)] * 5
        for i, row in enumerate(middles):
            centres[pl.ds(8 * (first + 8 * g) + i, 8, stride=8), :] = row
        for j in range(sz.tiles):
            cut = slice(128 * j, 128 * j + 128)
            y = [value[w : w + 8, cut] - m for w, m in zip(where, middles)]
            f = [forces[w : w + 8, cut] for w in where]
            norm = y[0] * y[0] + y[1] * y[1] + y[2] * y[2] + REGULARIZE
            along = y[0] * f[0] + y[1] * f[1] + y[2] * f[2]
            one, zero = jnp.ones((8, 128), F32), jnp.zeros((8, 128), F32)
            rows = [y[0], y[1], y[2], norm, one, zero, zero, zero]
            rows += f
            rows += [y[i] * f[k] for i in range(3) for k in range(3)]
            rows += [norm * f[i] + along * y[i] for i in range(3)]
            rows += [along]
            for k, row in enumerate(rows):
                place = pl.ds(SOURCE_ROWS * (first + 8 * g) + k, 8, stride=SOURCE_ROWS)
                source_rows.at[j][place, :] = row


def make_targets(sz, blocks, targets):
    targets[...] = jnp.zeros_like(targets)
    for g in range(sz.cells // 8):
        for i in range(3):
            block = blocks(i, g)
            for j in range(targets.shape[0]):
                cut = slice(128 * j, 128 * j + 128)
                targets.at[j][pl.ds(64 * g + i, 8, stride=8), :] = block[:, cut]


def source_operands(sz, source, source_rows):
    held = [
        source_rows[j, pl.ds(pl.multiple_of(SOURCE_ROWS * source, 8), SOURCE_ROWS), :]
        for j in range(sz.tiles)
    ]
    held = jnp.concatenate(held, axis=1)
    y1, y2, y3 = split3(held[:8])
    y_stack = jnp.concatenate([y1, y1, y2, y2, y1, y3], axis=0).astype(BF16)
    return y_stack, jnp.concatenate(split3(held[8:]), axis=0)


def pieces(points, step):
    return [(p, min(p + step, points)) for p in range(0, points, step)]


def twice(piece, count):
    if count % 128 == 0:
        return jnp.concatenate([piece.astype(BF16)] * 2, axis=1)
    return (piece + pltpu.roll(piece, count, 1)).astype(BF16)[:, : 2 * count]


def load_target(j, target, slot, centre, targets, offsets):
    row = lax.broadcasted_iota(jnp.int32, (8, 128), 0)
    x = targets[j, pl.ds(pl.multiple_of(8 * target, 8), 8), :] - centre
    square = x * x
    norm = pltpu.roll(square, 2, 0) + pltpu.roll(square, 3, 0) + pltpu.roll(square, 4, 0)
    side = jnp.where(row == 4, norm, jnp.where(row == 3, 1.0, 0.0))
    x_side = jnp.where(row < 3, -2.0 * x, side)
    x1, x2, x3 = split3(x_side)
    return x, jnp.concatenate([x1, x2, x1, x2, x3, x1], axis=0).astype(BF16)


def distances(one_stack, other_stack):
    return jnp.dot(one_stack, other_stack, preferred_element_type=F32)


def weights(shifted):
    inverse = lax.rsqrt(shifted)
    return split2(inverse * inverse * inverse)


def fold(result):
    return result[:SUM_ROWS] + result[SUM_ROWS : 2 * SUM_ROWS] + result[2 * SUM_ROWS :]


def skewed(stages):
    asked = []
    for q, (ask, _) in enumerate(stages):
        asked.append(ask())
        if q >= SKEW:
            stages[q - SKEW][1](asked[q - SKEW])
            asked[q - SKEW] = None
    for q in range(max(len(stages) - SKEW, 0), len(stages)):
        stages[q][1](asked[q])


def adder(totals, key):
    def add(value):
        totals[key] = totals[key] + value if key in totals else value

    return add


def tall_piece(targets, y_stack, m_stack, first, end, add):
    def ask():
        return distances(targets, y_stack[:, first:end])

    def take(shifted):
        stack = jnp.concatenate(weights(shifted), axis=1)
        m_piece = jnp.transpose(m_stack[:, first:end].astype(BF16))
        m_piece = jnp.concatenate([m_piece, m_piece], axis=0)
        add(jnp.dot(stack, m_piece, preferred_element_type=F32))

    return ask, take


def wide_piece(targets, y_turned, m_stack, first, end, add):
    def ask():
        return distances(y_turned, targets)

    def take(shifted):
        stack = jnp.concatenate(weights(shifted), axis=0)
        m_piece = twice(m_stack[:, first : up(end, 128)], end - first)
        add(jnp.dot(m_piece, stack, preferred_element_type=F32))

    return ask, take


def rest_piece(targets, y_stack, m_stack, add):
    def ask():
        return distances(targets, y_stack)

    def take(shifted):
        high, low = weights(shifted)
        m_whole = m_stack.astype(BF16)
        turned = (((1,), (1,)), ((), ()))
        result = lax.dot_general(m_whole, high, turned, preferred_element_type=F32)
        add(result + lax.dot_general(m_whole, low, turned, preferred_element_type=F32))

    return ask, take


def store_sums(slots, slot, j, x, result, offsets, sums):
    offsets.at[j][pl.ds(slot, 8, stride=slots), :] = x
    for h in range(0, SUM_ROWS, 8):
        sums.at[j][pl.ds(h * slots + slot, 8, stride=slots), :] = result[h : h + 8]


def mark(slot, target, hot):
    hot[pl.ds(slot, 1), :] = jnp.where(lane_iota(1) == target, 1.0, 0.0)


def combine(sz, slots, first, total, offsets, sums, speeds):
    live = lax.broadcasted_iota(jnp.int32, (8, 128), 0) + first < total
    for j in range(offsets.shape[0]):
        x = [offsets[j, pl.ds(i * slots + first, 8), :] for i in range(3)]
        s = [sums[j, pl.ds(k * slots + first, 8), :] for k in range(SUM_ROWS)]
        a, b, c = s[:3], [s[3:6], s[6:9], s[9:12]], s[12:15]
        norm = x[0] * x[0] + x[1] * x[1] + x[2] * x[2] + REGULARIZE
        along = x[0] * a[0] + x[1] * a[1] + x[2] * a[2] - s[15]
        for i in range(3):
            speed = norm * a[i] + c[i] + along * x[i]
            for k in range(3):
                speed = speed - x[k] * (2.0 * b[k][i] + b[i][k])
            speed = jnp.where(live, speed / sz.points, 0.0)
            speeds[i, pl.ds(first, 8), 128 * j : 128 * j + 128] = speed


def add_up(sz, slots, total, rows, offsets, sums, speeds, hot):
    def eight(q, carry):
        combine(sz, slots, pl.multiple_of(8 * q, 8), total, offsets, sums, speeds)
        return carry

    lax.fori_loop(0, lax.div(total + 7, 8), eight, 0)
    one_hot = hot[...].astype(BF16)
    result = []
    for i in range(3):
        first, second, third = split3(speeds[i])
        parts = [
            lax.dot_general(
                one_hot, part.astype(BF16), (((0,), (0,)), ((), ())), preferred_element_type=F32
            )
            for part in (first, second, third)
        ]
        result.append((parts[0] + parts[1] + parts[2])[:rows])
    return result


def task_operands(slot, pick, source_rows, centres, targets, offsets, sz):
    target, source = pick
    centre = centres[pl.ds(pl.multiple_of(8 * source, 8), 8), :]
    points = [
        load_target(j, target, slot, centre, targets, offsets) for j in range(targets.shape[0])
    ]
    return source_operands(sz, source, source_rows), points


def tiles_of_chunk(sz, total, tasks, source_rows, centres, targets, offsets, sums, hot):
    whole = 128 * (sz.points // 128)

    def several(q, carry):
        slots = [q * UNROLL + u for u in range(UNROLL)]
        picks = [(tasks[0, slot], tasks[1, slot]) for slot in slots]
        tall, wide, held, stages = {}, {}, [], []
        for u, (slot, pick) in enumerate(zip(slots, picks)):
            (y_stack, m_stack), points = task_operands(
                slot, pick, source_rows, centres, targets, offsets, sz
            )
            held.append(points)
            stack = jnp.concatenate([stack for _, stack in points], axis=1)[:, : sz.chunk]
            turned = jnp.transpose(stack)
            for first, end in pieces(whole, 256):
                stages.append(
                    tall_piece(turned, y_stack, m_stack, first, end, adder(tall, u))
                )
            if whole < sz.points:
                y_turned = jnp.transpose(y_stack[:, whole:])[: sz.points - whole]
                stages.append(
                    wide_piece(stack, y_turned, m_stack, whole, sz.points, adder(wide, u))
                )
        skewed(stages)
        for u, (slot, pick) in enumerate(zip(slots, picks)):
            result = jnp.transpose(tall[u])
            result = fold(result + wide[u] if u in wide else result)
            spare = -result.shape[1] % 128
            if spare:
                result = jnp.concatenate([result, jnp.zeros((SUM_ROWS, spare), F32)], axis=1)
            for j in range(sz.chunk_tiles):
                cut = result[:, 128 * j : 128 * j + 128]
                store_sums(sz.slots, slot, j, held[u][j][0], cut, offsets, sums)
            mark(slot, pick[0], hot)
        return carry

    lax.fori_loop(0, lax.div(total + UNROLL - 1, UNROLL), several, 0)


def tiles_of_cells(sz, base, total, mine, source_rows, centres, targets, offsets, sums, hot):
    whole = 128 * (sz.points // 128)

    def several(q, carry):
        slots = [q * PAIR + u for u in range(PAIR)]
        picks = [(jnp.maximum(mine[0, slot], 0) + base, mine[1, slot]) for slot in slots]
        parts, held, stages = {}, [], []
        for u, (slot, pick) in enumerate(zip(slots, picks)):
            (y_stack, m_stack), points = task_operands(
                slot, pick, source_rows, centres, targets, offsets, sz
            )
            held.append(points)
            y_turned = jnp.transpose(y_stack)
            for begin, end in pieces(whole, 256):
                stack = [stack for _, stack in points[begin // 128 : end // 128]]
                stack = jnp.concatenate(stack, axis=1)
                for first, last in pieces(sz.points, 128):
                    add = adder(parts, (u, begin))
                    rows = y_turned[first:last]
                    stages.append(wide_piece(stack, rows, m_stack, first, last, add))
            if whole < sz.points:
                rest = jnp.transpose(points[-1][1])[: sz.points - whole]
                stages.append(rest_piece(rest, y_stack, m_stack, adder(parts, (u, whole))))
        skewed(stages)
        for u, slot in enumerate(slots):
            results = [fold(parts[u, begin]) for begin, _ in pieces(whole, 256)]
            if whole < sz.points:
                result = fold(parts[u, whole])
                spare = jnp.zeros((SUM_ROWS, 128 - result.shape[1]), F32)
                results.append(jnp.concatenate([result, spare], axis=1))
            result = jnp.concatenate(results, axis=1)
            for j in range(sz.tiles):
                cut = result[:, 128 * j : 128 * j + 128]
                store_sums(sz.own, slot, j, held[u][j][0], cut, offsets, sums)
            mark(slot, mine[0, slot], hot)
        return carry

    lax.fori_loop(0, lax.div(total + PAIR - 1, PAIR), several, 0)


def packed(sz, blocks):
    rows = [b[:, : sz.main] for b in blocks] if sz.main else []
    lanes = lane_iota(8)
    for p in range(0, len(blocks), sz.per_pack):
        total = jnp.zeros((8, 128), F32)
        for q, block in enumerate(blocks[p : p + sz.per_pack]):
            rest = jnp.where(lanes < sz.rest, block[:, sz.main : sz.main + 128], 0.0)
            total = total + (pltpu.roll(rest, q * sz.rest, 1) if q else rest)
        rows.append(total)
    return rows


def store_packed(sz, out, blocks):
    first = 0
    count = len(blocks)
    values = packed(sz, blocks)
    if sz.main:
        for b in range(count):
            for m in range(sz.main // 128):
                out[pl.ds(first, 8), :] = values[b][:, 128 * m : 128 * m + 128]
                first += 8
        values = values[count:]
    for value in values:
        out[pl.ds(first, 8), :] = value
        first += 8


def place_packed(sz, lane, arrived, count, store_main, add_rest):
    first = 0
    if sz.main:
        for b in range(count):
            for m in range(sz.main // 128):
                store_main(b, m, arrived[pl.ds(first, 8), :])
                first += 8
    start = sz.rest * lane
    lanes = lane_iota(8)
    for b in range(count):
        pack, q = divmod(b, sz.per_pack)
        value = arrived[pl.ds(first + 8 * pack, 8), :]
        value = pltpu.roll(value, lax.rem(start - q * sz.rest + 128, 128), 1)
        for tile in range(sz.rest_tiles):
            inside = (lanes + 128 * tile >= start) & (lanes + 128 * tile < start + sz.rest)
            add_rest(b, tile, jnp.where(inside, value, 0.0))


def source_kernel(sz, *refs):
    inputs, (high_out, low_out, source_rows, centres), held, sems = (
        refs[:2],
        refs[2:6],
        refs[6:8],
        refs[8],
    )
    for copy in fetch(inputs, held, sems):
        copy.wait()
    positions, bend = held
    high_out[...], low_out[...] = split2(bend[...])
    value = jnp.concatenate([positions[i] for i in range(3)], axis=0)
    value = jnp.concatenate(
        [value, jnp.zeros((3 * sz.cells, sz.width - sz.points), F32)], axis=1
    )
    make_sources(sz, value, high_out[...], low_out[...], source_rows, centres, 0)


def first_kernel(sz, *refs):
    inputs, (chunk_out, ghost_out, tasks), refs = refs[:7], refs[7:10], refs[10:]
    source_rows, centres, targets, offsets, sums, speeds, hot, moved, pool = refs[:9]
    send, positions, arrived, high, low, staged, lists, sems = refs[9:]
    me, lane = lax.axis_index("space"), lax.axis_index("lane")
    own_rows = source_rows.at[:, pl.ds(0, SOURCE_ROWS * sz.cells)]
    own_centres = centres.at[pl.ds(0, 8 * sz.cells)]
    held = [arrived, send, positions, high, low, own_rows, own_centres]
    copies = fetch(inputs, held, sems)
    copies[0].wait()
    for other in range(sz.lanes):
        row = ((me * sz.lanes + other) * sz.group) * 4 + 3
        value = pltpu.roll(arrived[pl.ds(row, 1), :], 128 - 3 * sz.rest, 1)
        staged[pl.ds(other, 1), :] = value.astype(jnp.int32)
    copies.append(pltpu.make_async_copy(staged, lists, sems.at[7]))
    copies[7].start()
    pool[...] = jnp.zeros_like(pool)
    take_ghosts(sz, arrived, pool, up(sz.owners * sz.group, 8), 0)
    hot[...] = jnp.zeros_like(hot)
    speeds[...] = jnp.zeros_like(speeds)
    for copy in copies[1:5]:
        copy.wait()
    make_sources(sz, pool[...], high[...], low[...], source_rows, centres, sz.cells)
    make_targets(
        sz, lambda i, g: own_chunk(sz, lane, positions.at[i], pl.ds(8 * g, 8)), targets
    )
    for copy in copies[5:]:
        copy.wait()
    total = build_list(sz, lists, tasks)
    tiles_of_chunk(sz, total, tasks, source_rows, centres, targets, offsets, sums, hot)
    velocity = add_up(sz, sz.slots, total, sz.cells, offsets, sums, speeds, hot)
    blocks = []
    for i in range(3):
        for g in range(0, sz.cells, 8):
            chunk = own_chunk(sz, lane, positions.at[i], pl.ds(g, 8))
            block = chunk + TIME_STEP * velocity[i][g : g + 8]
            moved[pl.ds(i * sz.rows + g, 8), :] = block
            blocks.append(block)
    store_packed(sz, chunk_out, blocks)
    send_ghosts(sz, send, moved, ghost_out, jnp.zeros((1, 128), F32))


def second_kernel(sz, *refs):
    count = sz.lanes + 4
    inputs, (moved_out, velocity_out), refs = refs[:count], refs[count : count + 2], refs[count + 2 :]
    source_rows, centres, targets, offsets, sums, speeds, hot, pool, mine = refs[:9]
    held, sems = refs[9:-1], refs[-1]
    copies = fetch(inputs, held, sems)
    tasks, arrived, chunks, (high, low) = held[0], held[1], held[2:-2], held[-2:]
    hot[...] = jnp.zeros_like(hot)
    speeds[...] = jnp.zeros_like(speeds)
    lane = lax.axis_index("lane")
    pool[...] = jnp.zeros_like(pool)
    for copy in copies[:-2]:
        copy.wait()
    per = sz.cells // 8
    for k in range(sz.lanes):
        other = lane ^ k

        def row_of(b):
            return (b // per) * sz.pool + 8 * (b % per)

        def store_main(b, m, value):
            cut = pl.ds(pl.multiple_of(other * sz.main + 128 * m, 128), 128)
            pool[pl.ds(row_of(b), 8), cut] = value

        def add_rest(b, tile, value):
            offset = sz.main * sz.lanes + 128 * tile
            cut = (pl.ds(row_of(b), 8), slice(offset, offset + 128))
            pool[cut] = pool[cut] + value

        place_packed(sz, other, chunks[k], 3 * per, store_main, add_rest)
    take_ghosts(sz, arrived, pool, sz.pool, sz.cells)
    total = own_list(sz, lane, tasks, mine)
    for copy in copies[-2:]:
        copy.wait()
    make_sources(sz, pool[...], high[...], low[...], source_rows, centres, 0)
    make_targets(sz, lambda i, g: pool[pl.ds(i * sz.pool + 8 * g, 8), :], targets)
    first = lane * sz.share
    tiles_of_cells(sz, first, total, mine, source_rows, centres, targets, offsets, sums, hot)
    velocity = add_up(sz, sz.own, total, up(sz.share, 8), offsets, sums, speeds, hot)
    for i in range(3):
        speed = velocity[i]
        moved = share_rows(sz, pool, i * sz.pool, lane) + TIME_STEP * speed
        velocity_out[i] = speed[: sz.share, : sz.points]
        moved_out[i] = moved[: sz.share, : sz.points]


def share_rows(sz, ref, base, lane):
    if sz.share % 8 == 0:
        return ref[pl.ds(pl.multiple_of(base + lane * sz.share, 8), sz.share), :]
    rows = [ref[pl.ds(base + lane * sz.share + c, 1), :] for c in range(sz.share)]
    rows.append(jnp.zeros((8 - sz.share, rows[0].shape[1]), F32))
    return jnp.concatenate(rows, axis=0)


def scratch(sz, tiles, slots):
    return [
        pltpu.VMEM((sz.tiles, SOURCE_ROWS * sz.pool, 128), F32),
        pltpu.VMEM((8 * sz.pool, 128), F32),
        pltpu.VMEM((tiles, 8 * sz.rows, 128), F32),
        pltpu.VMEM((tiles, 8 * slots, 128), F32),
        pltpu.VMEM((tiles, SUM_ROWS * slots, 128), F32),
        pltpu.VMEM((3, slots, 128 * tiles), F32),
        pltpu.VMEM((slots, 128), F32),
    ]


def swap(value, axis, size, k):
    return lax.ppermute(value, axis, [(d, d ^ k) for d in range(size)])


def shards(positions, bend_op, send_list, task_target, task_source, task_count):
    owners, lanes = lax.axis_size("space"), lax.axis_size("lane")
    cells, points = positions.shape[0], positions.shape[2]
    sz = sizes(owners, lanes, cells, points, task_target.shape[1], send_list.shape[1])
    params = pltpu.CompilerParams(vmem_limit_bytes=60 << 20)
    shape = jax.ShapeDtypeStruct
    both = ("space", "lane")
    by_component = jnp.transpose(positions, (1, 0, 2))
    list_rows = up(lanes, 8)
    slot_shape = shape((4 * sz.group * owners * lanes, 128), F32)
    leaving, send = pl.pallas_call(
        functools.partial(pick_kernel, sz),
        out_shape=[slot_shape, shape(send_list.shape, jnp.int32)],
        in_specs=[HBM] * 5,
        out_specs=[VMEM, SMEM],
        scratch_shapes=[
            pltpu.SMEM(send_list.shape, jnp.int32),
            pltpu.VMEM(task_target.shape, jnp.int32),
            pltpu.VMEM(task_source.shape, jnp.int32),
            pltpu.SMEM(task_count.shape, jnp.int32),
            pltpu.VMEM(by_component.shape, F32),
            pltpu.VMEM((3 * sz.rows, sz.chunk_wide), F32),
            pltpu.SemaphoreType.DMA((5,)),
        ],
        compiler_params=params,
        name="pick_cells",
    )(send_list, task_target, task_source, task_count, by_component)
    arrived = lax.all_to_all(leaving, both, split_axis=0, concat_axis=0, tiled=True)
    high, low, own_rows, own_centres = pl.pallas_call(
        functools.partial(source_kernel, sz),
        out_shape=[
            shape(bend_op.shape, BF16),
            shape(bend_op.shape, BF16),
            shape((sz.tiles, SOURCE_ROWS * cells, 128), F32),
            shape((8 * cells, 128), F32),
        ],
        in_specs=[HBM] * 2,
        out_specs=[VMEM] * 4,
        scratch_shapes=[
            pltpu.VMEM(by_component.shape, F32),
            pltpu.VMEM(bend_op.shape, F32),
            pltpu.SemaphoreType.DMA((2,)),
        ],
        compiler_params=params,
        cost_estimate=pl.CostEstimate(flops=10**9, bytes_accessed=10**7, transcendentals=0),
        name="first_sources",
    )(by_component, bend_op)
    chunk, leaving, tasks = pl.pallas_call(
        functools.partial(first_kernel, sz),
        out_shape=[
            shape((pack_rows(sz, cells), 128), F32),
            slot_shape,
            shape((3, sz.slots), jnp.int32),
        ],
        in_specs=[HBM] * 7,
        out_specs=[VMEM, VMEM, SMEM],
        scratch_shapes=scratch(sz, sz.chunk_tiles, sz.slots)
        + [
            pltpu.VMEM((3 * sz.rows, sz.chunk_wide), F32),
            pltpu.VMEM((3 * up(sz.owners * sz.group, 8), sz.width), F32),
            pltpu.SMEM(send_list.shape, jnp.int32),
            pltpu.VMEM(by_component.shape, F32),
            pltpu.VMEM(slot_shape.shape, F32),
            pltpu.VMEM(bend_op.shape, BF16),
            pltpu.VMEM(bend_op.shape, BF16),
            pltpu.VMEM((list_rows, 128), jnp.int32),
            pltpu.SMEM((list_rows, 128), jnp.int32),
            pltpu.SemaphoreType.DMA((8,)),
        ],
        compiler_params=params,
        name="first_step",
    )(arrived, send, by_component, high, low, own_rows, own_centres)
    arrived = lax.all_to_all(leaving, both, split_axis=0, concat_axis=0, tiled=True)
    chunks = [chunk] + [swap(chunk, "lane", lanes, k) for k in range(1, lanes)]
    result = shape((3, sz.share, points), F32)
    outputs = pl.pallas_call(
        functools.partial(second_kernel, sz),
        out_shape=[result, result],
        in_specs=[HBM] * (lanes + 4),
        out_specs=[VMEM] * 2,
        scratch_shapes=scratch(sz, sz.tiles, sz.own)
        + [
            pltpu.VMEM((3 * sz.pool, sz.width), F32),
            pltpu.SMEM((2, sz.own + 8), jnp.int32),
            pltpu.SMEM(tasks.shape, jnp.int32),
            pltpu.VMEM(slot_shape.shape, F32),
        ]
        + [pltpu.VMEM(chunk.shape, F32)] * lanes
        + [pltpu.VMEM(bend_op.shape, BF16)] * 2
        + [pltpu.SemaphoreType.DMA((lanes + 4,))],
        compiler_params=params,
        name="second_step",
    )(tasks, arrived, *chunks, high, low)
    return tuple(jnp.transpose(output, (1, 0, 2)) for output in outputs)


def solution(mesh):
    in_specs = (
        P("space", None, None),
        P(),
        P("space", None),
        P(("space", "lane"), None),
        P(("space", "lane"), None),
        P(("space", "lane")),
    )
    out_specs = (P(("space", "lane"), None, None), P(("space", "lane"), None, None))
    return jax.shard_map(shards, mesh=mesh, in_specs=in_specs, out_specs=out_specs, check_vma=False)
```

```python
import functools
from types import SimpleNamespace

import jax
import jax.numpy as jnp
from jax import lax
from jax.experimental import pallas as pl
from jax.experimental.pallas import tpu as pltpu
from jax.sharding import PartitionSpec as P

REGULARIZE = 0.25
TIME_STEP = 0.5
UNROLL = 4
PAIR = 2
SOURCE_ROWS = 24
SUM_ROWS = 16

F32 = jnp.float32
BF16 = jnp.bfloat16
VMEM = pl.BlockSpec(memory_space=pltpu.VMEM)
SMEM = pl.BlockSpec(memory_space=pltpu.SMEM)
HBM = pl.BlockSpec(memory_space=pltpu.HBM)


def up(value, step):
    return -(-value // step) * step


def sizes(owners, lanes, cells, points, cap, listed):
    main = 128 * (points // (128 * lanes))
    rest = (points - main * lanes) // lanes
    group = listed // owners
    pool = up(cells + listed, 8)
    per_pack = 128 // rest
    return SimpleNamespace(
        owners=owners,
        lanes=lanes,
        cells=cells,
        points=points,
        cap=cap,
        group=group,
        width=up(points, 128),
        tiles=up(points, 128) // 128,
        main=main,
        rest=rest,
        rest_tiles=up(rest * lanes, 128) // 128,
        chunk=main + rest,
        chunk_wide=main + up(rest, 128),
        chunk_tiles=(main + up(rest, 128)) // 128,
        per_pack=per_pack,
        pool=pool,
        share=cells // lanes,
        slots=up(lanes * cap + UNROLL, 8),
        rows=cells + 8,
        own=up(lanes * cap + PAIR, 8),
    )


def pack_rows(sz, rows):
    return (3 * rows * sz.main // 128) + 8 * up(3 * rows // 8, sz.per_pack) // sz.per_pack


def split2(value):
    high = value.astype(BF16)
    return high, (value - high.astype(F32)).astype(BF16)


def split3(value):
    first = value.astype(BF16).astype(F32)
    left = value - first
    second = left.astype(BF16).astype(F32)
    return first, second, left - second


def lane_iota(rows):
    return lax.broadcasted_iota(jnp.int32, (rows, 128), 1)


def fetch(sources, targets, sems):
    copies = [
        pltpu.make_async_copy(source, target, sems.at[q])
        for q, (source, target) in enumerate(zip(sources, targets))
    ]
    for copy in copies:
        copy.start()
    return copies


def loop(count, body):
    if count <= 8:
        for q in range(count):
            body(q)
    else:

        def step(q, carry):
            body(q)
            return carry

        lax.fori_loop(0, count, step, 0)


def own_chunk(sz, lane, ref, rows):
    parts = []
    if sz.main:
        parts.append(ref[rows, pl.ds(pl.multiple_of(lane * sz.main, 128), sz.main)])
    start = sz.rest * lane
    lanes = lane_iota(8)
    rest = jnp.zeros((8, 128), F32)
    for tile in range(sz.rest_tiles):
        offset = sz.main * sz.lanes + 128 * tile
        block = ref[rows, offset : min(offset + 128, ref.shape[-1])]
        if block.shape[1] < 128:
            block = jnp.concatenate([block, jnp.zeros((8, 128 - block.shape[1]), F32)], axis=1)
        inside = (lanes + 128 * tile >= start) & (lanes + 128 * tile < start + sz.rest)
        rest = rest + jnp.where(inside, block, 0.0)
    rest = pltpu.roll(rest, lax.rem(128 * sz.rest_tiles - start, 128), 1)
    parts.append(rest)
    return jnp.concatenate(parts, axis=1) if len(parts) > 1 else parts[0]


def send_ghosts(sz, send, chunks, out, tasks):
    lanes = lane_iota(1)

    def one(d):
        for g in range(sz.group):
            cell = send[0, d * sz.group + g]
            rows = []
            last = tasks
            for i in range(3):
                row = chunks[pl.ds(i * sz.rows + cell, 1), :]
                rows.append(row[:, :128] if sz.main else jnp.zeros((1, 128), F32))
                piece = jnp.where(lanes < sz.rest, row[:, sz.main : sz.main + 128], 0.0)
                last = last + (pltpu.roll(piece, i * sz.rest, 1) if i else piece)
            rows.append(last)
            for other in range(sz.lanes):
                first = ((d * sz.lanes + other) * sz.group + g) * 4
                for q, row in enumerate(rows):
                    out[pl.ds(first + q, 1), :] = row

    loop(sz.owners, one)


def pick_kernel(sz, *refs):
    inputs, (out, send_out), held, (chunks, sems) = refs[:5], refs[5:7], refs[7:12], refs[12:]
    for copy in fetch(inputs, held, sems):
        copy.wait()
    send, target, source, count, positions = held
    for j in range(send_out.shape[1]):
        send_out[0, j] = send[0, j]
    lane = lax.axis_index("lane")
    for i in range(3):
        for g in range(0, sz.cells, 8):
            value = own_chunk(sz, lane, positions.at[i], pl.ds(g, 8))
            chunks[pl.ds(i * sz.rows + g, 8), :] = value
    spare = jnp.zeros((1, 128 - sz.cap), F32)
    tasks = jnp.where(lane_iota(1) == 3 * sz.rest + 2 * sz.cap, count[0].astype(F32), 0.0)
    for q, row in enumerate((target, source)):
        wide = jnp.concatenate([row[...].astype(F32), spare], axis=1)
        tasks = tasks + pltpu.roll(wide, 3 * sz.rest + q * sz.cap, 1)
    send_ghosts(sz, send, chunks, out, tasks)


def take_ghosts(sz, arrived, pool, stride, base):
    lanes = lane_iota(1)

    def one(d):
        for g in range(sz.group):
            first = [((d * sz.lanes + lane) * sz.group + g) * 4 for lane in range(sz.lanes)]
            last = [arrived[pl.ds(row + 3, 1), :] for row in first]
            for i in range(3):
                tiles = []
                if sz.main:
                    tiles += [arrived[pl.ds(row + i, 1), :] for row in first]
                for tile in range(sz.rest_tiles):
                    total = jnp.zeros((1, 128), F32)
                    for lane in range(sz.lanes):
                        start = sz.rest * lane
                        if start + sz.rest <= 128 * tile or start >= 128 * tile + 128:
                            continue
                        shift = (start - i * sz.rest) % 128
                        value = pltpu.roll(last[lane], shift, 1) if shift else last[lane]
                        at = lanes + 128 * tile
                        total = jnp.where((at >= start) & (at < start + sz.rest), value, total)
                    tiles.append(total)
                place = pl.ds(i * stride + base + d * sz.group + g, 1)
                pool[place, :] = jnp.concatenate(tiles, axis=1)

    loop(sz.owners, one)


def build_list(sz, lists, tasks):
    total = jnp.int32(0)
    for lane in range(sz.lanes):

        def step(j, total, lane=lane):
            tasks[0, total] = lists[lane, j]
            tasks[1, total] = lists[lane, sz.cap + j]
            return total + 1

        total = lax.fori_loop(0, lists[lane, 2 * sz.cap], step, total)
    for u in range(UNROLL):
        tasks[0, total + u] = jnp.int32(sz.cells)
        tasks[1, total + u] = jnp.int32(0)
    tasks[2, 0] = total
    return total


def own_list(sz, lane, tasks, mine):
    first = lane * sz.share

    def step(t, count):
        target = tasks[0, t] - first
        mine[0, count] = target
        mine[1, count] = tasks[1, t]
        return count + ((target >= 0) & (target < sz.share)).astype(jnp.int32)

    total = lax.fori_loop(0, tasks[2, 0], step, jnp.int32(0))
    for u in range(PAIR):
        mine[0, total + u] = jnp.int32(-1)
        mine[1, total + u] = jnp.int32(0)
    return total


def products(value, bend_high, bend_low):
    high, low = split2(value)
    dot = functools.partial(jnp.dot, preferred_element_type=F32)
    return dot(high, bend_high) + dot(low, bend_high) + dot(high, bend_low)


def make_sources(sz, value, bend_high, bend_low, source_rows, centres, first):
    count = value.shape[0] // 3
    forces = products(value[:, : sz.points], bend_high, bend_low)
    forces = jnp.concatenate(
        [forces, jnp.zeros((3 * count, sz.width - sz.points), F32)], axis=1
    )
    middle = jnp.sum(value, axis=1, keepdims=True) / sz.points
    for g in range(count // 8):
        where = [i * count + 8 * g for i in range(3)]
        middles = [jnp.broadcast_to(middle[w : w + 8], (8, 128)) for w in where]
        middles += [jnp.zeros((8, 128), F32)] * 5
        for i, row in enumerate(middles):
            centres[pl.ds(8 * (first + 8 * g) + i, 8, stride=8), :] = row
        for j in range(sz.tiles):
            cut = slice(128 * j, 128 * j + 128)
            y = [value[w : w + 8, cut] - m for w, m in zip(where, middles)]
            f = [forces[w : w + 8, cut] for w in where]
            norm = y[0] * y[0] + y[1] * y[1] + y[2] * y[2] + REGULARIZE
            along = y[0] * f[0] + y[1] * f[1] + y[2] * f[2]
            one, zero = jnp.ones((8, 128), F32), jnp.zeros((8, 128), F32)
            rows = [y[0], y[1], y[2], norm, one, zero, zero, zero]
            rows += f
            rows += [y[i] * f[k] for i in range(3) for k in range(3)]
            rows += [norm * f[i] + along * y[i] for i in range(3)]
            rows += [along]
            for k, row in enumerate(rows):
                place = pl.ds(SOURCE_ROWS * (first + 8 * g) + k, 8, stride=SOURCE_ROWS)
                source_rows.at[j][place, :] = row


def make_targets(sz, blocks, targets):
    targets[...] = jnp.zeros_like(targets)
    for g in range(sz.cells // 8):
        for i in range(3):
            block = blocks(i, g)
            for j in range(targets.shape[0]):
                cut = slice(128 * j, 128 * j + 128)
                targets.at[j][pl.ds(64 * g + i, 8, stride=8), :] = block[:, cut]


def source_operands(sz, source, source_rows):
    held = [
        source_rows[j, pl.ds(pl.multiple_of(SOURCE_ROWS * source, 8), SOURCE_ROWS), :]
        for j in range(sz.tiles)
    ]
    held = jnp.concatenate(held, axis=1)
    y1, y2, y3 = split3(held[:8])
    y_stack = jnp.concatenate([y1, y1, y2, y2, y1, y3], axis=0).astype(BF16)
    return y_stack, jnp.concatenate(split3(held[8:]), axis=0)


def pieces(points, step):
    starts = list(range(0, max(points // 128 * 128, 1), step))
    return list(zip(starts, starts[1:] + [points]))


def twice(piece, count):
    whole = count // 128 * 128
    parts = [piece[:, :whole].astype(BF16)] * 2 if whole else []
    if whole < count:
        last = piece[:, whole:]
        last = last + pltpu.roll(last, count - whole, 1)
        parts.append(last.astype(BF16)[:, : 2 * (count - whole)])
    return jnp.concatenate(parts, axis=1)


def load_target(j, target, slot, centre, targets, offsets):
    row = lax.broadcasted_iota(jnp.int32, (8, 128), 0)
    x = targets[j, pl.ds(pl.multiple_of(8 * target, 8), 8), :] - centre
    square = x * x
    norm = pltpu.roll(square, 2, 0) + pltpu.roll(square, 3, 0) + pltpu.roll(square, 4, 0)
    side = jnp.where(row == 4, norm, jnp.where(row == 3, 1.0, 0.0))
    x_side = jnp.where(row < 3, -2.0 * x, side)
    x1, x2, x3 = split3(x_side)
    return x, jnp.concatenate([x1, x2, x1, x2, x3, x1], axis=0).astype(BF16)


def distances(one_stack, other_stack):
    return jnp.dot(one_stack, other_stack, preferred_element_type=F32)


def weights(shifted):
    inverse = lax.rsqrt(shifted)
    return split2(inverse * inverse * inverse)


def fold(result):
    return result[:SUM_ROWS] + result[SUM_ROWS : 2 * SUM_ROWS] + result[2 * SUM_ROWS :]


def skewed(stages, skew):
    asked = []
    for q, (ask, _) in enumerate(stages):
        asked.append(ask())
        if q >= skew:
            stages[q - skew][1](asked[q - skew])
            asked[q - skew] = None
    for q in range(max(len(stages) - skew, 0), len(stages)):
        stages[q][1](asked[q])


def adder(totals, key):
    def add(value):
        totals[key] = totals[key] + value if key in totals else value

    return add


def wide_piece(targets, y_turned, m_stack, first, end, add):
    def ask():
        return distances(y_turned, targets)

    def take(shifted):
        high, low = weights(shifted)
        whole = (end - first) // 128 * 128
        parts = [high[:whole], low[:whole]] if whole else []
        parts += [high[whole:], low[whole:]] if whole < end - first else []
        stack = jnp.concatenate(parts, axis=0)
        m_piece = twice(m_stack[:, first : up(end, 128)], end - first)
        add(jnp.dot(m_piece, stack, preferred_element_type=F32))

    return ask, take


def rest_piece(targets, y_stack, m_stack, add):
    def ask():
        return distances(targets, y_stack)

    def take(shifted):
        high, low = weights(shifted)
        m_whole = m_stack.astype(BF16)
        turned = (((1,), (1,)), ((), ()))
        result = lax.dot_general(m_whole, high, turned, preferred_element_type=F32)
        add(result + lax.dot_general(m_whole, low, turned, preferred_element_type=F32))

    return ask, take


def store_sums(slots, slot, j, x, result, offsets, sums):
    offsets.at[j][pl.ds(slot, 8, stride=slots), :] = x
    for h in range(0, SUM_ROWS, 8):
        sums.at[j][pl.ds(h * slots + slot, 8, stride=slots), :] = result[h : h + 8]


def mark(slot, target, hot):
    hot[pl.ds(slot, 1), :] = jnp.where(lane_iota(1) == target, 1.0, 0.0)


def combine(sz, slots, first, total, offsets, sums, speeds):
    live = lax.broadcasted_iota(jnp.int32, (8, 128), 0) + first < total
    for j in range(offsets.shape[0]):
        x = [offsets[j, pl.ds(i * slots + first, 8), :] for i in range(3)]
        s = [sums[j, pl.ds(k * slots + first, 8), :] for k in range(SUM_ROWS)]
        a, b, c = s[:3], [s[3:6], s[6:9], s[9:12]], s[12:15]
        norm = x[0] * x[0] + x[1] * x[1] + x[2] * x[2] + REGULARIZE
        along = x[0] * a[0] + x[1] * a[1] + x[2] * a[2] - s[15]
        for i in range(3):
            speed = norm * a[i] + c[i] + along * x[i]
            for k in range(3):
                speed = speed - x[k] * (2.0 * b[k][i] + b[i][k])
            speed = jnp.where(live, speed / sz.points, 0.0)
            speeds[i, pl.ds(first, 8), 128 * j : 128 * j + 128] = speed


def add_up(sz, slots, total, rows, offsets, sums, speeds, hot):
    def eight(q, carry):
        combine(sz, slots, pl.multiple_of(8 * q, 8), total, offsets, sums, speeds)
        return carry

    lax.fori_loop(0, lax.div(total + 7, 8), eight, 0)
    one_hot = hot[...].astype(BF16)
    result = []
    for i in range(3):
        first, second, third = split3(speeds[i])
        parts = [
            lax.dot_general(
                one_hot, part.astype(BF16), (((0,), (0,)), ((), ())), preferred_element_type=F32
            )
            for part in (first, second, third)
        ]
        result.append((parts[0] + parts[1] + parts[2])[:rows])
    return result


def several_tasks(sz, slots, picks, marks, main, rest, wide, step, skew, refs):
    source_rows, centres, targets, offsets, sums, hot = refs
    parts, held, stages = {}, [], []
    for u, (slot, (target, source)) in enumerate(zip(slots, picks)):
        y_stack, m_stack = source_operands(sz, source, source_rows)
        centre = centres[pl.ds(pl.multiple_of(8 * source, 8), 8), :]
        points = [
            load_target(j, target, slot, centre, targets, offsets)
            for j in range(targets.shape[0])
        ]
        held.append(points)
        y_turned = jnp.transpose(y_stack)
        for begin in range(0, main, wide):
            stack = [stack for _, stack in points[begin // 128 : (begin + wide) // 128]]
            stack = jnp.concatenate(stack, axis=1)
            for first, last in pieces(sz.points, step):
                add = adder(parts, (u, begin))
                stages.append(wide_piece(stack, y_turned[first:last], m_stack, first, last, add))
        if rest:
            stack = jnp.transpose(points[main // 128][1])[:rest]
            stages.append(rest_piece(stack, y_stack, m_stack, adder(parts, (u, main))))
    skewed(stages, skew)
    for u, slot in enumerate(slots):
        results = [fold(parts[u, begin]) for begin in range(0, main, wide)]
        if rest:
            result = fold(parts[u, main])
            spare = jnp.zeros((SUM_ROWS, 128 - rest), F32)
            results.append(jnp.concatenate([result, spare], axis=1))
        result = jnp.concatenate(results, axis=1)
        for j in range(targets.shape[0]):
            cut = result[:, 128 * j : 128 * j + 128]
            store_sums(offsets.shape[1] // 8, slot, j, held[u][j][0], cut, offsets, sums)
        mark(slot, marks[u], hot)


def tiles_of_chunk(sz, total, tasks, *refs):
    def several(q, carry):
        slots = [q * UNROLL + u for u in range(UNROLL)]
        picks = [(tasks[0, slot], tasks[1, slot]) for slot in slots]
        marks = [target for target, _ in picks]
        several_tasks(sz, slots, picks, marks, sz.main, sz.rest, 128, 256, 3, refs)
        return carry

    lax.fori_loop(0, lax.div(total + UNROLL - 1, UNROLL), several, 0)


def tiles_of_cells(sz, base, total, mine, *refs):
    main = 256 * (sz.points // 256)

    def several(q, carry):
        slots = [q * PAIR + u for u in range(PAIR)]
        marks = [mine[0, slot] for slot in slots]
        picks = [(jnp.maximum(mark, 0) + base, mine[1, s]) for mark, s in zip(marks, slots)]
        several_tasks(sz, slots, picks, marks, main, sz.points - main, 256, 128, 2, refs)
        return carry

    lax.fori_loop(0, lax.div(total + PAIR - 1, PAIR), several, 0)


def packed(sz, blocks):
    rows = [b[:, : sz.main] for b in blocks] if sz.main else []
    lanes = lane_iota(8)
    for p in range(0, len(blocks), sz.per_pack):
        total = jnp.zeros((8, 128), F32)
        for q, block in enumerate(blocks[p : p + sz.per_pack]):
            rest = jnp.where(lanes < sz.rest, block[:, sz.main : sz.main + 128], 0.0)
            total = total + (pltpu.roll(rest, q * sz.rest, 1) if q else rest)
        rows.append(total)
    return rows


def store_packed(sz, out, blocks):
    first = 0
    count = len(blocks)
    values = packed(sz, blocks)
    if sz.main:
        for b in range(count):
            for m in range(sz.main // 128):
                out[pl.ds(first, 8), :] = values[b][:, 128 * m : 128 * m + 128]
                first += 8
        values = values[count:]
    for value in values:
        out[pl.ds(first, 8), :] = value
        first += 8


def place_packed(sz, lane, arrived, count, store_main, add_rest):
    first = 0
    if sz.main:
        for b in range(count):
            for m in range(sz.main // 128):
                store_main(b, m, arrived[pl.ds(first, 8), :])
                first += 8
    start = sz.rest * lane
    lanes = lane_iota(8)
    for b in range(count):
        pack, q = divmod(b, sz.per_pack)
        value = arrived[pl.ds(first + 8 * pack, 8), :]
        value = pltpu.roll(value, lax.rem(start - q * sz.rest + 128, 128), 1)
        for tile in range(sz.rest_tiles):
            inside = (lanes + 128 * tile >= start) & (lanes + 128 * tile < start + sz.rest)
            add_rest(b, tile, jnp.where(inside, value, 0.0))


def source_kernel(sz, *refs):
    inputs, (high_out, low_out, source_rows, centres), held, sems = (
        refs[:2],
        refs[2:6],
        refs[6:8],
        refs[8],
    )
    for copy in fetch(inputs, held, sems):
        copy.wait()
    positions, bend = held
    high_out[...], low_out[...] = split2(bend[...])
    value = jnp.concatenate([positions[i] for i in range(3)], axis=0)
    value = jnp.concatenate(
        [value, jnp.zeros((3 * sz.cells, sz.width - sz.points), F32)], axis=1
    )
    make_sources(sz, value, high_out[...], low_out[...], source_rows, centres, 0)


def first_kernel(sz, *refs):
    inputs, (chunk_out, ghost_out, tasks), refs = refs[:7], refs[7:10], refs[10:]
    source_rows, centres, targets, offsets, sums, speeds, hot, moved, pool = refs[:9]
    send, positions, arrived, high, low, staged, lists, sems = refs[9:]
    me, lane = lax.axis_index("space"), lax.axis_index("lane")
    own_rows = source_rows.at[:, pl.ds(0, SOURCE_ROWS * sz.cells)]
    own_centres = centres.at[pl.ds(0, 8 * sz.cells)]
    held = [arrived, send, positions, high, low, own_rows, own_centres]
    copies = fetch(inputs, held, sems)
    copies[0].wait()
    for other in range(sz.lanes):
        row = ((me * sz.lanes + other) * sz.group) * 4 + 3
        value = pltpu.roll(arrived[pl.ds(row, 1), :], 128 - 3 * sz.rest, 1)
        staged[pl.ds(other, 1), :] = value.astype(jnp.int32)
    copies.append(pltpu.make_async_copy(staged, lists, sems.at[7]))
    copies[7].start()
    pool[...] = jnp.zeros_like(pool)
    take_ghosts(sz, arrived, pool, up(sz.owners * sz.group, 8), 0)
    hot[...] = jnp.zeros_like(hot)
    speeds[...] = jnp.zeros_like(speeds)
    for copy in copies[1:5]:
        copy.wait()
    make_sources(sz, pool[...], high[...], low[...], source_rows, centres, sz.cells)
    make_targets(
        sz, lambda i, g: own_chunk(sz, lane, positions.at[i], pl.ds(8 * g, 8)), targets
    )
    for copy in copies[5:]:
        copy.wait()
    total = build_list(sz, lists, tasks)
    tiles_of_chunk(sz, total, tasks, source_rows, centres, targets, offsets, sums, hot)
    velocity = add_up(sz, sz.slots, total, sz.cells, offsets, sums, speeds, hot)
    blocks = []
    for i in range(3):
        for g in range(0, sz.cells, 8):
            chunk = own_chunk(sz, lane, positions.at[i], pl.ds(g, 8))
            block = chunk + TIME_STEP * velocity[i][g : g + 8]
            moved[pl.ds(i * sz.rows + g, 8), :] = block
            blocks.append(block)
    store_packed(sz, chunk_out, blocks)
    send_ghosts(sz, send, moved, ghost_out, jnp.zeros((1, 128), F32))


def second_kernel(sz, *refs):
    count = sz.lanes + 4
    inputs, (moved_out, velocity_out), refs = refs[:count], refs[count : count + 2], refs[count + 2 :]
    source_rows, centres, targets, offsets, sums, speeds, hot, pool, mine = refs[:9]
    held, sems = refs[9:-1], refs[-1]
    copies = fetch(inputs, held, sems)
    tasks, arrived, chunks, (high, low) = held[0], held[1], held[2:-2], held[-2:]
    hot[...] = jnp.zeros_like(hot)
    speeds[...] = jnp.zeros_like(speeds)
    lane = lax.axis_index("lane")
    pool[...] = jnp.zeros_like(pool)
    for copy in copies[:-2]:
        copy.wait()
    per = sz.cells // 8
    for k in range(sz.lanes):
        other = lane ^ k

        def row_of(b):
            return (b // per) * sz.pool + 8 * (b % per)

        def store_main(b, m, value):
            cut = pl.ds(pl.multiple_of(other * sz.main + 128 * m, 128), 128)
            pool[pl.ds(row_of(b), 8), cut] = value

        def add_rest(b, tile, value):
            offset = sz.main * sz.lanes + 128 * tile
            cut = (pl.ds(row_of(b), 8), slice(offset, offset + 128))
            pool[cut] = pool[cut] + value

        place_packed(sz, other, chunks[k], 3 * per, store_main, add_rest)
    take_ghosts(sz, arrived, pool, sz.pool, sz.cells)
    total = own_list(sz, lane, tasks, mine)
    for copy in copies[-2:]:
        copy.wait()
    make_sources(sz, pool[...], high[...], low[...], source_rows, centres, 0)
    make_targets(sz, lambda i, g: pool[pl.ds(i * sz.pool + 8 * g, 8), :], targets)
    first = lane * sz.share
    tiles_of_cells(sz, first, total, mine, source_rows, centres, targets, offsets, sums, hot)
    velocity = add_up(sz, sz.own, total, up(sz.share, 8), offsets, sums, speeds, hot)
    for i in range(3):
        speed = velocity[i]
        moved = share_rows(sz, pool, i * sz.pool, lane) + TIME_STEP * speed
        velocity_out[i] = speed[: sz.share, : sz.points]
        moved_out[i] = moved[: sz.share, : sz.points]


def share_rows(sz, ref, base, lane):
    if sz.share % 8 == 0:
        return ref[pl.ds(pl.multiple_of(base + lane * sz.share, 8), sz.share), :]
    rows = [ref[pl.ds(base + lane * sz.share + c, 1), :] for c in range(sz.share)]
    rows.append(jnp.zeros((8 - sz.share, rows[0].shape[1]), F32))
    return jnp.concatenate(rows, axis=0)


def scratch(sz, tiles, slots):
    return [
        pltpu.VMEM((sz.tiles, SOURCE_ROWS * sz.pool, 128), F32),
        pltpu.VMEM((8 * sz.pool, 128), F32),
        pltpu.VMEM((tiles, 8 * sz.rows, 128), F32),
        pltpu.VMEM((tiles, 8 * slots, 128), F32),
        pltpu.VMEM((tiles, SUM_ROWS * slots, 128), F32),
        pltpu.VMEM((3, slots, 128 * tiles), F32),
        pltpu.VMEM((slots, 128), F32),
    ]


def swap(value, axis, size, k):
    return lax.ppermute(value, axis, [(d, d ^ k) for d in range(size)])


def shards(positions, bend_op, send_list, task_target, task_source, task_count):
    owners, lanes = lax.axis_size("space"), lax.axis_size("lane")
    cells, points = positions.shape[0], positions.shape[2]
    sz = sizes(owners, lanes, cells, points, task_target.shape[1], send_list.shape[1])
    params = pltpu.CompilerParams(vmem_limit_bytes=60 << 20)
    shape = jax.ShapeDtypeStruct
    both = ("space", "lane")
    by_component = jnp.transpose(positions, (1, 0, 2))
    list_rows = up(lanes, 8)
    slot_shape = shape((4 * sz.group * owners * lanes, 128), F32)
    leaving, send = pl.pallas_call(
        functools.partial(pick_kernel, sz),
        out_shape=[slot_shape, shape(send_list.shape, jnp.int32)],
        in_specs=[HBM] * 5,
        out_specs=[VMEM, SMEM],
        scratch_shapes=[
            pltpu.SMEM(send_list.shape, jnp.int32),
            pltpu.VMEM(task_target.shape, jnp.int32),
            pltpu.VMEM(task_source.shape, jnp.int32),
            pltpu.SMEM(task_count.shape, jnp.int32),
            pltpu.VMEM(by_component.shape, F32),
            pltpu.VMEM((3 * sz.rows, sz.chunk_wide), F32),
            pltpu.SemaphoreType.DMA((5,)),
        ],
        compiler_params=params,
        name="pick_cells",
    )(send_list, task_target, task_source, task_count, by_component)
    arrived = lax.all_to_all(leaving, both, split_axis=0, concat_axis=0, tiled=True)
    high, low, own_rows, own_centres = pl.pallas_call(
        functools.partial(source_kernel, sz),
        out_shape=[
            shape(bend_op.shape, BF16),
            shape(bend_op.shape, BF16),
            shape((sz.tiles, SOURCE_ROWS * cells, 128), F32),
            shape((8 * cells, 128), F32),
        ],
        in_specs=[HBM] * 2,
        out_specs=[VMEM] * 4,
        scratch_shapes=[
            pltpu.VMEM(by_component.shape, F32),
            pltpu.VMEM(bend_op.shape, F32),
            pltpu.SemaphoreType.DMA((2,)),
        ],
        compiler_params=params,
        cost_estimate=pl.CostEstimate(flops=10**9, bytes_accessed=10**7, transcendentals=0),
        name="first_sources",
    )(by_component, bend_op)
    chunk, leaving, tasks = pl.pallas_call(
        functools.partial(first_kernel, sz),
        out_shape=[
            shape((pack_rows(sz, cells), 128), F32),
            slot_shape,
            shape((3, sz.slots), jnp.int32),
        ],
        in_specs=[HBM] * 7,
        out_specs=[VMEM, VMEM, SMEM],
        scratch_shapes=scratch(sz, sz.chunk_tiles, sz.slots)
        + [
            pltpu.VMEM((3 * sz.rows, sz.chunk_wide), F32),
            pltpu.VMEM((3 * up(sz.owners * sz.group, 8), sz.width), F32),
            pltpu.SMEM(send_list.shape, jnp.int32),
            pltpu.VMEM(by_component.shape, F32),
            pltpu.VMEM(slot_shape.shape, F32),
            pltpu.VMEM(bend_op.shape, BF16),
            pltpu.VMEM(bend_op.shape, BF16),
            pltpu.VMEM((list_rows, 128), jnp.int32),
            pltpu.SMEM((list_rows, 128), jnp.int32),
            pltpu.SemaphoreType.DMA((8,)),
        ],
        compiler_params=params,
        name="first_step",
    )(arrived, send, by_component, high, low, own_rows, own_centres)
    arrived = lax.all_to_all(leaving, both, split_axis=0, concat_axis=0, tiled=True)
    chunks = [chunk] + [swap(chunk, "lane", lanes, k) for k in range(1, lanes)]
    result = shape((3, sz.share, points), F32)
    outputs = pl.pallas_call(
        functools.partial(second_kernel, sz),
        out_shape=[result, result],
        in_specs=[HBM] * (lanes + 4),
        out_specs=[VMEM] * 2,
        scratch_shapes=scratch(sz, sz.tiles, sz.own)
        + [
            pltpu.VMEM((3 * sz.pool, sz.width), F32),
            pltpu.SMEM((2, sz.own + 8), jnp.int32),
            pltpu.SMEM(tasks.shape, jnp.int32),
            pltpu.VMEM(slot_shape.shape, F32),
        ]
        + [pltpu.VMEM(chunk.shape, F32)] * lanes
        + [pltpu.VMEM(bend_op.shape, BF16)] * 2
        + [pltpu.SemaphoreType.DMA((lanes + 4,))],
        compiler_params=params,
        name="second_step",
    )(tasks, arrived, *chunks, high, low)
    return tuple(jnp.transpose(output, (1, 0, 2)) for output in outputs)


def solution(mesh):
    in_specs = (
        P("space", None, None),
        P(),
        P("space", None),
        P(("space", "lane"), None),
        P(("space", "lane"), None),
        P(("space", "lane")),
    )
    out_specs = (P(("space", "lane"), None, None), P(("space", "lane"), None, None))
    return jax.shard_map(shards, mesh=mesh, in_specs=in_specs, out_specs=out_specs, check_vma=False)
```

```python
import functools
from types import SimpleNamespace

import jax
import jax.numpy as jnp
from jax import lax
from jax.experimental import pallas as pl
from jax.experimental.pallas import tpu as pltpu
from jax.sharding import PartitionSpec as P

REGULARIZE = 0.25
TIME_STEP = 0.5
UNROLL = 4
PAIR = 2
SOURCE_ROWS = 24
SUM_ROWS = 16

F32 = jnp.float32
BF16 = jnp.bfloat16
VMEM = pl.BlockSpec(memory_space=pltpu.VMEM)
SMEM = pl.BlockSpec(memory_space=pltpu.SMEM)
HBM = pl.BlockSpec(memory_space=pltpu.HBM)


def up(value, step):
    return -(-value // step) * step


def sizes(owners, lanes, cells, points, cap, listed):
    main = 128 * (points // (128 * lanes))
    rest = (points - main * lanes) // lanes
    group = listed // owners
    pool = up(cells + listed, 8)
    per_pack = 128 // rest
    return SimpleNamespace(
        owners=owners,
        lanes=lanes,
        cells=cells,
        points=points,
        cap=cap,
        group=group,
        width=up(points, 128),
        tiles=up(points, 128) // 128,
        main=main,
        rest=rest,
        rest_tiles=up(rest * lanes, 128) // 128,
        chunk=main + rest,
        chunk_wide=main + up(rest, 128),
        chunk_tiles=(main + up(rest, 128)) // 128,
        per_pack=per_pack,
        pool=pool,
        share=cells // lanes,
        slots=up(lanes * cap + UNROLL, 8),
        rows=cells + 8,
        own=up(lanes * cap + PAIR, 8),
    )


def pack_rows(sz, rows):
    return (3 * rows * sz.main // 128) + 8 * up(3 * rows // 8, sz.per_pack) // sz.per_pack


def split2(value):
    high = value.astype(BF16)
    return high, (value - high.astype(F32)).astype(BF16)


def split3(value):
    first = value.astype(BF16).astype(F32)
    left = value - first
    second = left.astype(BF16).astype(F32)
    return first, second, left - second


def lane_iota(rows):
    return lax.broadcasted_iota(jnp.int32, (rows, 128), 1)


def fetch(sources, targets, sems):
    copies = [
        pltpu.make_async_copy(source, target, sems.at[q])
        for q, (source, target) in enumerate(zip(sources, targets))
    ]
    for copy in copies:
        copy.start()
    return copies


def loop(count, body):
    if count <= 8:
        for q in range(count):
            body(q)
    else:

        def step(q, carry):
            body(q)
            return carry

        lax.fori_loop(0, count, step, 0)


def own_chunk(sz, lane, ref, rows):
    parts = []
    if sz.main:
        parts.append(ref[rows, pl.ds(pl.multiple_of(lane * sz.main, 128), sz.main)])
    start = sz.rest * lane
    lanes = lane_iota(8)
    rest = jnp.zeros((8, 128), F32)
    for tile in range(sz.rest_tiles):
        offset = sz.main * sz.lanes + 128 * tile
        block = ref[rows, offset : min(offset + 128, ref.shape[-1])]
        if block.shape[1] < 128:
            block = jnp.concatenate([block, jnp.zeros((8, 128 - block.shape[1]), F32)], axis=1)
        inside = (lanes + 128 * tile >= start) & (lanes + 128 * tile < start + sz.rest)
        rest = rest + jnp.where(inside, block, 0.0)
    rest = pltpu.roll(rest, lax.rem(128 * sz.rest_tiles - start, 128), 1)
    parts.append(rest)
    return jnp.concatenate(parts, axis=1) if len(parts) > 1 else parts[0]


def send_ghosts(sz, send, chunks, out, tasks):
    lanes = lane_iota(1)

    def one(d):
        for g in range(sz.group):
            cell = send[0, d * sz.group + g]
            rows = []
            last = tasks
            for i in range(3):
                row = chunks[pl.ds(i * sz.rows + cell, 1), :]
                rows.append(row[:, :128] if sz.main else jnp.zeros((1, 128), F32))
                piece = jnp.where(lanes < sz.rest, row[:, sz.main : sz.main + 128], 0.0)
                last = last + (pltpu.roll(piece, i * sz.rest, 1) if i else piece)
            rows.append(last)
            for other in range(sz.lanes):
                first = ((d * sz.lanes + other) * sz.group + g) * 4
                for q, row in enumerate(rows):
                    out[pl.ds(first + q, 1), :] = row

    loop(sz.owners, one)


def pick_kernel(sz, *refs):
    inputs, (out, send_out), held, (chunks, sems) = refs[:5], refs[5:7], refs[7:12], refs[12:]
    for copy in fetch(inputs, held, sems):
        copy.wait()
    send, target, source, count, positions = held
    for j in range(send_out.shape[1]):
        send_out[0, j] = send[0, j]
    lane = lax.axis_index("lane")
    for i in range(3):
        for g in range(0, sz.cells, 8):
            value = own_chunk(sz, lane, positions.at[i], pl.ds(g, 8))
            chunks[pl.ds(i * sz.rows + g, 8), :] = value
    spare = jnp.zeros((1, 128 - sz.cap), F32)
    tasks = jnp.where(lane_iota(1) == 3 * sz.rest + 2 * sz.cap, count[0].astype(F32), 0.0)
    for q, row in enumerate((target, source)):
        wide = jnp.concatenate([row[...].astype(F32), spare], axis=1)
        tasks = tasks + pltpu.roll(wide, 3 * sz.rest + q * sz.cap, 1)
    send_ghosts(sz, send, chunks, out, tasks)


def take_ghosts(sz, arrived, pool, stride, base):
    lanes = lane_iota(1)

    def one(d):
        for g in range(sz.group):
            first = [((d * sz.lanes + lane) * sz.group + g) * 4 for lane in range(sz.lanes)]
            last = [arrived[pl.ds(row + 3, 1), :] for row in first]
            for i in range(3):
                tiles = []
                if sz.main:
                    tiles += [arrived[pl.ds(row + i, 1), :] for row in first]
                for tile in range(sz.rest_tiles):
                    total = jnp.zeros((1, 128), F32)
                    for lane in range(sz.lanes):
                        start = sz.rest * lane
                        if start + sz.rest <= 128 * tile or start >= 128 * tile + 128:
                            continue
                        shift = (start - i * sz.rest) % 128
                        value = pltpu.roll(last[lane], shift, 1) if shift else last[lane]
                        at = lanes + 128 * tile
                        total = jnp.where((at >= start) & (at < start + sz.rest), value, total)
                    tiles.append(total)
                place = pl.ds(i * stride + base + d * sz.group + g, 1)
                pool[place, :] = jnp.concatenate(tiles, axis=1)

    loop(sz.owners, one)


def build_list(sz, lists, tasks):
    total = jnp.int32(0)
    for lane in range(sz.lanes):

        def step(j, total, lane=lane):
            tasks[0, total] = lists[lane, j]
            tasks[1, total] = lists[lane, sz.cap + j]
            return total + 1

        total = lax.fori_loop(0, lists[lane, 2 * sz.cap], step, total)
    for u in range(UNROLL):
        tasks[0, total + u] = jnp.int32(sz.cells)
        tasks[1, total + u] = jnp.int32(0)
    tasks[2, 0] = total
    return total


def own_list(sz, lane, tasks, mine):
    first = lane * sz.share

    def step(t, count):
        target = tasks[0, t] - first
        mine[0, count] = target
        mine[1, count] = tasks[1, t]
        return count + ((target >= 0) & (target < sz.share)).astype(jnp.int32)

    total = lax.fori_loop(0, tasks[2, 0], step, jnp.int32(0))
    for u in range(PAIR):
        mine[0, total + u] = jnp.int32(-1)
        mine[1, total + u] = jnp.int32(0)
    return total


def products(value, bend_high, bend_low):
    high, low = split2(value)
    dot = functools.partial(jnp.dot, preferred_element_type=F32)
    return dot(high, bend_high) + dot(low, bend_high) + dot(high, bend_low)


def make_sources(sz, value, bend_high, bend_low, source_rows, centres, first):
    count = value.shape[0] // 3
    forces = products(value[:, : sz.points], bend_high, bend_low)
    forces = jnp.concatenate(
        [forces, jnp.zeros((3 * count, sz.width - sz.points), F32)], axis=1
    )
    middle = jnp.sum(value, axis=1, keepdims=True) / sz.points
    for g in range(count // 8):
        where = [i * count + 8 * g for i in range(3)]
        middles = [jnp.broadcast_to(middle[w : w + 8], (8, 128)) for w in where]
        middles += [jnp.zeros((8, 128), F32)] * 5
        for i, row in enumerate(middles):
            centres[pl.ds(8 * (first + 8 * g) + i, 8, stride=8), :] = row
        for j in range(sz.tiles):
            cut = slice(128 * j, 128 * j + 128)
            y = [value[w : w + 8, cut] - m for w, m in zip(where, middles)]
            f = [forces[w : w + 8, cut] for w in where]
            norm = y[0] * y[0] + y[1] * y[1] + y[2] * y[2] + REGULARIZE
            along = y[0] * f[0] + y[1] * f[1] + y[2] * f[2]
            one, zero = jnp.ones((8, 128), F32), jnp.zeros((8, 128), F32)
            rows = [y[0], y[1], y[2], norm, one, zero, zero, zero]
            rows += f
            rows += [y[i] * f[k] for i in range(3) for k in range(3)]
            rows += [norm * f[i] + along * y[i] for i in range(3)]
            rows += [along]
            for k, row in enumerate(rows):
                place = pl.ds(SOURCE_ROWS * (first + 8 * g) + k, 8, stride=SOURCE_ROWS)
                source_rows.at[j][place, :] = row


def make_targets(sz, blocks, targets):
    targets[...] = jnp.zeros_like(targets)
    for g in range(sz.cells // 8):
        for i in range(3):
            block = blocks(i, g)
            for j in range(targets.shape[0]):
                cut = slice(128 * j, 128 * j + 128)
                targets.at[j][pl.ds(64 * g + i, 8, stride=8), :] = block[:, cut]


def source_operands(sz, source, source_rows):
    held = [
        source_rows[j, pl.ds(pl.multiple_of(SOURCE_ROWS * source, 8), SOURCE_ROWS), :]
        for j in range(sz.tiles)
    ]
    held = jnp.concatenate(held, axis=1)
    y1, y2, y3 = split3(held[:8])
    y_stack = jnp.concatenate([y1, y1, y2, y2, y1, y3], axis=0).astype(BF16)
    return y_stack, jnp.concatenate(split3(held[8:]), axis=0)


def pieces(points, step):
    starts = list(range(0, max(points // 128 * 128, 1), step))
    return list(zip(starts, starts[1:] + [points]))


def twice(piece, count):
    whole = count // 128 * 128
    parts = [piece[:, :whole].astype(BF16)] * 2 if whole else []
    if whole < count:
        last = piece[:, whole:]
        last = last + pltpu.roll(last, count - whole, 1)
        parts.append(last.astype(BF16)[:, : 2 * (count - whole)])
    return jnp.concatenate(parts, axis=1)


def load_target(j, target, slot, centre, targets, offsets):
    row = lax.broadcasted_iota(jnp.int32, (8, 128), 0)
    x = targets[j, pl.ds(pl.multiple_of(8 * target, 8), 8), :] - centre
    square = x * x
    norm = pltpu.roll(square, 2, 0) + pltpu.roll(square, 3, 0) + pltpu.roll(square, 4, 0)
    side = jnp.where(row == 4, norm, jnp.where(row == 3, 1.0, 0.0))
    x_side = jnp.where(row < 3, -2.0 * x, side)
    x1, x2, x3 = split3(x_side)
    return x, jnp.concatenate([x1, x2, x1, x2, x3, x1], axis=0).astype(BF16)


def distances(one_stack, other_stack):
    return jnp.dot(one_stack, other_stack, preferred_element_type=F32)


def weights(shifted):
    inverse = lax.rsqrt(shifted)
    return split2(inverse * inverse * inverse)


def fold(result):
    return result[:SUM_ROWS] + result[SUM_ROWS : 2 * SUM_ROWS] + result[2 * SUM_ROWS :]


def skewed(stages, skew):
    asked = []
    for q, (ask, _) in enumerate(stages):
        asked.append(ask())
        if q >= skew:
            stages[q - skew][1](asked[q - skew])
            asked[q - skew] = None
    for q in range(max(len(stages) - skew, 0), len(stages)):
        stages[q][1](asked[q])


def adder(totals, key):
    def add(value):
        totals[key] = totals[key] + value if key in totals else value

    return add


def wide_piece(targets, y_turned, m_stack, first, end, add):
    def ask():
        return distances(y_turned, targets)

    def take(shifted):
        high, low = weights(shifted)
        whole = (end - first) // 128 * 128
        parts = [high[:whole], low[:whole]] if whole else []
        parts += [high[whole:], low[whole:]] if whole < end - first else []
        stack = jnp.concatenate(parts, axis=0)
        m_piece = twice(m_stack[:, first : up(end, 128)], end - first)
        add(jnp.dot(m_piece, stack, preferred_element_type=F32))

    return ask, take


def rest_piece(targets, y_stack, m_stack, add):
    def ask():
        return distances(targets, y_stack)

    def take(shifted):
        high, low = weights(shifted)
        m_whole = m_stack.astype(BF16)
        turned = (((1,), (1,)), ((), ()))
        result = lax.dot_general(m_whole, high, turned, preferred_element_type=F32)
        add(result + lax.dot_general(m_whole, low, turned, preferred_element_type=F32))

    return ask, take


def store_sums(slots, slot, j, x, result, offsets, sums):
    offsets.at[j][pl.ds(slot, 8, stride=slots), :] = x
    for h in range(0, SUM_ROWS, 8):
        sums.at[j][pl.ds(h * slots + slot, 8, stride=slots), :] = result[h : h + 8]


def mark(slot, target, hot):
    hot[pl.ds(slot, 1), :] = jnp.where(lane_iota(1) == target, 1.0, 0.0)


def combine(sz, slots, first, total, offsets, sums, speeds):
    live = lax.broadcasted_iota(jnp.int32, (8, 128), 0) + first < total
    for j in range(offsets.shape[0]):
        x = [offsets[j, pl.ds(i * slots + first, 8), :] for i in range(3)]
        s = [sums[j, pl.ds(k * slots + first, 8), :] for k in range(SUM_ROWS)]
        a, b, c = s[:3], [s[3:6], s[6:9], s[9:12]], s[12:15]
        norm = x[0] * x[0] + x[1] * x[1] + x[2] * x[2] + REGULARIZE
        along = x[0] * a[0] + x[1] * a[1] + x[2] * a[2] - s[15]
        for i in range(3):
            speed = norm * a[i] + c[i] + along * x[i]
            for k in range(3):
                speed = speed - x[k] * (2.0 * b[k][i] + b[i][k])
            speed = jnp.where(live, speed / sz.points, 0.0)
            speeds[i, pl.ds(first, 8), 128 * j : 128 * j + 128] = speed


def add_up(sz, slots, total, rows, offsets, sums, speeds, hot):
    def eight(q, carry):
        combine(sz, slots, pl.multiple_of(8 * q, 8), total, offsets, sums, speeds)
        return carry

    lax.fori_loop(0, lax.div(total + 7, 8), eight, 0)
    one_hot = hot[...].astype(BF16)
    result = []
    for i in range(3):
        first, second, third = split3(speeds[i])
        parts = [
            lax.dot_general(
                one_hot, part.astype(BF16), (((0,), (0,)), ((), ())), preferred_element_type=F32
            )
            for part in (first, second, third)
        ]
        result.append((parts[0] + parts[1] + parts[2])[:rows])
    return result


def several_tasks(sz, slots, picks, marks, main, rest, wide, step, skew, refs):
    source_rows, centres, targets, offsets, sums, hot = refs
    parts, held, stages = {}, [], []
    for u, (slot, (target, source)) in enumerate(zip(slots, picks)):
        y_stack, m_stack = source_operands(sz, source, source_rows)
        centre = centres[pl.ds(pl.multiple_of(8 * source, 8), 8), :]
        points = [
            load_target(j, target, slot, centre, targets, offsets)
            for j in range(targets.shape[0])
        ]
        held.append(points)
        y_turned = jnp.transpose(y_stack)
        for begin in range(0, main, wide):
            stack = [stack for _, stack in points[begin // 128 : (begin + wide) // 128]]
            stack = jnp.concatenate(stack, axis=1)
            for first, last in pieces(sz.points, step):
                add = adder(parts, (u, begin))
                stages.append(wide_piece(stack, y_turned[first:last], m_stack, first, last, add))
        if rest:
            stack = jnp.transpose(points[main // 128][1])[:rest]
            stages.append(rest_piece(stack, y_stack, m_stack, adder(parts, (u, main))))
    skewed(stages, skew)
    for u, slot in enumerate(slots):
        results = [fold(parts[u, begin]) for begin in range(0, main, wide)]
        if rest:
            result = fold(parts[u, main])
            spare = jnp.zeros((SUM_ROWS, 128 - rest), F32)
            results.append(jnp.concatenate([result, spare], axis=1))
        result = jnp.concatenate(results, axis=1)
        for j in range(targets.shape[0]):
            cut = result[:, 128 * j : 128 * j + 128]
            store_sums(offsets.shape[1] // 8, slot, j, held[u][j][0], cut, offsets, sums)
        mark(slot, marks[u], hot)


def tiles_of_chunk(sz, total, tasks, *refs):
    def several(q, carry):
        slots = [q * UNROLL + u for u in range(UNROLL)]
        picks = [(tasks[0, slot], tasks[1, slot]) for slot in slots]
        marks = [target for target, _ in picks]
        several_tasks(sz, slots, picks, marks, sz.main, sz.rest, 128, 256, 3, refs)
        return carry

    lax.fori_loop(0, lax.div(total + UNROLL - 1, UNROLL), several, 0)


def tiles_of_cells(sz, base, total, mine, *refs):
    main = 256 * (sz.points // 256)

    def several(q, carry):
        slots = [q * PAIR + u for u in range(PAIR)]
        marks = [mine[0, slot] for slot in slots]
        picks = [(jnp.maximum(mark, 0) + base, mine[1, s]) for mark, s in zip(marks, slots)]
        several_tasks(sz, slots, picks, marks, main, sz.points - main, 256, 128, 2, refs)
        return carry

    lax.fori_loop(0, lax.div(total + PAIR - 1, PAIR), several, 0)


def packed(sz, blocks):
    rows = [b[:, : sz.main] for b in blocks] if sz.main else []
    lanes = lane_iota(8)
    for p in range(0, len(blocks), sz.per_pack):
        total = jnp.zeros((8, 128), F32)
        for q, block in enumerate(blocks[p : p + sz.per_pack]):
            rest = jnp.where(lanes < sz.rest, block[:, sz.main : sz.main + 128], 0.0)
            total = total + (pltpu.roll(rest, q * sz.rest, 1) if q else rest)
        rows.append(total)
    return rows


def store_packed(sz, out, blocks):
    first = 0
    count = len(blocks)
    values = packed(sz, blocks)
    if sz.main:
        for b in range(count):
            for m in range(sz.main // 128):
                out[pl.ds(first, 8), :] = values[b][:, 128 * m : 128 * m + 128]
                first += 8
        values = values[count:]
    for value in values:
        out[pl.ds(first, 8), :] = value
        first += 8


def place_packed(sz, lane, arrived, count, store_main, add_rest):
    first = 0
    if sz.main:
        for b in range(count):
            for m in range(sz.main // 128):
                store_main(b, m, arrived[pl.ds(first, 8), :])
                first += 8
    start = sz.rest * lane
    lanes = lane_iota(8)
    for b in range(count):
        pack, q = divmod(b, sz.per_pack)
        value = arrived[pl.ds(first + 8 * pack, 8), :]
        value = pltpu.roll(value, lax.rem(start - q * sz.rest + 128, 128), 1)
        for tile in range(sz.rest_tiles):
            inside = (lanes + 128 * tile >= start) & (lanes + 128 * tile < start + sz.rest)
            add_rest(b, tile, jnp.where(inside, value, 0.0))


def source_kernel(sz, *refs):
    inputs, (high_out, low_out, source_rows, centres), held, sems = (
        refs[:2],
        refs[2:6],
        refs[6:8],
        refs[8],
    )
    for copy in fetch(inputs, held, sems):
        copy.wait()
    positions, bend = held
    high_out[...], low_out[...] = split2(bend[...])
    value = jnp.concatenate([positions[i] for i in range(3)], axis=0)
    value = jnp.concatenate(
        [value, jnp.zeros((3 * sz.cells, sz.width - sz.points), F32)], axis=1
    )
    make_sources(sz, value, high_out[...], low_out[...], source_rows, centres, 0)


def first_kernel(sz, *refs):
    inputs, (chunk_out, ghost_out, tasks), refs = refs[:7], refs[7:10], refs[10:]
    source_rows, centres, targets, offsets, sums, speeds, hot, moved, pool = refs[:9]
    send, positions, arrived, high, low, staged, lists, sems = refs[9:]
    me, lane = lax.axis_index("space"), lax.axis_index("lane")
    own_rows = source_rows.at[:, pl.ds(0, SOURCE_ROWS * sz.cells)]
    own_centres = centres.at[pl.ds(0, 8 * sz.cells)]
    held = [arrived, send, positions, high, low, own_rows, own_centres]
    copies = fetch(inputs, held, sems)
    copies[0].wait()
    for other in range(sz.lanes):
        row = ((me * sz.lanes + other) * sz.group) * 4 + 3
        value = pltpu.roll(arrived[pl.ds(row, 1), :], 128 - 3 * sz.rest, 1)
        staged[pl.ds(other, 1), :] = value.astype(jnp.int32)
    copies.append(pltpu.make_async_copy(staged, lists, sems.at[7]))
    copies[7].start()
    pool[...] = jnp.zeros_like(pool)
    take_ghosts(sz, arrived, pool, up(sz.owners * sz.group, 8), 0)
    hot[...] = jnp.zeros_like(hot)
    speeds[...] = jnp.zeros_like(speeds)
    for copy in copies[1:5]:
        copy.wait()
    make_sources(sz, pool[...], high[...], low[...], source_rows, centres, sz.cells)
    make_targets(
        sz, lambda i, g: own_chunk(sz, lane, positions.at[i], pl.ds(8 * g, 8)), targets
    )
    for copy in copies[5:]:
        copy.wait()
    total = build_list(sz, lists, tasks)
    tiles_of_chunk(sz, total, tasks, source_rows, centres, targets, offsets, sums, hot)
    velocity = add_up(sz, sz.slots, total, sz.cells, offsets, sums, speeds, hot)
    blocks = []
    for i in range(3):
        for g in range(0, sz.cells, 8):
            chunk = own_chunk(sz, lane, positions.at[i], pl.ds(g, 8))
            block = chunk + TIME_STEP * velocity[i][g : g + 8]
            moved[pl.ds(i * sz.rows + g, 8), :] = block
            blocks.append(block)
    rows = chunk_out.shape[0] // sz.lanes
    for other in range(sz.lanes):
        store_packed(sz, chunk_out.at[pl.ds(rows * other, rows)], blocks)
    send_ghosts(sz, send, moved, ghost_out, jnp.zeros((1, 128), F32))


def second_kernel(sz, *refs):
    inputs, (moved_out, velocity_out), refs = refs[:5], refs[5:7], refs[7:]
    source_rows, centres, targets, offsets, sums, speeds, hot, pool, mine = refs[:9]
    held, sems = refs[9:-1], refs[-1]
    copies = fetch(inputs, held, sems)
    tasks, arrived, chunks, high, low = held
    hot[...] = jnp.zeros_like(hot)
    speeds[...] = jnp.zeros_like(speeds)
    lane = lax.axis_index("lane")
    pool[...] = jnp.zeros_like(pool)
    for copy in copies[:-2]:
        copy.wait()
    per = sz.cells // 8
    for k in range(sz.lanes):
        other = jnp.int32(k)

        def row_of(b):
            return (b // per) * sz.pool + 8 * (b % per)

        def store_main(b, m, value):
            cut = pl.ds(pl.multiple_of(other * sz.main + 128 * m, 128), 128)
            pool[pl.ds(row_of(b), 8), cut] = value

        def add_rest(b, tile, value):
            offset = sz.main * sz.lanes + 128 * tile
            cut = (pl.ds(row_of(b), 8), slice(offset, offset + 128))
            pool[cut] = pool[cut] + value

        rows = chunks.shape[0] // sz.lanes
        part = chunks.at[pl.ds(rows * k, rows)]
        place_packed(sz, other, part, 3 * per, store_main, add_rest)
    take_ghosts(sz, arrived, pool, sz.pool, sz.cells)
    total = own_list(sz, lane, tasks, mine)
    for copy in copies[-2:]:
        copy.wait()
    make_sources(sz, pool[...], high[...], low[...], source_rows, centres, 0)
    make_targets(sz, lambda i, g: pool[pl.ds(i * sz.pool + 8 * g, 8), :], targets)
    first = lane * sz.share
    tiles_of_cells(sz, first, total, mine, source_rows, centres, targets, offsets, sums, hot)
    velocity = add_up(sz, sz.own, total, up(sz.share, 8), offsets, sums, speeds, hot)
    for i in range(3):
        speed = velocity[i]
        moved = share_rows(sz, pool, i * sz.pool, lane) + TIME_STEP * speed
        velocity_out[i] = speed[: sz.share, : sz.points]
        moved_out[i] = moved[: sz.share, : sz.points]


def share_rows(sz, ref, base, lane):
    if sz.share % 8 == 0:
        return ref[pl.ds(pl.multiple_of(base + lane * sz.share, 8), sz.share), :]
    rows = [ref[pl.ds(base + lane * sz.share + c, 1), :] for c in range(sz.share)]
    rows.append(jnp.zeros((8 - sz.share, rows[0].shape[1]), F32))
    return jnp.concatenate(rows, axis=0)


def scratch(sz, tiles, slots):
    return [
        pltpu.VMEM((sz.tiles, SOURCE_ROWS * sz.pool, 128), F32),
        pltpu.VMEM((8 * sz.pool, 128), F32),
        pltpu.VMEM((tiles, 8 * sz.rows, 128), F32),
        pltpu.VMEM((tiles, 8 * slots, 128), F32),
        pltpu.VMEM((tiles, SUM_ROWS * slots, 128), F32),
        pltpu.VMEM((3, slots, 128 * tiles), F32),
        pltpu.VMEM((slots, 128), F32),
    ]


def shards(positions, bend_op, send_list, task_target, task_source, task_count):
    owners, lanes = lax.axis_size("space"), lax.axis_size("lane")
    cells, points = positions.shape[0], positions.shape[2]
    sz = sizes(owners, lanes, cells, points, task_target.shape[1], send_list.shape[1])
    params = pltpu.CompilerParams(vmem_limit_bytes=60 << 20)
    shape = jax.ShapeDtypeStruct
    both = ("space", "lane")
    by_component = jnp.transpose(positions, (1, 0, 2))
    list_rows = up(lanes, 8)
    slot_shape = shape((4 * sz.group * owners * lanes, 128), F32)
    leaving, send = pl.pallas_call(
        functools.partial(pick_kernel, sz),
        out_shape=[slot_shape, shape(send_list.shape, jnp.int32)],
        in_specs=[HBM] * 5,
        out_specs=[VMEM, SMEM],
        scratch_shapes=[
            pltpu.SMEM(send_list.shape, jnp.int32),
            pltpu.VMEM(task_target.shape, jnp.int32),
            pltpu.VMEM(task_source.shape, jnp.int32),
            pltpu.SMEM(task_count.shape, jnp.int32),
            pltpu.VMEM(by_component.shape, F32),
            pltpu.VMEM((3 * sz.rows, sz.chunk_wide), F32),
            pltpu.SemaphoreType.DMA((5,)),
        ],
        compiler_params=params,
        name="pick_cells",
    )(send_list, task_target, task_source, task_count, by_component)
    arrived = lax.all_to_all(leaving, both, split_axis=0, concat_axis=0, tiled=True)
    high, low, own_rows, own_centres = pl.pallas_call(
        functools.partial(source_kernel, sz),
        out_shape=[
            shape(bend_op.shape, BF16),
            shape(bend_op.shape, BF16),
            shape((sz.tiles, SOURCE_ROWS * cells, 128), F32),
            shape((8 * cells, 128), F32),
        ],
        in_specs=[HBM] * 2,
        out_specs=[VMEM] * 4,
        scratch_shapes=[
            pltpu.VMEM(by_component.shape, F32),
            pltpu.VMEM(bend_op.shape, F32),
            pltpu.SemaphoreType.DMA((2,)),
        ],
        compiler_params=params,
        cost_estimate=pl.CostEstimate(flops=10**9, bytes_accessed=10**7, transcendentals=0),
        name="first_sources",
    )(by_component, bend_op)
    chunk, leaving, tasks = pl.pallas_call(
        functools.partial(first_kernel, sz),
        out_shape=[
            shape((lanes * pack_rows(sz, cells), 128), F32),
            slot_shape,
            shape((3, sz.slots), jnp.int32),
        ],
        in_specs=[HBM] * 7,
        out_specs=[VMEM, VMEM, SMEM],
        scratch_shapes=scratch(sz, sz.chunk_tiles, sz.slots)
        + [
            pltpu.VMEM((3 * sz.rows, sz.chunk_wide), F32),
            pltpu.VMEM((3 * up(sz.owners * sz.group, 8), sz.width), F32),
            pltpu.SMEM(send_list.shape, jnp.int32),
            pltpu.VMEM(by_component.shape, F32),
            pltpu.VMEM(slot_shape.shape, F32),
            pltpu.VMEM(bend_op.shape, BF16),
            pltpu.VMEM(bend_op.shape, BF16),
            pltpu.VMEM((list_rows, 128), jnp.int32),
            pltpu.SMEM((list_rows, 128), jnp.int32),
            pltpu.SemaphoreType.DMA((8,)),
        ],
        compiler_params=params,
        name="first_step",
    )(arrived, send, by_component, high, low, own_rows, own_centres)
    arrived = lax.all_to_all(leaving, both, split_axis=0, concat_axis=0, tiled=True)
    chunks = lax.all_to_all(chunk, "lane", split_axis=0, concat_axis=0, tiled=True)
    result = shape((3, sz.share, points), F32)
    outputs = pl.pallas_call(
        functools.partial(second_kernel, sz),
        out_shape=[result, result],
        in_specs=[HBM] * 5,
        out_specs=[VMEM] * 2,
        scratch_shapes=scratch(sz, sz.tiles, sz.own)
        + [
            pltpu.VMEM((3 * sz.pool, sz.width), F32),
            pltpu.SMEM((2, sz.own + 8), jnp.int32),
            pltpu.SMEM(tasks.shape, jnp.int32),
            pltpu.VMEM(slot_shape.shape, F32),
        ]
        + [pltpu.VMEM(chunk.shape, F32)]
        + [pltpu.VMEM(bend_op.shape, BF16)] * 2
        + [pltpu.SemaphoreType.DMA((5,))],
        compiler_params=params,
        name="second_step",
    )(tasks, arrived, chunks, high, low)
    return tuple(jnp.transpose(output, (1, 0, 2)) for output in outputs)


def solution(mesh):
    in_specs = (
        P("space", None, None),
        P(),
        P("space", None),
        P(("space", "lane"), None),
        P(("space", "lane"), None),
        P(("space", "lane")),
    )
    out_specs = (P(("space", "lane"), None, None), P(("space", "lane"), None, None))
    return jax.shard_map(shards, mesh=mesh, in_specs=in_specs, out_specs=out_specs, check_vma=False)
```

```python
import functools
from types import SimpleNamespace

import jax
import jax.numpy as jnp
from jax import lax
from jax.experimental import pallas as pl
from jax.experimental.pallas import tpu as pltpu
from jax.sharding import PartitionSpec as P

REGULARIZE = 0.25
TIME_STEP = 0.5
UNROLL = 8
PAIR = 2
SOURCE_ROWS = 24
SUM_ROWS = 16

F32 = jnp.float32
BF16 = jnp.bfloat16
VMEM = pl.BlockSpec(memory_space=pltpu.VMEM)
SMEM = pl.BlockSpec(memory_space=pltpu.SMEM)
HBM = pl.BlockSpec(memory_space=pltpu.HBM)


def up(value, step):
    return -(-value // step) * step


def sizes(owners, lanes, cells, points, cap, listed):
    main = 128 * (points // (128 * lanes))
    rest = (points - main * lanes) // lanes
    group = listed // owners
    pool = up(cells + listed, 8)
    per_pack = 128 // rest
    return SimpleNamespace(
        owners=owners,
        lanes=lanes,
        cells=cells,
        points=points,
        cap=cap,
        group=group,
        width=up(points, 128),
        tiles=up(points, 128) // 128,
        main=main,
        rest=rest,
        rest_tiles=up(rest * lanes, 128) // 128,
        chunk=main + rest,
        chunk_wide=main + up(rest, 128),
        chunk_tiles=(main + up(rest, 128)) // 128,
        per_pack=per_pack,
        pool=pool,
        share=cells // lanes,
        slots=up(lanes * cap + UNROLL, 8),
        rows=cells + 8,
        own=up(lanes * cap + PAIR, 8),
    )


def pack_rows(sz, rows):
    return (3 * rows * sz.main // 128) + 8 * up(3 * rows // 8, sz.per_pack) // sz.per_pack


def split2(value):
    high = value.astype(BF16)
    return high, (value - high.astype(F32)).astype(BF16)


def split3(value):
    first = value.astype(BF16).astype(F32)
    left = value - first
    second = left.astype(BF16).astype(F32)
    return first, second, left - second


def lane_iota(rows):
    return lax.broadcasted_iota(jnp.int32, (rows, 128), 1)


def fetch(sources, targets, sems):
    copies = [
        pltpu.make_async_copy(source, target, sems.at[q])
        for q, (source, target) in enumerate(zip(sources, targets))
    ]
    for copy in copies:
        copy.start()
    return copies


def loop(count, body):
    if count <= 8:
        for q in range(count):
            body(q)
    else:

        def step(q, carry):
            body(q)
            return carry

        lax.fori_loop(0, count, step, 0)


def own_chunk(sz, lane, ref, rows):
    parts = []
    if sz.main:
        parts.append(ref[rows, pl.ds(pl.multiple_of(lane * sz.main, 128), sz.main)])
    start = sz.rest * lane
    lanes = lane_iota(8)
    rest = jnp.zeros((8, 128), F32)
    for tile in range(sz.rest_tiles):
        offset = sz.main * sz.lanes + 128 * tile
        block = ref[rows, offset : min(offset + 128, ref.shape[-1])]
        if block.shape[1] < 128:
            block = jnp.concatenate([block, jnp.zeros((8, 128 - block.shape[1]), F32)], axis=1)
        inside = (lanes + 128 * tile >= start) & (lanes + 128 * tile < start + sz.rest)
        rest = rest + jnp.where(inside, block, 0.0)
    rest = pltpu.roll(rest, lax.rem(128 * sz.rest_tiles - start, 128), 1)
    parts.append(rest)
    return jnp.concatenate(parts, axis=1) if len(parts) > 1 else parts[0]


def send_ghosts(sz, send, chunks, out, tasks):
    lanes = lane_iota(1)

    def one(d):
        for g in range(sz.group):
            cell = send[0, d * sz.group + g]
            rows = []
            last = tasks
            for i in range(3):
                row = chunks[pl.ds(i * sz.rows + cell, 1), :]
                rows.append(row[:, :128] if sz.main else jnp.zeros((1, 128), F32))
                piece = jnp.where(lanes < sz.rest, row[:, sz.main : sz.main + 128], 0.0)
                last = last + (pltpu.roll(piece, i * sz.rest, 1) if i else piece)
            rows.append(last)
            for other in range(sz.lanes):
                first = ((d * sz.lanes + other) * sz.group + g) * 4
                for q, row in enumerate(rows):
                    out[pl.ds(first + q, 1), :] = row

    loop(sz.owners, one)


def pick_kernel(sz, *refs):
    inputs, (out, send_out), held, (chunks, sems) = refs[:5], refs[5:7], refs[7:12], refs[12:]
    for copy in fetch(inputs, held, sems):
        copy.wait()
    send, target, source, count, positions = held
    for j in range(send_out.shape[1]):
        send_out[0, j] = send[0, j]
    lane = lax.axis_index("lane")
    for i in range(3):
        for g in range(0, sz.cells, 8):
            value = own_chunk(sz, lane, positions.at[i], pl.ds(g, 8))
            chunks[pl.ds(i * sz.rows + g, 8), :] = value
    spare = jnp.zeros((1, 128 - sz.cap), F32)
    tasks = jnp.where(lane_iota(1) == 3 * sz.rest + 2 * sz.cap, count[0].astype(F32), 0.0)
    for q, row in enumerate((target, source)):
        wide = jnp.concatenate([row[...].astype(F32), spare], axis=1)
        tasks = tasks + pltpu.roll(wide, 3 * sz.rest + q * sz.cap, 1)
    send_ghosts(sz, send, chunks, out, tasks)


def take_ghosts(sz, arrived, pool, stride, base):
    lanes = lane_iota(1)

    def one(d):
        for g in range(sz.group):
            first = [((d * sz.lanes + lane) * sz.group + g) * 4 for lane in range(sz.lanes)]
            last = [arrived[pl.ds(row + 3, 1), :] for row in first]
            for i in range(3):
                tiles = []
                if sz.main:
                    tiles += [arrived[pl.ds(row + i, 1), :] for row in first]
                for tile in range(sz.rest_tiles):
                    total = jnp.zeros((1, 128), F32)
                    for lane in range(sz.lanes):
                        start = sz.rest * lane
                        if start + sz.rest <= 128 * tile or start >= 128 * tile + 128:
                            continue
                        shift = (start - i * sz.rest) % 128
                        value = pltpu.roll(last[lane], shift, 1) if shift else last[lane]
                        at = lanes + 128 * tile
                        total = jnp.where((at >= start) & (at < start + sz.rest), value, total)
                    tiles.append(total)
                place = pl.ds(i * stride + base + d * sz.group + g, 1)
                pool[place, :] = jnp.concatenate(tiles, axis=1)

    loop(sz.owners, one)


def build_list(sz, lists, tasks):
    total = jnp.int32(0)
    for lane in range(sz.lanes):

        def step(j, total, lane=lane):
            tasks[0, total] = lists[lane, j]
            tasks[1, total] = lists[lane, sz.cap + j]
            return total + 1

        total = lax.fori_loop(0, lists[lane, 2 * sz.cap], step, total)
    for u in range(UNROLL):
        tasks[0, total + u] = jnp.int32(sz.cells)
        tasks[1, total + u] = jnp.int32(0)
    tasks[2, 0] = total
    return total


def own_list(sz, lane, tasks, mine):
    first = lane * sz.share

    def step(t, count):
        target = tasks[0, t] - first
        mine[0, count] = target
        mine[1, count] = tasks[1, t]
        return count + ((target >= 0) & (target < sz.share)).astype(jnp.int32)

    total = lax.fori_loop(0, tasks[2, 0], step, jnp.int32(0))
    for u in range(PAIR):
        mine[0, total + u] = jnp.int32(-1)
        mine[1, total + u] = jnp.int32(0)
    return total


def products(value, bend_high, bend_low):
    high, low = split2(value)
    dot = functools.partial(jnp.dot, preferred_element_type=F32)
    return dot(high, bend_high) + dot(low, bend_high) + dot(high, bend_low)


def make_sources(sz, value, bend_high, bend_low, source_rows, centres, first):
    count = value.shape[0] // 3
    forces = products(value[:, : sz.points], bend_high, bend_low)
    forces = jnp.concatenate(
        [forces, jnp.zeros((3 * count, sz.width - sz.points), F32)], axis=1
    )
    middle = jnp.sum(value, axis=1, keepdims=True) / sz.points
    for g in range(count // 8):
        where = [i * count + 8 * g for i in range(3)]
        middles = [jnp.broadcast_to(middle[w : w + 8], (8, 128)) for w in where]
        middles += [jnp.zeros((8, 128), F32)] * 5
        for i, row in enumerate(middles):
            centres[pl.ds(8 * (first + 8 * g) + i, 8, stride=8), :] = row
        for j in range(sz.tiles):
            cut = slice(128 * j, 128 * j + 128)
            y = [value[w : w + 8, cut] - m for w, m in zip(where, middles)]
            f = [forces[w : w + 8, cut] for w in where]
            norm = y[0] * y[0] + y[1] * y[1] + y[2] * y[2] + REGULARIZE
            along = y[0] * f[0] + y[1] * f[1] + y[2] * f[2]
            one, zero = jnp.ones((8, 128), F32), jnp.zeros((8, 128), F32)
            rows = [y[0], y[1], y[2], norm, one, zero, zero, zero]
            rows += f
            rows += [y[i] * f[k] for i in range(3) for k in range(3)]
            rows += [norm * f[i] + along * y[i] for i in range(3)]
            rows += [along]
            for k, row in enumerate(rows):
                place = pl.ds(SOURCE_ROWS * (first + 8 * g) + k, 8, stride=SOURCE_ROWS)
                source_rows.at[j][place, :] = row


def make_targets(sz, blocks, targets):
    targets[...] = jnp.zeros_like(targets)
    for g in range(sz.cells // 8):
        for i in range(3):
            block = blocks(i, g)
            for j in range(targets.shape[0]):
                cut = slice(128 * j, 128 * j + 128)
                targets.at[j][pl.ds(64 * g + i, 8, stride=8), :] = block[:, cut]


def source_operands(sz, source, source_rows):
    held = [
        source_rows[j, pl.ds(pl.multiple_of(SOURCE_ROWS * source, 8), SOURCE_ROWS), :]
        for j in range(sz.tiles)
    ]
    held = jnp.concatenate(held, axis=1)
    y1, y2, y3 = split3(held[:8])
    y_stack = jnp.concatenate([y1, y1, y2, y2, y1, y3], axis=0).astype(BF16)
    return y_stack, jnp.concatenate(split3(held[8:]), axis=0)


def pieces(points, step):
    starts = list(range(0, max(points // 128 * 128, 1), step))
    return list(zip(starts, starts[1:] + [points]))


def twice(piece, count):
    whole = count // 128 * 128
    parts = [piece[:, :whole].astype(BF16)] * 2 if whole else []
    if whole < count:
        last = piece[:, whole:]
        last = last + pltpu.roll(last, count - whole, 1)
        parts.append(last.astype(BF16)[:, : 2 * (count - whole)])
    return jnp.concatenate(parts, axis=1)


def load_target(j, target, slot, centre, targets, offsets):
    row = lax.broadcasted_iota(jnp.int32, (8, 128), 0)
    x = targets[j, pl.ds(pl.multiple_of(8 * target, 8), 8), :] - centre
    square = x * x
    norm = pltpu.roll(square, 2, 0) + pltpu.roll(square, 3, 0) + pltpu.roll(square, 4, 0)
    side = jnp.where(row == 4, norm, jnp.where(row == 3, 1.0, 0.0))
    x_side = jnp.where(row < 3, -2.0 * x, side)
    x1, x2, x3 = split3(x_side)
    return x, jnp.concatenate([x1, x2, x1, x2, x3, x1], axis=0).astype(BF16)


def distances(one_stack, other_stack):
    return jnp.dot(one_stack, other_stack, preferred_element_type=F32)


def weights(shifted):
    inverse = lax.rsqrt(shifted)
    return split2(inverse * inverse * inverse)


def fold(result):
    return result[:SUM_ROWS] + result[SUM_ROWS : 2 * SUM_ROWS] + result[2 * SUM_ROWS :]


def skewed(stages, skew):
    asked = []
    for q, (ask, _) in enumerate(stages):
        asked.append(ask())
        if q >= skew:
            stages[q - skew][1](asked[q - skew])
            asked[q - skew] = None
    for q in range(max(len(stages) - skew, 0), len(stages)):
        stages[q][1](asked[q])


def adder(totals, key):
    def add(value):
        totals[key] = totals[key] + value if key in totals else value

    return add


def wide_piece(operands, begin, first, end, add):
    def ask():
        _, y_turned, _, blocks = operands()
        return distances(y_turned[first:end], blocks[begin])

    def take(shifted):
        m_stack = operands()[2]
        high, low = weights(shifted)
        whole = (end - first) // 128 * 128
        parts = [high[:whole], low[:whole]] if whole else []
        parts += [high[whole:], low[whole:]] if whole < end - first else []
        stack = jnp.concatenate(parts, axis=0)
        m_piece = twice(m_stack[:, first : up(end, 128)], end - first)
        add(jnp.dot(m_piece, stack, preferred_element_type=F32))

    return ask, take


def rest_piece(operands, begin, add):
    def ask():
        y_stack, _, _, blocks = operands()
        return distances(blocks[begin], y_stack)

    def take(shifted):
        high, low = weights(shifted)
        m_whole = operands()[2].astype(BF16)
        turned = (((1,), (1,)), ((), ()))
        result = lax.dot_general(m_whole, high, turned, preferred_element_type=F32)
        add(result + lax.dot_general(m_whole, low, turned, preferred_element_type=F32))

    return ask, take


def store_sums(slots, slot, j, x, result, offsets, sums):
    offsets.at[j][pl.ds(slot, 8, stride=slots), :] = x
    for h in range(0, SUM_ROWS, 8):
        sums.at[j][pl.ds(h * slots + slot, 8, stride=slots), :] = result[h : h + 8]


def mark(slot, target, hot):
    hot[pl.ds(slot, 1), :] = jnp.where(lane_iota(1) == target, 1.0, 0.0)


def combine(sz, slots, first, total, offsets, sums, speeds):
    live = lax.broadcasted_iota(jnp.int32, (8, 128), 0) + first < total
    for j in range(offsets.shape[0]):
        x = [offsets[j, pl.ds(i * slots + first, 8), :] for i in range(3)]
        s = [sums[j, pl.ds(k * slots + first, 8), :] for k in range(SUM_ROWS)]
        a, b, c = s[:3], [s[3:6], s[6:9], s[9:12]], s[12:15]
        norm = x[0] * x[0] + x[1] * x[1] + x[2] * x[2] + REGULARIZE
        along = x[0] * a[0] + x[1] * a[1] + x[2] * a[2] - s[15]
        for i in range(3):
            speed = norm * a[i] + c[i] + along * x[i]
            for k in range(3):
                speed = speed - x[k] * (2.0 * b[k][i] + b[i][k])
            speed = jnp.where(live, speed / sz.points, 0.0)
            speeds[i, pl.ds(first, 8), 128 * j : 128 * j + 128] = speed


def add_up(sz, slots, total, rows, offsets, sums, speeds, hot):
    def eight(q, carry):
        combine(sz, slots, pl.multiple_of(8 * q, 8), total, offsets, sums, speeds)
        return carry

    lax.fori_loop(0, lax.div(total + 7, 8), eight, 0)
    one_hot = hot[...].astype(BF16)
    result = []
    for i in range(3):
        first, second, third = split3(speeds[i])
        parts = [
            lax.dot_general(
                one_hot, part.astype(BF16), (((0,), (0,)), ((), ())), preferred_element_type=F32
            )
            for part in (first, second, third)
        ]
        result.append((parts[0] + parts[1] + parts[2])[:rows])
    return result


def several_tasks(sz, slots, picks, marks, main, rest, wide, step, skew, refs):
    source_rows, centres, targets, offsets, sums, hot = refs
    stages = []

    def task(slot, pick, target_mark):
        target, source = pick
        made, parts, points = [], {}, []

        def operands():
            if made:
                return made[0]
            y_stack, m_stack = source_operands(sz, source, source_rows)
            centre = centres[pl.ds(pl.multiple_of(8 * source, 8), 8), :]
            points.extend(
                load_target(j, target, slot, centre, targets, offsets)
                for j in range(targets.shape[0])
            )
            blocks = {}
            for begin in range(0, main, wide):
                stack = [stack for _, stack in points[begin // 128 : (begin + wide) // 128]]
                blocks[begin] = jnp.concatenate(stack, axis=1)
            if rest:
                blocks[main] = jnp.transpose(points[main // 128][1])[:rest]
            made.append((y_stack, jnp.transpose(y_stack), m_stack, blocks))
            return made[0]

        def finish():
            results = [fold(parts[begin]) for begin in range(0, main, wide)]
            if rest:
                spare = jnp.zeros((SUM_ROWS, 128 - rest), F32)
                results.append(jnp.concatenate([fold(parts[main]), spare], axis=1))
            result = jnp.concatenate(results, axis=1)
            for j in range(targets.shape[0]):
                cut = result[:, 128 * j : 128 * j + 128]
                store_sums(offsets.shape[1] // 8, slot, j, points[j][0], cut, offsets, sums)
            mark(slot, target_mark, hot)

        own = []
        for begin in range(0, main, wide):
            for first, last in pieces(sz.points, step):
                own.append(wide_piece(operands, begin, first, last, adder(parts, begin)))
        if rest:
            own.insert(len(own) // 2, rest_piece(operands, main, adder(parts, main)))
        ask, take = own[-1]

        def last_take(shifted):
            take(shifted)
            finish()

        own[-1] = (ask, last_take)
        return own

    for slot, pick, target_mark in zip(slots, picks, marks):
        stages += task(slot, pick, target_mark)
    skewed(stages, skew)


def tiles_of_chunk(sz, total, tasks, *refs):
    def several(q, carry):
        slots = [q * UNROLL + u for u in range(UNROLL)]
        picks = [(tasks[0, slot], tasks[1, slot]) for slot in slots]
        marks = [target for target, _ in picks]
        several_tasks(sz, slots, picks, marks, sz.main, sz.rest, 128, 256, 3, refs)
        return carry

    lax.fori_loop(0, lax.div(total + UNROLL - 1, UNROLL), several, 0)


def tiles_of_cells(sz, base, total, mine, *refs):
    main = 256 * (sz.points // 256)

    def several(q, carry):
        slots = [q * PAIR + u for u in range(PAIR)]
        marks = [mine[0, slot] for slot in slots]
        picks = [(jnp.maximum(mark, 0) + base, mine[1, s]) for mark, s in zip(marks, slots)]
        several_tasks(sz, slots, picks, marks, main, sz.points - main, 256, 128, 2, refs)
        return carry

    lax.fori_loop(0, lax.div(total + PAIR - 1, PAIR), several, 0)


def packed(sz, blocks):
    rows = [b[:, : sz.main] for b in blocks] if sz.main else []
    lanes = lane_iota(8)
    for p in range(0, len(blocks), sz.per_pack):
        total = jnp.zeros((8, 128), F32)
        for q, block in enumerate(blocks[p : p + sz.per_pack]):
            rest = jnp.where(lanes < sz.rest, block[:, sz.main : sz.main + 128], 0.0)
            total = total + (pltpu.roll(rest, q * sz.rest, 1) if q else rest)
        rows.append(total)
    return rows


def store_packed(sz, out, blocks):
    first = 0
    count = len(blocks)
    values = packed(sz, blocks)
    if sz.main:
        for b in range(count):
            for m in range(sz.main // 128):
                out[pl.ds(first, 8), :] = values[b][:, 128 * m : 128 * m + 128]
                first += 8
        values = values[count:]
    for value in values:
        out[pl.ds(first, 8), :] = value
        first += 8


def place_packed(sz, lane, arrived, count, store_main, add_rest):
    first = 0
    if sz.main:
        for b in range(count):
            for m in range(sz.main // 128):
                store_main(b, m, arrived[pl.ds(first, 8), :])
                first += 8
    start = sz.rest * lane
    lanes = lane_iota(8)
    for b in range(count):
        pack, q = divmod(b, sz.per_pack)
        value = arrived[pl.ds(first + 8 * pack, 8), :]
        value = pltpu.roll(value, lax.rem(start - q * sz.rest + 128, 128), 1)
        for tile in range(sz.rest_tiles):
            inside = (lanes + 128 * tile >= start) & (lanes + 128 * tile < start + sz.rest)
            add_rest(b, tile, jnp.where(inside, value, 0.0))


def source_kernel(sz, *refs):
    inputs, (high_out, low_out, source_rows, centres), held, sems = (
        refs[:2],
        refs[2:6],
        refs[6:8],
        refs[8],
    )
    for copy in fetch(inputs, held, sems):
        copy.wait()
    positions, bend = held
    high_out[...], low_out[...] = split2(bend[...])
    value = jnp.concatenate([positions[i] for i in range(3)], axis=0)
    value = jnp.concatenate(
        [value, jnp.zeros((3 * sz.cells, sz.width - sz.points), F32)], axis=1
    )
    make_sources(sz, value, high_out[...], low_out[...], source_rows, centres, 0)


def first_kernel(sz, *refs):
    inputs, (chunk_out, ghost_out, tasks), refs = refs[:7], refs[7:10], refs[10:]
    source_rows, centres, targets, offsets, sums, speeds, hot, moved, pool = refs[:9]
    send, positions, arrived, high, low, staged, lists, sems = refs[9:]
    me, lane = lax.axis_index("space"), lax.axis_index("lane")
    own_rows = source_rows.at[:, pl.ds(0, SOURCE_ROWS * sz.cells)]
    own_centres = centres.at[pl.ds(0, 8 * sz.cells)]
    held = [arrived, send, positions, high, low, own_rows, own_centres]
    copies = fetch(inputs, held, sems)
    copies[0].wait()
    for other in range(sz.lanes):
        row = ((me * sz.lanes + other) * sz.group) * 4 + 3
        value = pltpu.roll(arrived[pl.ds(row, 1), :], 128 - 3 * sz.rest, 1)
        staged[pl.ds(other, 1), :] = value.astype(jnp.int32)
    copies.append(pltpu.make_async_copy(staged, lists, sems.at[7]))
    copies[7].start()
    pool[...] = jnp.zeros_like(pool)
    take_ghosts(sz, arrived, pool, up(sz.owners * sz.group, 8), 0)
    hot[...] = jnp.zeros_like(hot)
    speeds[...] = jnp.zeros_like(speeds)
    for copy in copies[1:5]:
        copy.wait()
    make_sources(sz, pool[...], high[...], low[...], source_rows, centres, sz.cells)
    make_targets(
        sz, lambda i, g: own_chunk(sz, lane, positions.at[i], pl.ds(8 * g, 8)), targets
    )
    for copy in copies[5:]:
        copy.wait()
    total = build_list(sz, lists, tasks)
    tiles_of_chunk(sz, total, tasks, source_rows, centres, targets, offsets, sums, hot)
    velocity = add_up(sz, sz.slots, total, sz.cells, offsets, sums, speeds, hot)
    blocks = []
    for i in range(3):
        for g in range(0, sz.cells, 8):
            chunk = own_chunk(sz, lane, positions.at[i], pl.ds(g, 8))
            block = chunk + TIME_STEP * velocity[i][g : g + 8]
            moved[pl.ds(i * sz.rows + g, 8), :] = block
            blocks.append(block)
    store_packed(sz, chunk_out, blocks)
    send_ghosts(sz, send, moved, ghost_out, jnp.zeros((1, 128), F32))


def second_kernel(sz, *refs):
    count = sz.lanes + 4
    inputs, (moved_out, velocity_out), refs = refs[:count], refs[count : count + 2], refs[count + 2 :]
    source_rows, centres, targets, offsets, sums, speeds, hot, pool, mine = refs[:9]
    held, sems = refs[9:-1], refs[-1]
    copies = fetch(inputs, held, sems)
    tasks, arrived, chunks, (high, low) = held[0], held[1], held[2:-2], held[-2:]
    hot[...] = jnp.zeros_like(hot)
    speeds[...] = jnp.zeros_like(speeds)
    lane = lax.axis_index("lane")
    pool[...] = jnp.zeros_like(pool)
    for copy in copies[:-2]:
        copy.wait()
    per = sz.cells // 8
    for k in range(sz.lanes):
        other = lane ^ k

        def row_of(b):
            return (b // per) * sz.pool + 8 * (b % per)

        def store_main(b, m, value):
            cut = pl.ds(pl.multiple_of(other * sz.main + 128 * m, 128), 128)
            pool[pl.ds(row_of(b), 8), cut] = value

        def add_rest(b, tile, value):
            offset = sz.main * sz.lanes + 128 * tile
            cut = (pl.ds(row_of(b), 8), slice(offset, offset + 128))
            pool[cut] = pool[cut] + value

        place_packed(sz, other, chunks[k], 3 * per, store_main, add_rest)
    take_ghosts(sz, arrived, pool, sz.pool, sz.cells)
    total = own_list(sz, lane, tasks, mine)
    for copy in copies[-2:]:
        copy.wait()
    make_sources(sz, pool[...], high[...], low[...], source_rows, centres, 0)
    make_targets(sz, lambda i, g: pool[pl.ds(i * sz.pool + 8 * g, 8), :], targets)
    first = lane * sz.share
    tiles_of_cells(sz, first, total, mine, source_rows, centres, targets, offsets, sums, hot)
    velocity = add_up(sz, sz.own, total, up(sz.share, 8), offsets, sums, speeds, hot)
    for i in range(3):
        speed = velocity[i]
        moved = share_rows(sz, pool, i * sz.pool, lane) + TIME_STEP * speed
        velocity_out[i] = speed[: sz.share, : sz.points]
        moved_out[i] = moved[: sz.share, : sz.points]


def share_rows(sz, ref, base, lane):
    if sz.share % 8 == 0:
        return ref[pl.ds(pl.multiple_of(base + lane * sz.share, 8), sz.share), :]
    rows = [ref[pl.ds(base + lane * sz.share + c, 1), :] for c in range(sz.share)]
    rows.append(jnp.zeros((8 - sz.share, rows[0].shape[1]), F32))
    return jnp.concatenate(rows, axis=0)


def scratch(sz, tiles, slots):
    return [
        pltpu.VMEM((sz.tiles, SOURCE_ROWS * sz.pool, 128), F32),
        pltpu.VMEM((8 * sz.pool, 128), F32),
        pltpu.VMEM((tiles, 8 * sz.rows, 128), F32),
        pltpu.VMEM((tiles, 8 * slots, 128), F32),
        pltpu.VMEM((tiles, SUM_ROWS * slots, 128), F32),
        pltpu.VMEM((3, slots, 128 * tiles), F32),
        pltpu.VMEM((slots, 128), F32),
    ]


def swap(value, axis, size, k):
    return lax.ppermute(value, axis, [(d, d ^ k) for d in range(size)])


def shards(positions, bend_op, send_list, task_target, task_source, task_count):
    owners, lanes = lax.axis_size("space"), lax.axis_size("lane")
    cells, points = positions.shape[0], positions.shape[2]
    sz = sizes(owners, lanes, cells, points, task_target.shape[1], send_list.shape[1])
    params = pltpu.CompilerParams(vmem_limit_bytes=60 << 20)
    shape = jax.ShapeDtypeStruct
    both = ("space", "lane")
    by_component = jnp.transpose(positions, (1, 0, 2))
    list_rows = up(lanes, 8)
    slot_shape = shape((4 * sz.group * owners * lanes, 128), F32)
    leaving, send = pl.pallas_call(
        functools.partial(pick_kernel, sz),
        out_shape=[slot_shape, shape(send_list.shape, jnp.int32)],
        in_specs=[HBM] * 5,
        out_specs=[VMEM, SMEM],
        scratch_shapes=[
            pltpu.SMEM(send_list.shape, jnp.int32),
            pltpu.VMEM(task_target.shape, jnp.int32),
            pltpu.VMEM(task_source.shape, jnp.int32),
            pltpu.SMEM(task_count.shape, jnp.int32),
            pltpu.VMEM(by_component.shape, F32),
            pltpu.VMEM((3 * sz.rows, sz.chunk_wide), F32),
            pltpu.SemaphoreType.DMA((5,)),
        ],
        compiler_params=params,
        name="pick_cells",
    )(send_list, task_target, task_source, task_count, by_component)
    arrived = lax.all_to_all(leaving, both, split_axis=0, concat_axis=0, tiled=True)
    high, low, own_rows, own_centres = pl.pallas_call(
        functools.partial(source_kernel, sz),
        out_shape=[
            shape(bend_op.shape, BF16),
            shape(bend_op.shape, BF16),
            shape((sz.tiles, SOURCE_ROWS * cells, 128), F32),
            shape((8 * cells, 128), F32),
        ],
        in_specs=[HBM] * 2,
        out_specs=[VMEM] * 4,
        scratch_shapes=[
            pltpu.VMEM(by_component.shape, F32),
            pltpu.VMEM(bend_op.shape, F32),
            pltpu.SemaphoreType.DMA((2,)),
        ],
        compiler_params=params,
        cost_estimate=pl.CostEstimate(flops=10**9, bytes_accessed=10**7, transcendentals=0),
        name="first_sources",
    )(by_component, bend_op)
    chunk, leaving, tasks = pl.pallas_call(
        functools.partial(first_kernel, sz),
        out_shape=[
            shape((pack_rows(sz, cells), 128), F32),
            slot_shape,
            shape((3, sz.slots), jnp.int32),
        ],
        in_specs=[HBM] * 7,
        out_specs=[VMEM, VMEM, SMEM],
        scratch_shapes=scratch(sz, sz.chunk_tiles, sz.slots)
        + [
            pltpu.VMEM((3 * sz.rows, sz.chunk_wide), F32),
            pltpu.VMEM((3 * up(sz.owners * sz.group, 8), sz.width), F32),
            pltpu.SMEM(send_list.shape, jnp.int32),
            pltpu.VMEM(by_component.shape, F32),
            pltpu.VMEM(slot_shape.shape, F32),
            pltpu.VMEM(bend_op.shape, BF16),
            pltpu.VMEM(bend_op.shape, BF16),
            pltpu.VMEM((list_rows, 128), jnp.int32),
            pltpu.SMEM((list_rows, 128), jnp.int32),
            pltpu.SemaphoreType.DMA((8,)),
        ],
        compiler_params=params,
        name="first_step",
    )(arrived, send, by_component, high, low, own_rows, own_centres)
    arrived = lax.all_to_all(leaving, both, split_axis=0, concat_axis=0, tiled=True)
    chunks = [chunk] + [swap(chunk, "lane", lanes, k) for k in range(1, lanes)]
    result = shape((3, sz.share, points), F32)
    outputs = pl.pallas_call(
        functools.partial(second_kernel, sz),
        out_shape=[result, result],
        in_specs=[HBM] * (lanes + 4),
        out_specs=[VMEM] * 2,
        scratch_shapes=scratch(sz, sz.tiles, sz.own)
        + [
            pltpu.VMEM((3 * sz.pool, sz.width), F32),
            pltpu.SMEM((2, sz.own + 8), jnp.int32),
            pltpu.SMEM(tasks.shape, jnp.int32),
            pltpu.VMEM(slot_shape.shape, F32),
        ]
        + [pltpu.VMEM(chunk.shape, F32)] * lanes
        + [pltpu.VMEM(bend_op.shape, BF16)] * 2
        + [pltpu.SemaphoreType.DMA((lanes + 4,))],
        compiler_params=params,
        name="second_step",
    )(tasks, arrived, *chunks, high, low)
    return tuple(jnp.transpose(output, (1, 0, 2)) for output in outputs)


def solution(mesh):
    in_specs = (
        P("space", None, None),
        P(),
        P("space", None),
        P(("space", "lane"), None),
        P(("space", "lane"), None),
        P(("space", "lane")),
    )
    out_specs = (P(("space", "lane"), None, None), P(("space", "lane"), None, None))
    return jax.shard_map(shards, mesh=mesh, in_specs=in_specs, out_specs=out_specs, check_vma=False)
```

```python
import functools
from types import SimpleNamespace

import jax
import jax.numpy as jnp
from jax import lax
from jax.experimental import pallas as pl
from jax.experimental.pallas import tpu as pltpu
from jax.sharding import PartitionSpec as P

REGULARIZE = 0.25
TIME_STEP = 0.5
UNROLL = 8
PAIR = 2
SOURCE_ROWS = 24
SUM_ROWS = 16

F32 = jnp.float32
BF16 = jnp.bfloat16
VMEM = pl.BlockSpec(memory_space=pltpu.VMEM)
SMEM = pl.BlockSpec(memory_space=pltpu.SMEM)
HBM = pl.BlockSpec(memory_space=pltpu.HBM)


def up(value, step):
    return -(-value // step) * step


def sizes(owners, lanes, cells, points, cap, listed):
    main = 128 * (points // (128 * lanes))
    rest = (points - main * lanes) // lanes
    group = listed // owners
    pool = up(cells + listed, 8)
    per_pack = 128 // rest
    return SimpleNamespace(
        owners=owners,
        lanes=lanes,
        cells=cells,
        points=points,
        cap=cap,
        group=group,
        width=up(points, 128),
        tiles=up(points, 128) // 128,
        main=main,
        rest=rest,
        rest_tiles=up(rest * lanes, 128) // 128,
        chunk=main + rest,
        chunk_wide=main + up(rest, 128),
        chunk_tiles=(main + up(rest, 128)) // 128,
        per_pack=per_pack,
        pool=pool,
        share=cells // lanes,
        slots=up(lanes * cap + UNROLL, 8),
        rows=cells + 8,
        own=up(lanes * cap + PAIR, 8),
    )


def pack_rows(sz, rows):
    return (3 * rows * sz.main // 128) + 8 * up(3 * rows // 8, sz.per_pack) // sz.per_pack


def split2(value):
    high = value.astype(BF16)
    return high, (value - high.astype(F32)).astype(BF16)


def split3(value):
    first = value.astype(BF16).astype(F32)
    left = value - first
    second = left.astype(BF16).astype(F32)
    return first, second, left - second


def lane_iota(rows):
    return lax.broadcasted_iota(jnp.int32, (rows, 128), 1)


def fetch(sources, targets, sems):
    copies = [
        pltpu.make_async_copy(source, target, sems.at[q])
        for q, (source, target) in enumerate(zip(sources, targets))
    ]
    for copy in copies:
        copy.start()
    return copies


def loop(count, body):
    if count <= 8:
        for q in range(count):
            body(q)
    else:

        def step(q, carry):
            body(q)
            return carry

        lax.fori_loop(0, count, step, 0)


def own_chunk(sz, lane, ref, rows):
    parts = []
    if sz.main:
        parts.append(ref[rows, pl.ds(pl.multiple_of(lane * sz.main, 128), sz.main)])
    start = sz.rest * lane
    lanes = lane_iota(8)
    rest = jnp.zeros((8, 128), F32)
    for tile in range(sz.rest_tiles):
        offset = sz.main * sz.lanes + 128 * tile
        block = ref[rows, offset : min(offset + 128, ref.shape[-1])]
        if block.shape[1] < 128:
            block = jnp.concatenate([block, jnp.zeros((8, 128 - block.shape[1]), F32)], axis=1)
        inside = (lanes + 128 * tile >= start) & (lanes + 128 * tile < start + sz.rest)
        rest = rest + jnp.where(inside, block, 0.0)
    rest = pltpu.roll(rest, lax.rem(128 * sz.rest_tiles - start, 128), 1)
    parts.append(rest)
    return jnp.concatenate(parts, axis=1) if len(parts) > 1 else parts[0]


def send_ghosts(sz, send, chunks, out, tasks):
    lanes = lane_iota(1)

    def one(d):
        for g in range(sz.group):
            cell = send[0, d * sz.group + g]
            rows = []
            last = tasks
            for i in range(3):
                row = chunks[pl.ds(i * sz.rows + cell, 1), :]
                rows.append(row[:, :128] if sz.main else jnp.zeros((1, 128), F32))
                piece = jnp.where(lanes < sz.rest, row[:, sz.main : sz.main + 128], 0.0)
                last = last + (pltpu.roll(piece, i * sz.rest, 1) if i else piece)
            rows.append(last)
            for other in range(sz.lanes):
                first = ((d * sz.lanes + other) * sz.group + g) * 4
                for q, row in enumerate(rows):
                    out[pl.ds(first + q, 1), :] = row

    loop(sz.owners, one)


def pick_kernel(sz, *refs):
    inputs, (out, send_out), held, (chunks, sems) = refs[:5], refs[5:7], refs[7:12], refs[12:]
    for copy in fetch(inputs, held, sems):
        copy.wait()
    send, target, source, count, positions = held
    for j in range(send_out.shape[1]):
        send_out[0, j] = send[0, j]
    lane = lax.axis_index("lane")
    for i in range(3):
        for g in range(0, sz.cells, 8):
            value = own_chunk(sz, lane, positions.at[i], pl.ds(g, 8))
            chunks[pl.ds(i * sz.rows + g, 8), :] = value
    spare = jnp.zeros((1, 128 - sz.cap), F32)
    tasks = jnp.where(lane_iota(1) == 3 * sz.rest + 2 * sz.cap, count[0].astype(F32), 0.0)
    for q, row in enumerate((target, source)):
        wide = jnp.concatenate([row[...].astype(F32), spare], axis=1)
        tasks = tasks + pltpu.roll(wide, 3 * sz.rest + q * sz.cap, 1)
    send_ghosts(sz, send, chunks, out, tasks)


def take_ghosts(sz, arrived, pool, stride, base):
    lanes = lane_iota(1)

    def one(d):
        for g in range(sz.group):
            first = [((d * sz.lanes + lane) * sz.group + g) * 4 for lane in range(sz.lanes)]
            last = [arrived[pl.ds(row + 3, 1), :] for row in first]
            for i in range(3):
                tiles = []
                if sz.main:
                    tiles += [arrived[pl.ds(row + i, 1), :] for row in first]
                for tile in range(sz.rest_tiles):
                    total = jnp.zeros((1, 128), F32)
                    for lane in range(sz.lanes):
                        start = sz.rest * lane
                        if start + sz.rest <= 128 * tile or start >= 128 * tile + 128:
                            continue
                        shift = (start - i * sz.rest) % 128
                        value = pltpu.roll(last[lane], shift, 1) if shift else last[lane]
                        at = lanes + 128 * tile
                        total = jnp.where((at >= start) & (at < start + sz.rest), value, total)
                    tiles.append(total)
                place = pl.ds(i * stride + base + d * sz.group + g, 1)
                pool[place, :] = jnp.concatenate(tiles, axis=1)

    loop(sz.owners, one)


def build_list(sz, lists, tasks):
    total = jnp.int32(0)
    for lane in range(sz.lanes):
        count = lists[lane, 2 * sz.cap]
        for j in range(sz.cap):
            tasks[0, total] = lists[lane, j]
            tasks[1, total] = lists[lane, sz.cap + j]
            total = total + (j < count).astype(jnp.int32)
    for u in range(UNROLL):
        tasks[0, total + u] = jnp.int32(sz.cells)
        tasks[1, total + u] = jnp.int32(0)
    tasks[2, 0] = total
    return total


def own_list(sz, lane, tasks, mine):
    first = lane * sz.share
    total = tasks[2, 0]
    count = jnp.int32(0)
    for t in range(sz.lanes * sz.cap):
        target = tasks[0, t] - first
        mine[0, count] = target
        mine[1, count] = tasks[1, t]
        taken = (target >= 0) & (target < sz.share) & (t < total)
        count = count + taken.astype(jnp.int32)
    for u in range(PAIR):
        mine[0, count + u] = jnp.int32(-1)
        mine[1, count + u] = jnp.int32(0)
    return count


def products(value, bend_high, bend_low):
    high, low = split2(value)
    dot = functools.partial(jnp.dot, preferred_element_type=F32)
    return dot(high, bend_high) + dot(low, bend_high) + dot(high, bend_low)


def make_sources(sz, value, bend_high, bend_low, source_rows, centres, first):
    count = value.shape[0] // 3
    forces = products(value[:, : sz.points], bend_high, bend_low)
    forces = jnp.concatenate(
        [forces, jnp.zeros((3 * count, sz.width - sz.points), F32)], axis=1
    )
    middle = jnp.sum(value, axis=1, keepdims=True) / sz.points
    for g in range(count // 8):
        where = [i * count + 8 * g for i in range(3)]
        middles = [jnp.broadcast_to(middle[w : w + 8], (8, 128)) for w in where]
        middles += [jnp.zeros((8, 128), F32)] * 5
        for i, row in enumerate(middles):
            centres[pl.ds(8 * (first + 8 * g) + i, 8, stride=8), :] = row
        for j in range(sz.tiles):
            cut = slice(128 * j, 128 * j + 128)
            y = [value[w : w + 8, cut] - m for w, m in zip(where, middles)]
            f = [forces[w : w + 8, cut] for w in where]
            norm = y[0] * y[0] + y[1] * y[1] + y[2] * y[2] + REGULARIZE
            along = y[0] * f[0] + y[1] * f[1] + y[2] * f[2]
            one, zero = jnp.ones((8, 128), F32), jnp.zeros((8, 128), F32)
            rows = [y[0], y[1], y[2], norm, one, zero, zero, zero]
            rows += f
            rows += [y[i] * f[k] for i in range(3) for k in range(3)]
            rows += [norm * f[i] + along * y[i] for i in range(3)]
            rows += [along]
            for k, row in enumerate(rows):
                place = pl.ds(SOURCE_ROWS * (first + 8 * g) + k, 8, stride=SOURCE_ROWS)
                source_rows.at[j][place, :] = row


def make_targets(sz, blocks, targets):
    targets[...] = jnp.zeros_like(targets)
    for g in range(sz.cells // 8):
        for i in range(3):
            block = blocks(i, g)
            for j in range(targets.shape[0]):
                cut = slice(128 * j, 128 * j + 128)
                targets.at[j][pl.ds(64 * g + i, 8, stride=8), :] = block[:, cut]


def source_operands(sz, source, source_rows):
    held = [
        source_rows[j, pl.ds(pl.multiple_of(SOURCE_ROWS * source, 8), SOURCE_ROWS), :]
        for j in range(sz.tiles)
    ]
    held = jnp.concatenate(held, axis=1)
    y1, y2, y3 = split3(held[:8])
    y_stack = jnp.concatenate([y1, y1, y2, y2, y1, y3], axis=0).astype(BF16)
    return y_stack, jnp.concatenate(split3(held[8:]), axis=0)


def pieces(points, step):
    starts = list(range(0, max(points // 128 * 128, 1), step))
    return list(zip(starts, starts[1:] + [points]))


def twice(piece, count):
    whole = count // 128 * 128
    parts = [piece[:, :whole].astype(BF16)] * 2 if whole else []
    if whole < count:
        last = piece[:, whole:]
        last = last + pltpu.roll(last, count - whole, 1)
        parts.append(last.astype(BF16)[:, : 2 * (count - whole)])
    return jnp.concatenate(parts, axis=1)


def load_target(j, target, slot, centre, targets, offsets):
    row = lax.broadcasted_iota(jnp.int32, (8, 128), 0)
    x = targets[j, pl.ds(pl.multiple_of(8 * target, 8), 8), :] - centre
    square = x * x
    norm = pltpu.roll(square, 2, 0) + pltpu.roll(square, 3, 0) + pltpu.roll(square, 4, 0)
    side = jnp.where(row == 4, norm, jnp.where(row == 3, 1.0, 0.0))
    x_side = jnp.where(row < 3, -2.0 * x, side)
    x1, x2, x3 = split3(x_side)
    return x, jnp.concatenate([x1, x2, x1, x2, x3, x1], axis=0).astype(BF16)


def distances(one_stack, other_stack):
    return jnp.dot(one_stack, other_stack, preferred_element_type=F32)


def weights(shifted):
    inverse = lax.rsqrt(shifted)
    return split2(inverse * inverse * inverse)


def fold(result):
    return result[:SUM_ROWS] + result[SUM_ROWS : 2 * SUM_ROWS] + result[2 * SUM_ROWS :]


def skewed(stages, skew):
    asked = []
    for q, (ask, _) in enumerate(stages):
        asked.append(ask())
        if q >= skew:
            stages[q - skew][1](asked[q - skew])
            asked[q - skew] = None
    for q in range(max(len(stages) - skew, 0), len(stages)):
        stages[q][1](asked[q])


def adder(totals, key):
    def add(value):
        totals[key] = totals[key] + value if key in totals else value

    return add


def wide_piece(operands, begin, first, end, add):
    def ask():
        _, y_turned, _, blocks = operands()
        return distances(y_turned[first:end], blocks[begin])

    def take(shifted):
        m_stack = operands()[2]
        high, low = weights(shifted)
        whole = (end - first) // 128 * 128
        parts = [high[:whole], low[:whole]] if whole else []
        parts += [high[whole:], low[whole:]] if whole < end - first else []
        stack = jnp.concatenate(parts, axis=0)
        m_piece = twice(m_stack[:, first : up(end, 128)], end - first)
        add(jnp.dot(m_piece, stack, preferred_element_type=F32))

    return ask, take


def rest_piece(operands, begin, add):
    def ask():
        y_stack, _, _, blocks = operands()
        return distances(blocks[begin], y_stack)

    def take(shifted):
        high, low = weights(shifted)
        m_whole = operands()[2].astype(BF16)
        turned = (((1,), (1,)), ((), ()))
        result = lax.dot_general(m_whole, high, turned, preferred_element_type=F32)
        add(result + lax.dot_general(m_whole, low, turned, preferred_element_type=F32))

    return ask, take


def store_sums(slots, slot, j, x, result, offsets, sums):
    offsets.at[j][pl.ds(slot, 8, stride=slots), :] = x
    for h in range(0, SUM_ROWS, 8):
        sums.at[j][pl.ds(h * slots + slot, 8, stride=slots), :] = result[h : h + 8]


def mark(slot, target, hot):
    hot[pl.ds(slot, 1), :] = jnp.where(lane_iota(1) == target, 1.0, 0.0)


def combine(sz, slots, first, total, offsets, sums, speeds):
    live = lax.broadcasted_iota(jnp.int32, (8, 128), 0) + first < total
    for j in range(offsets.shape[0]):
        x = [offsets[j, pl.ds(i * slots + first, 8), :] for i in range(3)]
        s = [sums[j, pl.ds(k * slots + first, 8), :] for k in range(SUM_ROWS)]
        a, b, c = s[:3], [s[3:6], s[6:9], s[9:12]], s[12:15]
        norm = x[0] * x[0] + x[1] * x[1] + x[2] * x[2] + REGULARIZE
        along = x[0] * a[0] + x[1] * a[1] + x[2] * a[2] - s[15]
        for i in range(3):
            speed = norm * a[i] + c[i] + along * x[i]
            for k in range(3):
                speed = speed - x[k] * (2.0 * b[k][i] + b[i][k])
            speed = jnp.where(live, speed / sz.points, 0.0)
            speeds[i, pl.ds(first, 8), 128 * j : 128 * j + 128] = speed


def add_up(sz, slots, total, rows, offsets, sums, speeds, hot):
    def eight(q, carry):
        combine(sz, slots, pl.multiple_of(8 * q, 8), total, offsets, sums, speeds)
        return carry

    lax.fori_loop(0, lax.div(total + 7, 8), eight, 0)
    one_hot = hot[...].astype(BF16)
    result = []
    for i in range(3):
        first, second, third = split3(speeds[i])
        parts = [
            lax.dot_general(
                one_hot, part.astype(BF16), (((0,), (0,)), ((), ())), preferred_element_type=F32
            )
            for part in (first, second, third)
        ]
        result.append((parts[0] + parts[1] + parts[2])[:rows])
    return result


def several_tasks(sz, slots, picks, marks, main, rest, wide, step, skew, refs):
    source_rows, centres, targets, offsets, sums, hot = refs

    def task(slot, pick, target_mark):
        target, source = pick
        made, parts, points = [], {}, []

        def operands():
            if made:
                return made[0]
            y_stack, m_stack = source_operands(sz, source, source_rows)
            centre = centres[pl.ds(pl.multiple_of(8 * source, 8), 8), :]
            points.extend(
                load_target(j, target, slot, centre, targets, offsets)
                for j in range(targets.shape[0])
            )
            blocks = {}
            for begin in range(0, main, wide):
                stack = [stack for _, stack in points[begin // 128 : (begin + wide) // 128]]
                blocks[begin] = jnp.concatenate(stack, axis=1)
            if rest:
                blocks[main] = jnp.transpose(points[main // 128][1])[:rest]
            made.append((y_stack, jnp.transpose(y_stack), m_stack, blocks))
            return made[0]

        def finish():
            results = [fold(parts[begin]) for begin in range(0, main, wide)]
            if rest:
                spare = jnp.zeros((SUM_ROWS, 128 - rest), F32)
                results.append(jnp.concatenate([fold(parts[main]), spare], axis=1))
            result = jnp.concatenate(results, axis=1)
            for j in range(targets.shape[0]):
                cut = result[:, 128 * j : 128 * j + 128]
                store_sums(offsets.shape[1] // 8, slot, j, points[j][0], cut, offsets, sums)
            mark(slot, target_mark, hot)

        own = []
        for begin in range(0, main, wide):
            for first, last in pieces(sz.points, step):
                own.append(wide_piece(operands, begin, first, last, adder(parts, begin)))
        if rest:
            own.insert(len(own) // 2, rest_piece(operands, main, adder(parts, main)))
        ask, take = own[-1]

        def last_take(shifted):
            take(shifted)
            finish()

        own[-1] = (ask, last_take)
        return own, operands

    made = [task(slot, pick, m) for slot, pick, m in zip(slots, picks, marks)]
    for (own, _), (_, after) in zip(made, made[1:]):
        ask, take = own[0]

        def ask_and_prepare(ask=ask, after=after):
            shifted = ask()
            after()
            return shifted

        own[0] = (ask_and_prepare, take)
    skewed([stage for own, _ in made for stage in own], skew)


def tiles_of_chunk(sz, total, tasks, *refs):
    def several(q, carry):
        slots = [q * UNROLL + u for u in range(UNROLL)]
        picks = [(tasks[0, slot], tasks[1, slot]) for slot in slots]
        marks = [target for target, _ in picks]
        several_tasks(sz, slots, picks, marks, sz.main, sz.rest, 128, 256, 4, refs)
        return carry

    lax.fori_loop(0, lax.div(total + UNROLL - 1, UNROLL), several, 0)


def tiles_of_cells(sz, base, total, mine, *refs):
    main = 256 * (sz.points // 256)

    def several(q, carry):
        slots = [q * PAIR + u for u in range(PAIR)]
        marks = [mine[0, slot] for slot in slots]
        picks = [(jnp.maximum(mark, 0) + base, mine[1, s]) for mark, s in zip(marks, slots)]
        several_tasks(sz, slots, picks, marks, main, sz.points - main, 256, 128, 3, refs)
        return carry

    lax.fori_loop(0, lax.div(total + PAIR - 1, PAIR), several, 0)


def packed(sz, blocks):
    rows = [b[:, : sz.main] for b in blocks] if sz.main else []
    lanes = lane_iota(8)
    for p in range(0, len(blocks), sz.per_pack):
        total = jnp.zeros((8, 128), F32)
        for q, block in enumerate(blocks[p : p + sz.per_pack]):
            rest = jnp.where(lanes < sz.rest, block[:, sz.main : sz.main + 128], 0.0)
            total = total + (pltpu.roll(rest, q * sz.rest, 1) if q else rest)
        rows.append(total)
    return rows


def store_packed(sz, out, blocks):
    first = 0
    count = len(blocks)
    values = packed(sz, blocks)
    if sz.main:
        for b in range(count):
            for m in range(sz.main // 128):
                out[pl.ds(first, 8), :] = values[b][:, 128 * m : 128 * m + 128]
                first += 8
        values = values[count:]
    for value in values:
        out[pl.ds(first, 8), :] = value
        first += 8


def place_packed(sz, lane, arrived, count, store_main, add_rest):
    first = 0
    if sz.main:
        for b in range(count):
            for m in range(sz.main // 128):
                store_main(b, m, arrived[pl.ds(first, 8), :])
                first += 8
    start = sz.rest * lane
    lanes = lane_iota(8)
    for b in range(count):
        pack, q = divmod(b, sz.per_pack)
        value = arrived[pl.ds(first + 8 * pack, 8), :]
        value = pltpu.roll(value, lax.rem(start - q * sz.rest + 128, 128), 1)
        for tile in range(sz.rest_tiles):
            inside = (lanes + 128 * tile >= start) & (lanes + 128 * tile < start + sz.rest)
            add_rest(b, tile, jnp.where(inside, value, 0.0))


def source_kernel(sz, *refs):
    inputs, (high_out, low_out, source_rows, centres), held, sems = (
        refs[:2],
        refs[2:6],
        refs[6:8],
        refs[8],
    )
    for copy in fetch(inputs, held, sems):
        copy.wait()
    positions, bend = held
    high_out[...], low_out[...] = split2(bend[...])
    value = jnp.concatenate([positions[i] for i in range(3)], axis=0)
    value = jnp.concatenate(
        [value, jnp.zeros((3 * sz.cells, sz.width - sz.points), F32)], axis=1
    )
    make_sources(sz, value, high_out[...], low_out[...], source_rows, centres, 0)


def first_kernel(sz, *refs):
    inputs, (chunk_out, ghost_out, tasks), refs = refs[:7], refs[7:10], refs[10:]
    source_rows, centres, targets, offsets, sums, speeds, hot, moved, pool = refs[:9]
    send, positions, arrived, high, low, staged, lists, sems = refs[9:]
    me, lane = lax.axis_index("space"), lax.axis_index("lane")
    own_rows = source_rows.at[:, pl.ds(0, SOURCE_ROWS * sz.cells)]
    own_centres = centres.at[pl.ds(0, 8 * sz.cells)]
    held = [arrived, send, positions, high, low, own_rows, own_centres]
    copies = fetch(inputs, held, sems)
    copies[0].wait()
    for other in range(sz.lanes):
        row = ((me * sz.lanes + other) * sz.group) * 4 + 3
        value = pltpu.roll(arrived[pl.ds(row, 1), :], 128 - 3 * sz.rest, 1)
        staged[pl.ds(other, 1), :] = value.astype(jnp.int32)
    copies.append(pltpu.make_async_copy(staged, lists, sems.at[7]))
    copies[7].start()
    pool[...] = jnp.zeros_like(pool)
    take_ghosts(sz, arrived, pool, up(sz.owners * sz.group, 8), 0)
    hot[...] = jnp.zeros_like(hot)
    speeds[...] = jnp.zeros_like(speeds)
    for copy in copies[1:5]:
        copy.wait()
    make_sources(sz, pool[...], high[...], low[...], source_rows, centres, sz.cells)
    make_targets(
        sz, lambda i, g: own_chunk(sz, lane, positions.at[i], pl.ds(8 * g, 8)), targets
    )
    for copy in copies[5:]:
        copy.wait()
    total = build_list(sz, lists, tasks)
    tiles_of_chunk(sz, total, tasks, source_rows, centres, targets, offsets, sums, hot)
    velocity = add_up(sz, sz.slots, total, sz.cells, offsets, sums, speeds, hot)
    blocks = []
    for i in range(3):
        for g in range(0, sz.cells, 8):
            chunk = own_chunk(sz, lane, positions.at[i], pl.ds(g, 8))
            block = chunk + TIME_STEP * velocity[i][g : g + 8]
            moved[pl.ds(i * sz.rows + g, 8), :] = block
            blocks.append(block)
    store_packed(sz, chunk_out, blocks)
    send_ghosts(sz, send, moved, ghost_out, jnp.zeros((1, 128), F32))


def second_kernel(sz, *refs):
    count = sz.lanes + 4
    inputs, (moved_out, velocity_out), refs = refs[:count], refs[count : count + 2], refs[count + 2 :]
    source_rows, centres, targets, offsets, sums, speeds, hot, pool, mine = refs[:9]
    held, sems = refs[9:-1], refs[-1]
    copies = fetch(inputs, held, sems)
    tasks, arrived, chunks, (high, low) = held[0], held[1], held[2:-2], held[-2:]
    hot[...] = jnp.zeros_like(hot)
    speeds[...] = jnp.zeros_like(speeds)
    lane = lax.axis_index("lane")
    pool[...] = jnp.zeros_like(pool)
    copies[0].wait()
    total = own_list(sz, lane, tasks, mine)
    for copy in copies[1:-2]:
        copy.wait()
    per = sz.cells // 8
    for k in range(sz.lanes):
        other = lane ^ k

        def row_of(b):
            return (b // per) * sz.pool + 8 * (b % per)

        def store_main(b, m, value):
            cut = pl.ds(pl.multiple_of(other * sz.main + 128 * m, 128), 128)
            pool[pl.ds(row_of(b), 8), cut] = value

        def add_rest(b, tile, value):
            offset = sz.main * sz.lanes + 128 * tile
            cut = (pl.ds(row_of(b), 8), slice(offset, offset + 128))
            pool[cut] = pool[cut] + value

        place_packed(sz, other, chunks[k], 3 * per, store_main, add_rest)
    take_ghosts(sz, arrived, pool, sz.pool, sz.cells)
    for copy in copies[-2:]:
        copy.wait()
    make_sources(sz, pool[...], high[...], low[...], source_rows, centres, 0)
    make_targets(sz, lambda i, g: pool[pl.ds(i * sz.pool + 8 * g, 8), :], targets)
    first = lane * sz.share
    tiles_of_cells(sz, first, total, mine, source_rows, centres, targets, offsets, sums, hot)
    velocity = add_up(sz, sz.own, total, up(sz.share, 8), offsets, sums, speeds, hot)
    for i in range(3):
        speed = velocity[i]
        moved = share_rows(sz, pool, i * sz.pool, lane) + TIME_STEP * speed
        velocity_out[i] = speed[: sz.share, : sz.points]
        moved_out[i] = moved[: sz.share, : sz.points]


def share_rows(sz, ref, base, lane):
    if sz.share % 8 == 0:
        return ref[pl.ds(pl.multiple_of(base + lane * sz.share, 8), sz.share), :]
    rows = [ref[pl.ds(base + lane * sz.share + c, 1), :] for c in range(sz.share)]
    rows.append(jnp.zeros((8 - sz.share, rows[0].shape[1]), F32))
    return jnp.concatenate(rows, axis=0)


def scratch(sz, tiles, slots):
    return [
        pltpu.VMEM((sz.tiles, SOURCE_ROWS * sz.pool, 128), F32),
        pltpu.VMEM((8 * sz.pool, 128), F32),
        pltpu.VMEM((tiles, 8 * sz.rows, 128), F32),
        pltpu.VMEM((tiles, 8 * slots, 128), F32),
        pltpu.VMEM((tiles, SUM_ROWS * slots, 128), F32),
        pltpu.VMEM((3, slots, 128 * tiles), F32),
        pltpu.VMEM((slots, 128), F32),
    ]


def swap(value, axis, size, k):
    return lax.ppermute(value, axis, [(d, d ^ k) for d in range(size)])


def shards(positions, bend_op, send_list, task_target, task_source, task_count):
    owners, lanes = lax.axis_size("space"), lax.axis_size("lane")
    cells, points = positions.shape[0], positions.shape[2]
    sz = sizes(owners, lanes, cells, points, task_target.shape[1], send_list.shape[1])
    params = pltpu.CompilerParams(vmem_limit_bytes=60 << 20)
    shape = jax.ShapeDtypeStruct
    both = ("space", "lane")
    by_component = jnp.transpose(positions, (1, 0, 2))
    list_rows = up(lanes, 8)
    slot_shape = shape((4 * sz.group * owners * lanes, 128), F32)
    leaving, send = pl.pallas_call(
        functools.partial(pick_kernel, sz),
        out_shape=[slot_shape, shape(send_list.shape, jnp.int32)],
        in_specs=[HBM] * 5,
        out_specs=[VMEM, SMEM],
        scratch_shapes=[
            pltpu.SMEM(send_list.shape, jnp.int32),
            pltpu.VMEM(task_target.shape, jnp.int32),
            pltpu.VMEM(task_source.shape, jnp.int32),
            pltpu.SMEM(task_count.shape, jnp.int32),
            pltpu.VMEM(by_component.shape, F32),
            pltpu.VMEM((3 * sz.rows, sz.chunk_wide), F32),
            pltpu.SemaphoreType.DMA((5,)),
        ],
        compiler_params=params,
        name="pick_cells",
    )(send_list, task_target, task_source, task_count, by_component)
    arrived = lax.all_to_all(leaving, both, split_axis=0, concat_axis=0, tiled=True)
    high, low, own_rows, own_centres = pl.pallas_call(
        functools.partial(source_kernel, sz),
        out_shape=[
            shape(bend_op.shape, BF16),
            shape(bend_op.shape, BF16),
            shape((sz.tiles, SOURCE_ROWS * cells, 128), F32),
            shape((8 * cells, 128), F32),
        ],
        in_specs=[HBM] * 2,
        out_specs=[VMEM] * 4,
        scratch_shapes=[
            pltpu.VMEM(by_component.shape, F32),
            pltpu.VMEM(bend_op.shape, F32),
            pltpu.SemaphoreType.DMA((2,)),
        ],
        compiler_params=params,
        cost_estimate=pl.CostEstimate(flops=10**9, bytes_accessed=10**7, transcendentals=0),
        name="first_sources",
    )(by_component, bend_op)
    chunk, leaving, tasks = pl.pallas_call(
        functools.partial(first_kernel, sz),
        out_shape=[
            shape((pack_rows(sz, cells), 128), F32),
            slot_shape,
            shape((3, sz.slots), jnp.int32),
        ],
        in_specs=[HBM] * 7,
        out_specs=[VMEM, VMEM, SMEM],
        scratch_shapes=scratch(sz, sz.chunk_tiles, sz.slots)
        + [
            pltpu.VMEM((3 * sz.rows, sz.chunk_wide), F32),
            pltpu.VMEM((3 * up(sz.owners * sz.group, 8), sz.width), F32),
            pltpu.SMEM(send_list.shape, jnp.int32),
            pltpu.VMEM(by_component.shape, F32),
            pltpu.VMEM(slot_shape.shape, F32),
            pltpu.VMEM(bend_op.shape, BF16),
            pltpu.VMEM(bend_op.shape, BF16),
            pltpu.VMEM((list_rows, 128), jnp.int32),
            pltpu.SMEM((list_rows, 128), jnp.int32),
            pltpu.SemaphoreType.DMA((8,)),
        ],
        compiler_params=params,
        name="first_step",
    )(arrived, send, by_component, high, low, own_rows, own_centres)
    arrived = lax.all_to_all(leaving, both, split_axis=0, concat_axis=0, tiled=True)
    chunks = [chunk] + [swap(chunk, "lane", lanes, k) for k in range(1, lanes)]
    result = shape((3, sz.share, points), F32)
    outputs = pl.pallas_call(
        functools.partial(second_kernel, sz),
        out_shape=[result, result],
        in_specs=[HBM] * (lanes + 4),
        out_specs=[VMEM] * 2,
        scratch_shapes=scratch(sz, sz.tiles, sz.own)
        + [
            pltpu.VMEM((3 * sz.pool, sz.width), F32),
            pltpu.SMEM((2, sz.own + 8), jnp.int32),
            pltpu.SMEM(tasks.shape, jnp.int32),
            pltpu.VMEM(slot_shape.shape, F32),
        ]
        + [pltpu.VMEM(chunk.shape, F32)] * lanes
        + [pltpu.VMEM(bend_op.shape, BF16)] * 2
        + [pltpu.SemaphoreType.DMA((lanes + 4,))],
        compiler_params=params,
        name="second_step",
    )(tasks, arrived, *chunks, high, low)
    return tuple(jnp.transpose(output, (1, 0, 2)) for output in outputs)


def solution(mesh):
    in_specs = (
        P("space", None, None),
        P(),
        P("space", None),
        P(("space", "lane"), None),
        P(("space", "lane"), None),
        P(("space", "lane")),
    )
    out_specs = (P(("space", "lane"), None, None), P(("space", "lane"), None, None))
    return jax.shard_map(shards, mesh=mesh, in_specs=in_specs, out_specs=out_specs, check_vma=False)
```

```python
import functools
from types import SimpleNamespace

import jax
import jax.numpy as jnp
from jax import lax
from jax.experimental import pallas as pl
from jax.experimental.pallas import tpu as pltpu
from jax.sharding import PartitionSpec as P

REGULARIZE = 0.25
TIME_STEP = 0.5
UNROLL = 8
PAIR = 2
SOURCE_ROWS = 24
SUM_ROWS = 16

F32 = jnp.float32
BF16 = jnp.bfloat16
VMEM = pl.BlockSpec(memory_space=pltpu.VMEM)
SMEM = pl.BlockSpec(memory_space=pltpu.SMEM)
HBM = pl.BlockSpec(memory_space=pltpu.HBM)
ANY = pl.BlockSpec(memory_space=pl.ANY)


def up(value, step):
    return -(-value // step) * step


def sizes(owners, lanes, cells, points, cap, listed):
    main = 128 * (points // (128 * lanes))
    rest = (points - main * lanes) // lanes
    group = listed // owners
    pool = up(cells + listed, 8)
    per_pack = 128 // rest
    return SimpleNamespace(
        owners=owners,
        lanes=lanes,
        cells=cells,
        points=points,
        cap=cap,
        group=group,
        width=up(points, 128),
        tiles=up(points, 128) // 128,
        main=main,
        rest=rest,
        rest_tiles=up(rest * lanes, 128) // 128,
        chunk=main + rest,
        chunk_wide=main + up(rest, 128),
        chunk_tiles=(main + up(rest, 128)) // 128,
        per_pack=per_pack,
        pool=pool,
        share=cells // lanes,
        slots=up(lanes * cap + UNROLL, 8),
        rows=cells + 8,
        own=up(lanes * cap + PAIR, 8),
    )


def pack_rows(sz, rows):
    return (3 * rows * sz.main // 128) + 8 * up(3 * rows // 8, sz.per_pack) // sz.per_pack


def split2(value):
    high = value.astype(BF16)
    return high, (value - high.astype(F32)).astype(BF16)


def split3(value):
    first = value.astype(BF16).astype(F32)
    left = value - first
    second = left.astype(BF16).astype(F32)
    return first, second, left - second


def lane_iota(rows):
    return lax.broadcasted_iota(jnp.int32, (rows, 128), 1)


def fetch(sources, targets, sems):
    copies = [
        pltpu.make_async_copy(source, target, sems.at[q])
        for q, (source, target) in enumerate(zip(sources, targets))
    ]
    for copy in copies:
        copy.start()
    return copies


def loop(count, body):
    if count <= 8:
        for q in range(count):
            body(q)
    else:

        def step(q, carry):
            body(q)
            return carry

        lax.fori_loop(0, count, step, 0)


def own_chunk(sz, lane, ref, rows):
    parts = []
    if sz.main:
        parts.append(ref[rows, pl.ds(pl.multiple_of(lane * sz.main, 128), sz.main)])
    start = sz.rest * lane
    lanes = lane_iota(8)
    rest = jnp.zeros((8, 128), F32)
    for tile in range(sz.rest_tiles):
        offset = sz.main * sz.lanes + 128 * tile
        block = ref[rows, offset : min(offset + 128, ref.shape[-1])]
        if block.shape[1] < 128:
            block = jnp.concatenate([block, jnp.zeros((8, 128 - block.shape[1]), F32)], axis=1)
        inside = (lanes + 128 * tile >= start) & (lanes + 128 * tile < start + sz.rest)
        rest = rest + jnp.where(inside, block, 0.0)
    rest = pltpu.roll(rest, lax.rem(128 * sz.rest_tiles - start, 128), 1)
    parts.append(rest)
    return jnp.concatenate(parts, axis=1) if len(parts) > 1 else parts[0]


def send_ghosts(sz, send, chunks, out, tasks):
    lanes = lane_iota(1)

    def one(d):
        for g in range(sz.group):
            cell = send[0, d * sz.group + g]
            rows = []
            last = tasks
            for i in range(3):
                row = chunks[pl.ds(i * sz.rows + cell, 1), :]
                rows.append(row[:, :128] if sz.main else jnp.zeros((1, 128), F32))
                piece = jnp.where(lanes < sz.rest, row[:, sz.main : sz.main + 128], 0.0)
                last = last + (pltpu.roll(piece, i * sz.rest, 1) if i else piece)
            rows.append(last)
            for other in range(sz.lanes):
                first = ((d * sz.lanes + other) * sz.group + g) * 4
                for q, row in enumerate(rows):
                    out[pl.ds(first + q, 1), :] = row

    loop(sz.owners, one)


def pick_kernel(sz, *refs):
    inputs, (out, send_out), held, (chunks, sems) = refs[:5], refs[5:7], refs[7:12], refs[12:]
    for copy in fetch(inputs, held, sems):
        copy.wait()
    send, target, source, count, positions = held
    for j in range(send_out.shape[1]):
        send_out[0, j] = send[0, j]
    lane = lax.axis_index("lane")
    for i in range(3):
        for g in range(0, sz.cells, 8):
            value = own_chunk(sz, lane, positions.at[i], pl.ds(g, 8))
            chunks[pl.ds(i * sz.rows + g, 8), :] = value
    spare = jnp.zeros((1, 128 - sz.cap), F32)
    tasks = jnp.where(lane_iota(1) == 3 * sz.rest + 2 * sz.cap, count[0].astype(F32), 0.0)
    for q, row in enumerate((target, source)):
        wide = jnp.concatenate([row[...].astype(F32), spare], axis=1)
        tasks = tasks + pltpu.roll(wide, 3 * sz.rest + q * sz.cap, 1)
    send_ghosts(sz, send, chunks, out, tasks)


def take_ghosts(sz, arrived, pool, stride, base):
    lanes = lane_iota(1)

    def one(d):
        for g in range(sz.group):
            first = [((d * sz.lanes + lane) * sz.group + g) * 4 for lane in range(sz.lanes)]
            last = [arrived[pl.ds(row + 3, 1), :] for row in first]
            for i in range(3):
                tiles = []
                if sz.main:
                    tiles += [arrived[pl.ds(row + i, 1), :] for row in first]
                for tile in range(sz.rest_tiles):
                    total = jnp.zeros((1, 128), F32)
                    for lane in range(sz.lanes):
                        start = sz.rest * lane
                        if start + sz.rest <= 128 * tile or start >= 128 * tile + 128:
                            continue
                        shift = (start - i * sz.rest) % 128
                        value = pltpu.roll(last[lane], shift, 1) if shift else last[lane]
                        at = lanes + 128 * tile
                        total = jnp.where((at >= start) & (at < start + sz.rest), value, total)
                    tiles.append(total)
                place = pl.ds(i * stride + base + d * sz.group + g, 1)
                pool[place, :] = jnp.concatenate(tiles, axis=1)

    loop(sz.owners, one)


def build_list(sz, lists, tasks):
    total = jnp.int32(0)
    for lane in range(sz.lanes):
        count = lists[lane, 2 * sz.cap]
        for j in range(sz.cap):
            tasks[0, total] = lists[lane, j]
            tasks[1, total] = lists[lane, sz.cap + j]
            total = total + (j < count).astype(jnp.int32)
    for u in range(UNROLL):
        tasks[0, total + u] = jnp.int32(sz.cells)
        tasks[1, total + u] = jnp.int32(0)
    tasks[2, 0] = total
    return total


def own_list(sz, lane, tasks, mine):
    first = lane * sz.share
    total = tasks[2, 0]
    count = jnp.int32(0)
    for t in range(sz.lanes * sz.cap):
        target = tasks[0, t] - first
        mine[0, count] = target
        mine[1, count] = tasks[1, t]
        taken = (target >= 0) & (target < sz.share) & (t < total)
        count = count + taken.astype(jnp.int32)
    for u in range(PAIR):
        mine[0, count + u] = jnp.int32(-1)
        mine[1, count + u] = jnp.int32(0)
    return count


def products(value, bend_high, bend_low):
    high, low = split2(value)
    dot = functools.partial(jnp.dot, preferred_element_type=F32)
    return dot(high, bend_high) + dot(low, bend_high) + dot(high, bend_low)


def make_sources(sz, value, bend_high, bend_low, source_rows, centres, first):
    count = value.shape[0] // 3
    forces = products(value[:, : sz.points], bend_high, bend_low)
    forces = jnp.concatenate(
        [forces, jnp.zeros((3 * count, sz.width - sz.points), F32)], axis=1
    )
    middle = jnp.sum(value, axis=1, keepdims=True) / sz.points
    for g in range(count // 8):
        where = [i * count + 8 * g for i in range(3)]
        middles = [jnp.broadcast_to(middle[w : w + 8], (8, 128)) for w in where]
        middles += [jnp.zeros((8, 128), F32)] * 5
        for i, row in enumerate(middles):
            centres[pl.ds(8 * (first + 8 * g) + i, 8, stride=8), :] = row
        for j in range(sz.tiles):
            cut = slice(128 * j, 128 * j + 128)
            y = [value[w : w + 8, cut] - m for w, m in zip(where, middles)]
            f = [forces[w : w + 8, cut] for w in where]
            norm = y[0] * y[0] + y[1] * y[1] + y[2] * y[2] + REGULARIZE
            along = y[0] * f[0] + y[1] * f[1] + y[2] * f[2]
            one, zero = jnp.ones((8, 128), F32), jnp.zeros((8, 128), F32)
            rows = [y[0], y[1], y[2], norm, one, zero, zero, zero]
            rows += f
            rows += [y[i] * f[k] for i in range(3) for k in range(3)]
            rows += [norm * f[i] + along * y[i] for i in range(3)]
            rows += [along]
            for k, row in enumerate(rows):
                place = pl.ds(SOURCE_ROWS * (first + 8 * g) + k, 8, stride=SOURCE_ROWS)
                source_rows.at[j][place, :] = row


def make_targets(sz, blocks, targets):
    targets[...] = jnp.zeros_like(targets)
    for g in range(sz.cells // 8):
        for i in range(3):
            block = blocks(i, g)
            for j in range(targets.shape[0]):
                cut = slice(128 * j, 128 * j + 128)
                targets.at[j][pl.ds(64 * g + i, 8, stride=8), :] = block[:, cut]


def source_operands(sz, source, source_rows):
    held = [
        source_rows[j, pl.ds(pl.multiple_of(SOURCE_ROWS * source, 8), SOURCE_ROWS), :]
        for j in range(sz.tiles)
    ]
    held = jnp.concatenate(held, axis=1)
    y1, y2, y3 = split3(held[:8])
    y_stack = jnp.concatenate([y1, y1, y2, y2, y1, y3], axis=0).astype(BF16)
    return y_stack, jnp.concatenate(split3(held[8:]), axis=0)


def pieces(points, step):
    starts = list(range(0, max(points // 128 * 128, 1), step))
    return list(zip(starts, starts[1:] + [points]))


def twice(piece, count):
    whole = count // 128 * 128
    parts = [piece[:, :whole].astype(BF16)] * 2 if whole else []
    if whole < count:
        last = piece[:, whole:]
        last = last + pltpu.roll(last, count - whole, 1)
        parts.append(last.astype(BF16)[:, : 2 * (count - whole)])
    return jnp.concatenate(parts, axis=1)


def load_target(j, target, slot, centre, targets, offsets):
    row = lax.broadcasted_iota(jnp.int32, (8, 128), 0)
    x = targets[j, pl.ds(pl.multiple_of(8 * target, 8), 8), :] - centre
    square = x * x
    norm = pltpu.roll(square, 2, 0) + pltpu.roll(square, 3, 0) + pltpu.roll(square, 4, 0)
    side = jnp.where(row == 4, norm, jnp.where(row == 3, 1.0, 0.0))
    x_side = jnp.where(row < 3, -2.0 * x, side)
    x1, x2, x3 = split3(x_side)
    return x, jnp.concatenate([x1, x2, x1, x2, x3, x1], axis=0).astype(BF16)


def distances(one_stack, other_stack):
    return jnp.dot(one_stack, other_stack, preferred_element_type=F32)


def weights(shifted):
    inverse = lax.rsqrt(shifted)
    return split2(inverse * inverse * inverse)


def fold(result):
    return result[:SUM_ROWS] + result[SUM_ROWS : 2 * SUM_ROWS] + result[2 * SUM_ROWS :]


def skewed(stages, skew):
    asked = []
    for q, (ask, _) in enumerate(stages):
        asked.append(ask())
        if q >= skew:
            stages[q - skew][1](asked[q - skew])
            asked[q - skew] = None
    for q in range(max(len(stages) - skew, 0), len(stages)):
        stages[q][1](asked[q])


def adder(totals, key):
    def add(value):
        totals[key] = totals[key] + value if key in totals else value

    return add


def wide_piece(operands, begin, first, end, add):
    def ask():
        _, y_turned, _, blocks = operands()
        return distances(y_turned[first:end], blocks[begin])

    def take(shifted):
        m_stack = operands()[2]
        high, low = weights(shifted)
        whole = (end - first) // 128 * 128
        parts = [high[:whole], low[:whole]] if whole else []
        parts += [high[whole:], low[whole:]] if whole < end - first else []
        stack = jnp.concatenate(parts, axis=0)
        m_piece = twice(m_stack[:, first : up(end, 128)], end - first)
        add(jnp.dot(m_piece, stack, preferred_element_type=F32))

    return ask, take


def rest_piece(operands, begin, add):
    def ask():
        y_stack, _, _, blocks = operands()
        return distances(blocks[begin], y_stack)

    def take(shifted):
        high, low = weights(shifted)
        m_whole = operands()[2].astype(BF16)
        turned = (((1,), (1,)), ((), ()))
        result = lax.dot_general(m_whole, high, turned, preferred_element_type=F32)
        add(result + lax.dot_general(m_whole, low, turned, preferred_element_type=F32))

    return ask, take


def store_sums(slots, slot, j, x, result, offsets, sums):
    offsets.at[j][pl.ds(slot, 8, stride=slots), :] = x
    for h in range(0, SUM_ROWS, 8):
        sums.at[j][pl.ds(h * slots + slot, 8, stride=slots), :] = result[h : h + 8]


def mark(slot, target, hot):
    hot[pl.ds(slot, 1), :] = jnp.where(lane_iota(1) == target, 1.0, 0.0)


def combine(sz, slots, first, total, offsets, sums, speeds):
    live = lax.broadcasted_iota(jnp.int32, (8, 128), 0) + first < total
    for j in range(offsets.shape[0]):
        x = [offsets[j, pl.ds(i * slots + first, 8), :] for i in range(3)]
        s = [sums[j, pl.ds(k * slots + first, 8), :] for k in range(SUM_ROWS)]
        a, b, c = s[:3], [s[3:6], s[6:9], s[9:12]], s[12:15]
        norm = x[0] * x[0] + x[1] * x[1] + x[2] * x[2] + REGULARIZE
        along = x[0] * a[0] + x[1] * a[1] + x[2] * a[2] - s[15]
        for i in range(3):
            speed = norm * a[i] + c[i] + along * x[i]
            for k in range(3):
                speed = speed - x[k] * (2.0 * b[k][i] + b[i][k])
            speed = jnp.where(live, speed / sz.points, 0.0)
            speeds[i, pl.ds(first, 8), 128 * j : 128 * j + 128] = speed


def add_up(sz, slots, total, rows, offsets, sums, speeds, hot):
    def eight(q, carry):
        combine(sz, slots, pl.multiple_of(8 * q, 8), total, offsets, sums, speeds)
        return carry

    lax.fori_loop(0, lax.div(total + 7, 8), eight, 0)
    one_hot = hot[...].astype(BF16)
    result = []
    for i in range(3):
        first, second, third = split3(speeds[i])
        parts = [
            lax.dot_general(
                one_hot, part.astype(BF16), (((0,), (0,)), ((), ())), preferred_element_type=F32
            )
            for part in (first, second, third)
        ]
        result.append((parts[0] + parts[1] + parts[2])[:rows])
    return result


def several_tasks(sz, slots, picks, marks, main, rest, wide, step, skew, refs):
    source_rows, centres, targets, offsets, sums, hot = refs

    def task(slot, pick, target_mark):
        target, source = pick
        made, parts, points = [], {}, []

        def operands():
            if made:
                return made[0]
            y_stack, m_stack = source_operands(sz, source, source_rows)
            centre = centres[pl.ds(pl.multiple_of(8 * source, 8), 8), :]
            points.extend(
                load_target(j, target, slot, centre, targets, offsets)
                for j in range(targets.shape[0])
            )
            blocks = {}
            for begin in range(0, main, wide):
                stack = [stack for _, stack in points[begin // 128 : (begin + wide) // 128]]
                blocks[begin] = jnp.concatenate(stack, axis=1)
            if rest:
                blocks[main] = jnp.transpose(points[main // 128][1])[:rest]
            made.append((y_stack, jnp.transpose(y_stack), m_stack, blocks))
            return made[0]

        def finish():
            results = [fold(parts[begin]) for begin in range(0, main, wide)]
            if rest:
                spare = jnp.zeros((SUM_ROWS, 128 - rest), F32)
                results.append(jnp.concatenate([fold(parts[main]), spare], axis=1))
            result = jnp.concatenate(results, axis=1)
            for j in range(targets.shape[0]):
                cut = result[:, 128 * j : 128 * j + 128]
                store_sums(offsets.shape[1] // 8, slot, j, points[j][0], cut, offsets, sums)
            mark(slot, target_mark, hot)

        own = []
        for begin in range(0, main, wide):
            for first, last in pieces(sz.points, step):
                own.append(wide_piece(operands, begin, first, last, adder(parts, begin)))
        if rest:
            own.insert(len(own) // 2, rest_piece(operands, main, adder(parts, main)))
        ask, take = own[-1]

        def last_take(shifted):
            take(shifted)
            finish()

        own[-1] = (ask, last_take)
        return own, operands

    made = [task(slot, pick, m) for slot, pick, m in zip(slots, picks, marks)]
    for (own, _), (_, after) in zip(made, made[1:]):
        ask, take = own[0]

        def ask_and_prepare(ask=ask, after=after):
            shifted = ask()
            after()
            return shifted

        own[0] = (ask_and_prepare, take)
    skewed([stage for own, _ in made for stage in own], skew)


def tiles_of_chunk(sz, total, tasks, *refs):
    def several(q, carry):
        slots = [q * UNROLL + u for u in range(UNROLL)]
        picks = [(tasks[0, slot], tasks[1, slot]) for slot in slots]
        marks = [target for target, _ in picks]
        several_tasks(sz, slots, picks, marks, sz.main, sz.rest, 128, 256, 4, refs)
        return carry

    lax.fori_loop(0, lax.div(total + UNROLL - 1, UNROLL), several, 0)


def tiles_of_cells(sz, base, total, mine, *refs):
    main = 256 * (sz.points // 256)

    def several(q, carry):
        slots = [q * PAIR + u for u in range(PAIR)]
        marks = [mine[0, slot] for slot in slots]
        picks = [(jnp.maximum(mark, 0) + base, mine[1, s]) for mark, s in zip(marks, slots)]
        several_tasks(sz, slots, picks, marks, main, sz.points - main, 256, 128, 3, refs)
        return carry

    lax.fori_loop(0, lax.div(total + PAIR - 1, PAIR), several, 0)


def packed(sz, blocks):
    rows = [b[:, : sz.main] for b in blocks] if sz.main else []
    lanes = lane_iota(8)
    for p in range(0, len(blocks), sz.per_pack):
        total = jnp.zeros((8, 128), F32)
        for q, block in enumerate(blocks[p : p + sz.per_pack]):
            rest = jnp.where(lanes < sz.rest, block[:, sz.main : sz.main + 128], 0.0)
            total = total + (pltpu.roll(rest, q * sz.rest, 1) if q else rest)
        rows.append(total)
    return rows


def store_packed(sz, out, blocks):
    first = 0
    count = len(blocks)
    values = packed(sz, blocks)
    if sz.main:
        for b in range(count):
            for m in range(sz.main // 128):
                out[pl.ds(first, 8), :] = values[b][:, 128 * m : 128 * m + 128]
                first += 8
        values = values[count:]
    for value in values:
        out[pl.ds(first, 8), :] = value
        first += 8


def place_packed(sz, lane, arrived, count, store_main, add_rest):
    first = 0
    if sz.main:
        for b in range(count):
            for m in range(sz.main // 128):
                store_main(b, m, arrived[pl.ds(first, 8), :])
                first += 8
    start = sz.rest * lane
    lanes = lane_iota(8)
    for b in range(count):
        pack, q = divmod(b, sz.per_pack)
        value = arrived[pl.ds(first + 8 * pack, 8), :]
        value = pltpu.roll(value, lax.rem(start - q * sz.rest + 128, 128), 1)
        for tile in range(sz.rest_tiles):
            inside = (lanes + 128 * tile >= start) & (lanes + 128 * tile < start + sz.rest)
            add_rest(b, tile, jnp.where(inside, value, 0.0))


def source_kernel(sz, *refs):
    inputs, (high_out, low_out, source_rows, centres), held, sems = (
        refs[:2],
        refs[2:6],
        refs[6:8],
        refs[8],
    )
    for copy in fetch(inputs, held, sems):
        copy.wait()
    positions, bend = held
    high_out[...], low_out[...] = split2(bend[...])
    value = jnp.concatenate([positions[i] for i in range(3)], axis=0)
    value = jnp.concatenate(
        [value, jnp.zeros((3 * sz.cells, sz.width - sz.points), F32)], axis=1
    )
    make_sources(sz, value, high_out[...], low_out[...], source_rows, centres, 0)


def first_kernel(sz, *refs):
    arrived, high, low, inputs = refs[0], refs[1], refs[2], refs[3:7]
    outputs, refs = refs[7:10], refs[10:]
    source_rows, centres, targets, offsets, sums, speeds, hot, moved, pool = refs[:9]
    send, positions, staged, lists, chunk_out, ghost_out, tasks, sems = refs[9:]
    me, lane = lax.axis_index("space"), lax.axis_index("lane")
    own_rows = source_rows.at[:, pl.ds(0, SOURCE_ROWS * sz.cells)]
    own_centres = centres.at[pl.ds(0, 8 * sz.cells)]
    copies = fetch(inputs, [send, positions, own_rows, own_centres], sems)
    for other in range(sz.lanes):
        row = ((me * sz.lanes + other) * sz.group) * 4 + 3
        value = pltpu.roll(arrived[pl.ds(row, 1), :], 128 - 3 * sz.rest, 1)
        staged[pl.ds(other, 1), :] = value.astype(jnp.int32)
    copies += fetch([staged], [lists], sems.at[pl.ds(4, 1)])
    pool[...] = jnp.zeros_like(pool)
    take_ghosts(sz, arrived, pool, up(sz.owners * sz.group, 8), 0)
    hot[...] = jnp.zeros_like(hot)
    speeds[...] = jnp.zeros_like(speeds)
    make_sources(sz, pool[...], high[...], low[...], source_rows, centres, sz.cells)
    for copy in copies[:2]:
        copy.wait()
    make_targets(
        sz, lambda i, g: own_chunk(sz, lane, positions.at[i], pl.ds(8 * g, 8)), targets
    )
    copies[4].wait()
    total = build_list(sz, lists, tasks)
    for copy in copies[2:4]:
        copy.wait()
    copies = fetch([tasks], outputs[2:], sems)
    tiles_of_chunk(sz, total, tasks, source_rows, centres, targets, offsets, sums, hot)
    velocity = add_up(sz, sz.slots, total, sz.cells, offsets, sums, speeds, hot)
    blocks = []
    for i in range(3):
        for g in range(0, sz.cells, 8):
            chunk = own_chunk(sz, lane, positions.at[i], pl.ds(g, 8))
            block = chunk + TIME_STEP * velocity[i][g : g + 8]
            moved[pl.ds(i * sz.rows + g, 8), :] = block
            blocks.append(block)
    store_packed(sz, chunk_out, blocks)
    copies += fetch([chunk_out], outputs[:1], sems.at[pl.ds(1, 1)])
    send_ghosts(sz, send, moved, ghost_out, jnp.zeros((1, 128), F32))
    copies += fetch([ghost_out], outputs[1:2], sems.at[pl.ds(2, 1)])
    for copy in copies:
        copy.wait()


def second_kernel(sz, *refs):
    (arrived, high, low), refs = refs[:3], refs[3:]
    others, refs = refs[: sz.lanes - 1], refs[sz.lanes - 1 :]
    inputs, (moved_out, velocity_out), refs = refs[:2], refs[2:4], refs[4:]
    source_rows, centres, targets, offsets, sums, speeds, hot, pool, mine = refs[:9]
    tasks, chunk, sems = refs[9:]
    copies = fetch(inputs, [tasks, chunk], sems)
    chunks = [chunk, *others]
    hot[...] = jnp.zeros_like(hot)
    speeds[...] = jnp.zeros_like(speeds)
    lane = lax.axis_index("lane")
    pool[...] = jnp.zeros_like(pool)
    copies[0].wait()
    total = own_list(sz, lane, tasks, mine)
    copies[1].wait()
    per = sz.cells // 8
    for k in range(sz.lanes):
        other = lane ^ k

        def row_of(b):
            return (b // per) * sz.pool + 8 * (b % per)

        def store_main(b, m, value):
            cut = pl.ds(pl.multiple_of(other * sz.main + 128 * m, 128), 128)
            pool[pl.ds(row_of(b), 8), cut] = value

        def add_rest(b, tile, value):
            offset = sz.main * sz.lanes + 128 * tile
            cut = (pl.ds(row_of(b), 8), slice(offset, offset + 128))
            pool[cut] = pool[cut] + value

        place_packed(sz, other, chunks[k], 3 * per, store_main, add_rest)
    take_ghosts(sz, arrived, pool, sz.pool, sz.cells)
    make_sources(sz, pool[...], high[...], low[...], source_rows, centres, 0)
    make_targets(sz, lambda i, g: pool[pl.ds(i * sz.pool + 8 * g, 8), :], targets)
    first = lane * sz.share
    tiles_of_cells(sz, first, total, mine, source_rows, centres, targets, offsets, sums, hot)
    velocity = add_up(sz, sz.own, total, up(sz.share, 8), offsets, sums, speeds, hot)
    for i in range(3):
        speed = velocity[i]
        moved = share_rows(sz, pool, i * sz.pool, lane) + TIME_STEP * speed
        velocity_out[i] = speed[: sz.share, : sz.points]
        moved_out[i] = moved[: sz.share, : sz.points]


def share_rows(sz, ref, base, lane):
    if sz.share % 8 == 0:
        return ref[pl.ds(pl.multiple_of(base + lane * sz.share, 8), sz.share), :]
    rows = [ref[pl.ds(base + lane * sz.share + c, 1), :] for c in range(sz.share)]
    rows.append(jnp.zeros((8 - sz.share, rows[0].shape[1]), F32))
    return jnp.concatenate(rows, axis=0)


def scratch(sz, tiles, slots):
    return [
        pltpu.VMEM((sz.tiles, SOURCE_ROWS * sz.pool, 128), F32),
        pltpu.VMEM((8 * sz.pool, 128), F32),
        pltpu.VMEM((tiles, 8 * sz.rows, 128), F32),
        pltpu.VMEM((tiles, 8 * slots, 128), F32),
        pltpu.VMEM((tiles, SUM_ROWS * slots, 128), F32),
        pltpu.VMEM((3, slots, 128 * tiles), F32),
        pltpu.VMEM((slots, 128), F32),
    ]


def swap(value, axis, size, k):
    return lax.ppermute(value, axis, [(d, d ^ k) for d in range(size)])


def in_hbm(value):
    return pltpu.with_memory_space_constraint(value, pltpu.HBM)


def shards(positions, bend_op, send_list, task_target, task_source, task_count):
    owners, lanes = lax.axis_size("space"), lax.axis_size("lane")
    cells, points = positions.shape[0], positions.shape[2]
    sz = sizes(owners, lanes, cells, points, task_target.shape[1], send_list.shape[1])
    params = pltpu.CompilerParams(vmem_limit_bytes=min(6 * lanes, 40) << 20)
    shape = jax.ShapeDtypeStruct
    both = ("space", "lane")
    by_component = jnp.transpose(positions, (1, 0, 2))
    list_rows = up(lanes, 8)
    slot_shape = shape((4 * sz.group * owners * lanes, 128), F32)
    leaving, send = pl.pallas_call(
        functools.partial(pick_kernel, sz),
        out_shape=[slot_shape, shape(send_list.shape, jnp.int32)],
        in_specs=[HBM] * 5,
        out_specs=[VMEM, SMEM],
        scratch_shapes=[
            pltpu.SMEM(send_list.shape, jnp.int32),
            pltpu.VMEM(task_target.shape, jnp.int32),
            pltpu.VMEM(task_source.shape, jnp.int32),
            pltpu.SMEM(task_count.shape, jnp.int32),
            pltpu.VMEM(by_component.shape, F32),
            pltpu.VMEM((3 * sz.rows, sz.chunk_wide), F32),
            pltpu.SemaphoreType.DMA((5,)),
        ],
        compiler_params=pltpu.CompilerParams(vmem_limit_bytes=60 << 20),
        name="pick_cells",
    )(send_list, task_target, task_source, task_count, by_component)
    arrived = lax.all_to_all(leaving, both, split_axis=0, concat_axis=0, tiled=True)
    high, low, own_rows, own_centres = pl.pallas_call(
        functools.partial(source_kernel, sz),
        out_shape=[
            shape(bend_op.shape, BF16),
            shape(bend_op.shape, BF16),
            shape((sz.tiles, SOURCE_ROWS * cells, 128), F32),
            shape((8 * cells, 128), F32),
        ],
        in_specs=[HBM] * 2,
        out_specs=[VMEM] * 4,
        scratch_shapes=[
            pltpu.VMEM(by_component.shape, F32),
            pltpu.VMEM(bend_op.shape, F32),
            pltpu.SemaphoreType.DMA((2,)),
        ],
        compiler_params=params,
        cost_estimate=pl.CostEstimate(flops=10**9, bytes_accessed=10**7, transcendentals=0),
        name="first_sources",
    )(in_hbm(by_component), in_hbm(bend_op))
    chunk_shape = (pack_rows(sz, cells), 128)
    chunk, leaving, tasks = pl.pallas_call(
        functools.partial(first_kernel, sz),
        out_shape=[
            pltpu.HBM(chunk_shape, F32),
            pltpu.HBM(slot_shape.shape, F32),
            pltpu.HBM((3, sz.slots), jnp.int32),
        ],
        in_specs=[VMEM] * 3 + [HBM] * 2 + [ANY] * 2,
        out_specs=[HBM] * 3,
        scratch_shapes=scratch(sz, sz.chunk_tiles, sz.slots)
        + [
            pltpu.VMEM((3 * sz.rows, sz.chunk_wide), F32),
            pltpu.VMEM((3 * up(sz.owners * sz.group, 8), sz.width), F32),
            pltpu.SMEM(send_list.shape, jnp.int32),
            pltpu.VMEM(by_component.shape, F32),
            pltpu.VMEM((list_rows, 128), jnp.int32),
            pltpu.SMEM((list_rows, 128), jnp.int32),
            pltpu.VMEM(chunk_shape, F32),
            pltpu.VMEM(slot_shape.shape, F32),
            pltpu.SMEM((3, sz.slots), jnp.int32),
            pltpu.SemaphoreType.DMA((5,)),
        ],
        compiler_params=params,
        name="first_step",
    )(arrived, high, low, in_hbm(send), in_hbm(by_component), own_rows, own_centres)
    arrived = lax.all_to_all(leaving, both, split_axis=0, concat_axis=0, tiled=True)
    chunks = [swap(chunk, "lane", lanes, k) for k in range(1, lanes)]
    result = shape((3, sz.share, points), F32)
    outputs = pl.pallas_call(
        functools.partial(second_kernel, sz),
        out_shape=[result, result],
        in_specs=[VMEM] * (lanes + 2) + [HBM] * 2,
        out_specs=[VMEM] * 2,
        scratch_shapes=scratch(sz, sz.tiles, sz.own)
        + [
            pltpu.VMEM((3 * sz.pool, sz.width), F32),
            pltpu.SMEM((2, sz.own + 8), jnp.int32),
            pltpu.SMEM(tasks.shape, jnp.int32),
            pltpu.VMEM(chunk.shape, F32),
            pltpu.SemaphoreType.DMA((2,)),
        ],
        compiler_params=params,
        name="second_step",
    )(arrived, high, low, *chunks, in_hbm(tasks), in_hbm(chunk))
    return tuple(jnp.transpose(output, (1, 0, 2)) for output in outputs)


def solution(mesh):
    in_specs = (
        P("space", None, None),
        P(),
        P("space", None),
        P(("space", "lane"), None),
        P(("space", "lane"), None),
        P(("space", "lane")),
    )
    out_specs = (P(("space", "lane"), None, None), P(("space", "lane"), None, None))
    return jax.shard_map(shards, mesh=mesh, in_specs=in_specs, out_specs=out_specs, check_vma=False)
```

```python
import functools
from types import SimpleNamespace

import jax
import jax.numpy as jnp
from jax import lax
from jax.experimental import pallas as pl
from jax.experimental.pallas import tpu as pltpu
from jax.sharding import PartitionSpec as P

REGULARIZE = 0.25
TIME_STEP = 0.5
UNROLL = 11
PAIR = 2
SOURCE_ROWS = 24
SUM_ROWS = 16

F32 = jnp.float32
BF16 = jnp.bfloat16
VMEM = pl.BlockSpec(memory_space=pltpu.VMEM)
SMEM = pl.BlockSpec(memory_space=pltpu.SMEM)
HBM = pl.BlockSpec(memory_space=pltpu.HBM)
ANY = pl.BlockSpec(memory_space=pl.ANY)


def up(value, step):
    return -(-value // step) * step


def sizes(owners, lanes, cells, points, cap, listed):
    main = 128 * (points // (128 * lanes))
    rest = (points - main * lanes) // lanes
    group = listed // owners
    pool = up(cells + listed, 8)
    per_pack = 128 // rest
    return SimpleNamespace(
        owners=owners,
        lanes=lanes,
        cells=cells,
        points=points,
        cap=cap,
        group=group,
        width=up(points, 128),
        tiles=up(points, 128) // 128,
        main=main,
        rest=rest,
        rest_tiles=up(rest * lanes, 128) // 128,
        chunk=main + rest,
        chunk_wide=main + up(rest, 128),
        chunk_tiles=(main + up(rest, 128)) // 128,
        per_pack=per_pack,
        pool=pool,
        share=cells // lanes,
        slots=up(lanes * cap + UNROLL, 8),
        rows=cells + 8,
        own=up(lanes * cap + PAIR, 8),
    )


def pack_rows(sz, rows):
    return (3 * rows * sz.main // 128) + 8 * up(3 * rows // 8, sz.per_pack) // sz.per_pack


def split2(value):
    high = value.astype(BF16)
    return high, (value - high.astype(F32)).astype(BF16)


def split3(value):
    first = value.astype(BF16).astype(F32)
    left = value - first
    second = left.astype(BF16).astype(F32)
    return first, second, left - second


def lane_iota(rows):
    return lax.broadcasted_iota(jnp.int32, (rows, 128), 1)


def fetch(sources, targets, sems):
    copies = [
        pltpu.make_async_copy(source, target, sems.at[q])
        for q, (source, target) in enumerate(zip(sources, targets))
    ]
    for copy in copies:
        copy.start()
    return copies


def loop(count, body):
    if count <= 8:
        for q in range(count):
            body(q)
    else:

        def step(q, carry):
            body(q)
            return carry

        lax.fori_loop(0, count, step, 0)


def own_chunk(sz, lane, ref, rows):
    parts = []
    if sz.main:
        parts.append(ref[rows, pl.ds(pl.multiple_of(lane * sz.main, 128), sz.main)])
    start = sz.rest * lane
    lanes = lane_iota(8)
    rest = jnp.zeros((8, 128), F32)
    for tile in range(sz.rest_tiles):
        offset = sz.main * sz.lanes + 128 * tile
        block = ref[rows, offset : min(offset + 128, ref.shape[-1])]
        if block.shape[1] < 128:
            block = jnp.concatenate([block, jnp.zeros((8, 128 - block.shape[1]), F32)], axis=1)
        inside = (lanes + 128 * tile >= start) & (lanes + 128 * tile < start + sz.rest)
        rest = rest + jnp.where(inside, block, 0.0)
    rest = pltpu.roll(rest, lax.rem(128 * sz.rest_tiles - start, 128), 1)
    parts.append(rest)
    return jnp.concatenate(parts, axis=1) if len(parts) > 1 else parts[0]


def send_ghosts(sz, send, chunks, out, tasks):
    lanes = lane_iota(1)

    def one(d):
        for g in range(sz.group):
            cell = send[0, d * sz.group + g]
            rows = []
            last = tasks
            for i in range(3):
                row = chunks[pl.ds(i * sz.rows + cell, 1), :]
                rows.append(row[:, :128] if sz.main else jnp.zeros((1, 128), F32))
                piece = jnp.where(lanes < sz.rest, row[:, sz.main : sz.main + 128], 0.0)
                last = last + (pltpu.roll(piece, i * sz.rest, 1) if i else piece)
            rows.append(last)
            for other in range(sz.lanes):
                first = ((d * sz.lanes + other) * sz.group + g) * 4
                for q, row in enumerate(rows):
                    out[pl.ds(first + q, 1), :] = row

    loop(sz.owners, one)


def pick_kernel(sz, *refs):
    inputs, (out, send_out), held, (chunks, sems) = refs[:5], refs[5:7], refs[7:12], refs[12:]
    for copy in fetch(inputs, held, sems):
        copy.wait()
    send, target, source, count, positions = held
    for j in range(send_out.shape[1]):
        send_out[0, j] = send[0, j]
    lane = lax.axis_index("lane")
    for i in range(3):
        for g in range(0, sz.cells, 8):
            value = own_chunk(sz, lane, positions.at[i], pl.ds(g, 8))
            chunks[pl.ds(i * sz.rows + g, 8), :] = value
    spare = jnp.zeros((1, 128 - sz.cap), F32)
    tasks = jnp.where(lane_iota(1) == 3 * sz.rest + 2 * sz.cap, count[0].astype(F32), 0.0)
    for q, row in enumerate((target, source)):
        wide = jnp.concatenate([row[...].astype(F32), spare], axis=1)
        tasks = tasks + pltpu.roll(wide, 3 * sz.rest + q * sz.cap, 1)
    send_ghosts(sz, send, chunks, out, tasks)


def take_ghosts(sz, arrived, pool, stride, base):
    lanes = lane_iota(1)

    def one(d):
        for g in range(sz.group):
            first = [((d * sz.lanes + lane) * sz.group + g) * 4 for lane in range(sz.lanes)]
            last = [arrived[pl.ds(row + 3, 1), :] for row in first]
            for i in range(3):
                tiles = []
                if sz.main:
                    tiles += [arrived[pl.ds(row + i, 1), :] for row in first]
                for tile in range(sz.rest_tiles):
                    total = jnp.zeros((1, 128), F32)
                    for lane in range(sz.lanes):
                        start = sz.rest * lane
                        if start + sz.rest <= 128 * tile or start >= 128 * tile + 128:
                            continue
                        shift = (start - i * sz.rest) % 128
                        value = pltpu.roll(last[lane], shift, 1) if shift else last[lane]
                        at = lanes + 128 * tile
                        total = jnp.where((at >= start) & (at < start + sz.rest), value, total)
                    tiles.append(total)
                place = pl.ds(i * stride + base + d * sz.group + g, 1)
                pool[place, :] = jnp.concatenate(tiles, axis=1)

    loop(sz.owners, one)


def build_list(sz, lists, tasks):
    total = jnp.int32(0)
    for lane in range(sz.lanes):
        count = lists[lane, 2 * sz.cap]
        for j in range(sz.cap):
            tasks[0, total] = lists[lane, j]
            tasks[1, total] = lists[lane, sz.cap + j]
            total = total + (j < count).astype(jnp.int32)
    for u in range(UNROLL):
        tasks[0, total + u] = jnp.int32(sz.cells)
        tasks[1, total + u] = jnp.int32(0)
    tasks[2, 0] = total
    return total


def own_list(sz, lane, tasks, mine):
    first = lane * sz.share
    total = tasks[2, 0]
    count = jnp.int32(0)
    for t in range(sz.lanes * sz.cap):
        target = tasks[0, t] - first
        mine[0, count] = target
        mine[1, count] = tasks[1, t]
        taken = (target >= 0) & (target < sz.share) & (t < total)
        count = count + taken.astype(jnp.int32)
    for u in range(PAIR):
        mine[0, count + u] = jnp.int32(-1)
        mine[1, count + u] = jnp.int32(0)
    return count


def products(value, bend_high, bend_low):
    high, low = split2(value)
    dot = functools.partial(jnp.dot, preferred_element_type=F32)
    return dot(high, bend_high) + dot(low, bend_high) + dot(high, bend_low)


def make_sources(sz, value, bend_high, bend_low, source_rows, centres, first):
    count = value.shape[0] // 3
    forces = products(value[:, : sz.points], bend_high, bend_low)
    forces = jnp.concatenate(
        [forces, jnp.zeros((3 * count, sz.width - sz.points), F32)], axis=1
    )
    middle = jnp.sum(value, axis=1, keepdims=True) / sz.points
    for g in range(count // 8):
        where = [i * count + 8 * g for i in range(3)]
        middles = [jnp.broadcast_to(middle[w : w + 8], (8, 128)) for w in where]
        middles += [jnp.zeros((8, 128), F32)] * 5
        for i, row in enumerate(middles):
            centres[pl.ds(8 * (first + 8 * g) + i, 8, stride=8), :] = row
        for j in range(sz.tiles):
            cut = slice(128 * j, 128 * j + 128)
            y = [value[w : w + 8, cut] - m for w, m in zip(where, middles)]
            f = [forces[w : w + 8, cut] for w in where]
            norm = y[0] * y[0] + y[1] * y[1] + y[2] * y[2] + REGULARIZE
            along = y[0] * f[0] + y[1] * f[1] + y[2] * f[2]
            one, zero = jnp.ones((8, 128), F32), jnp.zeros((8, 128), F32)
            rows = [y[0], y[1], y[2], norm, one, zero, zero, zero]
            rows += f
            rows += [y[i] * f[k] for i in range(3) for k in range(3)]
            rows += [norm * f[i] + along * y[i] for i in range(3)]
            rows += [along]
            for k, row in enumerate(rows):
                place = pl.ds(SOURCE_ROWS * (first + 8 * g) + k, 8, stride=SOURCE_ROWS)
                source_rows.at[j][place, :] = row


def make_targets(sz, blocks, targets):
    targets[...] = jnp.zeros_like(targets)
    for g in range(sz.cells // 8):
        for i in range(3):
            block = blocks(i, g)
            for j in range(targets.shape[0]):
                cut = slice(128 * j, 128 * j + 128)
                targets.at[j][pl.ds(64 * g + i, 8, stride=8), :] = block[:, cut]


def source_operands(sz, source, source_rows):
    held = [
        source_rows[j, pl.ds(pl.multiple_of(SOURCE_ROWS * source, 8), SOURCE_ROWS), :]
        for j in range(sz.tiles)
    ]
    held = jnp.concatenate(held, axis=1)
    y1, y2, y3 = split3(held[:8])
    y_stack = jnp.concatenate([y1, y1, y2, y2, y1, y3], axis=0).astype(BF16)
    return y_stack, jnp.concatenate(split3(held[8:]), axis=0)


def pieces(points, step):
    starts = list(range(0, max(points // 128 * 128, 1), step))
    return list(zip(starts, starts[1:] + [points]))


def twice(piece, count):
    whole = count // 128 * 128
    parts = [piece[:, :whole].astype(BF16)] * 2 if whole else []
    if whole < count:
        last = piece[:, whole:]
        last = last + pltpu.roll(last, count - whole, 1)
        parts.append(last.astype(BF16)[:, : 2 * (count - whole)])
    return jnp.concatenate(parts, axis=1)


def load_target(j, target, slot, centre, targets, offsets):
    row = lax.broadcasted_iota(jnp.int32, (8, 128), 0)
    x = targets[j, pl.ds(pl.multiple_of(8 * target, 8), 8), :] - centre
    square = x * x
    norm = pltpu.roll(square, 2, 0) + pltpu.roll(square, 3, 0) + pltpu.roll(square, 4, 0)
    side = jnp.where(row == 4, norm, jnp.where(row == 3, 1.0, 0.0))
    x_side = jnp.where(row < 3, -2.0 * x, side)
    x1, x2, x3 = split3(x_side)
    return x, jnp.concatenate([x1, x2, x1, x2, x3, x1], axis=0).astype(BF16)


def distances(one_stack, other_stack):
    return jnp.dot(one_stack, other_stack, preferred_element_type=F32)


def weights(shifted):
    inverse = lax.rsqrt(shifted)
    return split2(inverse * inverse * inverse)


def fold(result):
    return result[:SUM_ROWS] + result[SUM_ROWS : 2 * SUM_ROWS] + result[2 * SUM_ROWS :]


def skewed(stages, skew):
    asked = []
    for q, (ask, _) in enumerate(stages):
        asked.append(ask())
        if q >= skew:
            stages[q - skew][1](asked[q - skew])
            asked[q - skew] = None
    for q in range(max(len(stages) - skew, 0), len(stages)):
        stages[q][1](asked[q])


def adder(totals, key):
    def add(value):
        totals[key] = totals[key] + value if key in totals else value

    return add


def wide_piece(operands, begin, first, end, add):
    def ask():
        _, y_turned, _, blocks = operands()
        return distances(y_turned[first:end], blocks[begin])

    def take(shifted):
        m_stack = operands()[2]
        high, low = weights(shifted)
        whole = (end - first) // 128 * 128
        parts = [high[:whole], low[:whole]] if whole else []
        parts += [high[whole:], low[whole:]] if whole < end - first else []
        stack = jnp.concatenate(parts, axis=0)
        m_piece = twice(m_stack[:, first : up(end, 128)], end - first)
        add(jnp.dot(m_piece, stack, preferred_element_type=F32))

    return ask, take


def rest_piece(operands, begin, add):
    def ask():
        y_stack, _, _, blocks = operands()
        return distances(blocks[begin], y_stack)

    def take(shifted):
        high, low = weights(shifted)
        m_whole = operands()[2].astype(BF16)
        turned = (((1,), (1,)), ((), ()))
        result = lax.dot_general(m_whole, high, turned, preferred_element_type=F32)
        add(result + lax.dot_general(m_whole, low, turned, preferred_element_type=F32))

    return ask, take


def store_sums(slots, slot, j, x, result, offsets, sums):
    offsets.at[j][pl.ds(slot, 8, stride=slots), :] = x
    for h in range(0, SUM_ROWS, 8):
        sums.at[j][pl.ds(h * slots + slot, 8, stride=slots), :] = result[h : h + 8]


def mark(slot, target, hot):
    hot[pl.ds(slot, 1), :] = jnp.where(lane_iota(1) == target, 1.0, 0.0)


def combine(sz, slots, first, total, offsets, sums, speeds):
    live = lax.broadcasted_iota(jnp.int32, (8, 128), 0) + first < total
    for j in range(offsets.shape[0]):
        x = [offsets[j, pl.ds(i * slots + first, 8), :] for i in range(3)]
        s = [sums[j, pl.ds(k * slots + first, 8), :] for k in range(SUM_ROWS)]
        a, b, c = s[:3], [s[3:6], s[6:9], s[9:12]], s[12:15]
        norm = x[0] * x[0] + x[1] * x[1] + x[2] * x[2] + REGULARIZE
        along = x[0] * a[0] + x[1] * a[1] + x[2] * a[2] - s[15]
        for i in range(3):
            speed = norm * a[i] + c[i] + along * x[i]
            for k in range(3):
                speed = speed - x[k] * (2.0 * b[k][i] + b[i][k])
            speed = jnp.where(live, speed / sz.points, 0.0)
            speeds[i, pl.ds(first, 8), 128 * j : 128 * j + 128] = speed


def add_up(sz, slots, total, rows, offsets, sums, speeds, hot):
    def eight(q, carry):
        combine(sz, slots, pl.multiple_of(8 * q, 8), total, offsets, sums, speeds)
        return carry

    lax.fori_loop(0, lax.div(total + 7, 8), eight, 0)
    one_hot = hot[...].astype(BF16)
    result = []
    for i in range(3):
        first, second, third = split3(speeds[i])
        parts = [
            lax.dot_general(
                one_hot, part.astype(BF16), (((0,), (0,)), ((), ())), preferred_element_type=F32
            )
            for part in (first, second, third)
        ]
        result.append((parts[0] + parts[1] + parts[2])[:rows])
    return result


def several_tasks(sz, slots, picks, marks, main, rest, wide, step, skew, refs):
    source_rows, centres, targets, offsets, sums, hot = refs

    def task(slot, pick, target_mark):
        target, source = pick
        made, parts, points = [], {}, []

        def operands():
            if made:
                return made[0]
            y_stack, m_stack = source_operands(sz, source, source_rows)
            centre = centres[pl.ds(pl.multiple_of(8 * source, 8), 8), :]
            points.extend(
                load_target(j, target, slot, centre, targets, offsets)
                for j in range(targets.shape[0])
            )
            blocks = {}
            for begin in range(0, main, wide):
                stack = [stack for _, stack in points[begin // 128 : (begin + wide) // 128]]
                blocks[begin] = jnp.concatenate(stack, axis=1)
            if rest:
                blocks[main] = jnp.transpose(points[main // 128][1])[:rest]
            made.append((y_stack, jnp.transpose(y_stack), m_stack, blocks))
            return made[0]

        def finish():
            results = [fold(parts[begin]) for begin in range(0, main, wide)]
            if rest:
                spare = jnp.zeros((SUM_ROWS, 128 - rest), F32)
                results.append(jnp.concatenate([fold(parts[main]), spare], axis=1))
            result = jnp.concatenate(results, axis=1)
            for j in range(targets.shape[0]):
                cut = result[:, 128 * j : 128 * j + 128]
                store_sums(offsets.shape[1] // 8, slot, j, points[j][0], cut, offsets, sums)
            mark(slot, target_mark, hot)

        own = []
        for begin in range(0, main, wide):
            for first, last in pieces(sz.points, step):
                own.append(wide_piece(operands, begin, first, last, adder(parts, begin)))
        if rest:
            own.insert(len(own) // 2, rest_piece(operands, main, adder(parts, main)))
        ask, take = own[-1]

        def last_take(shifted):
            take(shifted)
            finish()

        own[-1] = (ask, last_take)
        return own, operands

    made = [task(slot, pick, m) for slot, pick, m in zip(slots, picks, marks)]
    for (own, _), (_, after) in zip(made, made[1:]):
        ask, take = own[0]

        def ask_and_prepare(ask=ask, after=after):
            shifted = ask()
            after()
            return shifted

        own[0] = (ask_and_prepare, take)
    skewed([stage for own, _ in made for stage in own], skew)


def tiles_of_chunk(sz, total, tasks, *refs):
    def several(q, carry):
        slots = [q * UNROLL + u for u in range(UNROLL)]
        picks = [(tasks[0, slot], tasks[1, slot]) for slot in slots]
        marks = [target for target, _ in picks]
        several_tasks(sz, slots, picks, marks, sz.main, sz.rest, 128, 256, 4, refs)
        return carry

    lax.fori_loop(0, lax.div(total + UNROLL - 1, UNROLL), several, 0)


def tiles_of_cells(sz, base, total, mine, *refs):
    main = 256 * (sz.points // 256)

    def several(q, carry):
        slots = [q * PAIR + u for u in range(PAIR)]
        marks = [mine[0, slot] for slot in slots]
        picks = [(jnp.maximum(mark, 0) + base, mine[1, s]) for mark, s in zip(marks, slots)]
        several_tasks(sz, slots, picks, marks, main, sz.points - main, 256, 128, 3, refs)
        return carry

    lax.fori_loop(0, lax.div(total + PAIR - 1, PAIR), several, 0)


def packed(sz, blocks):
    rows = [b[:, : sz.main] for b in blocks] if sz.main else []
    lanes = lane_iota(8)
    for p in range(0, len(blocks), sz.per_pack):
        total = jnp.zeros((8, 128), F32)
        for q, block in enumerate(blocks[p : p + sz.per_pack]):
            rest = jnp.where(lanes < sz.rest, block[:, sz.main : sz.main + 128], 0.0)
            total = total + (pltpu.roll(rest, q * sz.rest, 1) if q else rest)
        rows.append(total)
    return rows


def store_packed(sz, out, blocks):
    first = 0
    count = len(blocks)
    values = packed(sz, blocks)
    if sz.main:
        for b in range(count):
            for m in range(sz.main // 128):
                out[pl.ds(first, 8), :] = values[b][:, 128 * m : 128 * m + 128]
                first += 8
        values = values[count:]
    for value in values:
        out[pl.ds(first, 8), :] = value
        first += 8


def place_packed(sz, lane, arrived, count, store_main, add_rest):
    first = 0
    if sz.main:
        for b in range(count):
            for m in range(sz.main // 128):
                store_main(b, m, arrived[pl.ds(first, 8), :])
                first += 8
    start = sz.rest * lane
    lanes = lane_iota(8)
    for b in range(count):
        pack, q = divmod(b, sz.per_pack)
        value = arrived[pl.ds(first + 8 * pack, 8), :]
        value = pltpu.roll(value, lax.rem(start - q * sz.rest + 128, 128), 1)
        for tile in range(sz.rest_tiles):
            inside = (lanes + 128 * tile >= start) & (lanes + 128 * tile < start + sz.rest)
            add_rest(b, tile, jnp.where(inside, value, 0.0))


def source_kernel(sz, *refs):
    inputs, (high_out, low_out, source_rows, centres), held, sems = (
        refs[:2],
        refs[2:6],
        refs[6:8],
        refs[8],
    )
    for copy in fetch(inputs, held, sems):
        copy.wait()
    positions, bend = held
    high_out[...], low_out[...] = split2(bend[...])
    value = jnp.concatenate([positions[i] for i in range(3)], axis=0)
    value = jnp.concatenate(
        [value, jnp.zeros((3 * sz.cells, sz.width - sz.points), F32)], axis=1
    )
    make_sources(sz, value, high_out[...], low_out[...], source_rows, centres, 0)


def first_kernel(sz, *refs):
    arrived, high, low, inputs = refs[0], refs[1], refs[2], refs[3:7]
    outputs, refs = refs[7:10], refs[10:]
    source_rows, centres, targets, offsets, sums, speeds, hot, moved, pool = refs[:9]
    send, positions, staged, lists, chunk_out, ghost_out, tasks, sems = refs[9:]
    me, lane = lax.axis_index("space"), lax.axis_index("lane")
    own_rows = source_rows.at[:, pl.ds(0, SOURCE_ROWS * sz.cells)]
    own_centres = centres.at[pl.ds(0, 8 * sz.cells)]
    copies = fetch(inputs, [send, positions, own_rows, own_centres], sems)
    for other in range(sz.lanes):
        row = ((me * sz.lanes + other) * sz.group) * 4 + 3
        value = pltpu.roll(arrived[pl.ds(row, 1), :], 128 - 3 * sz.rest, 1)
        staged[pl.ds(other, 1), :] = value.astype(jnp.int32)
    copies += fetch([staged], [lists], sems.at[pl.ds(4, 1)])
    pool[...] = jnp.zeros_like(pool)
    take_ghosts(sz, arrived, pool, up(sz.owners * sz.group, 8), 0)
    hot[...] = jnp.zeros_like(hot)
    speeds[...] = jnp.zeros_like(speeds)
    make_sources(sz, pool[...], high[...], low[...], source_rows, centres, sz.cells)
    for copy in copies[:2]:
        copy.wait()
    make_targets(
        sz, lambda i, g: own_chunk(sz, lane, positions.at[i], pl.ds(8 * g, 8)), targets
    )
    copies[4].wait()
    total = build_list(sz, lists, tasks)
    for copy in copies[2:4]:
        copy.wait()
    copies = fetch([tasks], outputs[2:], sems)
    tiles_of_chunk(sz, total, tasks, source_rows, centres, targets, offsets, sums, hot)
    velocity = add_up(sz, sz.slots, total, sz.cells, offsets, sums, speeds, hot)
    blocks = []
    for i in range(3):
        for g in range(0, sz.cells, 8):
            chunk = own_chunk(sz, lane, positions.at[i], pl.ds(g, 8))
            block = chunk + TIME_STEP * velocity[i][g : g + 8]
            moved[pl.ds(i * sz.rows + g, 8), :] = block
            blocks.append(block)
    store_packed(sz, chunk_out, blocks)
    copies += fetch([chunk_out], outputs[:1], sems.at[pl.ds(1, 1)])
    send_ghosts(sz, send, moved, ghost_out, jnp.zeros((1, 128), F32))
    copies += fetch([ghost_out], outputs[1:2], sems.at[pl.ds(2, 1)])
    for copy in copies:
        copy.wait()


def second_kernel(sz, *refs):
    (arrived, high, low), refs = refs[:3], refs[3:]
    others, refs = refs[: sz.lanes - 1], refs[sz.lanes - 1 :]
    inputs, (moved_out, velocity_out), refs = refs[:2], refs[2:4], refs[4:]
    source_rows, centres, targets, offsets, sums, speeds, hot, pool, mine = refs[:9]
    tasks, chunk, sems = refs[9:]
    copies = fetch(inputs, [tasks, chunk], sems)
    chunks = [chunk, *others]
    hot[...] = jnp.zeros_like(hot)
    speeds[...] = jnp.zeros_like(speeds)
    lane = lax.axis_index("lane")
    pool[...] = jnp.zeros_like(pool)
    copies[0].wait()
    total = own_list(sz, lane, tasks, mine)
    copies[1].wait()
    per = sz.cells // 8
    for k in range(sz.lanes):
        other = lane ^ k

        def row_of(b):
            return (b // per) * sz.pool + 8 * (b % per)

        def store_main(b, m, value):
            cut = pl.ds(pl.multiple_of(other * sz.main + 128 * m, 128), 128)
            pool[pl.ds(row_of(b), 8), cut] = value

        def add_rest(b, tile, value):
            offset = sz.main * sz.lanes + 128 * tile
            cut = (pl.ds(row_of(b), 8), slice(offset, offset + 128))
            pool[cut] = pool[cut] + value

        place_packed(sz, other, chunks[k], 3 * per, store_main, add_rest)
    take_ghosts(sz, arrived, pool, sz.pool, sz.cells)
    make_sources(sz, pool[...], high[...], low[...], source_rows, centres, 0)
    make_targets(sz, lambda i, g: pool[pl.ds(i * sz.pool + 8 * g, 8), :], targets)
    first = lane * sz.share
    tiles_of_cells(sz, first, total, mine, source_rows, centres, targets, offsets, sums, hot)
    velocity = add_up(sz, sz.own, total, up(sz.share, 8), offsets, sums, speeds, hot)
    for i in range(3):
        speed = velocity[i]
        moved = share_rows(sz, pool, i * sz.pool, lane) + TIME_STEP * speed
        velocity_out[i] = speed[: sz.share, : sz.points]
        moved_out[i] = moved[: sz.share, : sz.points]


def share_rows(sz, ref, base, lane):
    if sz.share % 8 == 0:
        return ref[pl.ds(pl.multiple_of(base + lane * sz.share, 8), sz.share), :]
    rows = [ref[pl.ds(base + lane * sz.share + c, 1), :] for c in range(sz.share)]
    rows.append(jnp.zeros((8 - sz.share, rows[0].shape[1]), F32))
    return jnp.concatenate(rows, axis=0)


def scratch(sz, tiles, slots):
    return [
        pltpu.VMEM((sz.tiles, SOURCE_ROWS * sz.pool, 128), F32),
        pltpu.VMEM((8 * sz.pool, 128), F32),
        pltpu.VMEM((tiles, 8 * sz.rows, 128), F32),
        pltpu.VMEM((tiles, 8 * slots, 128), F32),
        pltpu.VMEM((tiles, SUM_ROWS * slots, 128), F32),
        pltpu.VMEM((3, slots, 128 * tiles), F32),
        pltpu.VMEM((slots, 128), F32),
    ]


def swap(value, axis, size, k):
    return lax.ppermute(value, axis, [(d, d ^ k) for d in range(size)])


def gather_by_halves(value, axis, size):
    held = {0: value}
    far = size // 2
    while far:
        held.update({k ^ far: swap(held[k], axis, size, far) for k in list(held)})
        far //= 2
    return [held[k] for k in range(1, size)]


def in_hbm(value):
    return pltpu.with_memory_space_constraint(value, pltpu.HBM)


def shards(positions, bend_op, send_list, task_target, task_source, task_count):
    owners, lanes = lax.axis_size("space"), lax.axis_size("lane")
    cells, points = positions.shape[0], positions.shape[2]
    sz = sizes(owners, lanes, cells, points, task_target.shape[1], send_list.shape[1])
    params = pltpu.CompilerParams(vmem_limit_bytes=min(6 * lanes, 40) << 20)
    shape = jax.ShapeDtypeStruct
    both = ("space", "lane")
    by_component = jnp.transpose(positions, (1, 0, 2))
    list_rows = up(lanes, 8)
    slot_shape = shape((4 * sz.group * owners * lanes, 128), F32)
    leaving, send = pl.pallas_call(
        functools.partial(pick_kernel, sz),
        out_shape=[slot_shape, shape(send_list.shape, jnp.int32)],
        in_specs=[HBM] * 5,
        out_specs=[VMEM, SMEM],
        scratch_shapes=[
            pltpu.SMEM(send_list.shape, jnp.int32),
            pltpu.VMEM(task_target.shape, jnp.int32),
            pltpu.VMEM(task_source.shape, jnp.int32),
            pltpu.SMEM(task_count.shape, jnp.int32),
            pltpu.VMEM(by_component.shape, F32),
            pltpu.VMEM((3 * sz.rows, sz.chunk_wide), F32),
            pltpu.SemaphoreType.DMA((5,)),
        ],
        compiler_params=pltpu.CompilerParams(vmem_limit_bytes=60 << 20),
        name="pick_cells",
    )(send_list, task_target, task_source, task_count, by_component)
    arrived = lax.all_to_all(leaving, both, split_axis=0, concat_axis=0, tiled=True)
    high, low, own_rows, own_centres = pl.pallas_call(
        functools.partial(source_kernel, sz),
        out_shape=[
            shape(bend_op.shape, BF16),
            shape(bend_op.shape, BF16),
            shape((sz.tiles, SOURCE_ROWS * cells, 128), F32),
            shape((8 * cells, 128), F32),
        ],
        in_specs=[HBM] * 2,
        out_specs=[VMEM] * 4,
        scratch_shapes=[
            pltpu.VMEM(by_component.shape, F32),
            pltpu.VMEM(bend_op.shape, F32),
            pltpu.SemaphoreType.DMA((2,)),
        ],
        compiler_params=params,
        cost_estimate=pl.CostEstimate(flops=10**9, bytes_accessed=10**7, transcendentals=0),
        name="first_sources",
    )(in_hbm(by_component), in_hbm(bend_op))
    chunk_shape = (pack_rows(sz, cells), 128)
    chunk, leaving, tasks = pl.pallas_call(
        functools.partial(first_kernel, sz),
        out_shape=[
            pltpu.HBM(chunk_shape, F32),
            pltpu.HBM(slot_shape.shape, F32),
            pltpu.HBM((3, sz.slots), jnp.int32),
        ],
        in_specs=[VMEM] * 3 + [HBM] * 2 + [ANY] * 2,
        out_specs=[HBM] * 3,
        scratch_shapes=scratch(sz, sz.chunk_tiles, sz.slots)
        + [
            pltpu.VMEM((3 * sz.rows, sz.chunk_wide), F32),
            pltpu.VMEM((3 * up(sz.owners * sz.group, 8), sz.width), F32),
            pltpu.SMEM(send_list.shape, jnp.int32),
            pltpu.VMEM(by_component.shape, F32),
            pltpu.VMEM((list_rows, 128), jnp.int32),
            pltpu.SMEM((list_rows, 128), jnp.int32),
            pltpu.VMEM(chunk_shape, F32),
            pltpu.VMEM(slot_shape.shape, F32),
            pltpu.SMEM((3, sz.slots), jnp.int32),
            pltpu.SemaphoreType.DMA((5,)),
        ],
        compiler_params=params,
        name="first_step",
    )(arrived, high, low, in_hbm(send), in_hbm(by_component), own_rows, own_centres)
    arrived = lax.all_to_all(leaving, both, split_axis=0, concat_axis=0, tiled=True)
    chunks = gather_by_halves(chunk, "lane", lanes)
    result = shape((3, sz.share, points), F32)
    outputs = pl.pallas_call(
        functools.partial(second_kernel, sz),
        out_shape=[result, result],
        in_specs=[VMEM] * (lanes + 2) + [HBM] * 2,
        out_specs=[VMEM] * 2,
        scratch_shapes=scratch(sz, sz.tiles, sz.own)
        + [
            pltpu.VMEM((3 * sz.pool, sz.width), F32),
            pltpu.SMEM((2, sz.own + 8), jnp.int32),
            pltpu.SMEM(tasks.shape, jnp.int32),
            pltpu.VMEM(chunk.shape, F32),
            pltpu.SemaphoreType.DMA((2,)),
        ],
        compiler_params=params,
        name="second_step",
    )(arrived, high, low, *chunks, in_hbm(tasks), in_hbm(chunk))
    return tuple(jnp.transpose(output, (1, 0, 2)) for output in outputs)


def solution(mesh):
    in_specs = (
        P("space", None, None),
        P(),
        P("space", None),
        P(("space", "lane"), None),
        P(("space", "lane"), None),
        P(("space", "lane")),
    )
    out_specs = (P(("space", "lane"), None, None), P(("space", "lane"), None, None))
    return jax.shard_map(shards, mesh=mesh, in_specs=in_specs, out_specs=out_specs, check_vma=False)
```

```python
import functools
from types import SimpleNamespace

import jax
import jax.numpy as jnp
from jax import lax
from jax.experimental import pallas as pl
from jax.experimental.pallas import tpu as pltpu
from jax.sharding import PartitionSpec as P

REGULARIZE = 0.25
TIME_STEP = 0.5
UNROLL = 11
PAIR = 2
SOURCE_ROWS = 24
SUM_ROWS = 16

F32 = jnp.float32
BF16 = jnp.bfloat16
VMEM = pl.BlockSpec(memory_space=pltpu.VMEM)
SMEM = pl.BlockSpec(memory_space=pltpu.SMEM)
HBM = pl.BlockSpec(memory_space=pltpu.HBM)
ANY = pl.BlockSpec(memory_space=pl.ANY)


def up(value, step):
    return -(-value // step) * step


def sizes(owners, lanes, cells, points, cap, listed):
    main = 128 * (points // (128 * lanes))
    rest = (points - main * lanes) // lanes
    group = listed // owners
    pool = up(cells + listed, 8)
    per_pack = 128 // rest
    return SimpleNamespace(
        owners=owners,
        lanes=lanes,
        cells=cells,
        points=points,
        cap=cap,
        group=group,
        width=up(points, 128),
        tiles=up(points, 128) // 128,
        main=main,
        rest=rest,
        rest_tiles=up(rest * lanes, 128) // 128,
        chunk=main + rest,
        chunk_wide=main + up(rest, 128),
        chunk_tiles=(main + up(rest, 128)) // 128,
        per_pack=per_pack,
        pool=pool,
        share=cells // lanes,
        slots=up(lanes * cap + UNROLL, 8),
        rows=cells + 8,
        own=up(lanes * cap + PAIR, 8),
    )


def pack_rows(sz, rows):
    return (3 * rows * sz.main // 128) + 8 * up(3 * rows // 8, sz.per_pack) // sz.per_pack


def split2(value):
    high = value.astype(BF16)
    return high, (value - high.astype(F32)).astype(BF16)


def split3(value):
    first = value.astype(BF16).astype(F32)
    left = value - first
    second = left.astype(BF16).astype(F32)
    return first, second, left - second


def lane_iota(rows):
    return lax.broadcasted_iota(jnp.int32, (rows, 128), 1)


def fetch(sources, targets, sems):
    copies = [
        pltpu.make_async_copy(source, target, sems.at[q])
        for q, (source, target) in enumerate(zip(sources, targets))
    ]
    for copy in copies:
        copy.start()
    return copies


def loop(count, body):
    if count <= 8:
        for q in range(count):
            body(q)
    else:

        def step(q, carry):
            body(q)
            return carry

        lax.fori_loop(0, count, step, 0)


def own_chunk(sz, lane, ref, rows):
    parts = []
    if sz.main:
        parts.append(ref[rows, pl.ds(pl.multiple_of(lane * sz.main, 128), sz.main)])
    start = sz.rest * lane
    lanes = lane_iota(8)
    rest = jnp.zeros((8, 128), F32)
    for tile in range(sz.rest_tiles):
        offset = sz.main * sz.lanes + 128 * tile
        block = ref[rows, offset : min(offset + 128, ref.shape[-1])]
        if block.shape[1] < 128:
            block = jnp.concatenate([block, jnp.zeros((8, 128 - block.shape[1]), F32)], axis=1)
        inside = (lanes + 128 * tile >= start) & (lanes + 128 * tile < start + sz.rest)
        rest = rest + jnp.where(inside, block, 0.0)
    rest = pltpu.roll(rest, lax.rem(128 * sz.rest_tiles - start, 128), 1)
    parts.append(rest)
    return jnp.concatenate(parts, axis=1) if len(parts) > 1 else parts[0]


def send_ghosts(sz, send, chunks, out, tasks):
    lanes = lane_iota(1)

    def one(d):
        for g in range(sz.group):
            cell = send[0, d * sz.group + g]
            rows = []
            last = tasks
            for i in range(3):
                row = chunks[pl.ds(i * sz.rows + cell, 1), :]
                rows.append(row[:, :128] if sz.main else jnp.zeros((1, 128), F32))
                piece = jnp.where(lanes < sz.rest, row[:, sz.main : sz.main + 128], 0.0)
                last = last + (pltpu.roll(piece, i * sz.rest, 1) if i else piece)
            rows.append(last)
            for other in range(sz.lanes):
                first = ((d * sz.lanes + other) * sz.group + g) * 4
                for q, row in enumerate(rows):
                    out[pl.ds(first + q, 1), :] = row

    loop(sz.owners, one)


def pick_kernel(sz, *refs):
    inputs, (out, send_out), held, (chunks, sems) = refs[:5], refs[5:7], refs[7:12], refs[12:]
    for copy in fetch(inputs, held, sems):
        copy.wait()
    send, target, source, count, positions = held
    for j in range(send_out.shape[1]):
        send_out[0, j] = send[0, j]
    lane = lax.axis_index("lane")
    for i in range(3):
        for g in range(0, sz.cells, 8):
            value = own_chunk(sz, lane, positions.at[i], pl.ds(g, 8))
            chunks[pl.ds(i * sz.rows + g, 8), :] = value
    spare = jnp.zeros((1, 128 - sz.cap), F32)
    tasks = jnp.where(lane_iota(1) == 3 * sz.rest + 2 * sz.cap, count[0].astype(F32), 0.0)
    for q, row in enumerate((target, source)):
        wide = jnp.concatenate([row[...].astype(F32), spare], axis=1)
        tasks = tasks + pltpu.roll(wide, 3 * sz.rest + q * sz.cap, 1)
    send_ghosts(sz, send, chunks, out, tasks)


def take_ghosts(sz, arrived, pool, stride, base):
    lanes = lane_iota(1)

    def one(d):
        for g in range(sz.group):
            first = [((d * sz.lanes + lane) * sz.group + g) * 4 for lane in range(sz.lanes)]
            last = [arrived[pl.ds(row + 3, 1), :] for row in first]
            for i in range(3):
                tiles = []
                if sz.main:
                    tiles += [arrived[pl.ds(row + i, 1), :] for row in first]
                for tile in range(sz.rest_tiles):
                    total = jnp.zeros((1, 128), F32)
                    for lane in range(sz.lanes):
                        start = sz.rest * lane
                        if start + sz.rest <= 128 * tile or start >= 128 * tile + 128:
                            continue
                        shift = (start - i * sz.rest) % 128
                        value = pltpu.roll(last[lane], shift, 1) if shift else last[lane]
                        at = lanes + 128 * tile
                        total = jnp.where((at >= start) & (at < start + sz.rest), value, total)
                    tiles.append(total)
                place = pl.ds(i * stride + base + d * sz.group + g, 1)
                pool[place, :] = jnp.concatenate(tiles, axis=1)

    loop(sz.owners, one)


def build_list(sz, lists, tasks):
    total = jnp.int32(0)
    for lane in range(sz.lanes):
        count = lists[lane, 2 * sz.cap]
        for j in range(sz.cap):
            tasks[0, total] = lists[lane, j]
            tasks[1, total] = lists[lane, sz.cap + j]
            total = total + (j < count).astype(jnp.int32)
    for u in range(UNROLL):
        tasks[0, total + u] = jnp.int32(sz.cells)
        tasks[1, total + u] = jnp.int32(0)
    tasks[2, 0] = total
    return total


def own_list(sz, lane, tasks, mine, low, high):
    first = lane * sz.share
    total = tasks[2, 0]
    count = jnp.int32(0)
    for t in range(sz.lanes * sz.cap):
        target = tasks[0, t] - first
        source = tasks[1, t]
        mine[0, count] = target
        mine[1, count] = source - low
        taken = (target >= 0) & (target < sz.share) & (t < total)
        taken = taken & (source >= low) & (source < high)
        count = count + taken.astype(jnp.int32)
    for u in range(PAIR):
        mine[0, count + u] = jnp.int32(-1)
        mine[1, count + u] = jnp.int32(0)
    return count


def products(value, bend_high, bend_low):
    high, low = split2(value)
    dot = functools.partial(jnp.dot, preferred_element_type=F32)
    return dot(high, bend_high) + dot(low, bend_high) + dot(high, bend_low)


def make_sources(sz, value, bend_high, bend_low, source_rows, centres, first):
    count = value.shape[0] // 3
    forces = products(value[:, : sz.points], bend_high, bend_low)
    forces = jnp.concatenate(
        [forces, jnp.zeros((3 * count, sz.width - sz.points), F32)], axis=1
    )
    middle = jnp.sum(value, axis=1, keepdims=True) / sz.points
    for g in range(count // 8):
        where = [i * count + 8 * g for i in range(3)]
        middles = [jnp.broadcast_to(middle[w : w + 8], (8, 128)) for w in where]
        middles += [jnp.zeros((8, 128), F32)] * 5
        for i, row in enumerate(middles):
            centres[pl.ds(8 * (first + 8 * g) + i, 8, stride=8), :] = row
        for j in range(sz.tiles):
            cut = slice(128 * j, 128 * j + 128)
            y = [value[w : w + 8, cut] - m for w, m in zip(where, middles)]
            f = [forces[w : w + 8, cut] for w in where]
            norm = y[0] * y[0] + y[1] * y[1] + y[2] * y[2] + REGULARIZE
            along = y[0] * f[0] + y[1] * f[1] + y[2] * f[2]
            one, zero = jnp.ones((8, 128), F32), jnp.zeros((8, 128), F32)
            rows = [y[0], y[1], y[2], norm, one, zero, zero, zero]
            rows += f
            rows += [y[i] * f[k] for i in range(3) for k in range(3)]
            rows += [norm * f[i] + along * y[i] for i in range(3)]
            rows += [along]
            for k, row in enumerate(rows):
                place = pl.ds(SOURCE_ROWS * (first + 8 * g) + k, 8, stride=SOURCE_ROWS)
                source_rows.at[j][place, :] = row


def make_targets(sz, blocks, targets):
    targets[...] = jnp.zeros_like(targets)
    for i in range(3):
        for g in range(blocks[i].shape[0] // 8):
            block = blocks[i][8 * g : 8 * g + 8]
            for j in range(targets.shape[0]):
                cut = slice(128 * j, 128 * j + 128)
                targets.at[j][pl.ds(64 * g + i, 8, stride=8), :] = block[:, cut]


def source_operands(sz, source, source_rows):
    held = [
        source_rows[j, pl.ds(pl.multiple_of(SOURCE_ROWS * source, 8), SOURCE_ROWS), :]
        for j in range(sz.tiles)
    ]
    held = jnp.concatenate(held, axis=1)
    y1, y2, y3 = split3(held[:8])
    y_stack = jnp.concatenate([y1, y1, y2, y2, y1, y3], axis=0).astype(BF16)
    return y_stack, jnp.concatenate(split3(held[8:]), axis=0)


def pieces(points, step):
    starts = list(range(0, max(points // 128 * 128, 1), step))
    return list(zip(starts, starts[1:] + [points]))


def twice(piece, count):
    whole = count // 128 * 128
    parts = [piece[:, :whole].astype(BF16)] * 2 if whole else []
    if whole < count:
        last = piece[:, whole:]
        last = last + pltpu.roll(last, count - whole, 1)
        parts.append(last.astype(BF16)[:, : 2 * (count - whole)])
    return jnp.concatenate(parts, axis=1)


def load_target(j, target, slot, centre, targets, offsets):
    row = lax.broadcasted_iota(jnp.int32, (8, 128), 0)
    x = targets[j, pl.ds(pl.multiple_of(8 * target, 8), 8), :] - centre
    square = x * x
    norm = pltpu.roll(square, 2, 0) + pltpu.roll(square, 3, 0) + pltpu.roll(square, 4, 0)
    side = jnp.where(row == 4, norm, jnp.where(row == 3, 1.0, 0.0))
    x_side = jnp.where(row < 3, -2.0 * x, side)
    x1, x2, x3 = split3(x_side)
    return x, jnp.concatenate([x1, x2, x1, x2, x3, x1], axis=0).astype(BF16)


def distances(one_stack, other_stack):
    return jnp.dot(one_stack, other_stack, preferred_element_type=F32)


def weights(shifted):
    inverse = lax.rsqrt(shifted)
    return split2(inverse * inverse * inverse)


def fold(result):
    return result[:SUM_ROWS] + result[SUM_ROWS : 2 * SUM_ROWS] + result[2 * SUM_ROWS :]


def skewed(stages, skew):
    asked = []
    for q, (ask, _) in enumerate(stages):
        asked.append(ask())
        if q >= skew:
            stages[q - skew][1](asked[q - skew])
            asked[q - skew] = None
    for q in range(max(len(stages) - skew, 0), len(stages)):
        stages[q][1](asked[q])


def adder(totals, key):
    def add(value):
        totals[key] = totals[key] + value if key in totals else value

    return add


def wide_piece(operands, begin, first, end, add):
    def ask():
        _, y_turned, _, blocks = operands()
        return distances(y_turned[first:end], blocks[begin])

    def take(shifted):
        m_stack = operands()[2]
        high, low = weights(shifted)
        whole = (end - first) // 128 * 128
        parts = [high[:whole], low[:whole]] if whole else []
        parts += [high[whole:], low[whole:]] if whole < end - first else []
        stack = jnp.concatenate(parts, axis=0)
        m_piece = twice(m_stack[:, first : up(end, 128)], end - first)
        add(jnp.dot(m_piece, stack, preferred_element_type=F32))

    return ask, take


def rest_piece(operands, begin, add):
    def ask():
        y_stack, _, _, blocks = operands()
        return distances(blocks[begin], y_stack)

    def take(shifted):
        high, low = weights(shifted)
        m_whole = operands()[2].astype(BF16)
        turned = (((1,), (1,)), ((), ()))
        result = lax.dot_general(m_whole, high, turned, preferred_element_type=F32)
        add(result + lax.dot_general(m_whole, low, turned, preferred_element_type=F32))

    return ask, take


def store_sums(slots, slot, j, x, result, offsets, sums):
    offsets.at[j][pl.ds(slot, 8, stride=slots), :] = x
    for h in range(0, SUM_ROWS, 8):
        sums.at[j][pl.ds(h * slots + slot, 8, stride=slots), :] = result[h : h + 8]


def mark(slot, target, hot):
    hot[pl.ds(slot, 1), :] = jnp.where(lane_iota(1) == target, 1.0, 0.0)


def combine(sz, slots, first, total, offsets, sums, speeds):
    live = lax.broadcasted_iota(jnp.int32, (8, 128), 0) + first < total
    for j in range(offsets.shape[0]):
        x = [offsets[j, pl.ds(i * slots + first, 8), :] for i in range(3)]
        s = [sums[j, pl.ds(k * slots + first, 8), :] for k in range(SUM_ROWS)]
        a, b, c = s[:3], [s[3:6], s[6:9], s[9:12]], s[12:15]
        norm = x[0] * x[0] + x[1] * x[1] + x[2] * x[2] + REGULARIZE
        along = x[0] * a[0] + x[1] * a[1] + x[2] * a[2] - s[15]
        for i in range(3):
            speed = norm * a[i] + c[i] + along * x[i]
            for k in range(3):
                speed = speed - x[k] * (2.0 * b[k][i] + b[i][k])
            speed = jnp.where(live, speed / sz.points, 0.0)
            speeds[i, pl.ds(first, 8), 128 * j : 128 * j + 128] = speed


def add_up(sz, slots, total, rows, offsets, sums, speeds, hot):
    def eight(q, carry):
        combine(sz, slots, pl.multiple_of(8 * q, 8), total, offsets, sums, speeds)
        return carry

    lax.fori_loop(0, lax.div(total + 7, 8), eight, 0)
    one_hot = hot[...].astype(BF16)
    result = []
    for i in range(3):
        first, second, third = split3(speeds[i])
        parts = [
            lax.dot_general(
                one_hot, part.astype(BF16), (((0,), (0,)), ((), ())), preferred_element_type=F32
            )
            for part in (first, second, third)
        ]
        result.append((parts[0] + parts[1] + parts[2])[:rows])
    return result


def several_tasks(sz, slots, picks, marks, main, rest, wide, step, skew, refs):
    source_rows, centres, targets, offsets, sums, hot = refs

    def task(slot, pick, target_mark):
        target, source = pick
        made, parts, points = [], {}, []

        def operands():
            if made:
                return made[0]
            y_stack, m_stack = source_operands(sz, source, source_rows)
            centre = centres[pl.ds(pl.multiple_of(8 * source, 8), 8), :]
            points.extend(
                load_target(j, target, slot, centre, targets, offsets)
                for j in range(targets.shape[0])
            )
            blocks = {}
            for begin in range(0, main, wide):
                stack = [stack for _, stack in points[begin // 128 : (begin + wide) // 128]]
                blocks[begin] = jnp.concatenate(stack, axis=1)
            if rest:
                blocks[main] = jnp.transpose(points[main // 128][1])[:rest]
            made.append((y_stack, jnp.transpose(y_stack), m_stack, blocks))
            return made[0]

        def finish():
            results = [fold(parts[begin]) for begin in range(0, main, wide)]
            if rest:
                spare = jnp.zeros((SUM_ROWS, 128 - rest), F32)
                results.append(jnp.concatenate([fold(parts[main]), spare], axis=1))
            result = jnp.concatenate(results, axis=1)
            for j in range(targets.shape[0]):
                cut = result[:, 128 * j : 128 * j + 128]
                store_sums(offsets.shape[1] // 8, slot, j, points[j][0], cut, offsets, sums)
            mark(slot, target_mark, hot)

        own = []
        for begin in range(0, main, wide):
            for first, last in pieces(sz.points, step):
                own.append(wide_piece(operands, begin, first, last, adder(parts, begin)))
        if rest:
            own.insert(len(own) // 2, rest_piece(operands, main, adder(parts, main)))
        ask, take = own[-1]

        def last_take(shifted):
            take(shifted)
            finish()

        own[-1] = (ask, last_take)
        return own, operands

    made = [task(slot, pick, m) for slot, pick, m in zip(slots, picks, marks)]
    for (own, _), (_, after) in zip(made, made[1:]):
        ask, take = own[0]

        def ask_and_prepare(ask=ask, after=after):
            shifted = ask()
            after()
            return shifted

        own[0] = (ask_and_prepare, take)
    skewed([stage for own, _ in made for stage in own], skew)


def tiles_of_chunk(sz, total, tasks, *refs):
    def several(q, carry):
        slots = [q * UNROLL + u for u in range(UNROLL)]
        picks = [(tasks[0, slot], tasks[1, slot]) for slot in slots]
        marks = [target for target, _ in picks]
        several_tasks(sz, slots, picks, marks, sz.main, sz.rest, 128, 256, 4, refs)
        return carry

    lax.fori_loop(0, lax.div(total + UNROLL - 1, UNROLL), several, 0)


def tiles_of_cells(sz, total, mine, *refs):
    main = 256 * (sz.points // 256)

    def several(q, carry):
        slots = [q * PAIR + u for u in range(PAIR)]
        marks = [mine[0, slot] for slot in slots]
        picks = [(jnp.maximum(mark, 0), mine[1, slot]) for mark, slot in zip(marks, slots)]
        several_tasks(sz, slots, picks, marks, main, sz.points - main, 256, 128, 3, refs)
        return carry

    lax.fori_loop(0, lax.div(total + PAIR - 1, PAIR), several, 0)


def packed(sz, blocks):
    rows = [b[:, : sz.main] for b in blocks] if sz.main else []
    lanes = lane_iota(8)
    for p in range(0, len(blocks), sz.per_pack):
        total = jnp.zeros((8, 128), F32)
        for q, block in enumerate(blocks[p : p + sz.per_pack]):
            rest = jnp.where(lanes < sz.rest, block[:, sz.main : sz.main + 128], 0.0)
            total = total + (pltpu.roll(rest, q * sz.rest, 1) if q else rest)
        rows.append(total)
    return rows


def store_packed(sz, out, blocks):
    first = 0
    count = len(blocks)
    values = packed(sz, blocks)
    if sz.main:
        for b in range(count):
            for m in range(sz.main // 128):
                out[pl.ds(first, 8), :] = values[b][:, 128 * m : 128 * m + 128]
                first += 8
        values = values[count:]
    for value in values:
        out[pl.ds(first, 8), :] = value
        first += 8


def place_packed(sz, lane, arrived, count, store_main, add_rest):
    first = 0
    if sz.main:
        for b in range(count):
            for m in range(sz.main // 128):
                store_main(b, m, arrived[pl.ds(first, 8), :])
                first += 8
    start = sz.rest * lane
    lanes = lane_iota(8)
    for b in range(count):
        pack, q = divmod(b, sz.per_pack)
        value = arrived[pl.ds(first + 8 * pack, 8), :]
        value = pltpu.roll(value, lax.rem(start - q * sz.rest + 128, 128), 1)
        for tile in range(sz.rest_tiles):
            inside = (lanes + 128 * tile >= start) & (lanes + 128 * tile < start + sz.rest)
            add_rest(b, tile, jnp.where(inside, value, 0.0))


def source_kernel(sz, *refs):
    inputs, (high_out, low_out, source_rows, centres), held, sems = (
        refs[:2],
        refs[2:6],
        refs[6:8],
        refs[8],
    )
    for copy in fetch(inputs, held, sems):
        copy.wait()
    positions, bend = held
    high_out[...], low_out[...] = split2(bend[...])
    value = jnp.concatenate([positions[i] for i in range(3)], axis=0)
    value = jnp.concatenate(
        [value, jnp.zeros((3 * sz.cells, sz.width - sz.points), F32)], axis=1
    )
    make_sources(sz, value, high_out[...], low_out[...], source_rows, centres, 0)


def first_kernel(sz, *refs):
    arrived, high, low, inputs = refs[0], refs[1], refs[2], refs[3:7]
    outputs, refs = refs[7:10], refs[10:]
    source_rows, centres, targets, offsets, sums, speeds, hot, moved, pool = refs[:9]
    send, positions, staged, lists, chunk_out, ghost_out, tasks, sems = refs[9:]
    me, lane = lax.axis_index("space"), lax.axis_index("lane")
    own_rows = source_rows.at[:, pl.ds(0, SOURCE_ROWS * sz.cells)]
    own_centres = centres.at[pl.ds(0, 8 * sz.cells)]
    copies = fetch(inputs, [send, positions, own_rows, own_centres], sems)
    for other in range(sz.lanes):
        row = ((me * sz.lanes + other) * sz.group) * 4 + 3
        value = pltpu.roll(arrived[pl.ds(row, 1), :], 128 - 3 * sz.rest, 1)
        staged[pl.ds(other, 1), :] = value.astype(jnp.int32)
    copies += fetch([staged], [lists], sems.at[pl.ds(4, 1)])
    pool[...] = jnp.zeros_like(pool)
    take_ghosts(sz, arrived, pool, up(sz.owners * sz.group, 8), 0)
    hot[...] = jnp.zeros_like(hot)
    speeds[...] = jnp.zeros_like(speeds)
    make_sources(sz, pool[...], high[...], low[...], source_rows, centres, sz.cells)
    for copy in copies[:2]:
        copy.wait()
    chunks = [
        [own_chunk(sz, lane, positions.at[i], pl.ds(g, 8)) for g in range(0, sz.cells, 8)]
        for i in range(3)
    ]
    make_targets(sz, [jnp.concatenate(blocks, axis=0) for blocks in chunks], targets)
    copies[4].wait()
    total = build_list(sz, lists, tasks)
    for copy in copies[2:4]:
        copy.wait()
    copies = fetch([tasks], outputs[2:], sems)
    tiles_of_chunk(sz, total, tasks, source_rows, centres, targets, offsets, sums, hot)
    velocity = add_up(sz, sz.slots, total, sz.cells, offsets, sums, speeds, hot)
    blocks = []
    for i in range(3):
        for g in range(0, sz.cells, 8):
            chunk = own_chunk(sz, lane, positions.at[i], pl.ds(g, 8))
            block = chunk + TIME_STEP * velocity[i][g : g + 8]
            moved[pl.ds(i * sz.rows + g, 8), :] = block
            blocks.append(block)
    store_packed(sz, chunk_out, blocks)
    copies += fetch([chunk_out], outputs[:1], sems.at[pl.ds(1, 1)])
    send_ghosts(sz, send, moved, ghost_out, jnp.zeros((1, 128), F32))
    copies += fetch([ghost_out], outputs[1:2], sems.at[pl.ds(2, 1)])
    for copy in copies:
        copy.wait()


def own_kernel(sz, *refs):
    (high, low), refs = refs[:2], refs[2:]
    others, refs = refs[: sz.lanes - 1], refs[sz.lanes - 1 :]
    inputs, (speed_out, share_out), refs = refs[:2], refs[2:4], refs[4:]
    source_rows, centres, targets, offsets, sums, speeds, hot, pool, mine = refs[:9]
    tasks, chunk, sems = refs[9:]
    copies = fetch(inputs, [tasks, chunk], sems)
    chunks = [chunk, *others]
    hot[...] = jnp.zeros_like(hot)
    speeds[...] = jnp.zeros_like(speeds)
    lane = lax.axis_index("lane")
    pool[...] = jnp.zeros_like(pool)
    copies[0].wait()
    total = own_list(sz, lane, tasks, mine, 0, sz.cells)
    copies[1].wait()
    per = sz.cells // 8
    for k in range(sz.lanes):
        other = lane ^ k

        def row_of(b):
            return (b // per) * sz.cells + 8 * (b % per)

        def store_main(b, m, value):
            cut = pl.ds(pl.multiple_of(other * sz.main + 128 * m, 128), 128)
            pool[pl.ds(row_of(b), 8), cut] = value

        def add_rest(b, tile, value):
            offset = sz.main * sz.lanes + 128 * tile
            cut = (pl.ds(row_of(b), 8), slice(offset, offset + 128))
            pool[cut] = pool[cut] + value

        place_packed(sz, other, chunks[k], 3 * per, store_main, add_rest)
    for i in range(3):
        share_out[i] = share_rows(sz, pool, i * sz.cells, lane)
    make_sources(sz, pool[...], high[...], low[...], source_rows, centres, 0)
    make_targets(sz, share_out, targets)
    tiles_of_cells(sz, total, mine, source_rows, centres, targets, offsets, sums, hot)
    velocity = add_up(sz, sz.own, total, up(sz.share, 8), offsets, sums, speeds, hot)
    for i in range(3):
        speed_out[i] = velocity[i]


def ghost_kernel(sz, *refs):
    arrived, high, low, speed_in, share, tasks_in = refs[:6]
    moved_out, velocity_out = refs[6:8]
    source_rows, centres, targets, offsets, sums, speeds, hot, pool, mine = refs[8:17]
    tasks, sems = refs[17:]
    copies = fetch([tasks_in], [tasks], sems)
    hot[...] = jnp.zeros_like(hot)
    speeds[...] = jnp.zeros_like(speeds)
    lane = lax.axis_index("lane")
    pool[...] = jnp.zeros_like(pool)
    ghosts = up(sz.owners * sz.group, 8)
    take_ghosts(sz, arrived, pool, ghosts, 0)
    make_sources(sz, pool[...], high[...], low[...], source_rows, centres, 0)
    make_targets(sz, share, targets)
    copies[0].wait()
    total = own_list(sz, lane, tasks, mine, sz.cells, sz.cells + sz.owners * sz.group)
    tiles_of_cells(sz, total, mine, source_rows, centres, targets, offsets, sums, hot)
    velocity = add_up(sz, sz.own, total, up(sz.share, 8), offsets, sums, speeds, hot)
    for i in range(3):
        speed = velocity[i] + speed_in[i]
        velocity_out[i] = speed[: sz.share, : sz.points]
        moved_out[i] = (share[i] + TIME_STEP * speed)[: sz.share, : sz.points]


def share_rows(sz, ref, base, lane):
    if sz.share % 8 == 0:
        return ref[pl.ds(pl.multiple_of(base + lane * sz.share, 8), sz.share), :]
    rows = [ref[pl.ds(base + lane * sz.share + c, 1), :] for c in range(sz.share)]
    rows.append(jnp.zeros((8 - sz.share, rows[0].shape[1]), F32))
    return jnp.concatenate(rows, axis=0)


def scratch(sz, cells, targets, tiles, slots):
    return [
        pltpu.VMEM((sz.tiles, SOURCE_ROWS * cells, 128), F32),
        pltpu.VMEM((8 * cells, 128), F32),
        pltpu.VMEM((tiles, 8 * targets, 128), F32),
        pltpu.VMEM((tiles, 8 * slots, 128), F32),
        pltpu.VMEM((tiles, SUM_ROWS * slots, 128), F32),
        pltpu.VMEM((3, slots, 128 * tiles), F32),
        pltpu.VMEM((slots, 128), F32),
    ]


def swap(value, axis, size, k):
    return lax.ppermute(value, axis, [(d, d ^ k) for d in range(size)])


def in_hbm(value):
    return pltpu.with_memory_space_constraint(value, pltpu.HBM)


def shards(positions, bend_op, send_list, task_target, task_source, task_count):
    owners, lanes = lax.axis_size("space"), lax.axis_size("lane")
    cells, points = positions.shape[0], positions.shape[2]
    sz = sizes(owners, lanes, cells, points, task_target.shape[1], send_list.shape[1])
    params = pltpu.CompilerParams(vmem_limit_bytes=min(6 * lanes, 40) << 20)
    shape = jax.ShapeDtypeStruct
    both = ("space", "lane")
    by_component = jnp.transpose(positions, (1, 0, 2))
    list_rows = up(lanes, 8)
    slot_shape = shape((4 * sz.group * owners * lanes, 128), F32)
    leaving, send = pl.pallas_call(
        functools.partial(pick_kernel, sz),
        out_shape=[slot_shape, shape(send_list.shape, jnp.int32)],
        in_specs=[HBM] * 5,
        out_specs=[VMEM, SMEM],
        scratch_shapes=[
            pltpu.SMEM(send_list.shape, jnp.int32),
            pltpu.VMEM(task_target.shape, jnp.int32),
            pltpu.VMEM(task_source.shape, jnp.int32),
            pltpu.SMEM(task_count.shape, jnp.int32),
            pltpu.VMEM(by_component.shape, F32),
            pltpu.VMEM((3 * sz.rows, sz.chunk_wide), F32),
            pltpu.SemaphoreType.DMA((5,)),
        ],
        compiler_params=pltpu.CompilerParams(vmem_limit_bytes=60 << 20),
        name="pick_cells",
    )(send_list, task_target, task_source, task_count, by_component)
    arrived = lax.all_to_all(leaving, both, split_axis=0, concat_axis=0, tiled=True)
    high, low, own_rows, own_centres = pl.pallas_call(
        functools.partial(source_kernel, sz),
        out_shape=[
            shape(bend_op.shape, BF16),
            shape(bend_op.shape, BF16),
            shape((sz.tiles, SOURCE_ROWS * cells, 128), F32),
            shape((8 * cells, 128), F32),
        ],
        in_specs=[HBM] * 2,
        out_specs=[VMEM] * 4,
        scratch_shapes=[
            pltpu.VMEM(by_component.shape, F32),
            pltpu.VMEM(bend_op.shape, F32),
            pltpu.SemaphoreType.DMA((2,)),
        ],
        compiler_params=params,
        cost_estimate=pl.CostEstimate(flops=10**9, bytes_accessed=10**7, transcendentals=0),
        name="first_sources",
    )(in_hbm(by_component), in_hbm(bend_op))
    chunk_shape = (pack_rows(sz, cells), 128)
    chunk, leaving, tasks = pl.pallas_call(
        functools.partial(first_kernel, sz),
        out_shape=[
            pltpu.HBM(chunk_shape, F32),
            pltpu.HBM(slot_shape.shape, F32),
            pltpu.HBM((3, sz.slots), jnp.int32),
        ],
        in_specs=[VMEM] * 3 + [HBM] * 2 + [ANY] * 2,
        out_specs=[HBM] * 3,
        scratch_shapes=scratch(sz, sz.pool, sz.rows, sz.chunk_tiles, sz.slots)
        + [
            pltpu.VMEM((3 * sz.rows, sz.chunk_wide), F32),
            pltpu.VMEM((3 * up(sz.owners * sz.group, 8), sz.width), F32),
            pltpu.SMEM(send_list.shape, jnp.int32),
            pltpu.VMEM(by_component.shape, F32),
            pltpu.VMEM((list_rows, 128), jnp.int32),
            pltpu.SMEM((list_rows, 128), jnp.int32),
            pltpu.VMEM(chunk_shape, F32),
            pltpu.VMEM(slot_shape.shape, F32),
            pltpu.SMEM((3, sz.slots), jnp.int32),
            pltpu.SemaphoreType.DMA((5,)),
        ],
        compiler_params=params,
        name="first_step",
    )(arrived, high, low, in_hbm(send), in_hbm(by_component), own_rows, own_centres)
    arrived = lax.all_to_all(leaving, both, split_axis=0, concat_axis=0, tiled=True)
    chunks = [swap(chunk, "lane", lanes, k) for k in range(1, lanes)]
    share = up(sz.share, 8)
    so_far = shape((3, share, sz.width), F32)
    speed, moved = pl.pallas_call(
        functools.partial(own_kernel, sz),
        out_shape=[so_far, so_far],
        in_specs=[VMEM] * (lanes + 1) + [HBM] * 2,
        out_specs=[VMEM] * 2,
        scratch_shapes=scratch(sz, cells, share, sz.tiles, sz.own)
        + [
            pltpu.VMEM((3 * cells, sz.width), F32),
            pltpu.SMEM((2, sz.own + 8), jnp.int32),
            pltpu.SMEM(tasks.shape, jnp.int32),
            pltpu.VMEM(chunk.shape, F32),
            pltpu.SemaphoreType.DMA((2,)),
        ],
        compiler_params=params,
        cost_estimate=pl.CostEstimate(flops=10**9, bytes_accessed=10**7, transcendentals=0),
        name="second_own",
    )(high, low, *chunks, in_hbm(tasks), in_hbm(chunk))
    result = shape((3, sz.share, points), F32)
    ghosts = up(owners * sz.group, 8)
    outputs = pl.pallas_call(
        functools.partial(ghost_kernel, sz),
        out_shape=[result, result],
        in_specs=[VMEM] * 5 + [HBM],
        out_specs=[VMEM] * 2,
        scratch_shapes=scratch(sz, ghosts, share, sz.tiles, sz.own)
        + [
            pltpu.VMEM((3 * ghosts, sz.width), F32),
            pltpu.SMEM((2, sz.own + 8), jnp.int32),
            pltpu.SMEM(tasks.shape, jnp.int32),
            pltpu.SemaphoreType.DMA((1,)),
        ],
        compiler_params=params,
        name="second_ghosts",
    )(arrived, high, low, speed, moved, in_hbm(tasks))
    return tuple(jnp.transpose(output, (1, 0, 2)) for output in outputs)


def solution(mesh):
    in_specs = (
        P("space", None, None),
        P(),
        P("space", None),
        P(("space", "lane"), None),
        P(("space", "lane"), None),
        P(("space", "lane")),
    )
    out_specs = (P(("space", "lane"), None, None), P(("space", "lane"), None, None))
    return jax.shard_map(shards, mesh=mesh, in_specs=in_specs, out_specs=out_specs, check_vma=False)
```

```python
import functools
from types import SimpleNamespace

import jax
import jax.numpy as jnp
from jax import lax
from jax.experimental import pallas as pl
from jax.experimental.pallas import tpu as pltpu
from jax.sharding import PartitionSpec as P

REGULARIZE = 0.25
TIME_STEP = 0.5
UNROLL = 11
PAIR = 2
SOURCE_ROWS = 24
SUM_ROWS = 16

F32 = jnp.float32
BF16 = jnp.bfloat16
VMEM = pl.BlockSpec(memory_space=pltpu.VMEM)
SMEM = pl.BlockSpec(memory_space=pltpu.SMEM)
HBM = pl.BlockSpec(memory_space=pltpu.HBM)
ANY = pl.BlockSpec(memory_space=pl.ANY)


def up(value, step):
    return -(-value // step) * step


def sizes(owners, lanes, cells, points, cap, listed):
    main = 128 * (points // (128 * lanes))
    rest = (points - main * lanes) // lanes
    group = listed // owners
    pool = up(cells + listed, 8)
    per_pack = 128 // rest
    return SimpleNamespace(
        owners=owners,
        lanes=lanes,
        cells=cells,
        points=points,
        cap=cap,
        group=group,
        width=up(points, 128),
        tiles=up(points, 128) // 128,
        main=main,
        rest=rest,
        rest_tiles=up(rest * lanes, 128) // 128,
        chunk=main + rest,
        chunk_wide=main + up(rest, 128),
        chunk_tiles=(main + up(rest, 128)) // 128,
        per_pack=per_pack,
        pool=pool,
        share=cells // lanes,
        slots=up(lanes * cap + UNROLL, 8),
        rows=cells + 8,
        own=up(lanes * cap + PAIR, 8),
    )


def pack_rows(sz, rows):
    return (3 * rows * sz.main // 128) + 8 * up(3 * rows // 8, sz.per_pack) // sz.per_pack


def split2(value):
    high = value.astype(BF16)
    return high, (value - high.astype(F32)).astype(BF16)


def split3(value):
    first = value.astype(BF16).astype(F32)
    left = value - first
    second = left.astype(BF16).astype(F32)
    return first, second, left - second


def lane_iota(rows):
    return lax.broadcasted_iota(jnp.int32, (rows, 128), 1)


def fetch(sources, targets, sems):
    copies = [
        pltpu.make_async_copy(source, target, sems.at[q])
        for q, (source, target) in enumerate(zip(sources, targets))
    ]
    for copy in copies:
        copy.start()
    return copies


def loop(count, body):
    if count <= 8:
        for q in range(count):
            body(q)
    else:

        def step(q, carry):
            body(q)
            return carry

        lax.fori_loop(0, count, step, 0)


def own_chunk(sz, lane, ref, rows):
    parts = []
    if sz.main:
        parts.append(ref[rows, pl.ds(pl.multiple_of(lane * sz.main, 128), sz.main)])
    start = sz.rest * lane
    lanes = lane_iota(8)
    rest = jnp.zeros((8, 128), F32)
    for tile in range(sz.rest_tiles):
        offset = sz.main * sz.lanes + 128 * tile
        block = ref[rows, offset : min(offset + 128, ref.shape[-1])]
        if block.shape[1] < 128:
            block = jnp.concatenate([block, jnp.zeros((8, 128 - block.shape[1]), F32)], axis=1)
        inside = (lanes + 128 * tile >= start) & (lanes + 128 * tile < start + sz.rest)
        rest = rest + jnp.where(inside, block, 0.0)
    rest = pltpu.roll(rest, lax.rem(128 * sz.rest_tiles - start, 128), 1)
    parts.append(rest)
    return jnp.concatenate(parts, axis=1) if len(parts) > 1 else parts[0]


def send_ghosts(sz, send, chunks, out, tasks):
    lanes = lane_iota(1)

    def one(d):
        for g in range(sz.group):
            cell = send[0, d * sz.group + g]
            rows = []
            last = tasks
            for i in range(3):
                row = chunks[pl.ds(i * sz.rows + cell, 1), :]
                rows.append(row[:, :128] if sz.main else jnp.zeros((1, 128), F32))
                piece = jnp.where(lanes < sz.rest, row[:, sz.main : sz.main + 128], 0.0)
                last = last + (pltpu.roll(piece, i * sz.rest, 1) if i else piece)
            rows.append(last)
            for other in range(sz.lanes):
                first = ((d * sz.lanes + other) * sz.group + g) * 4
                for q, row in enumerate(rows):
                    out[pl.ds(first + q, 1), :] = row

    loop(sz.owners, one)


def pick_kernel(sz, *refs):
    inputs, (out, send_out), held, (chunks, sems) = refs[:5], refs[5:7], refs[7:12], refs[12:]
    for copy in fetch(inputs, held, sems):
        copy.wait()
    send, target, source, count, positions = held
    for j in range(send_out.shape[1]):
        send_out[0, j] = send[0, j]
    lane = lax.axis_index("lane")
    for i in range(3):
        for g in range(0, sz.cells, 8):
            value = own_chunk(sz, lane, positions.at[i], pl.ds(g, 8))
            chunks[pl.ds(i * sz.rows + g, 8), :] = value
    spare = jnp.zeros((1, 128 - sz.cap), F32)
    tasks = jnp.where(lane_iota(1) == 3 * sz.rest + 2 * sz.cap, count[0].astype(F32), 0.0)
    for q, row in enumerate((target, source)):
        wide = jnp.concatenate([row[...].astype(F32), spare], axis=1)
        tasks = tasks + pltpu.roll(wide, 3 * sz.rest + q * sz.cap, 1)
    send_ghosts(sz, send, chunks, out, tasks)


def take_ghosts(sz, arrived, pool, stride, base):
    lanes = lane_iota(1)

    def one(d):
        for g in range(sz.group):
            first = [((d * sz.lanes + lane) * sz.group + g) * 4 for lane in range(sz.lanes)]
            last = [arrived[pl.ds(row + 3, 1), :] for row in first]
            for i in range(3):
                tiles = []
                if sz.main:
                    tiles += [arrived[pl.ds(row + i, 1), :] for row in first]
                for tile in range(sz.rest_tiles):
                    total = jnp.zeros((1, 128), F32)
                    for lane in range(sz.lanes):
                        start = sz.rest * lane
                        if start + sz.rest <= 128 * tile or start >= 128 * tile + 128:
                            continue
                        shift = (start - i * sz.rest) % 128
                        value = pltpu.roll(last[lane], shift, 1) if shift else last[lane]
                        at = lanes + 128 * tile
                        total = jnp.where((at >= start) & (at < start + sz.rest), value, total)
                    tiles.append(total)
                place = pl.ds(i * stride + base + d * sz.group + g, 1)
                pool[place, :] = jnp.concatenate(tiles, axis=1)

    loop(sz.owners, one)


def build_list(sz, lists, tasks):
    total = jnp.int32(0)
    for lane in range(sz.lanes):
        count = lists[lane, 2 * sz.cap]
        for j in range(sz.cap):
            tasks[0, total] = lists[lane, j]
            tasks[1, total] = lists[lane, sz.cap + j]
            total = total + (j < count).astype(jnp.int32)
    for u in range(UNROLL):
        tasks[0, total + u] = jnp.int32(sz.cells)
        tasks[1, total + u] = jnp.int32(0)
    tasks[2, 0] = total
    return total


def own_list(sz, lane, tasks, mine, low, high):
    first = lane * sz.share
    total = tasks[2, 0]
    count = jnp.int32(0)
    for t in range(sz.lanes * sz.cap):
        target = tasks[0, t] - first
        source = tasks[1, t]
        mine[0, count] = target
        mine[1, count] = source - low
        taken = (target >= 0) & (target < sz.share) & (t < total)
        taken = taken & (source >= low) & (source < high)
        count = count + taken.astype(jnp.int32)
    for u in range(PAIR):
        mine[0, count + u] = jnp.int32(-1)
        mine[1, count + u] = jnp.int32(0)
    return count


def products(value, bend_high, bend_low):
    high, low = split2(value)
    dot = functools.partial(jnp.dot, preferred_element_type=F32)
    return dot(high, bend_high) + dot(low, bend_high) + dot(high, bend_low)


def make_sources(sz, value, bend_high, bend_low, source_rows, centres, first):
    count = value.shape[0] // 3
    forces = products(value[:, : sz.points], bend_high, bend_low)
    forces = jnp.concatenate(
        [forces, jnp.zeros((3 * count, sz.width - sz.points), F32)], axis=1
    )
    middle = jnp.sum(value, axis=1, keepdims=True) / sz.points
    for g in range(count // 8):
        where = [i * count + 8 * g for i in range(3)]
        middles = [jnp.broadcast_to(middle[w : w + 8], (8, 128)) for w in where]
        middles += [jnp.zeros((8, 128), F32)] * 5
        for i, row in enumerate(middles):
            centres[pl.ds(8 * (first + 8 * g) + i, 8, stride=8), :] = row
        for j in range(sz.tiles):
            cut = slice(128 * j, 128 * j + 128)
            y = [value[w : w + 8, cut] - m for w, m in zip(where, middles)]
            f = [forces[w : w + 8, cut] for w in where]
            norm = y[0] * y[0] + y[1] * y[1] + y[2] * y[2] + REGULARIZE
            along = y[0] * f[0] + y[1] * f[1] + y[2] * f[2]
            one, zero = jnp.ones((8, 128), F32), jnp.zeros((8, 128), F32)
            rows = [y[0], y[1], y[2], norm, one, zero, zero, zero]
            rows += f
            rows += [y[i] * f[k] for i in range(3) for k in range(3)]
            rows += [norm * f[i] + along * y[i] for i in range(3)]
            rows += [along]
            for k, row in enumerate(rows):
                place = pl.ds(SOURCE_ROWS * (first + 8 * g) + k, 8, stride=SOURCE_ROWS)
                source_rows.at[j][place, :] = row


def make_targets(sz, blocks, targets):
    targets[...] = jnp.zeros_like(targets)
    for i in range(3):
        for g in range(blocks[i].shape[0] // 8):
            block = blocks[i][8 * g : 8 * g + 8]
            for j in range(targets.shape[0]):
                cut = slice(128 * j, 128 * j + 128)
                targets.at[j][pl.ds(64 * g + i, 8, stride=8), :] = block[:, cut]


def source_operands(sz, source, source_rows):
    held = [
        source_rows[j, pl.ds(pl.multiple_of(SOURCE_ROWS * source, 8), SOURCE_ROWS), :]
        for j in range(sz.tiles)
    ]
    held = jnp.concatenate(held, axis=1)
    y1, y2, y3 = split3(held[:8])
    y_stack = jnp.concatenate([y1, y1, y2, y2, y1, y3], axis=0).astype(BF16)
    return y_stack, jnp.concatenate(split3(held[8:]), axis=0)


def pieces(points, step):
    starts = list(range(0, max(points // 128 * 128, 1), step))
    return list(zip(starts, starts[1:] + [points]))


def twice(piece, count):
    whole = count // 128 * 128
    parts = [piece[:, :whole].astype(BF16)] * 2 if whole else []
    if whole < count:
        last = piece[:, whole:]
        last = last + pltpu.roll(last, count - whole, 1)
        parts.append(last.astype(BF16)[:, : 2 * (count - whole)])
    return jnp.concatenate(parts, axis=1)


def load_target(j, target, slot, centre, targets, offsets):
    row = lax.broadcasted_iota(jnp.int32, (8, 128), 0)
    x = targets[j, pl.ds(pl.multiple_of(8 * target, 8), 8), :] - centre
    square = x * x
    norm = pltpu.roll(square, 2, 0) + pltpu.roll(square, 3, 0) + pltpu.roll(square, 4, 0)
    side = jnp.where(row == 4, norm, jnp.where(row == 3, 1.0, 0.0))
    x_side = jnp.where(row < 3, -2.0 * x, side)
    x1, x2, x3 = split3(x_side)
    return x, jnp.concatenate([x1, x2, x1, x2, x3, x1], axis=0).astype(BF16)


def distances(one_stack, other_stack):
    return jnp.dot(one_stack, other_stack, preferred_element_type=F32)


def weights(shifted):
    inverse = lax.rsqrt(shifted)
    return split2(inverse * inverse * inverse)


def fold(result):
    return result[:SUM_ROWS] + result[SUM_ROWS : 2 * SUM_ROWS] + result[2 * SUM_ROWS :]


def skewed(stages, skew):
    asked = []
    for q, (ask, _) in enumerate(stages):
        asked.append(ask())
        if q >= skew:
            stages[q - skew][1](asked[q - skew])
            asked[q - skew] = None
    for q in range(max(len(stages) - skew, 0), len(stages)):
        stages[q][1](asked[q])


def adder(totals, key):
    def add(value):
        totals[key] = totals[key] + value if key in totals else value

    return add


def wide_piece(operands, begin, first, end, add):
    def ask():
        _, y_turned, _, blocks = operands()
        return distances(y_turned[first:end], blocks[begin])

    def take(shifted):
        m_piece = operands()[2][first]
        high, low = weights(shifted)
        whole = (end - first) // 128 * 128
        parts = [high[:whole], low[:whole]] if whole else []
        parts += [high[whole:], low[whole:]] if whole < end - first else []
        stack = jnp.concatenate(parts, axis=0)
        add(jnp.dot(m_piece, stack, preferred_element_type=F32))

    return ask, take


def rest_piece(operands, begin, add):
    def ask():
        y_stack, _, _, blocks = operands()
        return distances(blocks[begin], y_stack)

    def take(shifted):
        high, low = weights(shifted)
        m_whole = operands()[2][-1]
        turned = (((1,), (1,)), ((), ()))
        result = lax.dot_general(m_whole, high, turned, preferred_element_type=F32)
        add(result + lax.dot_general(m_whole, low, turned, preferred_element_type=F32))

    return ask, take


def store_sums(slots, slot, j, x, result, offsets, sums):
    offsets.at[j][pl.ds(slot, 8, stride=slots), :] = x
    for h in range(0, SUM_ROWS, 8):
        sums.at[j][pl.ds(h * slots + slot, 8, stride=slots), :] = result[h : h + 8]


def mark(slot, target, hot):
    hot[pl.ds(slot, 1), :] = jnp.where(lane_iota(1) == target, 1.0, 0.0)


def combine(sz, slots, first, total, offsets, sums, speeds):
    live = lax.broadcasted_iota(jnp.int32, (8, 128), 0) + first < total
    for j in range(offsets.shape[0]):
        x = [offsets[j, pl.ds(i * slots + first, 8), :] for i in range(3)]
        s = [sums[j, pl.ds(k * slots + first, 8), :] for k in range(SUM_ROWS)]
        a, b, c = s[:3], [s[3:6], s[6:9], s[9:12]], s[12:15]
        norm = x[0] * x[0] + x[1] * x[1] + x[2] * x[2] + REGULARIZE
        along = x[0] * a[0] + x[1] * a[1] + x[2] * a[2] - s[15]
        for i in range(3):
            speed = norm * a[i] + c[i] + along * x[i]
            for k in range(3):
                speed = speed - x[k] * (2.0 * b[k][i] + b[i][k])
            speed = jnp.where(live, speed / sz.points, 0.0)
            speeds[i, pl.ds(first, 8), 128 * j : 128 * j + 128] = speed


def add_up(sz, slots, total, rows, offsets, sums, speeds, hot):
    def eight(q, carry):
        combine(sz, slots, pl.multiple_of(8 * q, 8), total, offsets, sums, speeds)
        return carry

    if slots <= 64 and offsets.shape[0] <= 2:
        for q in range(slots // 8):
            combine(sz, slots, 8 * q, total, offsets, sums, speeds)
    else:
        lax.fori_loop(0, lax.div(total + 7, 8), eight, 0)
    one_hot = hot[...].astype(BF16)
    result = []
    for i in range(3):
        first, second, third = split3(speeds[i])
        parts = [
            lax.dot_general(
                one_hot, part.astype(BF16), (((0,), (0,)), ((), ())), preferred_element_type=F32
            )
            for part in (first, second, third)
        ]
        result.append((parts[0] + parts[1] + parts[2])[:rows])
    return result


def several_tasks(sz, slots, picks, marks, main, rest, wide, step, skew, refs):
    source_rows, centres, targets, offsets, sums, hot = refs

    def task(slot, pick, target_mark):
        target, source = pick
        made, parts, points = [], {}, []

        def operands():
            if made:
                return made[0]
            y_stack, m_stack = source_operands(sz, source, source_rows)
            centre = centres[pl.ds(pl.multiple_of(8 * source, 8), 8), :]
            points.extend(
                load_target(j, target, slot, centre, targets, offsets)
                for j in range(targets.shape[0])
            )
            blocks = {}
            for begin in range(0, main, wide):
                stack = [stack for _, stack in points[begin // 128 : (begin + wide) // 128]]
                blocks[begin] = jnp.concatenate(stack, axis=1)
            if rest:
                blocks[main] = jnp.transpose(points[main // 128][1])[:rest]
            sides = {-1: m_stack.astype(BF16)}
            if main:
                for first, last in pieces(sz.points, step):
                    sides[first] = twice(m_stack[:, first : up(last, 128)], last - first)
            made.append((y_stack, jnp.transpose(y_stack), sides, blocks))
            return made[0]

        def finish():
            results = [fold(parts[begin]) for begin in range(0, main, wide)]
            if rest:
                spare = jnp.zeros((SUM_ROWS, 128 - rest), F32)
                results.append(jnp.concatenate([fold(parts[main]), spare], axis=1))
            result = jnp.concatenate(results, axis=1)
            for j in range(targets.shape[0]):
                cut = result[:, 128 * j : 128 * j + 128]
                store_sums(offsets.shape[1] // 8, slot, j, points[j][0], cut, offsets, sums)
            mark(slot, target_mark, hot)

        own = []
        for begin in range(0, main, wide):
            for first, last in pieces(sz.points, step):
                own.append(wide_piece(operands, begin, first, last, adder(parts, begin)))
        if rest:
            own.insert(len(own) // 2, rest_piece(operands, main, adder(parts, main)))
        ask, take = own[-1]

        def last_take(shifted):
            take(shifted)
            finish()

        own[-1] = (ask, last_take)
        return own, operands

    made = [task(slot, pick, m) for slot, pick, m in zip(slots, picks, marks)]
    for (own, _), (_, after) in zip(made, made[1:]):
        ask, take = own[0]

        def ask_and_prepare(ask=ask, after=after):
            shifted = ask()
            after()
            return shifted

        own[0] = (ask_and_prepare, take)
    skewed([stage for own, _ in made for stage in own], skew)


def tiles_of_chunk(sz, total, tasks, *refs):
    def several(q, carry):
        slots = [q * UNROLL + u for u in range(UNROLL)]
        picks = [(tasks[0, slot], tasks[1, slot]) for slot in slots]
        marks = [target for target, _ in picks]
        several_tasks(sz, slots, picks, marks, sz.main, sz.rest, 128, 256, 4, refs)
        return carry

    lax.fori_loop(0, lax.div(total + UNROLL - 1, UNROLL), several, 0)


def tiles_of_cells(sz, total, mine, *refs):
    main = 256 * (sz.points // 256)

    def several(q, carry):
        slots = [q * PAIR + u for u in range(PAIR)]
        marks = [mine[0, slot] for slot in slots]
        picks = [(jnp.maximum(mark, 0), mine[1, slot]) for mark, slot in zip(marks, slots)]
        several_tasks(sz, slots, picks, marks, main, sz.points - main, 256, 256, 2, refs)
        return carry

    lax.fori_loop(0, lax.div(total + PAIR - 1, PAIR), several, 0)


def packed(sz, blocks):
    rows = [b[:, : sz.main] for b in blocks] if sz.main else []
    lanes = lane_iota(8)
    for p in range(0, len(blocks), sz.per_pack):
        total = jnp.zeros((8, 128), F32)
        for q, block in enumerate(blocks[p : p + sz.per_pack]):
            rest = jnp.where(lanes < sz.rest, block[:, sz.main : sz.main + 128], 0.0)
            total = total + (pltpu.roll(rest, q * sz.rest, 1) if q else rest)
        rows.append(total)
    return rows


def store_packed(sz, out, blocks):
    first = 0
    count = len(blocks)
    values = packed(sz, blocks)
    if sz.main:
        for b in range(count):
            for m in range(sz.main // 128):
                out[pl.ds(first, 8), :] = values[b][:, 128 * m : 128 * m + 128]
                first += 8
        values = values[count:]
    for value in values:
        out[pl.ds(first, 8), :] = value
        first += 8


def place_packed(sz, lane, arrived, count, store_main, add_rest):
    first = 0
    if sz.main:
        for b in range(count):
            for m in range(sz.main // 128):
                store_main(b, m, arrived[pl.ds(first, 8), :])
                first += 8
    start = sz.rest * lane
    lanes = lane_iota(8)
    for b in range(count):
        pack, q = divmod(b, sz.per_pack)
        value = arrived[pl.ds(first + 8 * pack, 8), :]
        value = pltpu.roll(value, lax.rem(start - q * sz.rest + 128, 128), 1)
        for tile in range(sz.rest_tiles):
            inside = (lanes + 128 * tile >= start) & (lanes + 128 * tile < start + sz.rest)
            add_rest(b, tile, jnp.where(inside, value, 0.0))


def source_kernel(sz, *refs):
    inputs, (high_out, low_out, source_rows, centres), held, sems = (
        refs[:2],
        refs[2:6],
        refs[6:8],
        refs[8],
    )
    for copy in fetch(inputs, held, sems):
        copy.wait()
    positions, bend = held
    high_out[...], low_out[...] = split2(bend[...])
    value = jnp.concatenate([positions[i] for i in range(3)], axis=0)
    value = jnp.concatenate(
        [value, jnp.zeros((3 * sz.cells, sz.width - sz.points), F32)], axis=1
    )
    make_sources(sz, value, high_out[...], low_out[...], source_rows, centres, 0)


def first_kernel(sz, *refs):
    arrived, high, low, inputs = refs[0], refs[1], refs[2], refs[3:7]
    outputs, refs = refs[7:10], refs[10:]
    source_rows, centres, targets, offsets, sums, speeds, hot, moved, pool = refs[:9]
    send, positions, staged, lists, chunk_out, ghost_out, tasks, sems = refs[9:]
    me, lane = lax.axis_index("space"), lax.axis_index("lane")
    own_rows = source_rows.at[:, pl.ds(0, SOURCE_ROWS * sz.cells)]
    own_centres = centres.at[pl.ds(0, 8 * sz.cells)]
    copies = fetch(inputs, [send, positions, own_rows, own_centres], sems)
    for other in range(sz.lanes):
        row = ((me * sz.lanes + other) * sz.group) * 4 + 3
        value = pltpu.roll(arrived[pl.ds(row, 1), :], 128 - 3 * sz.rest, 1)
        staged[pl.ds(other, 1), :] = value.astype(jnp.int32)
    copies += fetch([staged], [lists], sems.at[pl.ds(4, 1)])
    pool[...] = jnp.zeros_like(pool)
    take_ghosts(sz, arrived, pool, up(sz.owners * sz.group, 8), 0)
    hot[...] = jnp.zeros_like(hot)
    speeds[...] = jnp.zeros_like(speeds)
    make_sources(sz, pool[...], high[...], low[...], source_rows, centres, sz.cells)
    for copy in copies[:2]:
        copy.wait()
    chunks = [
        [own_chunk(sz, lane, positions.at[i], pl.ds(g, 8)) for g in range(0, sz.cells, 8)]
        for i in range(3)
    ]
    make_targets(sz, [jnp.concatenate(blocks, axis=0) for blocks in chunks], targets)
    copies[4].wait()
    total = build_list(sz, lists, tasks)
    for copy in copies[2:4]:
        copy.wait()
    copies = fetch([tasks], outputs[2:], sems)
    tiles_of_chunk(sz, total, tasks, source_rows, centres, targets, offsets, sums, hot)
    velocity = add_up(sz, sz.slots, total, sz.cells, offsets, sums, speeds, hot)
    blocks = []
    for i in range(3):
        for g in range(0, sz.cells, 8):
            chunk = own_chunk(sz, lane, positions.at[i], pl.ds(g, 8))
            block = chunk + TIME_STEP * velocity[i][g : g + 8]
            moved[pl.ds(i * sz.rows + g, 8), :] = block
            blocks.append(block)
    store_packed(sz, chunk_out, blocks)
    copies += fetch([chunk_out], outputs[:1], sems.at[pl.ds(1, 1)])
    send_ghosts(sz, send, moved, ghost_out, jnp.zeros((1, 128), F32))
    copies += fetch([ghost_out], outputs[1:2], sems.at[pl.ds(2, 1)])
    for copy in copies:
        copy.wait()


def own_kernel(sz, *refs):
    (high, low), refs = refs[:2], refs[2:]
    others, refs = refs[: sz.lanes - 1], refs[sz.lanes - 1 :]
    inputs, (speed_out, share_out), refs = refs[:2], refs[2:4], refs[4:]
    source_rows, centres, targets, offsets, sums, speeds, hot, pool, mine = refs[:9]
    tasks, chunk, sems = refs[9:]
    copies = fetch(inputs, [tasks, chunk], sems)
    chunks = [chunk, *others]
    hot[...] = jnp.zeros_like(hot)
    speeds[...] = jnp.zeros_like(speeds)
    lane = lax.axis_index("lane")
    pool[...] = jnp.zeros_like(pool)
    copies[0].wait()
    total = own_list(sz, lane, tasks, mine, 0, sz.cells)
    copies[1].wait()
    per = sz.cells // 8
    for k in range(sz.lanes):
        other = lane ^ k

        def row_of(b):
            return (b // per) * sz.cells + 8 * (b % per)

        def store_main(b, m, value):
            cut = pl.ds(pl.multiple_of(other * sz.main + 128 * m, 128), 128)
            pool[pl.ds(row_of(b), 8), cut] = value

        def add_rest(b, tile, value):
            offset = sz.main * sz.lanes + 128 * tile
            cut = (pl.ds(row_of(b), 8), slice(offset, offset + 128))
            pool[cut] = pool[cut] + value

        place_packed(sz, other, chunks[k], 3 * per, store_main, add_rest)
    for i in range(3):
        share_out[i] = share_rows(sz, pool, i * sz.cells, lane)
    make_sources(sz, pool[...], high[...], low[...], source_rows, centres, 0)
    make_targets(sz, share_out, targets)
    tiles_of_cells(sz, total, mine, source_rows, centres, targets, offsets, sums, hot)
    velocity = add_up(sz, sz.own, total, up(sz.share, 8), offsets, sums, speeds, hot)
    for i in range(3):
        speed_out[i] = velocity[i]


def ghost_kernel(sz, *refs):
    arrived, high, low, speed_in, share, tasks_in = refs[:6]
    moved_out, velocity_out = refs[6:8]
    source_rows, centres, targets, offsets, sums, speeds, hot, pool, mine = refs[8:17]
    tasks, sems = refs[17:]
    copies = fetch([tasks_in], [tasks], sems)
    hot[...] = jnp.zeros_like(hot)
    speeds[...] = jnp.zeros_like(speeds)
    lane = lax.axis_index("lane")
    pool[...] = jnp.zeros_like(pool)
    ghosts = up(sz.owners * sz.group, 8)
    take_ghosts(sz, arrived, pool, ghosts, 0)
    make_sources(sz, pool[...], high[...], low[...], source_rows, centres, 0)
    make_targets(sz, share, targets)
    copies[0].wait()
    total = own_list(sz, lane, tasks, mine, sz.cells, sz.cells + sz.owners * sz.group)
    tiles_of_cells(sz, total, mine, source_rows, centres, targets, offsets, sums, hot)
    velocity = add_up(sz, sz.own, total, up(sz.share, 8), offsets, sums, speeds, hot)
    for i in range(3):
        speed = velocity[i] + speed_in[i]
        velocity_out[i] = speed[: sz.share, : sz.points]
        moved_out[i] = (share[i] + TIME_STEP * speed)[: sz.share, : sz.points]


def share_rows(sz, ref, base, lane):
    if sz.share % 8 == 0:
        return ref[pl.ds(pl.multiple_of(base + lane * sz.share, 8), sz.share), :]
    rows = [ref[pl.ds(base + lane * sz.share + c, 1), :] for c in range(sz.share)]
    rows.append(jnp.zeros((8 - sz.share, rows[0].shape[1]), F32))
    return jnp.concatenate(rows, axis=0)


def scratch(sz, cells, targets, tiles, slots):
    return [
        pltpu.VMEM((sz.tiles, SOURCE_ROWS * cells, 128), F32),
        pltpu.VMEM((8 * cells, 128), F32),
        pltpu.VMEM((tiles, 8 * targets, 128), F32),
        pltpu.VMEM((tiles, 8 * slots, 128), F32),
        pltpu.VMEM((tiles, SUM_ROWS * slots, 128), F32),
        pltpu.VMEM((3, slots, 128 * tiles), F32),
        pltpu.VMEM((slots, 128), F32),
    ]


def swap(value, axis, size, k):
    return lax.ppermute(value, axis, [(d, d ^ k) for d in range(size)])


def in_hbm(value):
    return pltpu.with_memory_space_constraint(value, pltpu.HBM)


def shards(positions, bend_op, send_list, task_target, task_source, task_count):
    owners, lanes = lax.axis_size("space"), lax.axis_size("lane")
    cells, points = positions.shape[0], positions.shape[2]
    sz = sizes(owners, lanes, cells, points, task_target.shape[1], send_list.shape[1])
    params = pltpu.CompilerParams(vmem_limit_bytes=min(6 * lanes, 40) << 20)
    shape = jax.ShapeDtypeStruct
    both = ("space", "lane")
    by_component = jnp.transpose(positions, (1, 0, 2))
    list_rows = up(lanes, 8)
    slot_shape = shape((4 * sz.group * owners * lanes, 128), F32)
    leaving, send = pl.pallas_call(
        functools.partial(pick_kernel, sz),
        out_shape=[slot_shape, shape(send_list.shape, jnp.int32)],
        in_specs=[HBM] * 5,
        out_specs=[VMEM, SMEM],
        scratch_shapes=[
            pltpu.SMEM(send_list.shape, jnp.int32),
            pltpu.VMEM(task_target.shape, jnp.int32),
            pltpu.VMEM(task_source.shape, jnp.int32),
            pltpu.SMEM(task_count.shape, jnp.int32),
            pltpu.VMEM(by_component.shape, F32),
            pltpu.VMEM((3 * sz.rows, sz.chunk_wide), F32),
            pltpu.SemaphoreType.DMA((5,)),
        ],
        compiler_params=pltpu.CompilerParams(vmem_limit_bytes=60 << 20),
        name="pick_cells",
    )(send_list, task_target, task_source, task_count, by_component)
    arrived = lax.all_to_all(leaving, both, split_axis=0, concat_axis=0, tiled=True)
    high, low, own_rows, own_centres = pl.pallas_call(
        functools.partial(source_kernel, sz),
        out_shape=[
            shape(bend_op.shape, BF16),
            shape(bend_op.shape, BF16),
            shape((sz.tiles, SOURCE_ROWS * cells, 128), F32),
            shape((8 * cells, 128), F32),
        ],
        in_specs=[HBM] * 2,
        out_specs=[VMEM] * 4,
        scratch_shapes=[
            pltpu.VMEM(by_component.shape, F32),
            pltpu.VMEM(bend_op.shape, F32),
            pltpu.SemaphoreType.DMA((2,)),
        ],
        compiler_params=params,
        cost_estimate=pl.CostEstimate(flops=10**9, bytes_accessed=10**7, transcendentals=0),
        name="first_sources",
    )(in_hbm(by_component), in_hbm(bend_op))
    chunk_shape = (pack_rows(sz, cells), 128)
    chunk, leaving, tasks = pl.pallas_call(
        functools.partial(first_kernel, sz),
        out_shape=[
            pltpu.HBM(chunk_shape, F32),
            pltpu.HBM(slot_shape.shape, F32),
            pltpu.HBM((3, sz.slots), jnp.int32),
        ],
        in_specs=[VMEM] * 3 + [HBM] * 2 + [ANY] * 2,
        out_specs=[HBM] * 3,
        scratch_shapes=scratch(sz, sz.pool, sz.rows, sz.chunk_tiles, sz.slots)
        + [
            pltpu.VMEM((3 * sz.rows, sz.chunk_wide), F32),
            pltpu.VMEM((3 * up(sz.owners * sz.group, 8), sz.width), F32),
            pltpu.SMEM(send_list.shape, jnp.int32),
            pltpu.VMEM(by_component.shape, F32),
            pltpu.VMEM((list_rows, 128), jnp.int32),
            pltpu.SMEM((list_rows, 128), jnp.int32),
            pltpu.VMEM(chunk_shape, F32),
            pltpu.VMEM(slot_shape.shape, F32),
            pltpu.SMEM((3, sz.slots), jnp.int32),
            pltpu.SemaphoreType.DMA((5,)),
        ],
        compiler_params=params,
        name="first_step",
    )(arrived, high, low, in_hbm(send), in_hbm(by_component), own_rows, own_centres)
    arrived = lax.all_to_all(leaving, both, split_axis=0, concat_axis=0, tiled=True)
    chunks = [swap(chunk, "lane", lanes, k) for k in range(1, lanes)]
    share = up(sz.share, 8)
    so_far = shape((3, share, sz.width), F32)
    speed, moved = pl.pallas_call(
        functools.partial(own_kernel, sz),
        out_shape=[so_far, so_far],
        in_specs=[VMEM] * (lanes + 1) + [HBM] * 2,
        out_specs=[VMEM] * 2,
        scratch_shapes=scratch(sz, cells, share, sz.tiles, sz.own)
        + [
            pltpu.VMEM((3 * cells, sz.width), F32),
            pltpu.SMEM((2, sz.own + 8), jnp.int32),
            pltpu.SMEM(tasks.shape, jnp.int32),
            pltpu.VMEM(chunk.shape, F32),
            pltpu.SemaphoreType.DMA((2,)),
        ],
        compiler_params=params,
        cost_estimate=pl.CostEstimate(flops=10**9, bytes_accessed=10**7, transcendentals=0),
        name="second_own",
    )(high, low, *chunks, in_hbm(tasks), in_hbm(chunk))
    result = shape((3, sz.share, points), F32)
    ghosts = up(owners * sz.group, 8)
    outputs = pl.pallas_call(
        functools.partial(ghost_kernel, sz),
        out_shape=[result, result],
        in_specs=[VMEM] * 5 + [HBM],
        out_specs=[VMEM] * 2,
        scratch_shapes=scratch(sz, ghosts, share, sz.tiles, sz.own)
        + [
            pltpu.VMEM((3 * ghosts, sz.width), F32),
            pltpu.SMEM((2, sz.own + 8), jnp.int32),
            pltpu.SMEM(tasks.shape, jnp.int32),
            pltpu.SemaphoreType.DMA((1,)),
        ],
        compiler_params=params,
        name="second_ghosts",
    )(arrived, high, low, speed, moved, in_hbm(tasks))
    return tuple(jnp.transpose(output, (1, 0, 2)) for output in outputs)


def solution(mesh):
    in_specs = (
        P("space", None, None),
        P(),
        P("space", None),
        P(("space", "lane"), None),
        P(("space", "lane"), None),
        P(("space", "lane")),
    )
    out_specs = (P(("space", "lane"), None, None), P(("space", "lane"), None, None))
    return jax.shard_map(shards, mesh=mesh, in_specs=in_specs, out_specs=out_specs, check_vma=False)
```

```python
import functools
from types import SimpleNamespace

import jax
import jax.numpy as jnp
from jax import lax
from jax.experimental import pallas as pl
from jax.experimental.pallas import tpu as pltpu
from jax.sharding import PartitionSpec as P

REGULARIZE = 0.25
TIME_STEP = 0.5
UNROLL = 11
PAIR = 2
SOURCE_ROWS = 24
SUM_ROWS = 16

F32 = jnp.float32
BF16 = jnp.bfloat16
VMEM = pl.BlockSpec(memory_space=pltpu.VMEM)
SMEM = pl.BlockSpec(memory_space=pltpu.SMEM)
HBM = pl.BlockSpec(memory_space=pltpu.HBM)
ANY = pl.BlockSpec(memory_space=pl.ANY)


def up(value, step):
    return -(-value // step) * step


def sizes(owners, lanes, cells, points, cap, listed):
    main = 128 * (points // (128 * lanes))
    rest = (points - main * lanes) // lanes
    group = listed // owners
    pool = up(cells + listed, 8)
    per_pack = 128 // rest
    return SimpleNamespace(
        owners=owners,
        lanes=lanes,
        cells=cells,
        points=points,
        cap=cap,
        group=group,
        width=up(points, 128),
        tiles=up(points, 128) // 128,
        main=main,
        rest=rest,
        rest_tiles=up(rest * lanes, 128) // 128,
        chunk=main + rest,
        chunk_wide=main + up(rest, 128),
        chunk_tiles=(main + up(rest, 128)) // 128,
        per_pack=per_pack,
        pool=pool,
        share=cells // lanes,
        slots=up(lanes * cap + UNROLL, 8),
        rows=cells + 8,
        own=up(lanes * cap + PAIR, 8),
    )


def pack_rows(sz, rows):
    return (3 * rows * sz.main // 128) + 8 * up(3 * rows // 8, sz.per_pack) // sz.per_pack


def split2(value):
    high = value.astype(BF16)
    return high, (value - high.astype(F32)).astype(BF16)


def split3(value):
    first = value.astype(BF16).astype(F32)
    left = value - first
    second = left.astype(BF16).astype(F32)
    return first, second, left - second


def lane_iota(rows):
    return lax.broadcasted_iota(jnp.int32, (rows, 128), 1)


def fetch(sources, targets, sems):
    copies = [
        pltpu.make_async_copy(source, target, sems.at[q])
        for q, (source, target) in enumerate(zip(sources, targets))
    ]
    for copy in copies:
        copy.start()
    return copies


def loop(count, body):
    if count <= 8:
        for q in range(count):
            body(q)
    else:

        def step(q, carry):
            body(q)
            return carry

        lax.fori_loop(0, count, step, 0)


def own_chunk(sz, lane, ref, rows):
    parts = []
    if sz.main:
        parts.append(ref[rows, pl.ds(pl.multiple_of(lane * sz.main, 128), sz.main)])
    start = sz.rest * lane
    lanes = lane_iota(8)
    rest = jnp.zeros((8, 128), F32)
    for tile in range(sz.rest_tiles):
        offset = sz.main * sz.lanes + 128 * tile
        block = ref[rows, offset : min(offset + 128, ref.shape[-1])]
        if block.shape[1] < 128:
            block = jnp.concatenate([block, jnp.zeros((8, 128 - block.shape[1]), F32)], axis=1)
        inside = (lanes + 128 * tile >= start) & (lanes + 128 * tile < start + sz.rest)
        rest = rest + jnp.where(inside, block, 0.0)
    rest = pltpu.roll(rest, lax.rem(128 * sz.rest_tiles - start, 128), 1)
    parts.append(rest)
    return jnp.concatenate(parts, axis=1) if len(parts) > 1 else parts[0]


def send_ghosts(sz, send, chunks, out, tasks):
    lanes = lane_iota(1)

    def one(d):
        for g in range(sz.group):
            cell = send[0, d * sz.group + g]
            rows = []
            last = tasks
            for i in range(3):
                row = chunks[pl.ds(i * sz.rows + cell, 1), :]
                rows.append(row[:, :128] if sz.main else jnp.zeros((1, 128), F32))
                piece = jnp.where(lanes < sz.rest, row[:, sz.main : sz.main + 128], 0.0)
                last = last + (pltpu.roll(piece, i * sz.rest, 1) if i else piece)
            rows.append(last)
            for other in range(sz.lanes):
                first = ((d * sz.lanes + other) * sz.group + g) * 4
                for q, row in enumerate(rows):
                    out[pl.ds(first + q, 1), :] = row

    loop(sz.owners, one)


def pick_kernel(sz, *refs):
    inputs, (out, send_out), held, (chunks, sems) = refs[:5], refs[5:7], refs[7:12], refs[12:]
    for copy in fetch(inputs, held, sems):
        copy.wait()
    send, target, source, count, positions = held
    for j in range(send_out.shape[1]):
        send_out[0, j] = send[0, j]
    lane = lax.axis_index("lane")
    for i in range(3):
        for g in range(0, sz.cells, 8):
            value = own_chunk(sz, lane, positions.at[i], pl.ds(g, 8))
            chunks[pl.ds(i * sz.rows + g, 8), :] = value
    spare = jnp.zeros((1, 128 - sz.cap), F32)
    tasks = jnp.where(lane_iota(1) == 3 * sz.rest + 2 * sz.cap, count[0].astype(F32), 0.0)
    for q, row in enumerate((target, source)):
        wide = jnp.concatenate([row[...].astype(F32), spare], axis=1)
        tasks = tasks + pltpu.roll(wide, 3 * sz.rest + q * sz.cap, 1)
    send_ghosts(sz, send, chunks, out, tasks)


def take_ghosts(sz, arrived, pool, stride, base):
    lanes = lane_iota(1)

    def one(d):
        for g in range(sz.group):
            first = [((d * sz.lanes + lane) * sz.group + g) * 4 for lane in range(sz.lanes)]
            last = [arrived[pl.ds(row + 3, 1), :] for row in first]
            for i in range(3):
                tiles = []
                if sz.main:
                    tiles += [arrived[pl.ds(row + i, 1), :] for row in first]
                for tile in range(sz.rest_tiles):
                    total = jnp.zeros((1, 128), F32)
                    for lane in range(sz.lanes):
                        start = sz.rest * lane
                        if start + sz.rest <= 128 * tile or start >= 128 * tile + 128:
                            continue
                        shift = (start - i * sz.rest) % 128
                        value = pltpu.roll(last[lane], shift, 1) if shift else last[lane]
                        at = lanes + 128 * tile
                        total = jnp.where((at >= start) & (at < start + sz.rest), value, total)
                    tiles.append(total)
                place = pl.ds(i * stride + base + d * sz.group + g, 1)
                pool[place, :] = jnp.concatenate(tiles, axis=1)

    loop(sz.owners, one)


def build_list(sz, lists, tasks):
    total = jnp.int32(0)
    for lane in range(sz.lanes):
        count = lists[lane, 2 * sz.cap]
        for j in range(sz.cap):
            tasks[0, total] = lists[lane, j]
            tasks[1, total] = lists[lane, sz.cap + j]
            total = total + (j < count).astype(jnp.int32)
    for u in range(UNROLL):
        tasks[0, total + u] = jnp.int32(sz.cells)
        tasks[1, total + u] = jnp.int32(0)
    tasks[2, 0] = total
    return total


def own_list(sz, lane, tasks, mine, low, high):
    first = lane * sz.share
    total = tasks[2, 0]
    count = jnp.int32(0)
    for t in range(sz.lanes * sz.cap):
        target = tasks[0, t] - first
        source = tasks[1, t]
        mine[0, count] = target
        mine[1, count] = source - low
        taken = (target >= 0) & (target < sz.share) & (t < total)
        taken = taken & (source >= low) & (source < high)
        count = count + taken.astype(jnp.int32)
    for u in range(PAIR):
        mine[0, count + u] = jnp.int32(-1)
        mine[1, count + u] = jnp.int32(0)
    return count


def products(value, bend_high, bend_low):
    high, low = split2(value)
    dot = functools.partial(jnp.dot, preferred_element_type=F32)
    return dot(high, bend_high) + dot(low, bend_high) + dot(high, bend_low)


def make_sources(sz, value, bend_high, bend_low, source_rows, centres, first):
    count = value.shape[0] // 3
    forces = products(value[:, : sz.points], bend_high, bend_low)
    forces = jnp.concatenate(
        [forces, jnp.zeros((3 * count, sz.width - sz.points), F32)], axis=1
    )
    middle = jnp.sum(value, axis=1, keepdims=True) / sz.points
    for g in range(count // 8):
        where = [i * count + 8 * g for i in range(3)]
        middles = [jnp.broadcast_to(middle[w : w + 8], (8, 128)) for w in where]
        middles += [jnp.zeros((8, 128), F32)] * 5
        for i, row in enumerate(middles):
            centres[pl.ds(8 * (first + 8 * g) + i, 8, stride=8), :] = row
        for j in range(sz.tiles):
            cut = slice(128 * j, 128 * j + 128)
            y = [value[w : w + 8, cut] - m for w, m in zip(where, middles)]
            f = [forces[w : w + 8, cut] for w in where]
            norm = y[0] * y[0] + y[1] * y[1] + y[2] * y[2] + REGULARIZE
            along = y[0] * f[0] + y[1] * f[1] + y[2] * f[2]
            one, zero = jnp.ones((8, 128), F32), jnp.zeros((8, 128), F32)
            rows = [y[0], y[1], y[2], norm, one, zero, zero, zero]
            rows += f
            rows += [y[i] * f[k] for i in range(3) for k in range(3)]
            rows += [norm * f[i] + along * y[i] for i in range(3)]
            rows += [along]
            for k, row in enumerate(rows):
                place = pl.ds(SOURCE_ROWS * (first + 8 * g) + k, 8, stride=SOURCE_ROWS)
                source_rows.at[j][place, :] = row


def make_targets(sz, blocks, targets):
    targets[...] = jnp.zeros_like(targets)
    for i in range(3):
        for g in range(blocks[i].shape[0] // 8):
            block = blocks[i][8 * g : 8 * g + 8]
            for j in range(targets.shape[0]):
                cut = slice(128 * j, 128 * j + 128)
                targets.at[j][pl.ds(64 * g + i, 8, stride=8), :] = block[:, cut]


def source_operands(sz, source, source_rows):
    held = [
        source_rows[j, pl.ds(pl.multiple_of(SOURCE_ROWS * source, 8), SOURCE_ROWS), :]
        for j in range(sz.tiles)
    ]
    held = jnp.concatenate(held, axis=1)
    y1, y2, y3 = split3(held[:8])
    y_stack = jnp.concatenate([y1, y1, y2, y2, y1, y3], axis=0).astype(BF16)
    return y_stack, jnp.concatenate(split3(held[8:]), axis=0)


def pieces(points, step):
    starts = list(range(0, max(points // 128 * 128, 1), step))
    return list(zip(starts, starts[1:] + [points]))


def twice(piece, count):
    whole = count // 128 * 128
    parts = [piece[:, :whole].astype(BF16)] * 2 if whole else []
    if whole < count:
        last = piece[:, whole:]
        last = last + pltpu.roll(last, count - whole, 1)
        parts.append(last.astype(BF16)[:, : 2 * (count - whole)])
    return jnp.concatenate(parts, axis=1)


def load_target(j, target, slot, centre, targets, offsets):
    row = lax.broadcasted_iota(jnp.int32, (8, 128), 0)
    x = targets[j, pl.ds(pl.multiple_of(8 * target, 8), 8), :] - centre
    square = x * x
    norm = pltpu.roll(square, 2, 0) + pltpu.roll(square, 3, 0) + pltpu.roll(square, 4, 0)
    side = jnp.where(row == 4, norm, jnp.where(row == 3, 1.0, 0.0))
    x_side = jnp.where(row < 3, -2.0 * x, side)
    x1, x2, x3 = split3(x_side)
    return x, jnp.concatenate([x1, x2, x1, x2, x3, x1], axis=0).astype(BF16)


def distances(one_stack, other_stack):
    return jnp.dot(one_stack, other_stack, preferred_element_type=F32)


def weights(shifted):
    inverse = lax.rsqrt(shifted)
    return split2(inverse * inverse * inverse)


def fold(result):
    return result[:SUM_ROWS] + result[SUM_ROWS : 2 * SUM_ROWS] + result[2 * SUM_ROWS :]


def skewed(stages, skew):
    asked = []
    for q, (ask, _) in enumerate(stages):
        asked.append(ask())
        if q >= skew:
            stages[q - skew][1](asked[q - skew])
            asked[q - skew] = None
    for q in range(max(len(stages) - skew, 0), len(stages)):
        stages[q][1](asked[q])


def adder(totals, key):
    def add(value):
        totals[key] = totals[key] + value if key in totals else value

    return add


def wide_piece(operands, begin, first, end, add):
    def ask():
        _, y_turned, _, blocks = operands()
        return distances(y_turned[first:end], blocks[begin])

    def take(shifted):
        m_piece = operands()[2][first]
        high, low = weights(shifted)
        whole = (end - first) // 128 * 128
        parts = [high[:whole], low[:whole]] if whole else []
        parts += [high[whole:], low[whole:]] if whole < end - first else []
        stack = jnp.concatenate(parts, axis=0)
        add(jnp.dot(m_piece, stack, preferred_element_type=F32))

    return ask, take


def rest_piece(operands, begin, add):
    def ask():
        y_stack, _, _, blocks = operands()
        return distances(blocks[begin], y_stack)

    def take(shifted):
        high, low = weights(shifted)
        m_whole = operands()[2][-1]
        turned = (((1,), (1,)), ((), ()))
        result = lax.dot_general(m_whole, high, turned, preferred_element_type=F32)
        add(result + lax.dot_general(m_whole, low, turned, preferred_element_type=F32))

    return ask, take


def store_sums(slots, slot, j, x, result, offsets, sums):
    offsets.at[j][pl.ds(slot, 8, stride=slots), :] = x
    for h in range(0, SUM_ROWS, 8):
        sums.at[j][pl.ds(h * slots + slot, 8, stride=slots), :] = result[h : h + 8]


def mark(slot, target, hot):
    hot[pl.ds(slot, 1), :] = jnp.where(lane_iota(1) == target, 1.0, 0.0)


def combine(sz, slots, first, total, offsets, sums, speeds):
    live = lax.broadcasted_iota(jnp.int32, (8, 128), 0) + first < total
    for j in range(offsets.shape[0]):
        x = [offsets[j, pl.ds(i * slots + first, 8), :] for i in range(3)]
        s = [sums[j, pl.ds(k * slots + first, 8), :] for k in range(SUM_ROWS)]
        a, b, c = s[:3], [s[3:6], s[6:9], s[9:12]], s[12:15]
        norm = x[0] * x[0] + x[1] * x[1] + x[2] * x[2] + REGULARIZE
        along = x[0] * a[0] + x[1] * a[1] + x[2] * a[2] - s[15]
        for i in range(3):
            speed = norm * a[i] + c[i] + along * x[i]
            for k in range(3):
                speed = speed - x[k] * (2.0 * b[k][i] + b[i][k])
            speed = jnp.where(live, speed / sz.points, 0.0)
            speeds[i, pl.ds(first, 8), 128 * j : 128 * j + 128] = speed


def add_up(sz, slots, total, rows, offsets, sums, speeds, hot):
    def eight(q, carry):
        combine(sz, slots, pl.multiple_of(8 * q, 8), total, offsets, sums, speeds)
        return carry

    if slots <= 64 and offsets.shape[0] <= 2:
        for q in range(slots // 8):
            combine(sz, slots, 8 * q, total, offsets, sums, speeds)
    else:
        lax.fori_loop(0, lax.div(total + 7, 8), eight, 0)
    one_hot = hot[...].astype(BF16)
    result = []
    for i in range(3):
        first, second, third = split3(speeds[i])
        parts = [
            lax.dot_general(
                one_hot, part.astype(BF16), (((0,), (0,)), ((), ())), preferred_element_type=F32
            )
            for part in (first, second, third)
        ]
        result.append((parts[0] + parts[1] + parts[2])[:rows])
    return result


def several_tasks(sz, slots, picks, marks, main, rest, wide, step, skew, refs):
    source_rows, centres, targets, offsets, sums, hot = refs

    def task(slot, pick, target_mark):
        target, source = pick
        made, parts, points = [], {}, []

        def operands():
            if made:
                return made[0]
            y_stack, m_stack = source_operands(sz, source, source_rows)
            centre = centres[pl.ds(pl.multiple_of(8 * source, 8), 8), :]
            points.extend(
                load_target(j, target, slot, centre, targets, offsets)
                for j in range(targets.shape[0])
            )
            blocks = {}
            for begin in range(0, main, wide):
                stack = [stack for _, stack in points[begin // 128 : (begin + wide) // 128]]
                blocks[begin] = jnp.concatenate(stack, axis=1)
            if rest:
                blocks[main] = jnp.transpose(points[main // 128][1])[:rest]
            sides = {-1: m_stack.astype(BF16)}
            if main:
                for first, last in pieces(sz.points, step):
                    sides[first] = twice(m_stack[:, first : up(last, 128)], last - first)
            made.append((y_stack, jnp.transpose(y_stack), sides, blocks))
            return made[0]

        def finish():
            results = [fold(parts[begin]) for begin in range(0, main, wide)]
            if rest:
                spare = jnp.zeros((SUM_ROWS, 128 - rest), F32)
                results.append(jnp.concatenate([fold(parts[main]), spare], axis=1))
            result = jnp.concatenate(results, axis=1)
            for j in range(targets.shape[0]):
                cut = result[:, 128 * j : 128 * j + 128]
                store_sums(offsets.shape[1] // 8, slot, j, points[j][0], cut, offsets, sums)
            mark(slot, target_mark, hot)

        own = []
        for begin in range(0, main, wide):
            for first, last in pieces(sz.points, step):
                own.append(wide_piece(operands, begin, first, last, adder(parts, begin)))
        if rest:
            own.insert(len(own) // 2, rest_piece(operands, main, adder(parts, main)))
        ask, take = own[-1]

        def last_take(shifted):
            take(shifted)
            finish()

        own[-1] = (ask, last_take)
        return own, operands

    made = [task(slot, pick, m) for slot, pick, m in zip(slots, picks, marks)]
    for (own, _), (_, after) in zip(made, made[1:]):
        ask, take = own[0]

        def ask_and_prepare(ask=ask, after=after):
            shifted = ask()
            after()
            return shifted

        own[0] = (ask_and_prepare, take)
    skewed([stage for own, _ in made for stage in own], skew)


def tiles_of_chunk(sz, total, tasks, *refs):
    def several(q, carry):
        slots = [q * UNROLL + u for u in range(UNROLL)]
        picks = [(tasks[0, slot], tasks[1, slot]) for slot in slots]
        marks = [target for target, _ in picks]
        several_tasks(sz, slots, picks, marks, sz.main, sz.rest, 128, 256, 5, refs)
        return carry

    lax.fori_loop(0, lax.div(total + UNROLL - 1, UNROLL), several, 0)


def tiles_of_cells(sz, total, mine, *refs):
    main = 256 * (sz.points // 256)

    def several(q, carry):
        slots = [q * PAIR + u for u in range(PAIR)]
        marks = [mine[0, slot] for slot in slots]
        picks = [(jnp.maximum(mark, 0), mine[1, slot]) for mark, slot in zip(marks, slots)]
        several_tasks(sz, slots, picks, marks, main, sz.points - main, 256, 256, 3, refs)
        return carry

    lax.fori_loop(0, lax.div(total + PAIR - 1, PAIR), several, 0)


def packed(sz, blocks):
    rows = [b[:, : sz.main] for b in blocks] if sz.main else []
    lanes = lane_iota(8)
    for p in range(0, len(blocks), sz.per_pack):
        total = jnp.zeros((8, 128), F32)
        for q, block in enumerate(blocks[p : p + sz.per_pack]):
            rest = jnp.where(lanes < sz.rest, block[:, sz.main : sz.main + 128], 0.0)
            total = total + (pltpu.roll(rest, q * sz.rest, 1) if q else rest)
        rows.append(total)
    return rows


def store_packed(sz, out, blocks):
    first = 0
    count = len(blocks)
    values = packed(sz, blocks)
    if sz.main:
        for b in range(count):
            for m in range(sz.main // 128):
                out[pl.ds(first, 8), :] = values[b][:, 128 * m : 128 * m + 128]
                first += 8
        values = values[count:]
    for value in values:
        out[pl.ds(first, 8), :] = value
        first += 8


def place_packed(sz, lane, arrived, count, store_main, add_rest):
    first = 0
    if sz.main:
        for b in range(count):
            for m in range(sz.main // 128):
                store_main(b, m, arrived[pl.ds(first, 8), :])
                first += 8
    start = sz.rest * lane
    lanes = lane_iota(8)
    for b in range(count):
        pack, q = divmod(b, sz.per_pack)
        value = arrived[pl.ds(first + 8 * pack, 8), :]
        value = pltpu.roll(value, lax.rem(start - q * sz.rest + 128, 128), 1)
        for tile in range(sz.rest_tiles):
            inside = (lanes + 128 * tile >= start) & (lanes + 128 * tile < start + sz.rest)
            add_rest(b, tile, jnp.where(inside, value, 0.0))


def source_kernel(sz, *refs):
    inputs, (high_out, low_out, source_rows, centres), held, sems = (
        refs[:2],
        refs[2:6],
        refs[6:8],
        refs[8],
    )
    for copy in fetch(inputs, held, sems):
        copy.wait()
    positions, bend = held
    high_out[...], low_out[...] = split2(bend[...])
    value = jnp.concatenate([positions[i] for i in range(3)], axis=0)
    value = jnp.concatenate(
        [value, jnp.zeros((3 * sz.cells, sz.width - sz.points), F32)], axis=1
    )
    make_sources(sz, value, high_out[...], low_out[...], source_rows, centres, 0)


def first_kernel(sz, *refs):
    arrived, high, low, inputs = refs[0], refs[1], refs[2], refs[3:7]
    outputs, refs = refs[7:10], refs[10:]
    source_rows, centres, targets, offsets, sums, speeds, hot, moved, pool = refs[:9]
    send, positions, staged, lists, chunk_out, ghost_out, tasks, sems = refs[9:]
    me, lane = lax.axis_index("space"), lax.axis_index("lane")
    own_rows = source_rows.at[:, pl.ds(0, SOURCE_ROWS * sz.cells)]
    own_centres = centres.at[pl.ds(0, 8 * sz.cells)]
    copies = fetch(inputs, [send, positions, own_rows, own_centres], sems)
    for other in range(sz.lanes):
        row = ((me * sz.lanes + other) * sz.group) * 4 + 3
        value = pltpu.roll(arrived[pl.ds(row, 1), :], 128 - 3 * sz.rest, 1)
        staged[pl.ds(other, 1), :] = value.astype(jnp.int32)
    copies += fetch([staged], [lists], sems.at[pl.ds(4, 1)])
    pool[...] = jnp.zeros_like(pool)
    take_ghosts(sz, arrived, pool, up(sz.owners * sz.group, 8), 0)
    hot[...] = jnp.zeros_like(hot)
    speeds[...] = jnp.zeros_like(speeds)
    make_sources(sz, pool[...], high[...], low[...], source_rows, centres, sz.cells)
    for copy in copies[:2]:
        copy.wait()
    chunks = [
        [own_chunk(sz, lane, positions.at[i], pl.ds(g, 8)) for g in range(0, sz.cells, 8)]
        for i in range(3)
    ]
    make_targets(sz, [jnp.concatenate(blocks, axis=0) for blocks in chunks], targets)
    copies[4].wait()
    total = build_list(sz, lists, tasks)
    for copy in copies[2:4]:
        copy.wait()
    copies = fetch([tasks], outputs[2:], sems)
    tiles_of_chunk(sz, total, tasks, source_rows, centres, targets, offsets, sums, hot)
    velocity = add_up(sz, sz.slots, total, sz.cells, offsets, sums, speeds, hot)
    blocks = []
    for i in range(3):
        for g in range(0, sz.cells, 8):
            chunk = own_chunk(sz, lane, positions.at[i], pl.ds(g, 8))
            block = chunk + TIME_STEP * velocity[i][g : g + 8]
            moved[pl.ds(i * sz.rows + g, 8), :] = block
            blocks.append(block)
    store_packed(sz, chunk_out, blocks)
    copies += fetch([chunk_out], outputs[:1], sems.at[pl.ds(1, 1)])
    send_ghosts(sz, send, moved, ghost_out, jnp.zeros((1, 128), F32))
    copies += fetch([ghost_out], outputs[1:2], sems.at[pl.ds(2, 1)])
    for copy in copies:
        copy.wait()


def own_kernel(sz, *refs):
    (high, low), refs = refs[:2], refs[2:]
    others, refs = refs[: sz.lanes - 1], refs[sz.lanes - 1 :]
    inputs, (speed_out, share_out), refs = refs[:2], refs[2:4], refs[4:]
    source_rows, centres, targets, offsets, sums, speeds, hot, pool, mine = refs[:9]
    tasks, chunk, sems = refs[9:]
    copies = fetch(inputs, [tasks, chunk], sems)
    chunks = [chunk, *others]
    hot[...] = jnp.zeros_like(hot)
    speeds[...] = jnp.zeros_like(speeds)
    lane = lax.axis_index("lane")
    pool[...] = jnp.zeros_like(pool)
    copies[0].wait()
    total = own_list(sz, lane, tasks, mine, 0, sz.cells)
    copies[1].wait()
    per = sz.cells // 8
    for k in range(sz.lanes):
        other = lane ^ k

        def row_of(b):
            return (b // per) * sz.cells + 8 * (b % per)

        def store_main(b, m, value):
            cut = pl.ds(pl.multiple_of(other * sz.main + 128 * m, 128), 128)
            pool[pl.ds(row_of(b), 8), cut] = value

        def add_rest(b, tile, value):
            offset = sz.main * sz.lanes + 128 * tile
            cut = (pl.ds(row_of(b), 8), slice(offset, offset + 128))
            pool[cut] = pool[cut] + value

        place_packed(sz, other, chunks[k], 3 * per, store_main, add_rest)
    for i in range(3):
        share_out[i] = share_rows(sz, pool, i * sz.cells, lane)
    make_sources(sz, pool[...], high[...], low[...], source_rows, centres, 0)
    make_targets(sz, share_out, targets)
    tiles_of_cells(sz, total, mine, source_rows, centres, targets, offsets, sums, hot)
    velocity = add_up(sz, sz.own, total, up(sz.share, 8), offsets, sums, speeds, hot)
    for i in range(3):
        speed_out[i] = velocity[i]


def ghost_kernel(sz, *refs):
    arrived, high, low, speed_in, share, tasks_in = refs[:6]
    moved_out, velocity_out = refs[6:8]
    source_rows, centres, targets, offsets, sums, speeds, hot, pool, mine = refs[8:17]
    tasks, sems = refs[17:]
    copies = fetch([tasks_in], [tasks], sems)
    hot[...] = jnp.zeros_like(hot)
    speeds[...] = jnp.zeros_like(speeds)
    lane = lax.axis_index("lane")
    pool[...] = jnp.zeros_like(pool)
    ghosts = up(sz.owners * sz.group, 8)
    take_ghosts(sz, arrived, pool, ghosts, 0)
    make_sources(sz, pool[...], high[...], low[...], source_rows, centres, 0)
    make_targets(sz, share, targets)
    copies[0].wait()
    total = own_list(sz, lane, tasks, mine, sz.cells, sz.cells + sz.owners * sz.group)
    tiles_of_cells(sz, total, mine, source_rows, centres, targets, offsets, sums, hot)
    velocity = add_up(sz, sz.own, total, up(sz.share, 8), offsets, sums, speeds, hot)
    for i in range(3):
        speed = velocity[i] + speed_in[i]
        velocity_out[i] = speed[: sz.share, : sz.points]
        moved_out[i] = (share[i] + TIME_STEP * speed)[: sz.share, : sz.points]


def share_rows(sz, ref, base, lane):
    if sz.share % 8 == 0:
        return ref[pl.ds(pl.multiple_of(base + lane * sz.share, 8), sz.share), :]
    rows = [ref[pl.ds(base + lane * sz.share + c, 1), :] for c in range(sz.share)]
    rows.append(jnp.zeros((8 - sz.share, rows[0].shape[1]), F32))
    return jnp.concatenate(rows, axis=0)


def scratch(sz, cells, targets, tiles, slots):
    return [
        pltpu.VMEM((sz.tiles, SOURCE_ROWS * cells, 128), F32),
        pltpu.VMEM((8 * cells, 128), F32),
        pltpu.VMEM((tiles, 8 * targets, 128), F32),
        pltpu.VMEM((tiles, 8 * slots, 128), F32),
        pltpu.VMEM((tiles, SUM_ROWS * slots, 128), F32),
        pltpu.VMEM((3, slots, 128 * tiles), F32),
        pltpu.VMEM((slots, 128), F32),
    ]


def swap(value, axis, size, k):
    return lax.ppermute(value, axis, [(d, d ^ k) for d in range(size)])


def in_hbm(value):
    return pltpu.with_memory_space_constraint(value, pltpu.HBM)


def shards(positions, bend_op, send_list, task_target, task_source, task_count):
    owners, lanes = lax.axis_size("space"), lax.axis_size("lane")
    cells, points = positions.shape[0], positions.shape[2]
    sz = sizes(owners, lanes, cells, points, task_target.shape[1], send_list.shape[1])
    params = pltpu.CompilerParams(vmem_limit_bytes=min(6 * lanes, 40) << 20)
    shape = jax.ShapeDtypeStruct
    both = ("space", "lane")
    by_component = jnp.transpose(positions, (1, 0, 2))
    list_rows = up(lanes, 8)
    slot_shape = shape((4 * sz.group * owners * lanes, 128), F32)
    leaving, send = pl.pallas_call(
        functools.partial(pick_kernel, sz),
        out_shape=[slot_shape, shape(send_list.shape, jnp.int32)],
        in_specs=[HBM] * 5,
        out_specs=[VMEM, SMEM],
        scratch_shapes=[
            pltpu.SMEM(send_list.shape, jnp.int32),
            pltpu.VMEM(task_target.shape, jnp.int32),
            pltpu.VMEM(task_source.shape, jnp.int32),
            pltpu.SMEM(task_count.shape, jnp.int32),
            pltpu.VMEM(by_component.shape, F32),
            pltpu.VMEM((3 * sz.rows, sz.chunk_wide), F32),
            pltpu.SemaphoreType.DMA((5,)),
        ],
        compiler_params=pltpu.CompilerParams(vmem_limit_bytes=60 << 20),
        name="pick_cells",
    )(send_list, task_target, task_source, task_count, by_component)
    arrived = lax.all_to_all(leaving, both, split_axis=0, concat_axis=0, tiled=True)
    high, low, own_rows, own_centres = pl.pallas_call(
        functools.partial(source_kernel, sz),
        out_shape=[
            shape(bend_op.shape, BF16),
            shape(bend_op.shape, BF16),
            shape((sz.tiles, SOURCE_ROWS * cells, 128), F32),
            shape((8 * cells, 128), F32),
        ],
        in_specs=[HBM] * 2,
        out_specs=[VMEM] * 4,
        scratch_shapes=[
            pltpu.VMEM(by_component.shape, F32),
            pltpu.VMEM(bend_op.shape, F32),
            pltpu.SemaphoreType.DMA((2,)),
        ],
        compiler_params=params,
        cost_estimate=pl.CostEstimate(flops=10**9, bytes_accessed=10**7, transcendentals=0),
        name="first_sources",
    )(in_hbm(by_component), in_hbm(bend_op))
    chunk_shape = (pack_rows(sz, cells), 128)
    chunk, leaving, tasks = pl.pallas_call(
        functools.partial(first_kernel, sz),
        out_shape=[
            pltpu.HBM(chunk_shape, F32),
            pltpu.HBM(slot_shape.shape, F32),
            pltpu.HBM((3, sz.slots), jnp.int32),
        ],
        in_specs=[VMEM] * 3 + [HBM] * 2 + [ANY] * 2,
        out_specs=[HBM] * 3,
        scratch_shapes=scratch(sz, sz.pool, sz.rows, sz.chunk_tiles, sz.slots)
        + [
            pltpu.VMEM((3 * sz.rows, sz.chunk_wide), F32),
            pltpu.VMEM((3 * up(sz.owners * sz.group, 8), sz.width), F32),
            pltpu.SMEM(send_list.shape, jnp.int32),
            pltpu.VMEM(by_component.shape, F32),
            pltpu.VMEM((list_rows, 128), jnp.int32),
            pltpu.SMEM((list_rows, 128), jnp.int32),
            pltpu.VMEM(chunk_shape, F32),
            pltpu.VMEM(slot_shape.shape, F32),
            pltpu.SMEM((3, sz.slots), jnp.int32),
            pltpu.SemaphoreType.DMA((5,)),
        ],
        compiler_params=params,
        name="first_step",
    )(arrived, high, low, in_hbm(send), in_hbm(by_component), own_rows, own_centres)
    arrived = lax.all_to_all(leaving, both, split_axis=0, concat_axis=0, tiled=True)
    chunks = [swap(chunk, "lane", lanes, k) for k in range(1, lanes)]
    share = up(sz.share, 8)
    so_far = shape((3, share, sz.width), F32)
    speed, moved = pl.pallas_call(
        functools.partial(own_kernel, sz),
        out_shape=[so_far, so_far],
        in_specs=[VMEM] * (lanes + 1) + [HBM] * 2,
        out_specs=[VMEM] * 2,
        scratch_shapes=scratch(sz, cells, share, sz.tiles, sz.own)
        + [
            pltpu.VMEM((3 * cells, sz.width), F32),
            pltpu.SMEM((2, sz.own + 8), jnp.int32),
            pltpu.SMEM(tasks.shape, jnp.int32),
            pltpu.VMEM(chunk.shape, F32),
            pltpu.SemaphoreType.DMA((2,)),
        ],
        compiler_params=params,
        cost_estimate=pl.CostEstimate(flops=10**9, bytes_accessed=10**7, transcendentals=0),
        name="second_own",
    )(high, low, *chunks, in_hbm(tasks), in_hbm(chunk))
    result = shape((3, sz.share, points), F32)
    ghosts = up(owners * sz.group, 8)
    outputs = pl.pallas_call(
        functools.partial(ghost_kernel, sz),
        out_shape=[result, result],
        in_specs=[VMEM] * 5 + [HBM],
        out_specs=[VMEM] * 2,
        scratch_shapes=scratch(sz, ghosts, share, sz.tiles, sz.own)
        + [
            pltpu.VMEM((3 * ghosts, sz.width), F32),
            pltpu.SMEM((2, sz.own + 8), jnp.int32),
            pltpu.SMEM(tasks.shape, jnp.int32),
            pltpu.SemaphoreType.DMA((1,)),
        ],
        compiler_params=params,
        name="second_ghosts",
    )(arrived, high, low, speed, moved, in_hbm(tasks))
    return tuple(jnp.transpose(output, (1, 0, 2)) for output in outputs)


def solution(mesh):
    in_specs = (
        P("space", None, None),
        P(),
        P("space", None),
        P(("space", "lane"), None),
        P(("space", "lane"), None),
        P(("space", "lane")),
    )
    out_specs = (P(("space", "lane"), None, None), P(("space", "lane"), None, None))
    return jax.shard_map(shards, mesh=mesh, in_specs=in_specs, out_specs=out_specs, check_vma=False)
```

```python
import functools
from types import SimpleNamespace

import jax
import jax.numpy as jnp
from jax import lax
from jax.experimental import pallas as pl
from jax.experimental.pallas import tpu as pltpu
from jax.sharding import PartitionSpec as P

REGULARIZE = 0.25
TIME_STEP = 0.5
UNROLL = 11
PAIR = 2
SOURCE_ROWS = 24
SUM_ROWS = 16

F32 = jnp.float32
BF16 = jnp.bfloat16
VMEM = pl.BlockSpec(memory_space=pltpu.VMEM)
SMEM = pl.BlockSpec(memory_space=pltpu.SMEM)
HBM = pl.BlockSpec(memory_space=pltpu.HBM)
ANY = pl.BlockSpec(memory_space=pl.ANY)


def up(value, step):
    return -(-value // step) * step


def sizes(owners, lanes, cells, points, cap, listed):
    main = 128 * (points // (128 * lanes))
    rest = (points - main * lanes) // lanes
    group = listed // owners
    pool = up(cells + listed, 8)
    per_pack = 128 // rest
    return SimpleNamespace(
        owners=owners,
        lanes=lanes,
        cells=cells,
        points=points,
        cap=cap,
        group=group,
        width=up(points, 128),
        tiles=up(points, 128) // 128,
        main=main,
        rest=rest,
        rest_tiles=up(rest * lanes, 128) // 128,
        chunk=main + rest,
        chunk_wide=main + up(rest, 128),
        chunk_tiles=(main + up(rest, 128)) // 128,
        per_pack=per_pack,
        pool=pool,
        share=cells // lanes,
        slots=up(lanes * cap + UNROLL, 8),
        rows=cells + 8,
        own=up(lanes * cap + PAIR, 8),
    )


def pack_rows(sz, rows):
    return (3 * rows * sz.main // 128) + 8 * up(3 * rows // 8, sz.per_pack) // sz.per_pack


def split2(value):
    high = value.astype(BF16)
    return high, (value - high.astype(F32)).astype(BF16)


def split3(value):
    first = value.astype(BF16).astype(F32)
    left = value - first
    second = left.astype(BF16).astype(F32)
    return first, second, left - second


def lane_iota(rows):
    return lax.broadcasted_iota(jnp.int32, (rows, 128), 1)


def fetch(sources, targets, sems):
    copies = [
        pltpu.make_async_copy(source, target, sems.at[q])
        for q, (source, target) in enumerate(zip(sources, targets))
    ]
    for copy in copies:
        copy.start()
    return copies


def loop(count, body):
    if count <= 8:
        for q in range(count):
            body(q)
    else:

        def step(q, carry):
            body(q)
            return carry

        lax.fori_loop(0, count, step, 0)


def own_chunk(sz, lane, ref, rows):
    parts = []
    if sz.main:
        parts.append(ref[rows, pl.ds(pl.multiple_of(lane * sz.main, 128), sz.main)])
    start = sz.rest * lane
    lanes = lane_iota(8)
    rest = jnp.zeros((8, 128), F32)
    for tile in range(sz.rest_tiles):
        offset = sz.main * sz.lanes + 128 * tile
        block = ref[rows, offset : min(offset + 128, ref.shape[-1])]
        if block.shape[1] < 128:
            block = jnp.concatenate([block, jnp.zeros((8, 128 - block.shape[1]), F32)], axis=1)
        inside = (lanes + 128 * tile >= start) & (lanes + 128 * tile < start + sz.rest)
        rest = rest + jnp.where(inside, block, 0.0)
    rest = pltpu.roll(rest, lax.rem(128 * sz.rest_tiles - start, 128), 1)
    parts.append(rest)
    return jnp.concatenate(parts, axis=1) if len(parts) > 1 else parts[0]


def send_ghosts(sz, send, chunks, out, tasks):
    lanes = lane_iota(1)

    def one(d):
        for g in range(sz.group):
            cell = send[0, d * sz.group + g]
            rows = []
            last = tasks
            for i in range(3):
                row = chunks[pl.ds(i * sz.rows + cell, 1), :]
                rows.append(row[:, :128] if sz.main else jnp.zeros((1, 128), F32))
                piece = jnp.where(lanes < sz.rest, row[:, sz.main : sz.main + 128], 0.0)
                last = last + (pltpu.roll(piece, i * sz.rest, 1) if i else piece)
            rows.append(last)
            for other in range(sz.lanes):
                first = ((d * sz.lanes + other) * sz.group + g) * 4
                for q, row in enumerate(rows):
                    out[pl.ds(first + q, 1), :] = row

    loop(sz.owners, one)


def pick_kernel(sz, *refs):
    inputs, (out, send_out), held, (chunks, sems) = refs[:5], refs[5:7], refs[7:12], refs[12:]
    for copy in fetch(inputs, held, sems):
        copy.wait()
    send, target, source, count, positions = held
    for j in range(send_out.shape[1]):
        send_out[0, j] = send[0, j]
    lane = lax.axis_index("lane")
    for i in range(3):
        for g in range(0, sz.cells, 8):
            value = own_chunk(sz, lane, positions.at[i], pl.ds(g, 8))
            chunks[pl.ds(i * sz.rows + g, 8), :] = value
    spare = jnp.zeros((1, 128 - sz.cap), F32)
    tasks = jnp.where(lane_iota(1) == 3 * sz.rest + 2 * sz.cap, count[0].astype(F32), 0.0)
    for q, row in enumerate((target, source)):
        wide = jnp.concatenate([row[...].astype(F32), spare], axis=1)
        tasks = tasks + pltpu.roll(wide, 3 * sz.rest + q * sz.cap, 1)
    send_ghosts(sz, send, chunks, out, tasks)


def take_ghosts(sz, arrived, pool, stride, base):
    lanes = lane_iota(1)

    def one(d):
        for g in range(sz.group):
            first = [((d * sz.lanes + lane) * sz.group + g) * 4 for lane in range(sz.lanes)]
            last = [arrived[pl.ds(row + 3, 1), :] for row in first]
            for i in range(3):
                tiles = []
                if sz.main:
                    tiles += [arrived[pl.ds(row + i, 1), :] for row in first]
                for tile in range(sz.rest_tiles):
                    total = jnp.zeros((1, 128), F32)
                    for lane in range(sz.lanes):
                        start = sz.rest * lane
                        if start + sz.rest <= 128 * tile or start >= 128 * tile + 128:
                            continue
                        shift = (start - i * sz.rest) % 128
                        value = pltpu.roll(last[lane], shift, 1) if shift else last[lane]
                        at = lanes + 128 * tile
                        total = jnp.where((at >= start) & (at < start + sz.rest), value, total)
                    tiles.append(total)
                place = pl.ds(i * stride + base + d * sz.group + g, 1)
                pool[place, :] = jnp.concatenate(tiles, axis=1)

    loop(sz.owners, one)


def build_list(sz, lists, tasks):
    total = jnp.int32(0)
    for lane in range(sz.lanes):
        count = lists[lane, 2 * sz.cap]
        for j in range(sz.cap):
            tasks[0, total] = lists[lane, j]
            tasks[1, total] = lists[lane, sz.cap + j]
            total = total + (j < count).astype(jnp.int32)
    for u in range(UNROLL):
        tasks[0, total + u] = jnp.int32(sz.cells)
        tasks[1, total + u] = jnp.int32(0)
    tasks[2, 0] = total
    return total


def own_list(sz, lane, tasks, mine, low, high):
    first = lane * sz.share
    total = tasks[2, 0]
    count = jnp.int32(0)
    for t in range(sz.lanes * sz.cap):
        target = tasks[0, t] - first
        source = tasks[1, t]
        mine[0, count] = target
        mine[1, count] = source - low
        taken = (target >= 0) & (target < sz.share) & (t < total)
        taken = taken & (source >= low) & (source < high)
        count = count + taken.astype(jnp.int32)
    for u in range(PAIR):
        mine[0, count + u] = jnp.int32(-1)
        mine[1, count + u] = jnp.int32(0)
    return count


def products(value, bend_high, bend_low):
    high, low = split2(value)
    dot = functools.partial(jnp.dot, preferred_element_type=F32)
    return dot(high, bend_high) + dot(low, bend_high) + dot(high, bend_low)


def make_sources(sz, value, bend_high, bend_low, source_rows, centres, first):
    count = value.shape[0] // 3
    forces = products(value[:, : sz.points], bend_high, bend_low)
    forces = jnp.concatenate(
        [forces, jnp.zeros((3 * count, sz.width - sz.points), F32)], axis=1
    )
    middle = jnp.sum(value, axis=1, keepdims=True) / sz.points
    for g in range(count // 8):
        where = [i * count + 8 * g for i in range(3)]
        middles = [jnp.broadcast_to(middle[w : w + 8], (8, 128)) for w in where]
        middles += [jnp.zeros((8, 128), F32)] * 5
        for i, row in enumerate(middles):
            centres[pl.ds(8 * (first + 8 * g) + i, 8, stride=8), :] = row
        for j in range(sz.tiles):
            cut = slice(128 * j, 128 * j + 128)
            y = [value[w : w + 8, cut] - m for w, m in zip(where, middles)]
            f = [forces[w : w + 8, cut] for w in where]
            norm = y[0] * y[0] + y[1] * y[1] + y[2] * y[2] + REGULARIZE
            along = y[0] * f[0] + y[1] * f[1] + y[2] * f[2]
            one, zero = jnp.ones((8, 128), F32), jnp.zeros((8, 128), F32)
            rows = [y[0], y[1], y[2], norm, one, zero, zero, zero]
            rows += f
            rows += [y[i] * f[k] for i in range(3) for k in range(3)]
            rows += [norm * f[i] + along * y[i] for i in range(3)]
            rows += [along]
            for k, row in enumerate(rows):
                place = pl.ds(SOURCE_ROWS * (first + 8 * g) + k, 8, stride=SOURCE_ROWS)
                source_rows.at[j][place, :] = row


def make_targets(sz, blocks, targets):
    targets[...] = jnp.zeros_like(targets)
    for i in range(3):
        for g in range(blocks[i].shape[0] // 8):
            block = blocks[i][8 * g : 8 * g + 8]
            for j in range(targets.shape[0]):
                cut = slice(128 * j, 128 * j + 128)
                targets.at[j][pl.ds(64 * g + i, 8, stride=8), :] = block[:, cut]


def source_operands(sz, source, source_rows):
    held = [
        source_rows[j, pl.ds(pl.multiple_of(SOURCE_ROWS * source, 8), SOURCE_ROWS), :]
        for j in range(sz.tiles)
    ]
    held = jnp.concatenate(held, axis=1)
    y1, y2, y3 = split3(held[:8])
    y_stack = jnp.concatenate([y1, y1, y2, y2, y1, y3], axis=0).astype(BF16)
    return y_stack, jnp.concatenate(split3(held[8:]), axis=0)


def pieces(points, step):
    starts = list(range(0, max(points // 128 * 128, 1), step))
    return list(zip(starts, starts[1:] + [points]))


def twice(piece, count):
    whole = count // 128 * 128
    parts = [piece[:, :whole].astype(BF16)] * 2 if whole else []
    if whole < count:
        last = piece[:, whole:]
        last = last + pltpu.roll(last, count - whole, 1)
        parts.append(last.astype(BF16)[:, : 2 * (count - whole)])
    return jnp.concatenate(parts, axis=1)


def load_target(j, target, slot, centre, targets, offsets):
    row = lax.broadcasted_iota(jnp.int32, (8, 128), 0)
    x = targets[j, pl.ds(pl.multiple_of(8 * target, 8), 8), :] - centre
    square = x * x
    norm = pltpu.roll(square, 2, 0) + pltpu.roll(square, 3, 0) + pltpu.roll(square, 4, 0)
    side = jnp.where(row == 4, norm, jnp.where(row == 3, 1.0, 0.0))
    x_side = jnp.where(row < 3, -2.0 * x, side)
    x1, x2, x3 = split3(x_side)
    return x, jnp.concatenate([x1, x2, x1, x2, x3, x1], axis=0).astype(BF16)


def distances(one_stack, other_stack):
    return jnp.dot(one_stack, other_stack, preferred_element_type=F32)


def weights(shifted):
    inverse = lax.rsqrt(shifted)
    return split2(inverse * inverse * inverse)


def fold(result):
    return result[:SUM_ROWS] + result[SUM_ROWS : 2 * SUM_ROWS] + result[2 * SUM_ROWS :]


def skewed(stages, skew):
    asked = []
    for q, (ask, _) in enumerate(stages):
        asked.append(ask())
        if q >= skew:
            stages[q - skew][1](asked[q - skew])
            asked[q - skew] = None
    for q in range(max(len(stages) - skew, 0), len(stages)):
        stages[q][1](asked[q])


def adder(totals, key):
    def add(value):
        totals[key] = totals[key] + value if key in totals else value

    return add


def wide_piece(operands, begin, first, end, add):
    def ask():
        _, y_turned, _, blocks = operands()
        return distances(y_turned[first:end], blocks[begin])

    def take(shifted):
        m_piece = operands()[2][first]
        high, low = weights(shifted)
        whole = (end - first) // 128 * 128
        parts = [high[:whole], low[:whole]] if whole else []
        parts += [high[whole:], low[whole:]] if whole < end - first else []
        stack = jnp.concatenate(parts, axis=0)
        add(jnp.dot(m_piece, stack, preferred_element_type=F32))

    return ask, take


def rest_piece(operands, begin, add):
    def ask():
        y_stack, _, _, blocks = operands()
        return distances(blocks[begin], y_stack)

    def take(shifted):
        stack = jnp.concatenate(weights(shifted), axis=1)
        m_whole = jnp.concatenate([operands()[2][-1]] * 2, axis=1)
        turned = (((1,), (1,)), ((), ()))
        add(lax.dot_general(m_whole, stack, turned, preferred_element_type=F32))

    return ask, take


def store_sums(slots, slot, j, x, result, offsets, sums):
    offsets.at[j][pl.ds(slot, 8, stride=slots), :] = x
    for h in range(0, SUM_ROWS, 8):
        sums.at[j][pl.ds(h * slots + slot, 8, stride=slots), :] = result[h : h + 8]


def mark(slot, target, hot):
    hot[pl.ds(slot, 1), :] = jnp.where(lane_iota(1) == target, 1.0, 0.0)


def combine(sz, slots, first, total, offsets, sums, speeds):
    live = lax.broadcasted_iota(jnp.int32, (8, 128), 0) + first < total
    for j in range(offsets.shape[0]):
        x = [offsets[j, pl.ds(i * slots + first, 8), :] for i in range(3)]
        s = [sums[j, pl.ds(k * slots + first, 8), :] for k in range(SUM_ROWS)]
        a, b, c = s[:3], [s[3:6], s[6:9], s[9:12]], s[12:15]
        norm = x[0] * x[0] + x[1] * x[1] + x[2] * x[2] + REGULARIZE
        along = x[0] * a[0] + x[1] * a[1] + x[2] * a[2] - s[15]
        for i in range(3):
            speed = norm * a[i] + c[i] + along * x[i]
            for k in range(3):
                speed = speed - x[k] * (2.0 * b[k][i] + b[i][k])
            speed = jnp.where(live, speed / sz.points, 0.0)
            speeds[i, pl.ds(first, 8), 128 * j : 128 * j + 128] = speed


def add_up(sz, slots, total, rows, offsets, sums, speeds, hot):
    def eight(q, carry):
        combine(sz, slots, pl.multiple_of(8 * q, 8), total, offsets, sums, speeds)
        return carry

    if slots <= 64 and offsets.shape[0] <= 2:
        for q in range(slots // 8):
            combine(sz, slots, 8 * q, total, offsets, sums, speeds)
    else:
        lax.fori_loop(0, lax.div(total + 7, 8), eight, 0)
    one_hot = hot[...].astype(BF16)
    result = []
    for i in range(3):
        first, second, third = split3(speeds[i])
        parts = [
            lax.dot_general(
                one_hot, part.astype(BF16), (((0,), (0,)), ((), ())), preferred_element_type=F32
            )
            for part in (first, second, third)
        ]
        result.append((parts[0] + parts[1] + parts[2])[:rows])
    return result


def several_tasks(sz, slots, picks, marks, main, rest, wide, step, skew, refs):
    source_rows, centres, targets, offsets, sums, hot = refs

    def task(slot, pick, target_mark):
        target, source = pick
        made, parts, points = [], {}, []

        def operands():
            if made:
                return made[0]
            y_stack, m_stack = source_operands(sz, source, source_rows)
            centre = centres[pl.ds(pl.multiple_of(8 * source, 8), 8), :]
            points.extend(
                load_target(j, target, slot, centre, targets, offsets)
                for j in range(targets.shape[0])
            )
            blocks = {}
            for begin in range(0, main, wide):
                stack = [stack for _, stack in points[begin // 128 : (begin + wide) // 128]]
                blocks[begin] = jnp.concatenate(stack, axis=1)
            if rest:
                blocks[main] = jnp.transpose(points[main // 128][1])[:rest]
            sides = {-1: m_stack.astype(BF16)}
            if main:
                for first, last in pieces(sz.points, step):
                    sides[first] = twice(m_stack[:, first : up(last, 128)], last - first)
            made.append((y_stack, jnp.transpose(y_stack), sides, blocks))
            return made[0]

        def finish():
            results = [fold(parts[begin]) for begin in range(0, main, wide)]
            if rest:
                spare = jnp.zeros((SUM_ROWS, 128 - rest), F32)
                results.append(jnp.concatenate([fold(parts[main]), spare], axis=1))
            result = jnp.concatenate(results, axis=1)
            for j in range(targets.shape[0]):
                cut = result[:, 128 * j : 128 * j + 128]
                store_sums(offsets.shape[1] // 8, slot, j, points[j][0], cut, offsets, sums)
            mark(slot, target_mark, hot)

        own = []
        for begin in range(0, main, wide):
            for first, last in pieces(sz.points, step):
                own.append(wide_piece(operands, begin, first, last, adder(parts, begin)))
        if rest:
            own.insert(len(own) // 2, rest_piece(operands, main, adder(parts, main)))
        ask, take = own[-1]

        def last_take(shifted):
            take(shifted)
            finish()

        own[-1] = (ask, last_take)
        return own, operands

    made = [task(slot, pick, m) for slot, pick, m in zip(slots, picks, marks)]
    for (own, _), (_, after) in zip(made, made[1:]):
        ask, take = own[0]

        def ask_and_prepare(ask=ask, after=after):
            shifted = ask()
            after()
            return shifted

        own[0] = (ask_and_prepare, take)
    skewed([stage for own, _ in made for stage in own], skew)


def tiles_of_chunk(sz, total, tasks, *refs):
    def several(q, carry):
        slots = [q * UNROLL + u for u in range(UNROLL)]
        picks = [(tasks[0, slot], tasks[1, slot]) for slot in slots]
        marks = [target for target, _ in picks]
        several_tasks(sz, slots, picks, marks, sz.main, sz.rest, 128, 256, 7, refs)
        return carry

    lax.fori_loop(0, lax.div(total + UNROLL - 1, UNROLL), several, 0)


def tiles_of_cells(sz, total, mine, *refs):
    main = 256 * (sz.points // 256)

    def several(q, carry):
        slots = [q * PAIR + u for u in range(PAIR)]
        marks = [mine[0, slot] for slot in slots]
        picks = [(jnp.maximum(mark, 0), mine[1, slot]) for mark, slot in zip(marks, slots)]
        several_tasks(sz, slots, picks, marks, main, sz.points - main, 256, 256, 4, refs)
        return carry

    lax.fori_loop(0, lax.div(total + PAIR - 1, PAIR), several, 0)


def packed(sz, blocks):
    rows = [b[:, : sz.main] for b in blocks] if sz.main else []
    lanes = lane_iota(8)
    for p in range(0, len(blocks), sz.per_pack):
        total = jnp.zeros((8, 128), F32)
        for q, block in enumerate(blocks[p : p + sz.per_pack]):
            rest = jnp.where(lanes < sz.rest, block[:, sz.main : sz.main + 128], 0.0)
            total = total + (pltpu.roll(rest, q * sz.rest, 1) if q else rest)
        rows.append(total)
    return rows


def store_packed(sz, out, blocks):
    first = 0
    count = len(blocks)
    values = packed(sz, blocks)
    if sz.main:
        for b in range(count):
            for m in range(sz.main // 128):
                out[pl.ds(first, 8), :] = values[b][:, 128 * m : 128 * m + 128]
                first += 8
        values = values[count:]
    for value in values:
        out[pl.ds(first, 8), :] = value
        first += 8


def place_packed(sz, lane, arrived, count, store_main, add_rest):
    first = 0
    if sz.main:
        for b in range(count):
            for m in range(sz.main // 128):
                store_main(b, m, arrived[pl.ds(first, 8), :])
                first += 8
    start = sz.rest * lane
    lanes = lane_iota(8)
    for b in range(count):
        pack, q = divmod(b, sz.per_pack)
        value = arrived[pl.ds(first + 8 * pack, 8), :]
        value = pltpu.roll(value, lax.rem(start - q * sz.rest + 128, 128), 1)
        for tile in range(sz.rest_tiles):
            inside = (lanes + 128 * tile >= start) & (lanes + 128 * tile < start + sz.rest)
            add_rest(b, tile, jnp.where(inside, value, 0.0))


def source_kernel(sz, *refs):
    inputs, (high_out, low_out, source_rows, centres), held, sems = (
        refs[:2],
        refs[2:6],
        refs[6:8],
        refs[8],
    )
    for copy in fetch(inputs, held, sems):
        copy.wait()
    positions, bend = held
    high_out[...], low_out[...] = split2(bend[...])
    value = jnp.concatenate([positions[i] for i in range(3)], axis=0)
    value = jnp.concatenate(
        [value, jnp.zeros((3 * sz.cells, sz.width - sz.points), F32)], axis=1
    )
    make_sources(sz, value, high_out[...], low_out[...], source_rows, centres, 0)


def first_kernel(sz, *refs):
    arrived, high, low, inputs = refs[0], refs[1], refs[2], refs[3:7]
    outputs, refs = refs[7:10], refs[10:]
    source_rows, centres, targets, offsets, sums, speeds, hot, moved, pool = refs[:9]
    send, positions, staged, lists, chunk_out, ghost_out, tasks, sems = refs[9:]
    me, lane = lax.axis_index("space"), lax.axis_index("lane")
    own_rows = source_rows.at[:, pl.ds(0, SOURCE_ROWS * sz.cells)]
    own_centres = centres.at[pl.ds(0, 8 * sz.cells)]
    copies = fetch(inputs, [send, positions, own_rows, own_centres], sems)
    for other in range(sz.lanes):
        row = ((me * sz.lanes + other) * sz.group) * 4 + 3
        value = pltpu.roll(arrived[pl.ds(row, 1), :], 128 - 3 * sz.rest, 1)
        staged[pl.ds(other, 1), :] = value.astype(jnp.int32)
    copies += fetch([staged], [lists], sems.at[pl.ds(4, 1)])
    pool[...] = jnp.zeros_like(pool)
    take_ghosts(sz, arrived, pool, up(sz.owners * sz.group, 8), 0)
    hot[...] = jnp.zeros_like(hot)
    speeds[...] = jnp.zeros_like(speeds)
    make_sources(sz, pool[...], high[...], low[...], source_rows, centres, sz.cells)
    for copy in copies[:2]:
        copy.wait()
    chunks = [
        [own_chunk(sz, lane, positions.at[i], pl.ds(g, 8)) for g in range(0, sz.cells, 8)]
        for i in range(3)
    ]
    make_targets(sz, [jnp.concatenate(blocks, axis=0) for blocks in chunks], targets)
    copies[4].wait()
    total = build_list(sz, lists, tasks)
    for copy in copies[2:4]:
        copy.wait()
    copies = fetch([tasks], outputs[2:], sems)
    tiles_of_chunk(sz, total, tasks, source_rows, centres, targets, offsets, sums, hot)
    velocity = add_up(sz, sz.slots, total, sz.cells, offsets, sums, speeds, hot)
    blocks = []
    for i in range(3):
        for g in range(0, sz.cells, 8):
            chunk = own_chunk(sz, lane, positions.at[i], pl.ds(g, 8))
            block = chunk + TIME_STEP * velocity[i][g : g + 8]
            moved[pl.ds(i * sz.rows + g, 8), :] = block
            blocks.append(block)
    store_packed(sz, chunk_out, blocks)
    copies += fetch([chunk_out], outputs[:1], sems.at[pl.ds(1, 1)])
    send_ghosts(sz, send, moved, ghost_out, jnp.zeros((1, 128), F32))
    copies += fetch([ghost_out], outputs[1:2], sems.at[pl.ds(2, 1)])
    for copy in copies:
        copy.wait()


def own_kernel(sz, *refs):
    (high, low), refs = refs[:2], refs[2:]
    others, refs = refs[: sz.lanes - 1], refs[sz.lanes - 1 :]
    inputs, (speed_out, share_out), refs = refs[:2], refs[2:4], refs[4:]
    source_rows, centres, targets, offsets, sums, speeds, hot, pool, mine = refs[:9]
    tasks, chunk, sems = refs[9:]
    copies = fetch(inputs, [tasks, chunk], sems)
    chunks = [chunk, *others]
    hot[...] = jnp.zeros_like(hot)
    speeds[...] = jnp.zeros_like(speeds)
    lane = lax.axis_index("lane")
    pool[...] = jnp.zeros_like(pool)
    copies[0].wait()
    total = own_list(sz, lane, tasks, mine, 0, sz.cells)
    copies[1].wait()
    per = sz.cells // 8
    for k in range(sz.lanes):
        other = lane ^ k

        def row_of(b):
            return (b // per) * sz.cells + 8 * (b % per)

        def store_main(b, m, value):
            cut = pl.ds(pl.multiple_of(other * sz.main + 128 * m, 128), 128)
            pool[pl.ds(row_of(b), 8), cut] = value

        def add_rest(b, tile, value):
            offset = sz.main * sz.lanes + 128 * tile
            cut = (pl.ds(row_of(b), 8), slice(offset, offset + 128))
            pool[cut] = pool[cut] + value

        place_packed(sz, other, chunks[k], 3 * per, store_main, add_rest)
    for i in range(3):
        share_out[i] = share_rows(sz, pool, i * sz.cells, lane)
    make_sources(sz, pool[...], high[...], low[...], source_rows, centres, 0)
    make_targets(sz, share_out, targets)
    tiles_of_cells(sz, total, mine, source_rows, centres, targets, offsets, sums, hot)
    velocity = add_up(sz, sz.own, total, up(sz.share, 8), offsets, sums, speeds, hot)
    for i in range(3):
        speed_out[i] = velocity[i]


def ghost_kernel(sz, *refs):
    arrived, high, low, speed_in, share, tasks_in = refs[:6]
    moved_out, velocity_out = refs[6:8]
    source_rows, centres, targets, offsets, sums, speeds, hot, pool, mine = refs[8:17]
    tasks, sems = refs[17:]
    copies = fetch([tasks_in], [tasks], sems)
    hot[...] = jnp.zeros_like(hot)
    speeds[...] = jnp.zeros_like(speeds)
    lane = lax.axis_index("lane")
    pool[...] = jnp.zeros_like(pool)
    ghosts = up(sz.owners * sz.group, 8)
    take_ghosts(sz, arrived, pool, ghosts, 0)
    make_sources(sz, pool[...], high[...], low[...], source_rows, centres, 0)
    make_targets(sz, share, targets)
    copies[0].wait()
    total = own_list(sz, lane, tasks, mine, sz.cells, sz.cells + sz.owners * sz.group)
    tiles_of_cells(sz, total, mine, source_rows, centres, targets, offsets, sums, hot)
    velocity = add_up(sz, sz.own, total, up(sz.share, 8), offsets, sums, speeds, hot)
    for i in range(3):
        speed = velocity[i] + speed_in[i]
        velocity_out[i] = speed[: sz.share, : sz.points]
        moved_out[i] = (share[i] + TIME_STEP * speed)[: sz.share, : sz.points]


def share_rows(sz, ref, base, lane):
    if sz.share % 8 == 0:
        return ref[pl.ds(pl.multiple_of(base + lane * sz.share, 8), sz.share), :]
    rows = [ref[pl.ds(base + lane * sz.share + c, 1), :] for c in range(sz.share)]
    rows.append(jnp.zeros((8 - sz.share, rows[0].shape[1]), F32))
    return jnp.concatenate(rows, axis=0)


def scratch(sz, cells, targets, tiles, slots):
    return [
        pltpu.VMEM((sz.tiles, SOURCE_ROWS * cells, 128), F32),
        pltpu.VMEM((8 * cells, 128), F32),
        pltpu.VMEM((tiles, 8 * targets, 128), F32),
        pltpu.VMEM((tiles, 8 * slots, 128), F32),
        pltpu.VMEM((tiles, SUM_ROWS * slots, 128), F32),
        pltpu.VMEM((3, slots, 128 * tiles), F32),
        pltpu.VMEM((slots, 128), F32),
    ]


def swap(value, axis, size, k):
    return lax.ppermute(value, axis, [(d, d ^ k) for d in range(size)])


def in_hbm(value):
    return pltpu.with_memory_space_constraint(value, pltpu.HBM)


def shards(positions, bend_op, send_list, task_target, task_source, task_count):
    owners, lanes = lax.axis_size("space"), lax.axis_size("lane")
    cells, points = positions.shape[0], positions.shape[2]
    sz = sizes(owners, lanes, cells, points, task_target.shape[1], send_list.shape[1])
    params = pltpu.CompilerParams(vmem_limit_bytes=min(6 * lanes, 40) << 20)
    shape = jax.ShapeDtypeStruct
    both = ("space", "lane")
    by_component = jnp.transpose(positions, (1, 0, 2))
    list_rows = up(lanes, 8)
    slot_shape = shape((4 * sz.group * owners * lanes, 128), F32)
    leaving, send = pl.pallas_call(
        functools.partial(pick_kernel, sz),
        out_shape=[slot_shape, shape(send_list.shape, jnp.int32)],
        in_specs=[HBM] * 5,
        out_specs=[VMEM, SMEM],
        scratch_shapes=[
            pltpu.SMEM(send_list.shape, jnp.int32),
            pltpu.VMEM(task_target.shape, jnp.int32),
            pltpu.VMEM(task_source.shape, jnp.int32),
            pltpu.SMEM(task_count.shape, jnp.int32),
            pltpu.VMEM(by_component.shape, F32),
            pltpu.VMEM((3 * sz.rows, sz.chunk_wide), F32),
            pltpu.SemaphoreType.DMA((5,)),
        ],
        compiler_params=pltpu.CompilerParams(vmem_limit_bytes=60 << 20),
        name="pick_cells",
    )(send_list, task_target, task_source, task_count, by_component)
    arrived = lax.all_to_all(leaving, both, split_axis=0, concat_axis=0, tiled=True)
    high, low, own_rows, own_centres = pl.pallas_call(
        functools.partial(source_kernel, sz),
        out_shape=[
            shape(bend_op.shape, BF16),
            shape(bend_op.shape, BF16),
            shape((sz.tiles, SOURCE_ROWS * cells, 128), F32),
            shape((8 * cells, 128), F32),
        ],
        in_specs=[HBM] * 2,
        out_specs=[VMEM] * 4,
        scratch_shapes=[
            pltpu.VMEM(by_component.shape, F32),
            pltpu.VMEM(bend_op.shape, F32),
            pltpu.SemaphoreType.DMA((2,)),
        ],
        compiler_params=params,
        cost_estimate=pl.CostEstimate(flops=10**9, bytes_accessed=10**7, transcendentals=0),
        name="first_sources",
    )(in_hbm(by_component), in_hbm(bend_op))
    chunk_shape = (pack_rows(sz, cells), 128)
    chunk, leaving, tasks = pl.pallas_call(
        functools.partial(first_kernel, sz),
        out_shape=[
            pltpu.HBM(chunk_shape, F32),
            pltpu.HBM(slot_shape.shape, F32),
            pltpu.HBM((3, sz.slots), jnp.int32),
        ],
        in_specs=[VMEM] * 3 + [HBM] * 2 + [ANY] * 2,
        out_specs=[HBM] * 3,
        scratch_shapes=scratch(sz, sz.pool, sz.rows, sz.chunk_tiles, sz.slots)
        + [
            pltpu.VMEM((3 * sz.rows, sz.chunk_wide), F32),
            pltpu.VMEM((3 * up(sz.owners * sz.group, 8), sz.width), F32),
            pltpu.SMEM(send_list.shape, jnp.int32),
            pltpu.VMEM(by_component.shape, F32),
            pltpu.VMEM((list_rows, 128), jnp.int32),
            pltpu.SMEM((list_rows, 128), jnp.int32),
            pltpu.VMEM(chunk_shape, F32),
            pltpu.VMEM(slot_shape.shape, F32),
            pltpu.SMEM((3, sz.slots), jnp.int32),
            pltpu.SemaphoreType.DMA((5,)),
        ],
        compiler_params=params,
        name="first_step",
    )(arrived, high, low, in_hbm(send), in_hbm(by_component), own_rows, own_centres)
    arrived = lax.all_to_all(leaving, both, split_axis=0, concat_axis=0, tiled=True)
    chunks = [swap(chunk, "lane", lanes, k) for k in range(1, lanes)]
    share = up(sz.share, 8)
    so_far = shape((3, share, sz.width), F32)
    speed, moved = pl.pallas_call(
        functools.partial(own_kernel, sz),
        out_shape=[so_far, so_far],
        in_specs=[VMEM] * (lanes + 1) + [HBM] * 2,
        out_specs=[VMEM] * 2,
        scratch_shapes=scratch(sz, cells, share, sz.tiles, sz.own)
        + [
            pltpu.VMEM((3 * cells, sz.width), F32),
            pltpu.SMEM((2, sz.own + 8), jnp.int32),
            pltpu.SMEM(tasks.shape, jnp.int32),
            pltpu.VMEM(chunk.shape, F32),
            pltpu.SemaphoreType.DMA((2,)),
        ],
        compiler_params=params,
        cost_estimate=pl.CostEstimate(flops=10**9, bytes_accessed=10**7, transcendentals=0),
        name="second_own",
    )(high, low, *chunks, in_hbm(tasks), in_hbm(chunk))
    result = shape((3, sz.share, points), F32)
    ghosts = up(owners * sz.group, 8)
    outputs = pl.pallas_call(
        functools.partial(ghost_kernel, sz),
        out_shape=[result, result],
        in_specs=[VMEM] * 5 + [HBM],
        out_specs=[VMEM] * 2,
        scratch_shapes=scratch(sz, ghosts, share, sz.tiles, sz.own)
        + [
            pltpu.VMEM((3 * ghosts, sz.width), F32),
            pltpu.SMEM((2, sz.own + 8), jnp.int32),
            pltpu.SMEM(tasks.shape, jnp.int32),
            pltpu.SemaphoreType.DMA((1,)),
        ],
        compiler_params=params,
        name="second_ghosts",
    )(arrived, high, low, speed, moved, in_hbm(tasks))
    return tuple(jnp.transpose(output, (1, 0, 2)) for output in outputs)


def solution(mesh):
    in_specs = (
        P("space", None, None),
        P(),
        P("space", None),
        P(("space", "lane"), None),
        P(("space", "lane"), None),
        P(("space", "lane")),
    )
    out_specs = (P(("space", "lane"), None, None), P(("space", "lane"), None, None))
    return jax.shard_map(shards, mesh=mesh, in_specs=in_specs, out_specs=out_specs, check_vma=False)
```

```python
import functools
from types import SimpleNamespace

import jax
import jax.numpy as jnp
from jax import lax
from jax.experimental import pallas as pl
from jax.experimental.pallas import tpu as pltpu
from jax.sharding import PartitionSpec as P

REGULARIZE = 0.25
TIME_STEP = 0.5
UNROLL = 11
PAIR = 2
SOURCE_ROWS = 24
SUM_ROWS = 16

F32 = jnp.float32
BF16 = jnp.bfloat16
VMEM = pl.BlockSpec(memory_space=pltpu.VMEM)
SMEM = pl.BlockSpec(memory_space=pltpu.SMEM)
HBM = pl.BlockSpec(memory_space=pltpu.HBM)
ANY = pl.BlockSpec(memory_space=pl.ANY)


def up(value, step):
    return -(-value // step) * step


def sizes(owners, lanes, cells, points, cap, listed):
    main = 128 * (points // (128 * lanes))
    rest = (points - main * lanes) // lanes
    group = listed // owners
    pool = up(cells + listed, 8)
    per_pack = 128 // rest
    return SimpleNamespace(
        owners=owners,
        lanes=lanes,
        cells=cells,
        points=points,
        cap=cap,
        group=group,
        width=up(points, 128),
        tiles=up(points, 128) // 128,
        main=main,
        rest=rest,
        rest_tiles=up(rest * lanes, 128) // 128,
        chunk=main + rest,
        chunk_wide=main + up(rest, 128),
        chunk_tiles=(main + up(rest, 128)) // 128,
        per_pack=per_pack,
        pool=pool,
        share=cells // lanes,
        slots=up(lanes * cap + UNROLL, 8),
        rows=cells + 8,
        own=up(lanes * cap + PAIR, 8),
    )


def pack_rows(sz, rows):
    return (3 * rows * sz.main // 128) + 8 * up(3 * rows // 8, sz.per_pack) // sz.per_pack


def split2(value):
    high = value.astype(BF16)
    return high, (value - high.astype(F32)).astype(BF16)


def split3(value):
    first = value.astype(BF16).astype(F32)
    left = value - first
    second = left.astype(BF16).astype(F32)
    return first, second, left - second


def lane_iota(rows):
    return lax.broadcasted_iota(jnp.int32, (rows, 128), 1)


def fetch(sources, targets, sems):
    copies = [
        pltpu.make_async_copy(source, target, sems.at[q])
        for q, (source, target) in enumerate(zip(sources, targets))
    ]
    for copy in copies:
        copy.start()
    return copies


def loop(count, body):
    if count <= 8:
        for q in range(count):
            body(q)
    else:

        def step(q, carry):
            body(q)
            return carry

        lax.fori_loop(0, count, step, 0)


def own_chunk(sz, lane, ref, rows):
    parts = []
    if sz.main:
        parts.append(ref[rows, pl.ds(pl.multiple_of(lane * sz.main, 128), sz.main)])
    start = sz.rest * lane
    lanes = lane_iota(8)
    rest = jnp.zeros((8, 128), F32)
    for tile in range(sz.rest_tiles):
        offset = sz.main * sz.lanes + 128 * tile
        block = ref[rows, offset : min(offset + 128, ref.shape[-1])]
        if block.shape[1] < 128:
            block = jnp.concatenate([block, jnp.zeros((8, 128 - block.shape[1]), F32)], axis=1)
        inside = (lanes + 128 * tile >= start) & (lanes + 128 * tile < start + sz.rest)
        rest = rest + jnp.where(inside, block, 0.0)
    rest = pltpu.roll(rest, lax.rem(128 * sz.rest_tiles - start, 128), 1)
    parts.append(rest)
    return jnp.concatenate(parts, axis=1) if len(parts) > 1 else parts[0]


def send_ghosts(sz, send, chunks, out, tasks):
    lanes = lane_iota(1)

    def one(d):
        for g in range(sz.group):
            cell = send[0, d * sz.group + g]
            rows = []
            last = tasks
            for i in range(3):
                row = chunks[pl.ds(i * sz.rows + cell, 1), :]
                rows.append(row[:, :128] if sz.main else jnp.zeros((1, 128), F32))
                piece = jnp.where(lanes < sz.rest, row[:, sz.main : sz.main + 128], 0.0)
                last = last + (pltpu.roll(piece, i * sz.rest, 1) if i else piece)
            rows.append(last)
            for other in range(sz.lanes):
                first = ((d * sz.lanes + other) * sz.group + g) * 4
                for q, row in enumerate(rows):
                    out[pl.ds(first + q, 1), :] = row

    loop(sz.owners, one)


def pick_kernel(sz, *refs):
    inputs, (out, send_out), held, (chunks, sems) = refs[:5], refs[5:7], refs[7:12], refs[12:]
    for copy in fetch(inputs, held, sems):
        copy.wait()
    send, target, source, count, positions = held
    for j in range(send_out.shape[1]):
        send_out[0, j] = send[0, j]
    lane = lax.axis_index("lane")
    for i in range(3):
        for g in range(0, sz.cells, 8):
            value = own_chunk(sz, lane, positions.at[i], pl.ds(g, 8))
            chunks[pl.ds(i * sz.rows + g, 8), :] = value
    spare = jnp.zeros((1, 128 - sz.cap), F32)
    tasks = jnp.where(lane_iota(1) == 3 * sz.rest + 2 * sz.cap, count[0].astype(F32), 0.0)
    for q, row in enumerate((target, source)):
        wide = jnp.concatenate([row[...].astype(F32), spare], axis=1)
        tasks = tasks + pltpu.roll(wide, 3 * sz.rest + q * sz.cap, 1)
    send_ghosts(sz, send, chunks, out, tasks)


def take_ghosts(sz, arrived, pool, stride, base):
    lanes = lane_iota(1)

    def one(d):
        for g in range(sz.group):
            first = [((d * sz.lanes + lane) * sz.group + g) * 4 for lane in range(sz.lanes)]
            last = [arrived[pl.ds(row + 3, 1), :] for row in first]
            for i in range(3):
                tiles = []
                if sz.main:
                    tiles += [arrived[pl.ds(row + i, 1), :] for row in first]
                for tile in range(sz.rest_tiles):
                    total = jnp.zeros((1, 128), F32)
                    for lane in range(sz.lanes):
                        start = sz.rest * lane
                        if start + sz.rest <= 128 * tile or start >= 128 * tile + 128:
                            continue
                        shift = (start - i * sz.rest) % 128
                        value = pltpu.roll(last[lane], shift, 1) if shift else last[lane]
                        at = lanes + 128 * tile
                        total = jnp.where((at >= start) & (at < start + sz.rest), value, total)
                    tiles.append(total)
                place = pl.ds(i * stride + base + d * sz.group + g, 1)
                pool[place, :] = jnp.concatenate(tiles, axis=1)

    loop(sz.owners, one)


def build_list(sz, lists, tasks):
    total = jnp.int32(0)
    for lane in range(sz.lanes):
        count = lists[lane, 2 * sz.cap]
        for j in range(sz.cap):
            tasks[0, total] = lists[lane, j]
            tasks[1, total] = lists[lane, sz.cap + j]
            total = total + (j < count).astype(jnp.int32)
    for u in range(UNROLL):
        tasks[0, total + u] = jnp.int32(sz.cells)
        tasks[1, total + u] = jnp.int32(0)
    tasks[2, 0] = total
    return total


def own_list(sz, lane, tasks, mine, low, high):
    first = lane * sz.share
    total = tasks[2, 0]
    count = jnp.int32(0)
    for t in range(sz.lanes * sz.cap):
        target = tasks[0, t] - first
        source = tasks[1, t]
        mine[0, count] = target
        mine[1, count] = source - low
        taken = (target >= 0) & (target < sz.share) & (t < total)
        taken = taken & (source >= low) & (source < high)
        count = count + taken.astype(jnp.int32)
    for u in range(PAIR):
        mine[0, count + u] = jnp.int32(-1)
        mine[1, count + u] = jnp.int32(0)
    return count


def products(value, bend_high, bend_low):
    high, low = split2(value)
    dot = functools.partial(jnp.dot, preferred_element_type=F32)
    return dot(high, bend_high) + dot(low, bend_high) + dot(high, bend_low)


def make_sources(sz, value, bend_high, bend_low, source_rows, centres, first):
    count = value.shape[0] // 3
    forces = products(value[:, : sz.points], bend_high, bend_low)
    forces = jnp.concatenate(
        [forces, jnp.zeros((3 * count, sz.width - sz.points), F32)], axis=1
    )
    middle = jnp.sum(value, axis=1, keepdims=True) / sz.points
    for g in range(count // 8):
        where = [i * count + 8 * g for i in range(3)]
        middles = [jnp.broadcast_to(middle[w : w + 8], (8, 128)) for w in where]
        middles += [jnp.zeros((8, 128), F32)] * 5
        for i, row in enumerate(middles):
            centres[pl.ds(8 * (first + 8 * g) + i, 8, stride=8), :] = row
        for j in range(sz.tiles):
            cut = slice(128 * j, 128 * j + 128)
            y = [value[w : w + 8, cut] - m for w, m in zip(where, middles)]
            f = [forces[w : w + 8, cut] for w in where]
            norm = y[0] * y[0] + y[1] * y[1] + y[2] * y[2] + REGULARIZE
            along = y[0] * f[0] + y[1] * f[1] + y[2] * f[2]
            one, zero = jnp.ones((8, 128), F32), jnp.zeros((8, 128), F32)
            rows = [y[0], y[1], y[2], norm, one, zero, zero, zero]
            rows += f
            rows += [y[i] * f[k] for i in range(3) for k in range(3)]
            rows += [norm * f[i] + along * y[i] for i in range(3)]
            rows += [along]
            for k, row in enumerate(rows):
                place = pl.ds(SOURCE_ROWS * (first + 8 * g) + k, 8, stride=SOURCE_ROWS)
                source_rows.at[j][place, :] = row


def make_targets(sz, blocks, targets):
    targets[...] = jnp.zeros_like(targets)
    for i in range(3):
        for g in range(blocks[i].shape[0] // 8):
            block = blocks[i][8 * g : 8 * g + 8]
            for j in range(targets.shape[0]):
                cut = slice(128 * j, 128 * j + 128)
                targets.at[j][pl.ds(64 * g + i, 8, stride=8), :] = block[:, cut]


def source_operands(sz, source, source_rows):
    held = [
        source_rows[j, pl.ds(pl.multiple_of(SOURCE_ROWS * source, 8), SOURCE_ROWS), :]
        for j in range(sz.tiles)
    ]
    held = jnp.concatenate(held, axis=1)
    y1, y2, y3 = split3(held[:8])
    y_stack = jnp.concatenate([y1, y1, y2, y2, y1, y3], axis=0).astype(BF16)
    return y_stack, jnp.concatenate(split3(held[8:]), axis=0)


def pieces(points, step):
    starts = list(range(0, max(points // 128 * 128, 1), step))
    return list(zip(starts, starts[1:] + [points]))


def twice(piece, count):
    whole = count // 128 * 128
    parts = [piece[:, :whole].astype(BF16)] * 2 if whole else []
    if whole < count:
        last = piece[:, whole:]
        last = last + pltpu.roll(last, count - whole, 1)
        parts.append(last.astype(BF16)[:, : 2 * (count - whole)])
    return jnp.concatenate(parts, axis=1)


def load_target(j, target, slot, centre, targets, offsets):
    row = lax.broadcasted_iota(jnp.int32, (8, 128), 0)
    x = targets[j, pl.ds(pl.multiple_of(8 * target, 8), 8), :] - centre
    square = x * x
    norm = pltpu.roll(square, 2, 0) + pltpu.roll(square, 3, 0) + pltpu.roll(square, 4, 0)
    side = jnp.where(row == 4, norm, jnp.where(row == 3, 1.0, 0.0))
    x_side = jnp.where(row < 3, -2.0 * x, side)
    x1, x2, x3 = split3(x_side)
    return x, jnp.concatenate([x1, x2, x1, x2, x3, x1], axis=0).astype(BF16)


def distances(one_stack, other_stack):
    return jnp.dot(one_stack, other_stack, preferred_element_type=F32)


def weights(shifted):
    inverse = lax.rsqrt(shifted)
    return split2(inverse * inverse * inverse)


def fold(result):
    return result[:SUM_ROWS] + result[SUM_ROWS : 2 * SUM_ROWS] + result[2 * SUM_ROWS :]


def skewed(stages, skew):
    asked = []
    for q, (ask, _) in enumerate(stages):
        asked.append(ask())
        if q >= skew:
            stages[q - skew][1](asked[q - skew])
            asked[q - skew] = None
    for q in range(max(len(stages) - skew, 0), len(stages)):
        stages[q][1](asked[q])


def adder(totals, key):
    def add(value):
        totals[key] = totals[key] + value if key in totals else value

    return add


def wide_piece(operands, begin, first, end, add):
    def ask():
        _, y_turned, _, blocks = operands()
        return distances(y_turned[first:end], blocks[begin])

    def take(shifted):
        m_piece = operands()[2][first]
        high, low = weights(shifted)
        whole = (end - first) // 128 * 128
        parts = [high[:whole], low[:whole]] if whole else []
        parts += [high[whole:], low[whole:]] if whole < end - first else []
        stack = jnp.concatenate(parts, axis=0)
        add(jnp.dot(m_piece, stack, preferred_element_type=F32))

    return ask, take


def rest_piece(operands, begin, add):
    def ask():
        y_stack, _, _, blocks = operands()
        return distances(blocks[begin], y_stack)

    def take(shifted):
        stack = jnp.concatenate(weights(shifted), axis=1)
        m_whole = jnp.concatenate([operands()[2][-1]] * 2, axis=1)
        turned = (((1,), (1,)), ((), ()))
        add(lax.dot_general(m_whole, stack, turned, preferred_element_type=F32))

    return ask, take


def store_sums(slots, slot, j, x, result, offsets, sums):
    offsets.at[j][pl.ds(slot, 8, stride=slots), :] = x
    for h in range(0, SUM_ROWS, 8):
        sums.at[j][pl.ds(h * slots + slot, 8, stride=slots), :] = result[h : h + 8]


def mark(slot, target, hot):
    hot[pl.ds(slot, 1), :] = jnp.where(lane_iota(1) == target, 1.0, 0.0)


def combine(sz, slots, first, total, offsets, sums, speeds):
    live = lax.broadcasted_iota(jnp.int32, (8, 128), 0) + first < total
    for j in range(offsets.shape[0]):
        x = [offsets[j, pl.ds(i * slots + first, 8), :] for i in range(3)]
        s = [sums[j, pl.ds(k * slots + first, 8), :] for k in range(SUM_ROWS)]
        a, b, c = s[:3], [s[3:6], s[6:9], s[9:12]], s[12:15]
        norm = x[0] * x[0] + x[1] * x[1] + x[2] * x[2] + REGULARIZE
        along = x[0] * a[0] + x[1] * a[1] + x[2] * a[2] - s[15]
        for i in range(3):
            speed = norm * a[i] + c[i] + along * x[i]
            for k in range(3):
                speed = speed - x[k] * (2.0 * b[k][i] + b[i][k])
            speed = jnp.where(live, speed / sz.points, 0.0)
            speeds[i, pl.ds(first, 8), 128 * j : 128 * j + 128] = speed


def add_up(sz, slots, total, rows, offsets, sums, speeds, hot):
    def eight(q, carry):
        combine(sz, slots, pl.multiple_of(8 * q, 8), total, offsets, sums, speeds)
        return carry

    if slots <= 64 and offsets.shape[0] <= 2:
        for q in range(slots // 8):
            combine(sz, slots, 8 * q, total, offsets, sums, speeds)
    else:
        lax.fori_loop(0, lax.div(total + 7, 8), eight, 0)
    one_hot = hot[...].astype(BF16)
    result = []
    for i in range(3):
        first, second, third = split3(speeds[i])
        parts = [
            lax.dot_general(
                one_hot, part.astype(BF16), (((0,), (0,)), ((), ())), preferred_element_type=F32
            )
            for part in (first, second, third)
        ]
        result.append((parts[0] + parts[1] + parts[2])[:rows])
    return result


def several_tasks(sz, slots, picks, marks, main, rest, wide, step, skew, refs):
    source_rows, centres, targets, offsets, sums, hot = refs

    def task(slot, pick, target_mark):
        target, source = pick
        made, parts, points = [], {}, []

        def operands():
            if made:
                return made[0]
            y_stack, m_stack = source_operands(sz, source, source_rows)
            centre = centres[pl.ds(pl.multiple_of(8 * source, 8), 8), :]
            points.extend(
                load_target(j, target, slot, centre, targets, offsets)
                for j in range(targets.shape[0])
            )
            blocks = {}
            for begin in range(0, main, wide):
                stack = [stack for _, stack in points[begin // 128 : (begin + wide) // 128]]
                blocks[begin] = jnp.concatenate(stack, axis=1)
            if rest:
                blocks[main] = jnp.transpose(points[main // 128][1])[:rest]
            sides = {-1: m_stack.astype(BF16)}
            if main:
                for first, last in pieces(sz.points, step):
                    sides[first] = twice(m_stack[:, first : up(last, 128)], last - first)
            made.append((y_stack, jnp.transpose(y_stack), sides, blocks))
            return made[0]

        def finish():
            results = [fold(parts[begin]) for begin in range(0, main, wide)]
            if rest:
                spare = jnp.zeros((SUM_ROWS, 128 - rest), F32)
                results.append(jnp.concatenate([fold(parts[main]), spare], axis=1))
            result = jnp.concatenate(results, axis=1)
            for j in range(targets.shape[0]):
                cut = result[:, 128 * j : 128 * j + 128]
                store_sums(offsets.shape[1] // 8, slot, j, points[j][0], cut, offsets, sums)
            mark(slot, target_mark, hot)

        own = []
        for begin in range(0, main, wide):
            for first, last in pieces(sz.points, step):
                own.append(wide_piece(operands, begin, first, last, adder(parts, begin)))
        if rest:
            own.insert(len(own) // 2, rest_piece(operands, main, adder(parts, main)))
        ask, take = own[-1]

        def last_take(shifted):
            take(shifted)
            finish()

        own[-1] = (ask, last_take)
        return own, operands

    made = [task(slot, pick, m) for slot, pick, m in zip(slots, picks, marks)]
    for (own, _), (_, after) in zip(made, made[1:]):
        ask, take = own[0]

        def ask_and_prepare(ask=ask, after=after):
            shifted = ask()
            after()
            return shifted

        own[0] = (ask_and_prepare, take)
    skewed([stage for own, _ in made for stage in own], skew)


def tiles_of_chunk(sz, total, tasks, *refs):
    def several(q, carry):
        slots = [q * UNROLL + u for u in range(UNROLL)]
        picks = [(tasks[0, slot], tasks[1, slot]) for slot in slots]
        marks = [target for target, _ in picks]
        several_tasks(sz, slots, picks, marks, sz.main, sz.rest, 128, 256, 9, refs)
        return carry

    lax.fori_loop(0, lax.div(total + UNROLL - 1, UNROLL), several, 0)


def tiles_of_cells(sz, total, mine, *refs):
    main = 256 * (sz.points // 256)

    def several(q, carry):
        slots = [q * PAIR + u for u in range(PAIR)]
        marks = [mine[0, slot] for slot in slots]
        picks = [(jnp.maximum(mark, 0), mine[1, slot]) for mark, slot in zip(marks, slots)]
        several_tasks(sz, slots, picks, marks, main, sz.points - main, 256, 256, 3, refs)
        return carry

    lax.fori_loop(0, lax.div(total + PAIR - 1, PAIR), several, 0)


def packed(sz, blocks):
    rows = [b[:, : sz.main] for b in blocks] if sz.main else []
    lanes = lane_iota(8)
    for p in range(0, len(blocks), sz.per_pack):
        total = jnp.zeros((8, 128), F32)
        for q, block in enumerate(blocks[p : p + sz.per_pack]):
            rest = jnp.where(lanes < sz.rest, block[:, sz.main : sz.main + 128], 0.0)
            total = total + (pltpu.roll(rest, q * sz.rest, 1) if q else rest)
        rows.append(total)
    return rows


def store_packed(sz, out, blocks):
    first = 0
    count = len(blocks)
    values = packed(sz, blocks)
    if sz.main:
        for b in range(count):
            for m in range(sz.main // 128):
                out[pl.ds(first, 8), :] = values[b][:, 128 * m : 128 * m + 128]
                first += 8
        values = values[count:]
    for value in values:
        out[pl.ds(first, 8), :] = value
        first += 8


def place_packed(sz, lane, arrived, count, store_main, add_rest):
    first = 0
    if sz.main:
        for b in range(count):
            for m in range(sz.main // 128):
                store_main(b, m, arrived[pl.ds(first, 8), :])
                first += 8
    start = sz.rest * lane
    lanes = lane_iota(8)
    for b in range(count):
        pack, q = divmod(b, sz.per_pack)
        value = arrived[pl.ds(first + 8 * pack, 8), :]
        value = pltpu.roll(value, lax.rem(start - q * sz.rest + 128, 128), 1)
        for tile in range(sz.rest_tiles):
            inside = (lanes + 128 * tile >= start) & (lanes + 128 * tile < start + sz.rest)
            add_rest(b, tile, jnp.where(inside, value, 0.0))


def source_kernel(sz, *refs):
    inputs, (high_out, low_out, source_rows, centres), held, sems = (
        refs[:2],
        refs[2:6],
        refs[6:8],
        refs[8],
    )
    for copy in fetch(inputs, held, sems):
        copy.wait()
    positions, bend = held
    high_out[...], low_out[...] = split2(bend[...])
    value = jnp.concatenate([positions[i] for i in range(3)], axis=0)
    value = jnp.concatenate(
        [value, jnp.zeros((3 * sz.cells, sz.width - sz.points), F32)], axis=1
    )
    make_sources(sz, value, high_out[...], low_out[...], source_rows, centres, 0)


def first_kernel(sz, *refs):
    arrived, high, low, inputs = refs[0], refs[1], refs[2], refs[3:7]
    outputs, refs = refs[7:10], refs[10:]
    source_rows, centres, targets, offsets, sums, speeds, hot, moved, pool = refs[:9]
    send, positions, staged, lists, chunk_out, ghost_out, tasks, sems = refs[9:]
    me, lane = lax.axis_index("space"), lax.axis_index("lane")
    own_rows = source_rows.at[:, pl.ds(0, SOURCE_ROWS * sz.cells)]
    own_centres = centres.at[pl.ds(0, 8 * sz.cells)]
    copies = fetch(inputs, [send, positions, own_rows, own_centres], sems)
    for other in range(sz.lanes):
        row = ((me * sz.lanes + other) * sz.group) * 4 + 3
        value = pltpu.roll(arrived[pl.ds(row, 1), :], 128 - 3 * sz.rest, 1)
        staged[pl.ds(other, 1), :] = value.astype(jnp.int32)
    copies += fetch([staged], [lists], sems.at[pl.ds(4, 1)])
    pool[...] = jnp.zeros_like(pool)
    take_ghosts(sz, arrived, pool, up(sz.owners * sz.group, 8), 0)
    hot[...] = jnp.zeros_like(hot)
    speeds[...] = jnp.zeros_like(speeds)
    make_sources(sz, pool[...], high[...], low[...], source_rows, centres, sz.cells)
    for copy in copies[:2]:
        copy.wait()
    chunks = [
        [own_chunk(sz, lane, positions.at[i], pl.ds(g, 8)) for g in range(0, sz.cells, 8)]
        for i in range(3)
    ]
    make_targets(sz, [jnp.concatenate(blocks, axis=0) for blocks in chunks], targets)
    copies[4].wait()
    total = build_list(sz, lists, tasks)
    for copy in copies[2:4]:
        copy.wait()
    copies = fetch([tasks], outputs[2:], sems)
    tiles_of_chunk(sz, total, tasks, source_rows, centres, targets, offsets, sums, hot)
    velocity = add_up(sz, sz.slots, total, sz.cells, offsets, sums, speeds, hot)
    blocks = []
    for i in range(3):
        for g in range(0, sz.cells, 8):
            chunk = own_chunk(sz, lane, positions.at[i], pl.ds(g, 8))
            block = chunk + TIME_STEP * velocity[i][g : g + 8]
            moved[pl.ds(i * sz.rows + g, 8), :] = block
            blocks.append(block)
    store_packed(sz, chunk_out, blocks)
    copies += fetch([chunk_out], outputs[:1], sems.at[pl.ds(1, 1)])
    send_ghosts(sz, send, moved, ghost_out, jnp.zeros((1, 128), F32))
    copies += fetch([ghost_out], outputs[1:2], sems.at[pl.ds(2, 1)])
    for copy in copies:
        copy.wait()


def own_kernel(sz, *refs):
    (high, low), refs = refs[:2], refs[2:]
    others, refs = refs[: sz.lanes - 1], refs[sz.lanes - 1 :]
    inputs, (speed_out, share_out), refs = refs[:2], refs[2:4], refs[4:]
    source_rows, centres, targets, offsets, sums, speeds, hot, pool, mine = refs[:9]
    tasks, chunk, sems = refs[9:]
    copies = fetch(inputs, [tasks, chunk], sems)
    chunks = [chunk, *others]
    hot[...] = jnp.zeros_like(hot)
    speeds[...] = jnp.zeros_like(speeds)
    lane = lax.axis_index("lane")
    pool[...] = jnp.zeros_like(pool)
    copies[0].wait()
    total = own_list(sz, lane, tasks, mine, 0, sz.cells)
    copies[1].wait()
    per = sz.cells // 8
    for k in range(sz.lanes):
        other = lane ^ k

        def row_of(b):
            return (b // per) * sz.cells + 8 * (b % per)

        def store_main(b, m, value):
            cut = pl.ds(pl.multiple_of(other * sz.main + 128 * m, 128), 128)
            pool[pl.ds(row_of(b), 8), cut] = value

        def add_rest(b, tile, value):
            offset = sz.main * sz.lanes + 128 * tile
            cut = (pl.ds(row_of(b), 8), slice(offset, offset + 128))
            pool[cut] = pool[cut] + value

        place_packed(sz, other, chunks[k], 3 * per, store_main, add_rest)
    for i in range(3):
        share_out[i] = share_rows(sz, pool, i * sz.cells, lane)
    make_sources(sz, pool[...], high[...], low[...], source_rows, centres, 0)
    make_targets(sz, share_out, targets)
    tiles_of_cells(sz, total, mine, source_rows, centres, targets, offsets, sums, hot)
    velocity = add_up(sz, sz.own, total, up(sz.share, 8), offsets, sums, speeds, hot)
    for i in range(3):
        speed_out[i] = velocity[i]


def ghost_kernel(sz, *refs):
    arrived, high, low, speed_in, share, tasks_in = refs[:6]
    moved_out, velocity_out = refs[6:8]
    source_rows, centres, targets, offsets, sums, speeds, hot, pool, mine = refs[8:17]
    tasks, sems = refs[17:]
    copies = fetch([tasks_in], [tasks], sems)
    hot[...] = jnp.zeros_like(hot)
    speeds[...] = jnp.zeros_like(speeds)
    lane = lax.axis_index("lane")
    pool[...] = jnp.zeros_like(pool)
    ghosts = up(sz.owners * sz.group, 8)
    take_ghosts(sz, arrived, pool, ghosts, 0)
    make_sources(sz, pool[...], high[...], low[...], source_rows, centres, 0)
    make_targets(sz, share, targets)
    copies[0].wait()
    total = own_list(sz, lane, tasks, mine, sz.cells, sz.cells + sz.owners * sz.group)
    tiles_of_cells(sz, total, mine, source_rows, centres, targets, offsets, sums, hot)
    velocity = add_up(sz, sz.own, total, up(sz.share, 8), offsets, sums, speeds, hot)
    for i in range(3):
        speed = velocity[i] + speed_in[i]
        velocity_out[i] = speed[: sz.share, : sz.points]
        moved_out[i] = (share[i] + TIME_STEP * speed)[: sz.share, : sz.points]


def share_rows(sz, ref, base, lane):
    if sz.share % 8 == 0:
        return ref[pl.ds(pl.multiple_of(base + lane * sz.share, 8), sz.share), :]
    rows = [ref[pl.ds(base + lane * sz.share + c, 1), :] for c in range(sz.share)]
    rows.append(jnp.zeros((8 - sz.share, rows[0].shape[1]), F32))
    return jnp.concatenate(rows, axis=0)


def scratch(sz, cells, targets, tiles, slots):
    return [
        pltpu.VMEM((sz.tiles, SOURCE_ROWS * cells, 128), F32),
        pltpu.VMEM((8 * cells, 128), F32),
        pltpu.VMEM((tiles, 8 * targets, 128), F32),
        pltpu.VMEM((tiles, 8 * slots, 128), F32),
        pltpu.VMEM((tiles, SUM_ROWS * slots, 128), F32),
        pltpu.VMEM((3, slots, 128 * tiles), F32),
        pltpu.VMEM((slots, 128), F32),
    ]


def swap(value, axis, size, k):
    return lax.ppermute(value, axis, [(d, d ^ k) for d in range(size)])


def in_hbm(value):
    return pltpu.with_memory_space_constraint(value, pltpu.HBM)


def shards(positions, bend_op, send_list, task_target, task_source, task_count):
    owners, lanes = lax.axis_size("space"), lax.axis_size("lane")
    cells, points = positions.shape[0], positions.shape[2]
    sz = sizes(owners, lanes, cells, points, task_target.shape[1], send_list.shape[1])
    params = pltpu.CompilerParams(vmem_limit_bytes=min(6 * lanes, 40) << 20)
    shape = jax.ShapeDtypeStruct
    both = ("space", "lane")
    by_component = jnp.transpose(positions, (1, 0, 2))
    list_rows = up(lanes, 8)
    slot_shape = shape((4 * sz.group * owners * lanes, 128), F32)
    leaving, send = pl.pallas_call(
        functools.partial(pick_kernel, sz),
        out_shape=[slot_shape, shape(send_list.shape, jnp.int32)],
        in_specs=[HBM] * 5,
        out_specs=[VMEM, SMEM],
        scratch_shapes=[
            pltpu.SMEM(send_list.shape, jnp.int32),
            pltpu.VMEM(task_target.shape, jnp.int32),
            pltpu.VMEM(task_source.shape, jnp.int32),
            pltpu.SMEM(task_count.shape, jnp.int32),
            pltpu.VMEM(by_component.shape, F32),
            pltpu.VMEM((3 * sz.rows, sz.chunk_wide), F32),
            pltpu.SemaphoreType.DMA((5,)),
        ],
        compiler_params=pltpu.CompilerParams(vmem_limit_bytes=60 << 20),
        name="pick_cells",
    )(send_list, task_target, task_source, task_count, by_component)
    arrived = lax.all_to_all(leaving, both, split_axis=0, concat_axis=0, tiled=True)
    high, low, own_rows, own_centres = pl.pallas_call(
        functools.partial(source_kernel, sz),
        out_shape=[
            shape(bend_op.shape, BF16),
            shape(bend_op.shape, BF16),
            shape((sz.tiles, SOURCE_ROWS * cells, 128), F32),
            shape((8 * cells, 128), F32),
        ],
        in_specs=[HBM] * 2,
        out_specs=[VMEM] * 4,
        scratch_shapes=[
            pltpu.VMEM(by_component.shape, F32),
            pltpu.VMEM(bend_op.shape, F32),
            pltpu.SemaphoreType.DMA((2,)),
        ],
        compiler_params=params,
        cost_estimate=pl.CostEstimate(flops=10**9, bytes_accessed=10**7, transcendentals=0),
        name="first_sources",
    )(in_hbm(by_component), in_hbm(bend_op))
    chunk_shape = (pack_rows(sz, cells), 128)
    chunk, leaving, tasks = pl.pallas_call(
        functools.partial(first_kernel, sz),
        out_shape=[
            pltpu.HBM(chunk_shape, F32),
            pltpu.HBM(slot_shape.shape, F32),
            pltpu.HBM((3, sz.slots), jnp.int32),
        ],
        in_specs=[VMEM] * 3 + [HBM] * 2 + [ANY] * 2,
        out_specs=[HBM] * 3,
        scratch_shapes=scratch(sz, sz.pool, sz.rows, sz.chunk_tiles, sz.slots)
        + [
            pltpu.VMEM((3 * sz.rows, sz.chunk_wide), F32),
            pltpu.VMEM((3 * up(sz.owners * sz.group, 8), sz.width), F32),
            pltpu.SMEM(send_list.shape, jnp.int32),
            pltpu.VMEM(by_component.shape, F32),
            pltpu.VMEM((list_rows, 128), jnp.int32),
            pltpu.SMEM((list_rows, 128), jnp.int32),
            pltpu.VMEM(chunk_shape, F32),
            pltpu.VMEM(slot_shape.shape, F32),
            pltpu.SMEM((3, sz.slots), jnp.int32),
            pltpu.SemaphoreType.DMA((5,)),
        ],
        compiler_params=params,
        name="first_step",
    )(arrived, high, low, in_hbm(send), in_hbm(by_component), own_rows, own_centres)
    arrived = lax.all_to_all(leaving, both, split_axis=0, concat_axis=0, tiled=True)
    chunks = [swap(chunk, "lane", lanes, k) for k in range(1, lanes)]
    share = up(sz.share, 8)
    so_far = shape((3, share, sz.width), F32)
    speed, moved = pl.pallas_call(
        functools.partial(own_kernel, sz),
        out_shape=[so_far, so_far],
        in_specs=[VMEM] * (lanes + 1) + [HBM] * 2,
        out_specs=[VMEM] * 2,
        scratch_shapes=scratch(sz, cells, share, sz.tiles, sz.own)
        + [
            pltpu.VMEM((3 * cells, sz.width), F32),
            pltpu.SMEM((2, sz.own + 8), jnp.int32),
            pltpu.SMEM(tasks.shape, jnp.int32),
            pltpu.VMEM(chunk.shape, F32),
            pltpu.SemaphoreType.DMA((2,)),
        ],
        compiler_params=params,
        cost_estimate=pl.CostEstimate(flops=10**9, bytes_accessed=10**7, transcendentals=0),
        name="second_own",
    )(high, low, *chunks, in_hbm(tasks), in_hbm(chunk))
    result = shape((3, sz.share, points), F32)
    ghosts = up(owners * sz.group, 8)
    outputs = pl.pallas_call(
        functools.partial(ghost_kernel, sz),
        out_shape=[result, result],
        in_specs=[VMEM] * 5 + [HBM],
        out_specs=[VMEM] * 2,
        scratch_shapes=scratch(sz, ghosts, share, sz.tiles, sz.own)
        + [
            pltpu.VMEM((3 * ghosts, sz.width), F32),
            pltpu.SMEM((2, sz.own + 8), jnp.int32),
            pltpu.SMEM(tasks.shape, jnp.int32),
            pltpu.SemaphoreType.DMA((1,)),
        ],
        compiler_params=params,
        name="second_ghosts",
    )(arrived, high, low, speed, moved, in_hbm(tasks))
    return tuple(jnp.transpose(output, (1, 0, 2)) for output in outputs)


def solution(mesh):
    in_specs = (
        P("space", None, None),
        P(),
        P("space", None),
        P(("space", "lane"), None),
        P(("space", "lane"), None),
        P(("space", "lane")),
    )
    out_specs = (P(("space", "lane"), None, None), P(("space", "lane"), None, None))
    return jax.shard_map(shards, mesh=mesh, in_specs=in_specs, out_specs=out_specs, check_vma=False)
```

```python
import functools
from types import SimpleNamespace

import jax
import jax.numpy as jnp
from jax import lax
from jax.experimental import pallas as pl
from jax.experimental.pallas import tpu as pltpu
from jax.sharding import PartitionSpec as P

REGULARIZE = 0.25
TIME_STEP = 0.5
UNROLL = 11
PAIR = 2
SOURCE_ROWS = 24
SUM_ROWS = 16

F32 = jnp.float32
BF16 = jnp.bfloat16
VMEM = pl.BlockSpec(memory_space=pltpu.VMEM)
SMEM = pl.BlockSpec(memory_space=pltpu.SMEM)
HBM = pl.BlockSpec(memory_space=pltpu.HBM)


def up(value, step):
    return -(-value // step) * step


def sizes(owners, lanes, cells, points, cap, listed):
    main = 128 * (points // (128 * lanes))
    rest = (points - main * lanes) // lanes
    group = listed // owners
    pool = up(cells + listed, 8)
    per_pack = 128 // rest
    return SimpleNamespace(
        owners=owners,
        lanes=lanes,
        cells=cells,
        points=points,
        cap=cap,
        group=group,
        width=up(points, 128),
        tiles=up(points, 128) // 128,
        main=main,
        rest=rest,
        rest_tiles=up(rest * lanes, 128) // 128,
        chunk=main + rest,
        chunk_wide=main + up(rest, 128),
        chunk_tiles=(main + up(rest, 128)) // 128,
        per_pack=per_pack,
        pool=pool,
        share=cells // lanes,
        slots=up(lanes * cap + UNROLL, 8),
        rows=cells + 8,
        own=up(lanes * cap + PAIR, 8),
    )


def pack_rows(sz, rows):
    return (3 * rows * sz.main // 128) + 8 * up(3 * rows // 8, sz.per_pack) // sz.per_pack


def split2(value):
    high = value.astype(BF16)
    return high, (value - high.astype(F32)).astype(BF16)


def split3(value):
    first = value.astype(BF16).astype(F32)
    left = value - first
    second = left.astype(BF16).astype(F32)
    return first, second, left - second


def lane_iota(rows):
    return lax.broadcasted_iota(jnp.int32, (rows, 128), 1)


def fetch(sources, targets, sems):
    copies = [
        pltpu.make_async_copy(source, target, sems.at[q])
        for q, (source, target) in enumerate(zip(sources, targets))
    ]
    for copy in copies:
        copy.start()
    return copies


def loop(count, body):
    if count <= 8:
        for q in range(count):
            body(q)
    else:

        def step(q, carry):
            body(q)
            return carry

        lax.fori_loop(0, count, step, 0)


def own_chunk(sz, lane, ref, rows):
    parts = []
    if sz.main:
        parts.append(ref[rows, pl.ds(pl.multiple_of(lane * sz.main, 128), sz.main)])
    start = sz.rest * lane
    lanes = lane_iota(8)
    rest = jnp.zeros((8, 128), F32)
    for tile in range(sz.rest_tiles):
        offset = sz.main * sz.lanes + 128 * tile
        block = ref[rows, offset : min(offset + 128, ref.shape[-1])]
        if block.shape[1] < 128:
            block = jnp.concatenate([block, jnp.zeros((8, 128 - block.shape[1]), F32)], axis=1)
        inside = (lanes + 128 * tile >= start) & (lanes + 128 * tile < start + sz.rest)
        rest = rest + jnp.where(inside, block, 0.0)
    rest = pltpu.roll(rest, lax.rem(128 * sz.rest_tiles - start, 128), 1)
    parts.append(rest)
    return jnp.concatenate(parts, axis=1) if len(parts) > 1 else parts[0]


def send_ghosts(sz, send, chunks, out, tasks):
    lanes = lane_iota(1)

    def one(d):
        for g in range(sz.group):
            cell = send[0, d * sz.group + g]
            rows = []
            last = tasks
            for i in range(3):
                row = chunks[pl.ds(i * sz.rows + cell, 1), :]
                rows.append(row[:, :128] if sz.main else jnp.zeros((1, 128), F32))
                piece = jnp.where(lanes < sz.rest, row[:, sz.main : sz.main + 128], 0.0)
                last = last + (pltpu.roll(piece, i * sz.rest, 1) if i else piece)
            rows.append(last)
            for other in range(sz.lanes):
                first = ((d * sz.lanes + other) * sz.group + g) * 4
                for q, row in enumerate(rows):
                    out[pl.ds(first + q, 1), :] = row

    loop(sz.owners, one)


def pick_kernel(sz, *refs):
    inputs, (out, send_out), held, (chunks, sems) = refs[:5], refs[5:7], refs[7:12], refs[12:]
    for copy in fetch(inputs, held, sems):
        copy.wait()
    send, target, source, count, positions = held
    for j in range(send_out.shape[1]):
        send_out[0, j] = send[0, j]
    lane = lax.axis_index("lane")
    for i in range(3):
        for g in range(0, sz.cells, 8):
            value = own_chunk(sz, lane, positions.at[i], pl.ds(g, 8))
            chunks[pl.ds(i * sz.rows + g, 8), :] = value
    spare = jnp.zeros((1, 128 - sz.cap), F32)
    tasks = jnp.where(lane_iota(1) == 3 * sz.rest + 2 * sz.cap, count[0].astype(F32), 0.0)
    for q, row in enumerate((target, source)):
        wide = jnp.concatenate([row[...].astype(F32), spare], axis=1)
        tasks = tasks + pltpu.roll(wide, 3 * sz.rest + q * sz.cap, 1)
    send_ghosts(sz, send, chunks, out, tasks)


def take_ghosts(sz, arrived, pool, stride, base):
    lanes = lane_iota(1)

    def one(d):
        for g in range(sz.group):
            first = [((d * sz.lanes + lane) * sz.group + g) * 4 for lane in range(sz.lanes)]
            last = [arrived[pl.ds(row + 3, 1), :] for row in first]
            for i in range(3):
                tiles = []
                if sz.main:
                    tiles += [arrived[pl.ds(row + i, 1), :] for row in first]
                for tile in range(sz.rest_tiles):
                    total = jnp.zeros((1, 128), F32)
                    for lane in range(sz.lanes):
                        start = sz.rest * lane
                        if start + sz.rest <= 128 * tile or start >= 128 * tile + 128:
                            continue
                        shift = (start - i * sz.rest) % 128
                        value = pltpu.roll(last[lane], shift, 1) if shift else last[lane]
                        at = lanes + 128 * tile
                        total = jnp.where((at >= start) & (at < start + sz.rest), value, total)
                    tiles.append(total)
                place = pl.ds(i * stride + base + d * sz.group + g, 1)
                pool[place, :] = jnp.concatenate(tiles, axis=1)

    loop(sz.owners, one)


def build_list(sz, lists, tasks):
    total = jnp.int32(0)
    for lane in range(sz.lanes):
        count = lists[lane, 2 * sz.cap]
        for j in range(sz.cap):
            tasks[0, total] = lists[lane, j]
            tasks[1, total] = lists[lane, sz.cap + j]
            total = total + (j < count).astype(jnp.int32)
    for u in range(UNROLL):
        tasks[0, total + u] = jnp.int32(sz.cells)
        tasks[1, total + u] = jnp.int32(0)
    tasks[2, 0] = total
    return total


def own_list(sz, lane, tasks, mine, low, high):
    first = lane * sz.share
    total = tasks[2, 0]
    count = jnp.int32(0)
    for t in range(sz.lanes * sz.cap):
        target = tasks[0, t] - first
        source = tasks[1, t]
        mine[0, count] = target
        mine[1, count] = source - low
        taken = (target >= 0) & (target < sz.share) & (t < total)
        taken = taken & (source >= low) & (source < high)
        count = count + taken.astype(jnp.int32)
    for u in range(PAIR):
        mine[0, count + u] = jnp.int32(-1)
        mine[1, count + u] = jnp.int32(0)
    return count


def products(value, bend_high, bend_low):
    high, low = split2(value)
    dot = functools.partial(jnp.dot, preferred_element_type=F32)
    return dot(high, bend_high) + dot(low, bend_high) + dot(high, bend_low)


def make_sources(sz, value, bend_high, bend_low, source_rows, centres, first):
    count = value.shape[0] // 3
    forces = products(value[:, : sz.points], bend_high, bend_low)
    forces = jnp.concatenate(
        [forces, jnp.zeros((3 * count, sz.width - sz.points), F32)], axis=1
    )
    middle = jnp.sum(value, axis=1, keepdims=True) / sz.points
    for g in range(count // 8):
        where = [i * count + 8 * g for i in range(3)]
        middles = [jnp.broadcast_to(middle[w : w + 8], (8, 128)) for w in where]
        middles += [jnp.zeros((8, 128), F32)] * 5
        for i, row in enumerate(middles):
            centres[pl.ds(8 * (first + 8 * g) + i, 8, stride=8), :] = row
        for j in range(sz.tiles):
            cut = slice(128 * j, 128 * j + 128)
            y = [value[w : w + 8, cut] - m for w, m in zip(where, middles)]
            f = [forces[w : w + 8, cut] for w in where]
            norm = y[0] * y[0] + y[1] * y[1] + y[2] * y[2] + REGULARIZE
            along = y[0] * f[0] + y[1] * f[1] + y[2] * f[2]
            one, zero = jnp.ones((8, 128), F32), jnp.zeros((8, 128), F32)
            rows = [y[0], y[1], y[2], norm, one, zero, zero, zero]
            rows += f
            rows += [y[i] * f[k] for i in range(3) for k in range(3)]
            rows += [norm * f[i] + along * y[i] for i in range(3)]
            rows += [along]
            for k, row in enumerate(rows):
                place = pl.ds(SOURCE_ROWS * (first + 8 * g) + k, 8, stride=SOURCE_ROWS)
                source_rows.at[j][place, :] = row


def make_targets(sz, blocks, targets):
    targets[...] = jnp.zeros_like(targets)
    for i in range(3):
        for g in range(blocks[i].shape[0] // 8):
            block = blocks[i][8 * g : 8 * g + 8]
            for j in range(targets.shape[0]):
                cut = slice(128 * j, 128 * j + 128)
                targets.at[j][pl.ds(64 * g + i, 8, stride=8), :] = block[:, cut]


def rows_of(refs, cell, rows, tile=None):
    def load(ref, at):
        place = pl.ds(pl.multiple_of(rows * at, 8), rows)
        return ref[place, :] if tile is None else ref[tile, place, :]

    if not isinstance(refs, tuple):
        return load(refs, cell)
    first, second = refs
    count = first.shape[-2] // rows
    own = load(first, jnp.minimum(cell, count - 1))
    return jnp.where(cell < count, own, load(second, jnp.maximum(cell - count, 0)))


def source_operands(sz, source, source_rows):
    held = [rows_of(source_rows, source, SOURCE_ROWS, j) for j in range(sz.tiles)]
    held = jnp.concatenate(held, axis=1)
    y1, y2, y3 = split3(held[:8])
    y_stack = jnp.concatenate([y1, y1, y2, y2, y1, y3], axis=0).astype(BF16)
    return y_stack, jnp.concatenate(split3(held[8:]), axis=0)


def pieces(points, step):
    starts = list(range(0, max(points // 128 * 128, 1), step))
    return list(zip(starts, starts[1:] + [points]))


def twice(piece, count):
    whole = count // 128 * 128
    parts = [piece[:, :whole].astype(BF16)] * 2 if whole else []
    if whole < count:
        last = piece[:, whole:]
        last = last + pltpu.roll(last, count - whole, 1)
        parts.append(last.astype(BF16)[:, : 2 * (count - whole)])
    return jnp.concatenate(parts, axis=1)


def load_target(j, target, slot, centre, targets, offsets):
    row = lax.broadcasted_iota(jnp.int32, (8, 128), 0)
    x = targets[j, pl.ds(pl.multiple_of(8 * target, 8), 8), :] - centre
    square = x * x
    norm = pltpu.roll(square, 2, 0) + pltpu.roll(square, 3, 0) + pltpu.roll(square, 4, 0)
    side = jnp.where(row == 4, norm, jnp.where(row == 3, 1.0, 0.0))
    x_side = jnp.where(row < 3, -2.0 * x, side)
    x1, x2, x3 = split3(x_side)
    return x, jnp.concatenate([x1, x2, x1, x2, x3, x1], axis=0).astype(BF16)


def distances(one_stack, other_stack):
    return jnp.dot(one_stack, other_stack, preferred_element_type=F32)


def weights(shifted):
    inverse = lax.rsqrt(shifted)
    return split2(inverse * inverse * inverse)


def fold(result):
    return result[:SUM_ROWS] + result[SUM_ROWS : 2 * SUM_ROWS] + result[2 * SUM_ROWS :]


def skewed(stages, skew):
    asked = []
    for q, (ask, _) in enumerate(stages):
        asked.append(ask())
        if q >= skew:
            stages[q - skew][1](asked[q - skew])
            asked[q - skew] = None
    for q in range(max(len(stages) - skew, 0), len(stages)):
        stages[q][1](asked[q])


def adder(totals, key):
    def add(value):
        totals[key] = totals[key] + value if key in totals else value

    return add


def wide_piece(operands, begin, first, end, add):
    def ask():
        _, y_turned, _, blocks = operands()
        return distances(y_turned[first:end], blocks[begin])

    def take(shifted):
        m_piece = operands()[2][first]
        high, low = weights(shifted)
        whole = (end - first) // 128 * 128
        parts = [high[:whole], low[:whole]] if whole else []
        parts += [high[whole:], low[whole:]] if whole < end - first else []
        stack = jnp.concatenate(parts, axis=0)
        add(jnp.dot(m_piece, stack, preferred_element_type=F32))

    return ask, take


def rest_piece(operands, begin, add):
    def ask():
        y_stack, _, _, blocks = operands()
        return distances(blocks[begin], y_stack)

    def take(shifted):
        stack = jnp.concatenate(weights(shifted), axis=1)
        m_whole = jnp.concatenate([operands()[2][-1]] * 2, axis=1)
        turned = (((1,), (1,)), ((), ()))
        add(lax.dot_general(m_whole, stack, turned, preferred_element_type=F32))

    return ask, take


def store_sums(slots, slot, j, x, result, offsets, sums):
    offsets.at[j][pl.ds(slot, 8, stride=slots), :] = x
    for h in range(0, SUM_ROWS, 8):
        sums.at[j][pl.ds(h * slots + slot, 8, stride=slots), :] = result[h : h + 8]


def mark(slot, target, hot):
    hot[pl.ds(slot, 1), :] = jnp.where(lane_iota(1) == target, 1.0, 0.0)


def combine(sz, slots, first, total, offsets, sums, speeds):
    live = lax.broadcasted_iota(jnp.int32, (8, 128), 0) + first < total
    for j in range(offsets.shape[0]):
        x = [offsets[j, pl.ds(i * slots + first, 8), :] for i in range(3)]
        s = [sums[j, pl.ds(k * slots + first, 8), :] for k in range(SUM_ROWS)]
        a, b, c = s[:3], [s[3:6], s[6:9], s[9:12]], s[12:15]
        norm = x[0] * x[0] + x[1] * x[1] + x[2] * x[2] + REGULARIZE
        along = x[0] * a[0] + x[1] * a[1] + x[2] * a[2] - s[15]
        for i in range(3):
            speed = norm * a[i] + c[i] + along * x[i]
            for k in range(3):
                speed = speed - x[k] * (2.0 * b[k][i] + b[i][k])
            speed = jnp.where(live, speed / sz.points, 0.0)
            speeds[i, pl.ds(first, 8), 128 * j : 128 * j + 128] = speed


def add_up(sz, slots, total, rows, offsets, sums, speeds, hot):
    def eight(q, carry):
        combine(sz, slots, pl.multiple_of(8 * q, 8), total, offsets, sums, speeds)
        return carry

    if slots <= 64 and offsets.shape[0] <= 2:
        for q in range(slots // 8):
            combine(sz, slots, 8 * q, total, offsets, sums, speeds)
    else:
        lax.fori_loop(0, lax.div(total + 7, 8), eight, 0)
    one_hot = hot[...].astype(BF16)
    result = []
    for i in range(3):
        first, second, third = split3(speeds[i])
        parts = [
            lax.dot_general(
                one_hot, part.astype(BF16), (((0,), (0,)), ((), ())), preferred_element_type=F32
            )
            for part in (first, second, third)
        ]
        result.append((parts[0] + parts[1] + parts[2])[:rows])
    return result


def several_tasks(sz, slots, picks, marks, main, rest, wide, step, skew, refs):
    source_rows, centres, targets, offsets, sums, hot = refs

    def task(slot, pick, target_mark):
        target, source = pick
        made, parts, points = [], {}, []

        def operands():
            if made:
                return made[0]
            y_stack, m_stack = source_operands(sz, source, source_rows)
            centre = rows_of(centres, source, 8)
            points.extend(
                load_target(j, target, slot, centre, targets, offsets)
                for j in range(targets.shape[0])
            )
            blocks = {}
            for begin in range(0, main, wide):
                stack = [stack for _, stack in points[begin // 128 : (begin + wide) // 128]]
                blocks[begin] = jnp.concatenate(stack, axis=1)
            if rest:
                blocks[main] = jnp.transpose(points[main // 128][1])[:rest]
            sides = {-1: m_stack.astype(BF16)}
            if main:
                for first, last in pieces(sz.points, step):
                    sides[first] = twice(m_stack[:, first : up(last, 128)], last - first)
            made.append((y_stack, jnp.transpose(y_stack), sides, blocks))
            return made[0]

        def finish():
            results = [fold(parts[begin]) for begin in range(0, main, wide)]
            if rest:
                spare = jnp.zeros((SUM_ROWS, 128 - rest), F32)
                results.append(jnp.concatenate([fold(parts[main]), spare], axis=1))
            result = jnp.concatenate(results, axis=1)
            for j in range(targets.shape[0]):
                cut = result[:, 128 * j : 128 * j + 128]
                store_sums(offsets.shape[1] // 8, slot, j, points[j][0], cut, offsets, sums)
            mark(slot, target_mark, hot)

        own = []
        for begin in range(0, main, wide):
            for first, last in pieces(sz.points, step):
                own.append(wide_piece(operands, begin, first, last, adder(parts, begin)))
        if rest:
            own.insert(len(own) // 2, rest_piece(operands, main, adder(parts, main)))
        ask, take = own[-1]

        def last_take(shifted):
            take(shifted)
            finish()

        own[-1] = (ask, last_take)
        return own, operands

    made = [task(slot, pick, m) for slot, pick, m in zip(slots, picks, marks)]
    for (own, _), (_, after) in zip(made, made[1:]):
        ask, take = own[0]

        def ask_and_prepare(ask=ask, after=after):
            shifted = ask()
            after()
            return shifted

        own[0] = (ask_and_prepare, take)
    skewed([stage for own, _ in made for stage in own], skew)


def tiles_of_chunk(sz, total, tasks, *refs):
    def several(q, carry):
        slots = [q * UNROLL + u for u in range(UNROLL)]
        picks = [(tasks[0, slot], tasks[1, slot]) for slot in slots]
        marks = [target for target, _ in picks]
        several_tasks(sz, slots, picks, marks, sz.main, sz.rest, 128, 256, 9, refs)
        return carry

    lax.fori_loop(0, lax.div(total + UNROLL - 1, UNROLL), several, 0)


def tiles_of_cells(sz, total, mine, *refs):
    main = 256 * (sz.points // 256)

    def several(q, carry):
        slots = [q * PAIR + u for u in range(PAIR)]
        marks = [mine[0, slot] for slot in slots]
        picks = [(jnp.maximum(mark, 0), mine[1, slot]) for mark, slot in zip(marks, slots)]
        several_tasks(sz, slots, picks, marks, main, sz.points - main, 256, 256, 3, refs)
        return carry

    lax.fori_loop(0, lax.div(total + PAIR - 1, PAIR), several, 0)


def packed(sz, blocks):
    rows = [b[:, : sz.main] for b in blocks] if sz.main else []
    lanes = lane_iota(8)
    for p in range(0, len(blocks), sz.per_pack):
        total = jnp.zeros((8, 128), F32)
        for q, block in enumerate(blocks[p : p + sz.per_pack]):
            rest = jnp.where(lanes < sz.rest, block[:, sz.main : sz.main + 128], 0.0)
            total = total + (pltpu.roll(rest, q * sz.rest, 1) if q else rest)
        rows.append(total)
    return rows


def store_packed(sz, out, blocks):
    first = 0
    count = len(blocks)
    values = packed(sz, blocks)
    if sz.main:
        for b in range(count):
            for m in range(sz.main // 128):
                out[pl.ds(first, 8), :] = values[b][:, 128 * m : 128 * m + 128]
                first += 8
        values = values[count:]
    for value in values:
        out[pl.ds(first, 8), :] = value
        first += 8


def place_packed(sz, lane, arrived, count, store_main, add_rest):
    first = 0
    if sz.main:
        for b in range(count):
            for m in range(sz.main // 128):
                store_main(b, m, arrived[pl.ds(first, 8), :])
                first += 8
    start = sz.rest * lane
    lanes = lane_iota(8)
    for b in range(count):
        pack, q = divmod(b, sz.per_pack)
        value = arrived[pl.ds(first + 8 * pack, 8), :]
        value = pltpu.roll(value, lax.rem(start - q * sz.rest + 128, 128), 1)
        for tile in range(sz.rest_tiles):
            inside = (lanes + 128 * tile >= start) & (lanes + 128 * tile < start + sz.rest)
            add_rest(b, tile, jnp.where(inside, value, 0.0))


def source_kernel(sz, *refs):
    inputs, (high_out, low_out, source_rows, centres), held, sems = (
        refs[:2],
        refs[2:6],
        refs[6:8],
        refs[8],
    )
    for copy in fetch(inputs, held, sems):
        copy.wait()
    positions, bend = held
    high_out[...], low_out[...] = split2(bend[...])
    value = jnp.concatenate([positions[i] for i in range(3)], axis=0)
    value = jnp.concatenate(
        [value, jnp.zeros((3 * sz.cells, sz.width - sz.points), F32)], axis=1
    )
    make_sources(sz, value, high_out[...], low_out[...], source_rows, centres, 0)


def first_kernel(sz, *refs):
    arrived, high, low, own_rows, own_centres = refs[:5]
    inputs, outputs, refs = refs[5:7], refs[7:10], refs[10:]
    source_rows, centres, targets, offsets, sums, speeds, hot, moved, pool = refs[:9]
    send, positions, staged, lists, chunk_out, ghost_out, tasks, sems = refs[9:]
    me, lane = lax.axis_index("space"), lax.axis_index("lane")
    copies = fetch(inputs, [send, positions], sems)
    for other in range(sz.lanes):
        row = ((me * sz.lanes + other) * sz.group) * 4 + 3
        value = pltpu.roll(arrived[pl.ds(row, 1), :], 128 - 3 * sz.rest, 1)
        staged[pl.ds(other, 1), :] = value.astype(jnp.int32)
    copies += fetch([staged], [lists], sems.at[pl.ds(2, 1)])
    pool[...] = jnp.zeros_like(pool)
    take_ghosts(sz, arrived, pool, up(sz.owners * sz.group, 8), 0)
    hot[...] = jnp.zeros_like(hot)
    speeds[...] = jnp.zeros_like(speeds)
    make_sources(sz, pool[...], high[...], low[...], source_rows, centres, 0)
    for copy in copies[:2]:
        copy.wait()
    chunks = [
        [own_chunk(sz, lane, positions.at[i], pl.ds(g, 8)) for g in range(0, sz.cells, 8)]
        for i in range(3)
    ]
    make_targets(sz, [jnp.concatenate(blocks, axis=0) for blocks in chunks], targets)
    copies[2].wait()
    total = build_list(sz, lists, tasks)
    copies = fetch([tasks], outputs[2:], sems)
    rows, middles = (own_rows, source_rows), (own_centres, centres)
    tiles_of_chunk(sz, total, tasks, rows, middles, targets, offsets, sums, hot)
    velocity = add_up(sz, sz.slots, total, sz.cells, offsets, sums, speeds, hot)
    blocks = []
    for i in range(3):
        for g in range(0, sz.cells, 8):
            chunk = own_chunk(sz, lane, positions.at[i], pl.ds(g, 8))
            block = chunk + TIME_STEP * velocity[i][g : g + 8]
            moved[pl.ds(i * sz.rows + g, 8), :] = block
            blocks.append(block)
    store_packed(sz, chunk_out, blocks)
    copies += fetch([chunk_out], outputs[:1], sems.at[pl.ds(1, 1)])
    send_ghosts(sz, send, moved, ghost_out, jnp.zeros((1, 128), F32))
    copies += fetch([ghost_out], outputs[1:2], sems.at[pl.ds(2, 1)])
    for copy in copies:
        copy.wait()


def own_kernel(sz, *refs):
    (high, low), refs = refs[:2], refs[2:]
    others, refs = refs[: sz.lanes - 1], refs[sz.lanes - 1 :]
    inputs, (speed_out, share_out), refs = refs[:2], refs[2:4], refs[4:]
    source_rows, centres, targets, offsets, sums, speeds, hot, pool, mine = refs[:9]
    tasks, chunk, sems = refs[9:]
    copies = fetch(inputs, [tasks, chunk], sems)
    chunks = [chunk, *others]
    hot[...] = jnp.zeros_like(hot)
    speeds[...] = jnp.zeros_like(speeds)
    lane = lax.axis_index("lane")
    pool[...] = jnp.zeros_like(pool)
    copies[0].wait()
    total = own_list(sz, lane, tasks, mine, 0, sz.cells)
    copies[1].wait()
    per = sz.cells // 8
    for k in range(sz.lanes):
        other = lane ^ k

        def row_of(b):
            return (b // per) * sz.cells + 8 * (b % per)

        def store_main(b, m, value):
            cut = pl.ds(pl.multiple_of(other * sz.main + 128 * m, 128), 128)
            pool[pl.ds(row_of(b), 8), cut] = value

        def add_rest(b, tile, value):
            offset = sz.main * sz.lanes + 128 * tile
            cut = (pl.ds(row_of(b), 8), slice(offset, offset + 128))
            pool[cut] = pool[cut] + value

        place_packed(sz, other, chunks[k], 3 * per, store_main, add_rest)
    for i in range(3):
        share_out[i] = share_rows(sz, pool, i * sz.cells, lane)
    make_sources(sz, pool[...], high[...], low[...], source_rows, centres, 0)
    make_targets(sz, share_out, targets)
    tiles_of_cells(sz, total, mine, source_rows, centres, targets, offsets, sums, hot)
    velocity = add_up(sz, sz.own, total, up(sz.share, 8), offsets, sums, speeds, hot)
    for i in range(3):
        speed_out[i] = velocity[i]


def ghost_kernel(sz, *refs):
    arrived, high, low, speed_in, share, tasks_in = refs[:6]
    moved_out, velocity_out = refs[6:8]
    source_rows, centres, targets, offsets, sums, speeds, hot, pool, mine = refs[8:17]
    tasks, sems = refs[17:]
    copies = fetch([tasks_in], [tasks], sems)
    hot[...] = jnp.zeros_like(hot)
    speeds[...] = jnp.zeros_like(speeds)
    lane = lax.axis_index("lane")
    pool[...] = jnp.zeros_like(pool)
    ghosts = up(sz.owners * sz.group, 8)
    take_ghosts(sz, arrived, pool, ghosts, 0)
    make_sources(sz, pool[...], high[...], low[...], source_rows, centres, 0)
    make_targets(sz, share, targets)
    copies[0].wait()
    total = own_list(sz, lane, tasks, mine, sz.cells, sz.cells + sz.owners * sz.group)
    tiles_of_cells(sz, total, mine, source_rows, centres, targets, offsets, sums, hot)
    velocity = add_up(sz, sz.own, total, up(sz.share, 8), offsets, sums, speeds, hot)
    for i in range(3):
        speed = velocity[i] + speed_in[i]
        velocity_out[i] = speed[: sz.share, : sz.points]
        moved_out[i] = (share[i] + TIME_STEP * speed)[: sz.share, : sz.points]


def share_rows(sz, ref, base, lane):
    if sz.share % 8 == 0:
        return ref[pl.ds(pl.multiple_of(base + lane * sz.share, 8), sz.share), :]
    rows = [ref[pl.ds(base + lane * sz.share + c, 1), :] for c in range(sz.share)]
    rows.append(jnp.zeros((8 - sz.share, rows[0].shape[1]), F32))
    return jnp.concatenate(rows, axis=0)


def scratch(sz, cells, targets, tiles, slots):
    return [
        pltpu.VMEM((sz.tiles, SOURCE_ROWS * cells, 128), F32),
        pltpu.VMEM((8 * cells, 128), F32),
        pltpu.VMEM((tiles, 8 * targets, 128), F32),
        pltpu.VMEM((tiles, 8 * slots, 128), F32),
        pltpu.VMEM((tiles, SUM_ROWS * slots, 128), F32),
        pltpu.VMEM((3, slots, 128 * tiles), F32),
        pltpu.VMEM((slots, 128), F32),
    ]


def swap(value, axis, size, k):
    return lax.ppermute(value, axis, [(d, d ^ k) for d in range(size)])


def in_hbm(value):
    return pltpu.with_memory_space_constraint(value, pltpu.HBM)


def shards(positions, bend_op, send_list, task_target, task_source, task_count):
    owners, lanes = lax.axis_size("space"), lax.axis_size("lane")
    cells, points = positions.shape[0], positions.shape[2]
    sz = sizes(owners, lanes, cells, points, task_target.shape[1], send_list.shape[1])
    params = pltpu.CompilerParams(vmem_limit_bytes=min(6 * lanes, 40) << 20)
    shape = jax.ShapeDtypeStruct
    both = ("space", "lane")
    by_component = jnp.transpose(positions, (1, 0, 2))
    list_rows = up(lanes, 8)
    slot_shape = shape((4 * sz.group * owners * lanes, 128), F32)
    leaving, send = pl.pallas_call(
        functools.partial(pick_kernel, sz),
        out_shape=[slot_shape, shape(send_list.shape, jnp.int32)],
        in_specs=[HBM] * 5,
        out_specs=[VMEM, SMEM],
        scratch_shapes=[
            pltpu.SMEM(send_list.shape, jnp.int32),
            pltpu.VMEM(task_target.shape, jnp.int32),
            pltpu.VMEM(task_source.shape, jnp.int32),
            pltpu.SMEM(task_count.shape, jnp.int32),
            pltpu.VMEM(by_component.shape, F32),
            pltpu.VMEM((3 * sz.rows, sz.chunk_wide), F32),
            pltpu.SemaphoreType.DMA((5,)),
        ],
        compiler_params=pltpu.CompilerParams(vmem_limit_bytes=60 << 20),
        name="pick_cells",
    )(send_list, task_target, task_source, task_count, by_component)
    arrived = lax.all_to_all(leaving, both, split_axis=0, concat_axis=0, tiled=True)
    high, low, own_rows, own_centres = pl.pallas_call(
        functools.partial(source_kernel, sz),
        out_shape=[
            shape(bend_op.shape, BF16),
            shape(bend_op.shape, BF16),
            shape((sz.tiles, SOURCE_ROWS * cells, 128), F32),
            shape((8 * cells, 128), F32),
        ],
        in_specs=[HBM] * 2,
        out_specs=[VMEM] * 4,
        scratch_shapes=[
            pltpu.VMEM(by_component.shape, F32),
            pltpu.VMEM(bend_op.shape, F32),
            pltpu.SemaphoreType.DMA((2,)),
        ],
        compiler_params=params,
        cost_estimate=pl.CostEstimate(flops=10**9, bytes_accessed=10**7, transcendentals=0),
        name="first_sources",
    )(in_hbm(by_component), in_hbm(bend_op))
    chunk_shape = (pack_rows(sz, cells), 128)
    chunk, leaving, tasks = pl.pallas_call(
        functools.partial(first_kernel, sz),
        out_shape=[
            pltpu.HBM(chunk_shape, F32),
            pltpu.HBM(slot_shape.shape, F32),
            pltpu.HBM((3, sz.slots), jnp.int32),
        ],
        in_specs=[VMEM] * 5 + [HBM] * 2,
        out_specs=[HBM] * 3,
        scratch_shapes=scratch(sz, sz.pool - cells, sz.rows, sz.chunk_tiles, sz.slots)
        + [
            pltpu.VMEM((3 * sz.rows, sz.chunk_wide), F32),
            pltpu.VMEM((3 * up(sz.owners * sz.group, 8), sz.width), F32),
            pltpu.SMEM(send_list.shape, jnp.int32),
            pltpu.VMEM(by_component.shape, F32),
            pltpu.VMEM((list_rows, 128), jnp.int32),
            pltpu.SMEM((list_rows, 128), jnp.int32),
            pltpu.VMEM(chunk_shape, F32),
            pltpu.VMEM(slot_shape.shape, F32),
            pltpu.SMEM((3, sz.slots), jnp.int32),
            pltpu.SemaphoreType.DMA((3,)),
        ],
        compiler_params=params,
        name="first_step",
    )(arrived, high, low, own_rows, own_centres, in_hbm(send), in_hbm(by_component))
    arrived = lax.all_to_all(leaving, both, split_axis=0, concat_axis=0, tiled=True)
    chunks = [swap(chunk, "lane", lanes, k) for k in range(1, lanes)]
    share = up(sz.share, 8)
    so_far = shape((3, share, sz.width), F32)
    speed, moved = pl.pallas_call(
        functools.partial(own_kernel, sz),
        out_shape=[so_far, so_far],
        in_specs=[VMEM] * (lanes + 1) + [HBM] * 2,
        out_specs=[VMEM] * 2,
        scratch_shapes=scratch(sz, cells, share, sz.tiles, sz.own)
        + [
            pltpu.VMEM((3 * cells, sz.width), F32),
            pltpu.SMEM((2, sz.own + 8), jnp.int32),
            pltpu.SMEM(tasks.shape, jnp.int32),
            pltpu.VMEM(chunk.shape, F32),
            pltpu.SemaphoreType.DMA((2,)),
        ],
        compiler_params=params,
        cost_estimate=pl.CostEstimate(flops=10**9, bytes_accessed=10**7, transcendentals=0),
        name="second_own",
    )(high, low, *chunks, in_hbm(tasks), in_hbm(chunk))
    result = shape((3, sz.share, points), F32)
    ghosts = up(owners * sz.group, 8)
    outputs = pl.pallas_call(
        functools.partial(ghost_kernel, sz),
        out_shape=[result, result],
        in_specs=[VMEM] * 5 + [HBM],
        out_specs=[VMEM] * 2,
        scratch_shapes=scratch(sz, ghosts, share, sz.tiles, sz.own)
        + [
            pltpu.VMEM((3 * ghosts, sz.width), F32),
            pltpu.SMEM((2, sz.own + 8), jnp.int32),
            pltpu.SMEM(tasks.shape, jnp.int32),
            pltpu.SemaphoreType.DMA((1,)),
        ],
        compiler_params=params,
        name="second_ghosts",
    )(arrived, high, low, speed, moved, in_hbm(tasks))
    return tuple(jnp.transpose(output, (1, 0, 2)) for output in outputs)


def solution(mesh):
    in_specs = (
        P("space", None, None),
        P(),
        P("space", None),
        P(("space", "lane"), None),
        P(("space", "lane"), None),
        P(("space", "lane")),
    )
    out_specs = (P(("space", "lane"), None, None), P(("space", "lane"), None, None))
    return jax.shard_map(shards, mesh=mesh, in_specs=in_specs, out_specs=out_specs, check_vma=False)
```

```python
import functools
from types import SimpleNamespace

import jax
import jax.numpy as jnp
from jax import lax
from jax.experimental import pallas as pl
from jax.experimental.pallas import tpu as pltpu
from jax.sharding import PartitionSpec as P

REGULARIZE = 0.25
TIME_STEP = 0.5
UNROLL = 11
PAIR = 2
SOURCE_ROWS = 24
SUM_ROWS = 16

F32 = jnp.float32
BF16 = jnp.bfloat16
VMEM = pl.BlockSpec(memory_space=pltpu.VMEM)
SMEM = pl.BlockSpec(memory_space=pltpu.SMEM)
HBM = pl.BlockSpec(memory_space=pltpu.HBM)
ANY = pl.BlockSpec(memory_space=pl.ANY)


def up(value, step):
    return -(-value // step) * step


def sizes(owners, lanes, cells, points, cap, listed):
    main = 128 * (points // (128 * lanes))
    rest = (points - main * lanes) // lanes
    group = listed // owners
    pool = up(cells + listed, 8)
    per_pack = 128 // rest
    return SimpleNamespace(
        owners=owners,
        lanes=lanes,
        cells=cells,
        points=points,
        cap=cap,
        group=group,
        width=up(points, 128),
        tiles=up(points, 128) // 128,
        main=main,
        rest=rest,
        rest_tiles=up(rest * lanes, 128) // 128,
        chunk=main + rest,
        chunk_wide=main + up(rest, 128),
        chunk_tiles=(main + up(rest, 128)) // 128,
        per_pack=per_pack,
        pool=pool,
        share=cells // lanes,
        slots=up(lanes * cap + UNROLL, 8),
        rows=cells + 8,
        own=up(lanes * cap + PAIR, 8),
    )


def pack_rows(sz, rows):
    return (3 * rows * sz.main // 128) + 8 * up(3 * rows // 8, sz.per_pack) // sz.per_pack


def split2(value):
    high = value.astype(BF16)
    return high, (value - high.astype(F32)).astype(BF16)


def split3(value):
    first = value.astype(BF16).astype(F32)
    left = value - first
    second = left.astype(BF16).astype(F32)
    return first, second, left - second


def lane_iota(rows):
    return lax.broadcasted_iota(jnp.int32, (rows, 128), 1)


def fetch(sources, targets, sems):
    copies = [
        pltpu.make_async_copy(source, target, sems.at[q])
        for q, (source, target) in enumerate(zip(sources, targets))
    ]
    for copy in copies:
        copy.start()
    return copies


def loop(count, body):
    if count <= 8:
        for q in range(count):
            body(q)
    else:

        def step(q, carry):
            body(q)
            return carry

        lax.fori_loop(0, count, step, 0)


def own_chunk(sz, lane, ref, rows):
    parts = []
    if sz.main:
        parts.append(ref[rows, pl.ds(pl.multiple_of(lane * sz.main, 128), sz.main)])
    start = sz.rest * lane
    lanes = lane_iota(8)
    rest = jnp.zeros((8, 128), F32)
    for tile in range(sz.rest_tiles):
        offset = sz.main * sz.lanes + 128 * tile
        block = ref[rows, offset : min(offset + 128, ref.shape[-1])]
        if block.shape[1] < 128:
            block = jnp.concatenate([block, jnp.zeros((8, 128 - block.shape[1]), F32)], axis=1)
        inside = (lanes + 128 * tile >= start) & (lanes + 128 * tile < start + sz.rest)
        rest = rest + jnp.where(inside, block, 0.0)
    rest = pltpu.roll(rest, lax.rem(128 * sz.rest_tiles - start, 128), 1)
    parts.append(rest)
    return jnp.concatenate(parts, axis=1) if len(parts) > 1 else parts[0]


def send_ghosts(sz, send, chunks, out, tasks):
    lanes = lane_iota(1)

    def one(d):
        for g in range(sz.group):
            cell = send[0, d * sz.group + g]
            rows = []
            last = tasks
            for i in range(3):
                row = chunks[pl.ds(i * sz.rows + cell, 1), :]
                rows.append(row[:, :128] if sz.main else jnp.zeros((1, 128), F32))
                piece = jnp.where(lanes < sz.rest, row[:, sz.main : sz.main + 128], 0.0)
                last = last + (pltpu.roll(piece, i * sz.rest, 1) if i else piece)
            rows.append(last)
            for other in range(sz.lanes):
                first = ((d * sz.lanes + other) * sz.group + g) * 4
                for q, row in enumerate(rows):
                    out[pl.ds(first + q, 1), :] = row

    loop(sz.owners, one)


def pick_kernel(sz, *refs):
    inputs, (out, send_out), held, (chunks, sems) = refs[:5], refs[5:7], refs[7:12], refs[12:]
    for copy in fetch(inputs, held, sems):
        copy.wait()
    send, target, source, count, positions = held
    for j in range(send_out.shape[1]):
        send_out[0, j] = send[0, j]
    lane = lax.axis_index("lane")
    for i in range(3):
        for g in range(0, sz.cells, 8):
            value = own_chunk(sz, lane, positions.at[i], pl.ds(g, 8))
            chunks[pl.ds(i * sz.rows + g, 8), :] = value
    spare = jnp.zeros((1, 128 - sz.cap), F32)
    tasks = jnp.where(lane_iota(1) == 3 * sz.rest + 2 * sz.cap, count[0].astype(F32), 0.0)
    for q, row in enumerate((target, source)):
        wide = jnp.concatenate([row[...].astype(F32), spare], axis=1)
        tasks = tasks + pltpu.roll(wide, 3 * sz.rest + q * sz.cap, 1)
    send_ghosts(sz, send, chunks, out, tasks)


def take_ghosts(sz, arrived, pool, stride, base):
    lanes = lane_iota(1)

    def one(d):
        for g in range(sz.group):
            first = [((d * sz.lanes + lane) * sz.group + g) * 4 for lane in range(sz.lanes)]
            last = [arrived[pl.ds(row + 3, 1), :] for row in first]
            for i in range(3):
                tiles = []
                if sz.main:
                    tiles += [arrived[pl.ds(row + i, 1), :] for row in first]
                for tile in range(sz.rest_tiles):
                    total = jnp.zeros((1, 128), F32)
                    for lane in range(sz.lanes):
                        start = sz.rest * lane
                        if start + sz.rest <= 128 * tile or start >= 128 * tile + 128:
                            continue
                        shift = (start - i * sz.rest) % 128
                        value = pltpu.roll(last[lane], shift, 1) if shift else last[lane]
                        at = lanes + 128 * tile
                        total = jnp.where((at >= start) & (at < start + sz.rest), value, total)
                    tiles.append(total)
                place = pl.ds(i * stride + base + d * sz.group + g, 1)
                pool[place, :] = jnp.concatenate(tiles, axis=1)

    loop(sz.owners, one)


def build_list(sz, lists, tasks):
    total = jnp.int32(0)
    for lane in range(sz.lanes):
        count = lists[lane, 2 * sz.cap]
        for j in range(sz.cap):
            tasks[0, total] = lists[lane, j]
            tasks[1, total] = lists[lane, sz.cap + j]
            total = total + (j < count).astype(jnp.int32)
    for u in range(UNROLL):
        tasks[0, total + u] = jnp.int32(sz.cells)
        tasks[1, total + u] = jnp.int32(0)
    tasks[2, 0] = total
    return total


def own_list(sz, lane, tasks, mine, low, high):
    first = lane * sz.share
    total = tasks[2, 0]
    count = jnp.int32(0)
    for t in range(sz.lanes * sz.cap):
        target = tasks[0, t] - first
        source = tasks[1, t]
        mine[0, count] = target
        mine[1, count] = source - low
        taken = (target >= 0) & (target < sz.share) & (t < total)
        taken = taken & (source >= low) & (source < high)
        count = count + taken.astype(jnp.int32)
    for u in range(PAIR):
        mine[0, count + u] = jnp.int32(-1)
        mine[1, count + u] = jnp.int32(0)
    return count


def products(value, bend_high, bend_low):
    high, low = split2(value)
    dot = functools.partial(jnp.dot, preferred_element_type=F32)
    return dot(high, bend_high) + dot(low, bend_high) + dot(high, bend_low)


def make_sources(sz, value, bend_high, bend_low, source_rows, centres, first):
    count = value.shape[0] // 3
    forces = products(value[:, : sz.points], bend_high, bend_low)
    forces = jnp.concatenate(
        [forces, jnp.zeros((3 * count, sz.width - sz.points), F32)], axis=1
    )
    middle = jnp.sum(value, axis=1, keepdims=True) / sz.points
    for g in range(count // 8):
        where = [i * count + 8 * g for i in range(3)]
        middles = [jnp.broadcast_to(middle[w : w + 8], (8, 128)) for w in where]
        middles += [jnp.zeros((8, 128), F32)] * 5
        for i, row in enumerate(middles):
            centres[pl.ds(8 * (first + 8 * g) + i, 8, stride=8), :] = row
        for j in range(sz.tiles):
            cut = slice(128 * j, 128 * j + 128)
            y = [value[w : w + 8, cut] - m for w, m in zip(where, middles)]
            f = [forces[w : w + 8, cut] for w in where]
            norm = y[0] * y[0] + y[1] * y[1] + y[2] * y[2] + REGULARIZE
            along = y[0] * f[0] + y[1] * f[1] + y[2] * f[2]
            one, zero = jnp.ones((8, 128), F32), jnp.zeros((8, 128), F32)
            rows = [y[0], y[1], y[2], norm, one, zero, zero, zero]
            rows += f
            rows += [y[i] * f[k] for i in range(3) for k in range(3)]
            rows += [norm * f[i] + along * y[i] for i in range(3)]
            rows += [along]
            for k, row in enumerate(rows):
                place = pl.ds(SOURCE_ROWS * (first + 8 * g) + k, 8, stride=SOURCE_ROWS)
                source_rows.at[j][place, :] = row


def make_targets(sz, blocks, targets):
    targets[...] = jnp.zeros_like(targets)
    for i in range(3):
        for g in range(blocks[i].shape[0] // 8):
            block = blocks[i][8 * g : 8 * g + 8]
            for j in range(targets.shape[0]):
                cut = slice(128 * j, 128 * j + 128)
                targets.at[j][pl.ds(64 * g + i, 8, stride=8), :] = block[:, cut]


def source_operands(sz, source, source_rows):
    held = [
        source_rows[j, pl.ds(pl.multiple_of(SOURCE_ROWS * source, 8), SOURCE_ROWS), :]
        for j in range(sz.tiles)
    ]
    held = jnp.concatenate(held, axis=1)
    y1, y2, y3 = split3(held[:8])
    y_stack = jnp.concatenate([y1, y1, y2, y2, y1, y3], axis=0).astype(BF16)
    return y_stack, jnp.concatenate(split3(held[8:]), axis=0)


def pieces(points, step):
    starts = list(range(0, max(points // 128 * 128, 1), step))
    return list(zip(starts, starts[1:] + [points]))


def twice(piece, count):
    whole = count // 128 * 128
    parts = [piece[:, :whole].astype(BF16)] * 2 if whole else []
    if whole < count:
        last = piece[:, whole:]
        last = last + pltpu.roll(last, count - whole, 1)
        parts.append(last.astype(BF16)[:, : 2 * (count - whole)])
    return jnp.concatenate(parts, axis=1)


def load_target(j, target, slot, centre, targets, offsets):
    row = lax.broadcasted_iota(jnp.int32, (8, 128), 0)
    x = targets[j, pl.ds(pl.multiple_of(8 * target, 8), 8), :] - centre
    square = x * x
    norm = pltpu.roll(square, 2, 0) + pltpu.roll(square, 3, 0) + pltpu.roll(square, 4, 0)
    side = jnp.where(row == 4, norm, jnp.where(row == 3, 1.0, 0.0))
    x_side = jnp.where(row < 3, -2.0 * x, side)
    x1, x2, x3 = split3(x_side)
    return x, jnp.concatenate([x1, x2, x1, x2, x3, x1], axis=0).astype(BF16)


def distances(one_stack, other_stack):
    return jnp.dot(one_stack, other_stack, preferred_element_type=F32)


def weights(shifted):
    inverse = lax.rsqrt(shifted)
    return split2(inverse * inverse * inverse)


def fold(result):
    return result[:SUM_ROWS] + result[SUM_ROWS : 2 * SUM_ROWS] + result[2 * SUM_ROWS :]


def skewed(stages, skew):
    asked = []
    for q, (ask, _) in enumerate(stages):
        asked.append(ask())
        if q >= skew:
            stages[q - skew][1](asked[q - skew])
            asked[q - skew] = None
    for q in range(max(len(stages) - skew, 0), len(stages)):
        stages[q][1](asked[q])


def adder(totals, key):
    def add(value):
        totals[key] = totals[key] + value if key in totals else value

    return add


def wide_piece(operands, begin, first, end, add):
    def ask():
        _, y_turned, _, blocks = operands()
        return distances(y_turned[first:end], blocks[begin])

    def take(shifted):
        m_piece = operands()[2][first]
        high, low = weights(shifted)
        whole = (end - first) // 128 * 128
        parts = [high[:whole], low[:whole]] if whole else []
        parts += [high[whole:], low[whole:]] if whole < end - first else []
        stack = jnp.concatenate(parts, axis=0)
        add(jnp.dot(m_piece, stack, preferred_element_type=F32))

    return ask, take


def rest_piece(operands, begin, add):
    def ask():
        y_stack, _, _, blocks = operands()
        return distances(blocks[begin], y_stack)

    def take(shifted):
        stack = jnp.concatenate(weights(shifted), axis=1)
        m_whole = jnp.concatenate([operands()[2][-1]] * 2, axis=1)
        turned = (((1,), (1,)), ((), ()))
        add(lax.dot_general(m_whole, stack, turned, preferred_element_type=F32))

    return ask, take


def store_sums(slots, slot, j, x, result, offsets, sums):
    offsets.at[j][pl.ds(slot, 8, stride=slots), :] = x
    for h in range(0, SUM_ROWS, 8):
        sums.at[j][pl.ds(h * slots + slot, 8, stride=slots), :] = result[h : h + 8]


def mark(slot, target, hot):
    hot[pl.ds(slot, 1), :] = jnp.where(lane_iota(1) == target, 1.0, 0.0)


def combine(sz, slots, first, total, offsets, sums, speeds):
    live = lax.broadcasted_iota(jnp.int32, (8, 128), 0) + first < total
    for j in range(offsets.shape[0]):
        x = [offsets[j, pl.ds(i * slots + first, 8), :] for i in range(3)]
        s = [sums[j, pl.ds(k * slots + first, 8), :] for k in range(SUM_ROWS)]
        a, b, c = s[:3], [s[3:6], s[6:9], s[9:12]], s[12:15]
        norm = x[0] * x[0] + x[1] * x[1] + x[2] * x[2] + REGULARIZE
        along = x[0] * a[0] + x[1] * a[1] + x[2] * a[2] - s[15]
        for i in range(3):
            speed = norm * a[i] + c[i] + along * x[i]
            for k in range(3):
                speed = speed - x[k] * (2.0 * b[k][i] + b[i][k])
            speed = jnp.where(live, speed / sz.points, 0.0)
            speeds[i, pl.ds(first, 8), 128 * j : 128 * j + 128] = speed


def add_up(sz, slots, total, rows, offsets, sums, speeds, hot):
    def eight(q, carry):
        combine(sz, slots, pl.multiple_of(8 * q, 8), total, offsets, sums, speeds)
        return carry

    if slots <= 64 and offsets.shape[0] <= 2:
        for q in range(slots // 8):
            combine(sz, slots, 8 * q, total, offsets, sums, speeds)
    else:
        lax.fori_loop(0, lax.div(total + 7, 8), eight, 0)
    one_hot = hot[...].astype(BF16)
    result = []
    for i in range(3):
        first, second, third = split3(speeds[i])
        parts = [
            lax.dot_general(
                one_hot, part.astype(BF16), (((0,), (0,)), ((), ())), preferred_element_type=F32
            )
            for part in (first, second, third)
        ]
        result.append((parts[0] + parts[1] + parts[2])[:rows])
    return result


def several_tasks(sz, slots, picks, marks, main, rest, wide, step, skew, refs):
    source_rows, centres, targets, offsets, sums, hot = refs

    def task(slot, pick, target_mark):
        target, source = pick
        made, parts, points = [], {}, []

        def operands():
            if made:
                return made[0]
            y_stack, m_stack = source_operands(sz, source, source_rows)
            centre = centres[pl.ds(pl.multiple_of(8 * source, 8), 8), :]
            points.extend(
                load_target(j, target, slot, centre, targets, offsets)
                for j in range(targets.shape[0])
            )
            blocks = {}
            for begin in range(0, main, wide):
                stack = [stack for _, stack in points[begin // 128 : (begin + wide) // 128]]
                blocks[begin] = jnp.concatenate(stack, axis=1)
            if rest:
                blocks[main] = jnp.transpose(points[main // 128][1])[:rest]
            sides = {-1: m_stack.astype(BF16)}
            if main:
                for first, last in pieces(sz.points, step):
                    sides[first] = twice(m_stack[:, first : up(last, 128)], last - first)
            made.append((y_stack, jnp.transpose(y_stack), sides, blocks))
            return made[0]

        def finish():
            results = [fold(parts[begin]) for begin in range(0, main, wide)]
            if rest:
                spare = jnp.zeros((SUM_ROWS, 128 - rest), F32)
                results.append(jnp.concatenate([fold(parts[main]), spare], axis=1))
            result = jnp.concatenate(results, axis=1)
            for j in range(targets.shape[0]):
                cut = result[:, 128 * j : 128 * j + 128]
                store_sums(hot.shape[0], slot, j, points[j][0], cut, offsets, sums)
            mark(slot, target_mark, hot)

        own = []
        for begin in range(0, main, wide):
            for first, last in pieces(sz.points, step):
                own.append(wide_piece(operands, begin, first, last, adder(parts, begin)))
        if rest:
            own.insert(len(own) // 2, rest_piece(operands, main, adder(parts, main)))
        ask, take = own[-1]

        def last_take(shifted):
            take(shifted)
            finish()

        own[-1] = (ask, last_take)
        return own, operands

    made = [task(slot, pick, m) for slot, pick, m in zip(slots, picks, marks)]
    for (own, _), (_, after) in zip(made, made[1:]):
        ask, take = own[0]

        def ask_and_prepare(ask=ask, after=after):
            shifted = ask()
            after()
            return shifted

        own[0] = (ask_and_prepare, take)
    skewed([stage for own, _ in made for stage in own], skew)


def tiles_of_chunk(sz, total, tasks, *refs):
    def several(q, carry):
        slots = [q * UNROLL + u for u in range(UNROLL)]
        picks = [(tasks[0, slot], tasks[1, slot]) for slot in slots]
        marks = [target for target, _ in picks]
        several_tasks(sz, slots, picks, marks, sz.main, sz.rest, 128, 256, 9, refs)
        return carry

    lax.fori_loop(0, lax.div(total + UNROLL - 1, UNROLL), several, 0)


def tiles_of_cells(sz, total, mine, *refs):
    main = 256 * (sz.points // 256)

    def several(q, carry):
        slots = [q * PAIR + u for u in range(PAIR)]
        marks = [mine[0, slot] for slot in slots]
        picks = [(jnp.maximum(mark, 0), mine[1, slot]) for mark, slot in zip(marks, slots)]
        several_tasks(sz, slots, picks, marks, main, sz.points - main, 256, 256, 3, refs)
        return carry

    lax.fori_loop(0, lax.div(total + PAIR - 1, PAIR), several, 0)


def packed(sz, blocks):
    rows = [b[:, : sz.main] for b in blocks] if sz.main else []
    lanes = lane_iota(8)
    for p in range(0, len(blocks), sz.per_pack):
        total = jnp.zeros((8, 128), F32)
        for q, block in enumerate(blocks[p : p + sz.per_pack]):
            rest = jnp.where(lanes < sz.rest, block[:, sz.main : sz.main + 128], 0.0)
            total = total + (pltpu.roll(rest, q * sz.rest, 1) if q else rest)
        rows.append(total)
    return rows


def store_packed(sz, out, blocks):
    first = 0
    count = len(blocks)
    values = packed(sz, blocks)
    if sz.main:
        for b in range(count):
            for m in range(sz.main // 128):
                out[pl.ds(first, 8), :] = values[b][:, 128 * m : 128 * m + 128]
                first += 8
        values = values[count:]
    for value in values:
        out[pl.ds(first, 8), :] = value
        first += 8


def place_packed(sz, lane, arrived, count, store_main, add_rest):
    first = 0
    if sz.main:
        for b in range(count):
            for m in range(sz.main // 128):
                store_main(b, m, arrived[pl.ds(first, 8), :])
                first += 8
    start = sz.rest * lane
    lanes = lane_iota(8)
    for b in range(count):
        pack, q = divmod(b, sz.per_pack)
        value = arrived[pl.ds(first + 8 * pack, 8), :]
        value = pltpu.roll(value, lax.rem(start - q * sz.rest + 128, 128), 1)
        for tile in range(sz.rest_tiles):
            inside = (lanes + 128 * tile >= start) & (lanes + 128 * tile < start + sz.rest)
            add_rest(b, tile, jnp.where(inside, value, 0.0))


def source_kernel(sz, *refs):
    inputs, (high_out, low_out, source_rows, centres), held, sems = (
        refs[:2],
        refs[2:6],
        refs[6:8],
        refs[8],
    )
    for copy in fetch(inputs, held, sems):
        copy.wait()
    positions, bend = held
    high_out[...], low_out[...] = split2(bend[...])
    value = jnp.concatenate([positions[i] for i in range(3)], axis=0)
    value = jnp.concatenate(
        [value, jnp.zeros((3 * sz.cells, sz.width - sz.points), F32)], axis=1
    )
    make_sources(sz, value, high_out[...], low_out[...], source_rows, centres, 0)


def first_kernel(sz, *refs):
    arrived, high, low, inputs = refs[0], refs[1], refs[2], refs[3:7]
    outputs, refs = refs[7:10], refs[10:]
    source_rows, centres, targets, offsets, sums, speeds, hot, moved, pool = refs[:9]
    send, positions, staged, lists, chunk_out, ghost_out, tasks, sems = refs[9:]
    me, lane = lax.axis_index("space"), lax.axis_index("lane")
    own_rows = source_rows.at[:, pl.ds(0, SOURCE_ROWS * sz.cells)]
    own_centres = centres.at[pl.ds(0, 8 * sz.cells)]
    copies = fetch(inputs, [send, positions, own_rows, own_centres], sems)
    count = 4 * sz.lanes * sz.group
    slots = arrived[pl.ds(pl.multiple_of(me * count, 8), count), :]
    for other in range(sz.lanes):
        row = 4 * other * sz.group + 3
        value = pltpu.roll(slots[row : row + 1], 128 - 3 * sz.rest, 1)
        staged[pl.ds(other, 1), :] = value.astype(jnp.int32)
    copies += fetch([staged], [lists], sems.at[pl.ds(4, 1)])
    pool[...] = jnp.zeros_like(pool)
    take_ghosts(sz, arrived, pool, up(sz.owners * sz.group, 8), 0)
    hot[...] = jnp.zeros_like(hot)
    speeds[...] = jnp.zeros_like(speeds)
    make_sources(sz, pool[...], high[...], low[...], source_rows, centres, sz.cells)
    for copy in copies[:2]:
        copy.wait()
    chunks = [
        [own_chunk(sz, lane, positions.at[i], pl.ds(g, 8)) for g in range(0, sz.cells, 8)]
        for i in range(3)
    ]
    make_targets(sz, [jnp.concatenate(blocks, axis=0) for blocks in chunks], targets)
    copies[4].wait()
    total = build_list(sz, lists, tasks)
    for copy in copies[2:4]:
        copy.wait()
    copies = fetch([tasks], outputs[2:], sems)
    tiles_of_chunk(sz, total, tasks, source_rows, centres, targets, offsets, sums, hot)
    velocity = add_up(sz, sz.slots, total, sz.cells, offsets, sums, speeds, hot)
    blocks = []
    for i in range(3):
        for g in range(0, sz.cells, 8):
            chunk = own_chunk(sz, lane, positions.at[i], pl.ds(g, 8))
            block = chunk + TIME_STEP * velocity[i][g : g + 8]
            moved[pl.ds(i * sz.rows + g, 8), :] = block
            blocks.append(block)
    store_packed(sz, chunk_out, blocks)
    copies += fetch([chunk_out], outputs[:1], sems.at[pl.ds(1, 1)])
    send_ghosts(sz, send, moved, ghost_out, jnp.zeros((1, 128), F32))
    copies += fetch([ghost_out], outputs[1:2], sems.at[pl.ds(2, 1)])
    for copy in copies:
        copy.wait()


def own_kernel(sz, *refs):
    (high, low), refs = refs[:2], refs[2:]
    others, refs = refs[: sz.lanes - 1], refs[sz.lanes - 1 :]
    inputs, (speed_out, share_out), refs = refs[:2], refs[2:4], refs[4:]
    source_rows, centres, targets, offsets, sums, speeds, hot, pool, mine = refs[:9]
    tasks, chunk, sems = refs[9:]
    copies = fetch(inputs, [tasks, chunk], sems)
    chunks = [chunk, *others]
    hot[...] = jnp.zeros_like(hot)
    speeds[...] = jnp.zeros_like(speeds)
    lane = lax.axis_index("lane")
    pool[...] = jnp.zeros_like(pool)
    copies[0].wait()
    total = own_list(sz, lane, tasks, mine, 0, sz.cells)
    copies[1].wait()
    per = sz.cells // 8
    for k in range(sz.lanes):
        other = lane ^ k

        def row_of(b):
            return (b // per) * sz.cells + 8 * (b % per)

        def store_main(b, m, value):
            cut = pl.ds(pl.multiple_of(other * sz.main + 128 * m, 128), 128)
            pool[pl.ds(row_of(b), 8), cut] = value

        def add_rest(b, tile, value):
            offset = sz.main * sz.lanes + 128 * tile
            cut = (pl.ds(row_of(b), 8), slice(offset, offset + 128))
            pool[cut] = pool[cut] + value

        place_packed(sz, other, chunks[k], 3 * per, store_main, add_rest)
    for i in range(3):
        share_out[i] = share_rows(sz, pool, i * sz.cells, lane)
    make_sources(sz, pool[...], high[...], low[...], source_rows, centres, 0)
    make_targets(sz, share_out, targets)
    tiles_of_cells(sz, total, mine, source_rows, centres, targets, offsets, sums, hot)
    velocity = add_up(sz, sz.own, total, up(sz.share, 8), offsets, sums, speeds, hot)
    for i in range(3):
        speed_out[i] = velocity[i]


def ghost_kernel(sz, *refs):
    arrived, high, low, speed_in, share, tasks_in = refs[:6]
    moved_out, velocity_out = refs[6:8]
    source_rows, centres, targets, offsets, sums, speeds, hot, pool, mine = refs[8:17]
    tasks, sems = refs[17:]
    copies = fetch([tasks_in], [tasks], sems)
    hot[...] = jnp.zeros_like(hot)
    speeds[...] = jnp.zeros_like(speeds)
    lane = lax.axis_index("lane")
    pool[...] = jnp.zeros_like(pool)
    ghosts = up(sz.owners * sz.group, 8)
    take_ghosts(sz, arrived, pool, ghosts, 0)
    make_sources(sz, pool[...], high[...], low[...], source_rows, centres, 0)
    make_targets(sz, share, targets)
    copies[0].wait()
    total = own_list(sz, lane, tasks, mine, sz.cells, sz.cells + sz.owners * sz.group)
    tiles_of_cells(sz, total, mine, source_rows, centres, targets, offsets, sums, hot)
    velocity = add_up(sz, sz.own, total, up(sz.share, 8), offsets, sums, speeds, hot)
    for i in range(3):
        speed = velocity[i] + speed_in[i]
        velocity_out[i] = speed[: sz.share, : sz.points]
        moved_out[i] = (share[i] + TIME_STEP * speed)[: sz.share, : sz.points]


def share_rows(sz, ref, base, lane):
    if sz.share % 8 == 0:
        return ref[pl.ds(pl.multiple_of(base + lane * sz.share, 8), sz.share), :]
    rows = [ref[pl.ds(base + lane * sz.share + c, 1), :] for c in range(sz.share)]
    rows.append(jnp.zeros((8 - sz.share, rows[0].shape[1]), F32))
    return jnp.concatenate(rows, axis=0)


def scratch(sz, cells, targets, tiles, slots):
    return [
        pltpu.VMEM((sz.tiles, SOURCE_ROWS * cells, 128), F32),
        pltpu.VMEM((8 * cells, 128), F32),
        pltpu.VMEM((tiles, 8 * targets, 128), F32),
        pltpu.VMEM((tiles, 9 * slots, 128), F32),
        pltpu.VMEM((tiles, (SUM_ROWS + 1) * slots, 128), F32),
        pltpu.VMEM((3, slots, 128 * tiles), F32),
        pltpu.VMEM((slots, 128), F32),
    ]


def swap(value, axis, size, k):
    return lax.ppermute(value, axis, [(d, d ^ k) for d in range(size)])


def in_hbm(value):
    return pltpu.with_memory_space_constraint(value, pltpu.HBM)


def shards(positions, bend_op, send_list, task_target, task_source, task_count):
    owners, lanes = lax.axis_size("space"), lax.axis_size("lane")
    cells, points = positions.shape[0], positions.shape[2]
    sz = sizes(owners, lanes, cells, points, task_target.shape[1], send_list.shape[1])
    params = pltpu.CompilerParams(vmem_limit_bytes=min(6 * lanes, 40) << 20)
    shape = jax.ShapeDtypeStruct
    both = ("space", "lane")
    by_component = jnp.transpose(positions, (1, 0, 2))
    list_rows = up(lanes, 8)
    slot_shape = shape((4 * sz.group * owners * lanes, 128), F32)
    leaving, send = pl.pallas_call(
        functools.partial(pick_kernel, sz),
        out_shape=[slot_shape, shape(send_list.shape, jnp.int32)],
        in_specs=[HBM] * 5,
        out_specs=[VMEM, SMEM],
        scratch_shapes=[
            pltpu.SMEM(send_list.shape, jnp.int32),
            pltpu.VMEM(task_target.shape, jnp.int32),
            pltpu.VMEM(task_source.shape, jnp.int32),
            pltpu.SMEM(task_count.shape, jnp.int32),
            pltpu.VMEM(by_component.shape, F32),
            pltpu.VMEM((3 * sz.rows, sz.chunk_wide), F32),
            pltpu.SemaphoreType.DMA((5,)),
        ],
        compiler_params=pltpu.CompilerParams(vmem_limit_bytes=60 << 20),
        name="pick_cells",
    )(send_list, task_target, task_source, task_count, by_component)
    arrived = lax.all_to_all(leaving, both, split_axis=0, concat_axis=0, tiled=True)
    high, low, own_rows, own_centres = pl.pallas_call(
        functools.partial(source_kernel, sz),
        out_shape=[
            shape(bend_op.shape, BF16),
            shape(bend_op.shape, BF16),
            shape((sz.tiles, SOURCE_ROWS * cells, 128), F32),
            shape((8 * cells, 128), F32),
        ],
        in_specs=[HBM] * 2,
        out_specs=[VMEM] * 4,
        scratch_shapes=[
            pltpu.VMEM(by_component.shape, F32),
            pltpu.VMEM(bend_op.shape, F32),
            pltpu.SemaphoreType.DMA((2,)),
        ],
        compiler_params=params,
        cost_estimate=pl.CostEstimate(flops=10**9, bytes_accessed=10**7, transcendentals=0),
        name="first_sources",
    )(in_hbm(by_component), in_hbm(bend_op))
    chunk_shape = (pack_rows(sz, cells), 128)
    chunk, leaving, tasks = pl.pallas_call(
        functools.partial(first_kernel, sz),
        out_shape=[
            pltpu.HBM(chunk_shape, F32),
            pltpu.HBM(slot_shape.shape, F32),
            pltpu.HBM((3, sz.slots), jnp.int32),
        ],
        in_specs=[VMEM] * 3 + [HBM] * 2 + [ANY] * 2,
        out_specs=[HBM] * 3,
        scratch_shapes=scratch(sz, sz.pool, sz.rows, sz.chunk_tiles, sz.slots)
        + [
            pltpu.VMEM((3 * sz.rows, sz.chunk_wide), F32),
            pltpu.VMEM((3 * up(sz.owners * sz.group, 8), sz.width), F32),
            pltpu.SMEM(send_list.shape, jnp.int32),
            pltpu.VMEM(by_component.shape, F32),
            pltpu.VMEM((list_rows, 128), jnp.int32),
            pltpu.SMEM((list_rows, 128), jnp.int32),
            pltpu.VMEM(chunk_shape, F32),
            pltpu.VMEM(slot_shape.shape, F32),
            pltpu.SMEM((3, sz.slots), jnp.int32),
            pltpu.SemaphoreType.DMA((5,)),
        ],
        compiler_params=params,
        name="first_step",
    )(arrived, high, low, in_hbm(send), in_hbm(by_component), own_rows, own_centres)
    arrived = lax.all_to_all(leaving, both, split_axis=0, concat_axis=0, tiled=True)
    chunks = [swap(chunk, "lane", lanes, k) for k in range(1, lanes)]
    share = up(sz.share, 8)
    so_far = shape((3, share, sz.width), F32)
    speed, moved = pl.pallas_call(
        functools.partial(own_kernel, sz),
        out_shape=[so_far, so_far],
        in_specs=[VMEM] * (lanes + 1) + [HBM] * 2,
        out_specs=[VMEM] * 2,
        scratch_shapes=scratch(sz, cells, share, sz.tiles, sz.own)
        + [
            pltpu.VMEM((3 * cells, sz.width), F32),
            pltpu.SMEM((2, sz.own + 8), jnp.int32),
            pltpu.SMEM(tasks.shape, jnp.int32),
            pltpu.VMEM(chunk.shape, F32),
            pltpu.SemaphoreType.DMA((2,)),
        ],
        compiler_params=params,
        cost_estimate=pl.CostEstimate(flops=10**9, bytes_accessed=10**7, transcendentals=0),
        name="second_own",
    )(high, low, *chunks, in_hbm(tasks), in_hbm(chunk))
    result = shape((3, sz.share, points), F32)
    ghosts = up(owners * sz.group, 8)
    outputs = pl.pallas_call(
        functools.partial(ghost_kernel, sz),
        out_shape=[result, result],
        in_specs=[VMEM] * 5 + [HBM],
        out_specs=[VMEM] * 2,
        scratch_shapes=scratch(sz, ghosts, share, sz.tiles, sz.own)
        + [
            pltpu.VMEM((3 * ghosts, sz.width), F32),
            pltpu.SMEM((2, sz.own + 8), jnp.int32),
            pltpu.SMEM(tasks.shape, jnp.int32),
            pltpu.SemaphoreType.DMA((1,)),
        ],
        compiler_params=params,
        name="second_ghosts",
    )(arrived, high, low, speed, moved, in_hbm(tasks))
    return tuple(jnp.transpose(output, (1, 0, 2)) for output in outputs)


def solution(mesh):
    in_specs = (
        P("space", None, None),
        P(),
        P("space", None),
        P(("space", "lane"), None),
        P(("space", "lane"), None),
        P(("space", "lane")),
    )
    out_specs = (P(("space", "lane"), None, None), P(("space", "lane"), None, None))
    return jax.shard_map(shards, mesh=mesh, in_specs=in_specs, out_specs=out_specs, check_vma=False)
```
